32 devices in a mesh: slab: 4 (over y, core), seq: 8 (over z, x).
Axes of the slice: x: 2, y: 2, z: 4, core: 2. Of those that a mesh axis runs over, the one named last changes fastest.
Arguments:
- query: bfloat16 [8192, 3072], P(('slab', 'seq')), may hold values from -9 to 9
- key: bfloat16 [8192, 3072], P(('slab', 'seq')), may hold values from -9 to 9
- value: bfloat16 [8192, 3072], P(('slab', 'seq')), may hold values from -6 to 6
- d_out: bfloat16 [8192, 3072], P(('slab', 'seq')), may hold values from -6 to 6
- pattern: int32 [48, 64, 8], P('seq', 'slab'), may hold values from 0 to 63, as said below
Outputs:
- attended: bfloat16 [8192, 3072], P(('slab', 'seq'))
- grad_query: bfloat16 [8192, 3072], P(('slab', 'seq'))
- grad_key: bfloat16 [8192, 3072], P(('slab', 'seq'))
- grad_value: bfloat16 [8192, 3072], P(('slab', 'seq'))
The draws below stay inside these ranges and needn't reach their ends.
Inputs may be any that keep to these rules, and one draw needn't show every extreme that they name: Every list pattern[h, b] holds 8 distinct blocks: first b itself, then blocks of b's own slab, and blocks of the adjacent slabs only (slab of block k is k // 16). A list of a slab with two neighbours holds 2 blocks of each; a list of the first or the last slab holds 2 blocks of its one neighbour. For each slab and each adjacent slab, the lists of every head together reference exactly 4 blocks of that adjacent slab, the same set for all heads.
All inputs are finite; a program needn't handle non-finite values.
Results may differ from the reference program's by a relative error of at most 0.0081.
Values may be sent and summed in bfloat16 or wider, within the bound.
No kernel may reach another device: no remote copies, remote signals or barrier semaphores. Data moves between devices by JAX's collectives and lax.ppermute only.
A program may use at most 128 MiB of HBM per device.

```python
import jax
import jax.numpy as jnp
from jax import lax

HEADS = 48
HDIM = 64
BLOCK = 128
KSEL = 8
CROSS = 4
D = 3072
SLAB_BLOCKS = 16
QBLOCKS = 64
TOKENS = 8192
N_SLAB = 4


def draw_query(key, part):
    values = jnp.clip(jax.random.normal(jax.random.fold_in(key, 1), (TOKENS, HEADS * HDIM), jnp.float32), -6.0, 6.0)
    return values.astype(jnp.bfloat16)


def draw_key(key, part):
    values = jnp.clip(jax.random.normal(jax.random.fold_in(key, 3), (TOKENS, HEADS * HDIM), jnp.float32), -6.0, 6.0)
    return values.astype(jnp.bfloat16)


def cross_sets(key):
    scores = jax.random.randint(key, (N_SLAB, SLAB_BLOCKS), 0, 65536, jnp.int32) * SLAB_BLOCKS
    scores = scores + jnp.arange(SLAB_BLOCKS, dtype=jnp.int32)[None, :]
    return lax.top_k(scores, CROSS)[1].astype(jnp.int32)


def neighbour_picks(key, salt, slab_ids, inside, shift_slab):
    sets = cross_sets(jax.random.fold_in(key, salt))
    offsets = jax.random.randint(jax.random.fold_in(key, salt + 10), (HEADS, N_SLAB), 0, CROSS, jnp.int32)
    half = CROSS // 2
    step_ids = jnp.arange(half, dtype=jnp.int32)
    positions = (offsets[:, slab_ids][:, :, None] + inside[None, :, None] + step_ids[None, None, :]) % CROSS
    per_block = jnp.broadcast_to(sets[slab_ids][None, :, :], (HEADS, QBLOCKS, CROSS))
    picked = jnp.take_along_axis(per_block, positions, axis=-1)
    return picked + ((slab_ids + shift_slab) * SLAB_BLOCKS)[None, :, None]


def draw_pattern(key, part):
    half = CROSS // 2
    locals_count = KSEL - 1 - CROSS
    block_ids = jnp.arange(QBLOCKS, dtype=jnp.int32)
    slab_ids = block_ids // SLAB_BLOCKS
    inside = block_ids % SLAB_BLOCKS
    below = neighbour_picks(key, 21, slab_ids, inside, -1)
    above = neighbour_picks(key, 22, slab_ids, inside, 1)
    nearby = jnp.arange(SLAB_BLOCKS, dtype=jnp.int32)
    scores = jax.random.randint(jax.random.fold_in(key, 24), (HEADS, QBLOCKS, SLAB_BLOCKS), 0, 65536, jnp.int32) * SLAB_BLOCKS
    scores = scores + nearby[None, None, :]
    scores = jnp.where((nearby[None, :] == inside[:, None])[None, :, :], -1, scores)
    own_picks = lax.top_k(scores, locals_count + half)[1].astype(jnp.int32) + (slab_ids * SLAB_BLOCKS)[None, :, None]
    first = own_picks[:, :, :locals_count]
    extra = own_picks[:, :, locals_count:]
    low_part = jnp.where((slab_ids == 0)[None, :, None], extra, below)
    high_part = jnp.where((slab_ids == N_SLAB - 1)[None, :, None], extra, above)
    own_block = jnp.broadcast_to(block_ids[None, :, None], (HEADS, QBLOCKS, 1))
    return jnp.concatenate([own_block, first, low_part, high_part], axis=-1).astype(jnp.int32)


def block_levels(stream_key, dims, shards, smallest, top_value):
    def one(dim, parts):
        steps = jax.random.uniform(jax.random.fold_in(jax.random.fold_in(stream_key, 6), dim), (parts,), jnp.float32, smallest / len(shards), top_value / len(shards))
        return jnp.repeat(jnp.exp(steps), dims[dim] // parts).reshape((-1,) + (1,) * (len(dims) - dim - 1))

    loudness = one(*shards[0])
    for cut in shards[1:]:
        loudness = loudness * one(*cut)
    return loudness


def scatter_about(stream_key, extent, width, limit, split=(), kind=jnp.bfloat16):
    result = jax.random.normal(stream_key, extent, jnp.float32) * width
    if len(split) > 0:
        result = block_levels(stream_key, extent, split, -0.22, 0.18) * result
    return jnp.clip(result, min=-limit, max=limit).astype(kind)


def setup_inputs(seed: int = 0) -> dict:
    keys = jax.random.split(jax.random.key(seed), 6)
    return {
        "query": draw_query(jax.random.fold_in(keys[5], 71), 0),
        "key": draw_key(jax.random.fold_in(keys[5], 71), 0),
        "value": scatter_about(keys[2], (TOKENS, D), 1.0, 6.0, ((0, 32),)),
        "d_out": scatter_about(keys[3], (TOKENS, D), 1.0, 6.0, ((0, 32),)),
        "pattern": draw_pattern(jax.random.fold_in(keys[5], 71), 0),
    }


def rounded(values):
    return lax.optimization_barrier(values.astype(jnp.bfloat16)).astype(jnp.float32)


def spread(contrib, lists, keep):
    masked = jnp.where(keep[:, :, None, None], contrib, jnp.zeros_like(contrib))
    flat_rows = masked.reshape(QBLOCKS * KSEL, BLOCK, HDIM)
    empty = jnp.zeros((QBLOCKS, BLOCK, HDIM), jnp.float32)
    return empty.at[lists.reshape(-1)].add(flat_rows)


def one_head(inputs):
    query_h, key_h, value_h, grad_h, lists = inputs
    scaling = HDIM ** -0.5
    query_f = query_h.astype(jnp.float32)
    key_f = key_h.astype(jnp.float32)
    value_f = value_h.astype(jnp.float32)
    grad_f = grad_h.astype(jnp.float32)
    key_sel = key_f[lists].reshape(QBLOCKS, KSEL * BLOCK, HDIM)
    value_sel = value_f[lists].reshape(QBLOCKS, KSEL * BLOCK, HDIM)
    scores = jnp.einsum("qid,qjd->qij", query_f, key_sel) * scaling
    row_max = jnp.max(scores, axis=-1, keepdims=True)
    weights = jnp.exp(scores - row_max)
    weights = weights / jnp.sum(weights, axis=-1, keepdims=True)
    weights_low = rounded(weights)
    attended = jnp.einsum("qij,qjd->qid", weights_low, value_sel).astype(jnp.bfloat16)
    grad_prob = jnp.einsum("qid,qjd->qij", grad_f, value_sel)
    correction = jnp.sum(weights * grad_prob, axis=-1, keepdims=True)
    grad_score = rounded(weights * (grad_prob - correction))
    grad_query = (jnp.einsum("qij,qjd->qid", grad_score, key_sel) * scaling).astype(jnp.bfloat16)
    key_terms = (jnp.einsum("qij,qid->qjd", grad_score, query_f) * scaling).reshape(QBLOCKS, KSEL, BLOCK, HDIM)
    value_terms = jnp.einsum("qij,qid->qjd", weights_low, grad_f).reshape(QBLOCKS, KSEL, BLOCK, HDIM)
    offset_slab = lists // SLAB_BLOCKS - (jnp.arange(QBLOCKS, dtype=jnp.int32) // SLAB_BLOCKS)[:, None]

    def combine(contrib):
        same_sum = spread(contrib, lists, offset_slab == 0)
        later_sum = spread(contrib, lists, offset_slab == -1)
        earlier_sum = spread(contrib, lists, offset_slab == 1)
        return (same_sum + rounded(later_sum) + rounded(earlier_sum)).astype(jnp.bfloat16)

    return attended, grad_query, combine(key_terms), combine(value_terms)


def heads_first(array):
    return array.reshape(QBLOCKS, BLOCK, HEADS, HDIM).transpose(2, 0, 1, 3)


def tokens_back(array):
    return array.transpose(1, 2, 0, 3).reshape(TOKENS, HEADS * HDIM)


def reference(query, key, value, d_out, pattern):
    results = lax.map(one_head, (heads_first(query), heads_first(key), heads_first(value), heads_first(d_out), pattern))
    return (tokens_back(results[0]), tokens_back(results[1]), tokens_back(results[2]), tokens_back(results[3]))
```

```python
import functools

import jax
import jax.numpy as jnp
from jax import lax
from jax.experimental import pallas as pl
from jax.experimental.pallas import tpu as pltpu
from jax.sharding import PartitionSpec as P

CROSS = 4
VMEM_LIMIT = 48 * 1024 * 1024


def from_behind(x, axis, by):
    count = lax.axis_size(axis)
    pairs = [(i, i + by) for i in range(count) if 0 <= i + by < count]
    return lax.ppermute(x, axis, pairs)


def pair_halves(left, right, head_dim):
    first = jnp.concatenate([left[:, :head_dim], right[:, :head_dim]], axis=1)
    second = jnp.concatenate([left[:, head_dim:], right[:, head_dim:]], axis=1)
    return first, second


def pack_kernel(query, key, value, d_out, message, *, head_dim):
    for pair in range(message.shape[1] // 2):
        lanes = pl.ds(pair * 2 * head_dim, 2 * head_dim)
        key_value = pair_halves(key[:, lanes], value[:, lanes], head_dim)
        query_grad = pair_halves(query[:, lanes], d_out[:, lanes], head_dim)
        for side in range(2):
            message[0, 2 * pair + side, 0] = key_value[side]
            message[0, 2 * pair + side, 1] = query_grad[side]


def pack(arrays, chunk, chunk_heads, heads_here, peers, head_dim):
    rows = arrays[0].shape[0]
    chunks = heads_here // chunk_heads
    shape = (peers, chunk_heads, 2, rows, 2 * head_dim)
    if chunk_heads % 2:
        low = chunk * chunk_heads
        cut = [
            x.reshape(rows, peers, heads_here, head_dim)[:, :, low : low + chunk_heads]
            for x in arrays
        ]
        query, key, value, d_out = cut
        both = jnp.stack(
            [jnp.concatenate([key, value], -1), jnp.concatenate([query, d_out], -1)]
        )
        return both.transpose(2, 3, 0, 1, 4)
    source = pl.BlockSpec(
        (rows, chunk_heads * head_dim), lambda peer: (0, peer * chunks + chunk)
    )
    return pl.pallas_call(
        functools.partial(pack_kernel, head_dim=head_dim),
        grid=(peers,),
        in_specs=[source] * 4,
        out_specs=pl.BlockSpec((1,) + shape[1:], lambda peer: (peer, 0, 0, 0, 0)),
        out_shape=jax.ShapeDtypeStruct(shape, arrays[0].dtype),
        compiler_params=pltpu.CompilerParams(vmem_limit_bytes=VMEM_LIMIT),
        name="pack",
    )(*arrays)


def unpack_kernel(message, *refs, head_dim):
    attended, grad_query, grad_key, grad_value = refs[-4:]
    for pair in range(message.shape[1] // 2):
        lanes = pl.ds(pair * 2 * head_dim, 2 * head_dim)
        key_grad, value_grad = pair_halves(
            message[0, 2 * pair, 0], message[0, 2 * pair + 1, 0], head_dim
        )
        query_grad, out = pair_halves(
            message[0, 2 * pair, 1], message[0, 2 * pair + 1, 1], head_dim
        )
        attended[:, lanes] = out
        grad_query[:, lanes] = query_grad
        grad_key[:, lanes] = key_grad
        grad_value[:, lanes] = value_grad


def unpack(message, chunk, heads_here, earlier):
    peers, chunk_heads, _, rows, pair_dim = message.shape
    head_dim = pair_dim // 2
    chunks = heads_here // chunk_heads
    columns = peers * heads_here * head_dim
    target = pl.BlockSpec(
        (rows, chunk_heads * head_dim), lambda peer: (0, peer * chunks + chunk)
    )
    return pl.pallas_call(
        functools.partial(unpack_kernel, head_dim=head_dim),
        grid=(peers,),
        in_specs=[pl.BlockSpec((1,) + message.shape[1:], lambda peer: (peer, 0, 0, 0, 0))]
        + [pl.BlockSpec(memory_space=pl.ANY)] * len(earlier),
        out_specs=[target] * 4,
        out_shape=[jax.ShapeDtypeStruct((rows, columns), message.dtype)] * 4,
        input_output_aliases={1 + i: i for i in range(len(earlier))},
        compiler_params=pltpu.CompilerParams(vmem_limit_bytes=VMEM_LIMIT),
        name="unpack",
    )(message, *earlier)


def unpack_all(messages, heads_here):
    if messages[0].shape[1] % 2 == 0:
        outs = ()
        for chunk, message in enumerate(messages):
            outs = unpack(message, chunk, heads_here, outs)
        return tuple(outs)
    whole = jnp.concatenate(messages, axis=1)
    peers, _, _, rows, pair_dim = whole.shape
    head_dim = pair_dim // 2
    parts = whole.reshape(peers, heads_here, 2, rows, 2, head_dim)
    parts = parts.transpose(2, 4, 3, 0, 1, 5).reshape(2, 2, rows, -1)
    return (parts[1, 1], parts[1, 0], parts[0, 0], parts[0, 1])


def pick_kernel(asked, message, picked):
    picked[0] = message[0, :, 0]


def pick(message, asked, block_rows):
    _, chunk_heads, _, rows, lanes = message.shape
    each = rows // block_rows
    return pl.pallas_call(
        pick_kernel,
        grid_spec=pltpu.PrefetchScalarGridSpec(
            num_scalar_prefetch=1,
            grid=(asked.shape[0],),
            in_specs=[
                pl.BlockSpec(
                    (1, chunk_heads, 1, block_rows, lanes),
                    lambda i, ids: (
                        lax.div(ids[i], each),
                        0,
                        0,
                        lax.rem(ids[i], each),
                        0,
                    ),
                )
            ],
            out_specs=pl.BlockSpec(
                (1, chunk_heads, block_rows, lanes), lambda i, ids: (i, 0, 0, 0)
            ),
        ),
        out_shape=jax.ShapeDtypeStruct(
            (asked.shape[0], chunk_heads, block_rows, lanes), message.dtype
        ),
        name="pick",
    )(asked, message)


def attend_kernel(
    lists,
    message,
    came_prev,
    came_next,
    back,
    own,
    to_prev,
    to_next,
    table,
    turned,
    sums,
    *,
    block_rows,
    head_dim,
    per_list,
):
    head = pl.program_id(0)
    peers, _, _, rows, lanes = message.shape
    each = rows // block_rows
    blocks = peers * each
    window = blocks + 2 * CROSS
    scaling = head_dim ** (-0.5)
    for i in range(CROSS):
        table[i] = came_prev[i, 0]
        table[CROSS + blocks + i] = came_next[i, 0]
    for peer in range(peers):
        for i in range(each):
            table[CROSS + peer * each + i] = message[
                peer, 0, 0, i * block_rows : (i + 1) * block_rows
            ]

    def turn(i, carry):
        turned[i] = table[i].T
        sums[i] = jnp.zeros(sums.shape[1:], sums.dtype)
        return carry

    lax.fori_loop(0, window, turn, 0)
    left = lax.broadcasted_iota(jnp.int32, (block_rows, lanes), 1) < head_dim

    def one_block(block, carry):
        ids = [lists[head, block, j] for j in range(per_list)]
        peer = lax.div(block, each)
        start = pl.multiple_of(lax.rem(block, each) * block_rows, block_rows)
        query_grad = message[peer, 0, 1, pl.ds(start, block_rows)]
        nothing = jnp.zeros_like(query_grad)
        apart = jnp.concatenate(
            [jnp.where(left, query_grad, nothing), jnp.where(left, nothing, query_grad)],
            axis=0,
        )
        key_value = jnp.concatenate([table[i] for i in ids], axis=0)
        both = lax.dot_general(
            key_value, apart, (((1,), (1,)), ((), ())), preferred_element_type=jnp.float32
        )
        scores = both[:, :block_rows]
        grad_prob = both[:, block_rows:]
        top = jnp.max(scores, axis=0, keepdims=True)
        weights = jnp.exp((scores - top) * scaling)
        weights = weights * (1.0 / jnp.sum(weights, axis=0, keepdims=True))
        correction = jnp.sum(weights * grad_prob, axis=0, keepdims=True)
        grad_score = weights * (grad_prob - correction)
        low = jnp.concatenate(
            [grad_score.astype(jnp.bfloat16), weights.astype(jnp.bfloat16)], axis=1
        )
        terms = jnp.dot(low, apart, preferred_element_type=jnp.float32)
        for j, i in enumerate(ids):
            sums[i] += terms[j * block_rows : (j + 1) * block_rows]
        key_value_turned = jnp.concatenate([turned[i] for i in ids], axis=1)
        out = jnp.dot(key_value_turned, low, preferred_element_type=jnp.float32)
        out = jnp.concatenate(
            [out[:head_dim, :block_rows] * scaling, out[head_dim:, block_rows:]], axis=0
        )
        back[peer, 0, 0, pl.ds(start, block_rows)] = out.T.astype(back.dtype)
        return carry

    lax.fori_loop(0, blocks, one_block, 0)
    factor = jnp.where(left, scaling, 1.0)
    for i in range(CROSS):
        to_prev[i, 0] = (sums[i] * factor).astype(to_prev.dtype)
        to_next[i, 0] = (sums[CROSS + blocks + i] * factor).astype(to_next.dtype)

    def finish(i, carry):
        own[0, i] = sums[CROSS + i] * factor
        return carry

    lax.fori_loop(0, blocks, finish, 0)


def attend(message, came_prev, came_next, lists, block_rows):
    peers, chunk_heads, _, rows, lanes = message.shape
    per_list = lists.shape[-1]
    blocks = peers * rows // block_rows
    window = blocks + 2 * CROSS
    cross_spec = pl.BlockSpec(
        (CROSS, 1, block_rows, lanes), lambda head, ids: (0, head, 0, 0)
    )
    cross_shape = jax.ShapeDtypeStruct(came_prev.shape, message.dtype)
    return pl.pallas_call(
        functools.partial(
            attend_kernel, block_rows=block_rows, head_dim=lanes // 2, per_list=per_list
        ),
        grid_spec=pltpu.PrefetchScalarGridSpec(
            num_scalar_prefetch=1,
            grid=(chunk_heads,),
            in_specs=[
                pl.BlockSpec(
                    (peers, 1, 2, rows, lanes), lambda head, ids: (0, head, 0, 0, 0)
                ),
                cross_spec,
                cross_spec,
            ],
            out_specs=[
                pl.BlockSpec(
                    (peers, 1, 1, rows, lanes), lambda head, ids: (0, head, 1, 0, 0)
                ),
                pl.BlockSpec(
                    (1, blocks, block_rows, lanes), lambda head, ids: (head, 0, 0, 0)
                ),
                cross_spec,
                cross_spec,
            ],
            scratch_shapes=[
                pltpu.VMEM((window, block_rows, lanes), message.dtype),
                pltpu.VMEM((window, lanes, block_rows), message.dtype),
                pltpu.VMEM((window, block_rows, lanes), jnp.float32),
            ],
        ),
        out_shape=[
            jax.ShapeDtypeStruct(message.shape, message.dtype),
            jax.ShapeDtypeStruct((chunk_heads, blocks, block_rows, lanes), jnp.float32),
            cross_shape,
            cross_shape,
        ],
        compiler_params=pltpu.CompilerParams(vmem_limit_bytes=VMEM_LIMIT),
        name="attend",
    )(lists, message, came_prev, came_next)


def finish_kernel(asked, own, later, earlier, back_in, back, sums, *, block_rows):
    del back_in
    peers, _, _, rows, _ = back.shape
    each = rows // block_rows
    sums[...] = own[0]
    for i in range(CROSS):
        sums[asked[i]] += later[i, 0].astype(jnp.float32)
    for i in range(CROSS):
        sums[asked[CROSS + i]] += earlier[i, 0].astype(jnp.float32)
    for peer in range(peers):
        for i in range(each):
            back[peer, 0, 0, i * block_rows : (i + 1) * block_rows] = sums[
                peer * each + i
            ].astype(back.dtype)


def finish(back, own, later, earlier, asked):
    peers, chunk_heads, _, rows, lanes = back.shape
    _, blocks, block_rows, _ = own.shape
    cross_spec = pl.BlockSpec(
        (CROSS, 1, block_rows, lanes), lambda head, ids: (0, head, 0, 0)
    )
    return pl.pallas_call(
        functools.partial(finish_kernel, block_rows=block_rows),
        grid_spec=pltpu.PrefetchScalarGridSpec(
            num_scalar_prefetch=1,
            grid=(chunk_heads,),
            in_specs=[
                pl.BlockSpec(
                    (1, blocks, block_rows, lanes), lambda head, ids: (head, 0, 0, 0)
                ),
                cross_spec,
                cross_spec,
                pl.BlockSpec(memory_space=pl.ANY),
            ],
            out_specs=pl.BlockSpec(
                (peers, 1, 1, rows, lanes), lambda head, ids: (0, head, 0, 0, 0)
            ),
            scratch_shapes=[pltpu.VMEM((blocks, block_rows, lanes), jnp.float32)],
        ),
        out_shape=jax.ShapeDtypeStruct(back.shape, back.dtype),
        input_output_aliases={4: 0},
        compiler_params=pltpu.CompilerParams(vmem_limit_bytes=VMEM_LIMIT),
        name="finish",
    )(asked, own, later, earlier, back)


def exchange(message):
    return lax.all_to_all(message, "seq", split_axis=0, concat_axis=0, tiled=True)


def local(query, key, value, d_out, pattern):
    heads_here, blocks, _ = pattern.shape
    peers = lax.axis_size("seq")
    rows, columns = query.shape
    head_dim = columns // (peers * heads_here)
    block_rows = rows * peers // blocks
    chunks = 3 if heads_here % 3 == 0 else 1
    chunk_heads = heads_here // chunks
    arrays = (query, key, value, d_out)

    own_base = lax.axis_index("slab") * blocks
    block_ids = jnp.arange(blocks, dtype=jnp.int32)
    flat_lists = pattern.reshape(-1)
    reverse_rank = blocks - 1 - block_ids
    hits_prev = jnp.any(flat_lists[:, None] == (own_base - blocks + block_ids)[None, :], axis=0)
    hits_next = jnp.any(flat_lists[:, None] == (own_base + blocks + block_ids)[None, :], axis=0)
    need_prev = lax.top_k(hits_prev.astype(jnp.int32) * blocks + reverse_rank, CROSS)[1]
    need_next = lax.top_k(hits_next.astype(jnp.int32) * blocks + reverse_rank, CROSS)[1]
    asked_next = from_behind(need_prev, "slab", -1)
    asked_prev = from_behind(need_next, "slab", 1)
    asked = jnp.concatenate([asked_next, asked_prev])
    rank_ids = jnp.arange(CROSS, dtype=jnp.int32)
    prev_global = own_base - blocks + need_prev
    next_global = own_base + blocks + need_next
    pos_prev = jnp.sum(jnp.where(pattern[..., None] == prev_global, rank_ids, 0), axis=-1)
    pos_next = jnp.sum(jnp.where(pattern[..., None] == next_global, rank_ids, 0), axis=-1)
    in_own = (pattern >= own_base) & (pattern < own_base + blocks)
    local_ids = jnp.where(
        in_own,
        CROSS + pattern - own_base,
        jnp.where(pattern < own_base, pos_prev, CROSS + blocks + pos_next),
    )

    came = [
        exchange(pack(arrays, chunk, chunk_heads, heads_here, peers, head_dim))
        for chunk in range(chunks)
    ]
    sent = []
    for chunk in range(chunks):
        picked = pick(came[chunk], asked, block_rows)
        came_prev = from_behind(picked[:CROSS], "slab", 1)
        came_next = from_behind(picked[CROSS:], "slab", -1)
        lists = local_ids[chunk * chunk_heads : (chunk + 1) * chunk_heads]
        back, own, to_prev, to_next = attend(
            came[chunk], came_prev, came_next, lists, block_rows
        )
        later = from_behind(to_prev, "slab", -1)
        earlier = from_behind(to_next, "slab", 1)
        sent.append(exchange(finish(back, own, later, earlier, asked)))
    return unpack_all(sent, heads_here)


def solution(mesh):
    tokens = P(("slab", "seq"), None)
    return jax.shard_map(
        local,
        mesh=mesh,
        in_specs=(tokens, tokens, tokens, tokens, P("seq", "slab", None)),
        out_specs=(tokens, tokens, tokens, tokens),
        check_vma=False,
    )
```

```python
import functools
import math

import jax
import jax.numpy as jnp
from jax import lax
from jax.experimental import pallas as pl
from jax.experimental.pallas import tpu as pltpu
from jax.sharding import PartitionSpec as P

CROSS = 4
CHUNKS = 2
LANES = 128
SMALL_VMEM = 24 * 1024 * 1024
LARGE_VMEM = 40 * 1024 * 1024


def from_behind(x, axis, by):
    count = lax.axis_size(axis)
    pairs = [(i, i + by) for i in range(count) if 0 <= i + by < count]
    return lax.ppermute(x, axis, pairs)


def pack_kernel(query, key, value, d_out, message, stage, ready, in_sems, out_sems, *, spans):
    sources = (key, value, query, d_out)
    head_dim = ready.shape[-1] // 2

    def fetch(peer, i):
        _, low, high = spans[peer]
        width = high - low
        return pltpu.make_async_copy(
            sources[i].at[:, pl.ds(low, width)],
            stage.at[i, peer, :, pl.ds(0, width)],
            in_sems.at[i, peer],
        )

    def send(peer):
        return pltpu.make_async_copy(ready.at[peer], message.at[peer], out_sems.at[peer])

    for peer in range(len(spans)):
        for i in range(4):
            fetch(peer, i).start()
    for peer, (first, low, _) in enumerate(spans):
        for i in range(4):
            fetch(peer, i).wait()
        for head in range(ready.shape[1]):
            at = first + head * head_dim - low
            for kind in range(2):
                ready[peer, head, kind] = jnp.concatenate(
                    [
                        stage[2 * kind, peer, :, at : at + head_dim],
                        stage[2 * kind + 1, peer, :, at : at + head_dim],
                    ],
                    axis=1,
                )
        send(peer).start()
    for peer in range(len(spans)):
        send(peer).wait()


def pack(arrays, start, chunk_heads, heads_here, peers, head_dim):
    rows = arrays[0].shape[0]
    shape = (peers, chunk_heads, 2, rows, 2 * head_dim)
    spans = []
    for peer in range(peers):
        first = (peer * heads_here + start) * head_dim
        last = first + chunk_heads * head_dim
        spans.append((first, first // LANES * LANES, -(-last // LANES) * LANES))
    width = max(high - low for _, low, high in spans)
    dtype = arrays[0].dtype
    anywhere = pl.BlockSpec(memory_space=pltpu.HBM)
    return pl.pallas_call(
        functools.partial(pack_kernel, spans=spans),
        in_specs=[anywhere] * 4,
        out_specs=pl.BlockSpec(memory_space=pl.ANY),
        out_shape=jax.ShapeDtypeStruct(shape, dtype),
        scratch_shapes=[
            pltpu.VMEM((4, peers, rows, width), dtype),
            pltpu.VMEM(shape, dtype),
            pltpu.SemaphoreType.DMA((4, peers)),
            pltpu.SemaphoreType.DMA((peers,)),
        ],
        compiler_params=pltpu.CompilerParams(vmem_limit_bytes=SMALL_VMEM),
        name="pack",
    )(*arrays)


def unpack_kernel(*refs, chunk, chunks_before, jobs):
    messages = refs[: chunk + 1]
    outs = refs[chunk + 1 + 4 * chunks_before :][:4]
    stages = refs[-2 - chunk - 1 : -2]
    ready, sems = refs[-2], refs[-1]
    in_sems, out_sems = sems.at[0], sems.at[1]
    head_dim = ready.shape[-1] // 2
    needed = sorted({place for job in jobs for place in job[1:]})
    slots = {place: i for i, place in enumerate(needed)}

    def fetch(place):
        which, peer, head = place
        return pltpu.make_async_copy(
            messages[which].at[peer, head],
            stages[which].at[peer, head],
            in_sems.at[slots[place]],
        )

    def send(job, i):
        tile = jobs[job][0]
        return pltpu.make_async_copy(
            ready.at[i, job],
            outs[i].at[:, pl.ds(tile * LANES, LANES)],
            out_sems.at[4 * job + i],
        )

    for place in needed:
        fetch(place).start()
    waited = set()
    for job, (tile, left, right) in enumerate(jobs):
        for place in (left, right):
            if place not in waited:
                fetch(place).wait()
                waited.add(place)
        sides = [stages[which][peer, head] for which, peer, head in (left, right)]
        for i, (kind, at) in enumerate(((1, head_dim), (1, 0), (0, 0), (0, head_dim))):
            ready[i, job] = jnp.concatenate(
                [side[kind, :, at : at + head_dim] for side in sides], axis=1
            )
            send(job, i).start()
    for job in range(len(jobs)):
        for i in range(4):
            send(job, i).wait()


def unpack(messages, starts, heads_here, earlier):
    chunk = len(messages) - 1
    peers, _, _, rows, pair_dim = messages[0].shape
    head_dim = pair_dim // 2
    columns = peers * heads_here * head_dim
    dtype = messages[0].dtype

    def place_of(head):
        peer, local_head = divmod(head, heads_here)
        which = max(c for c, start in enumerate(starts) if start <= local_head)
        return which, peer, local_head - starts[which]

    jobs = []
    for tile in range(columns // LANES):
        left, right = place_of(2 * tile), place_of(2 * tile + 1)
        if max(left[0], right[0]) == chunk:
            jobs.append((tile, left, right))
    if not jobs:
        return earlier
    copies = max(2 * len(jobs), 4 * len(jobs))
    return pl.pallas_call(
        functools.partial(
            unpack_kernel,
            chunk=chunk,
            chunks_before=1 if earlier else 0,
            jobs=jobs,
        ),
        in_specs=[pl.BlockSpec(memory_space=pl.ANY)] * (chunk + 1 + len(earlier)),
        out_specs=[pl.BlockSpec(memory_space=pltpu.HBM)] * 4,
        out_shape=[jax.ShapeDtypeStruct((rows, columns), dtype)] * 4,
        input_output_aliases={chunk + 1 + i: i for i in range(len(earlier))},
        scratch_shapes=[pltpu.VMEM(m.shape, dtype) for m in messages]
        + [
            pltpu.VMEM((4, len(jobs), rows, LANES), dtype),
            pltpu.SemaphoreType.DMA((2, copies)),
        ],
        compiler_params=pltpu.CompilerParams(vmem_limit_bytes=SMALL_VMEM),
        name="unpack",
    )(*messages, *earlier)


def pick_kernel(asked, message, for_next, for_prev, sems, *, block_rows):
    each = message.shape[3] // block_rows

    def copy(i):
        target = for_next if i < CROSS else for_prev
        start = pl.multiple_of(lax.rem(asked[i], each) * block_rows, block_rows)
        return pltpu.make_async_copy(
            message.at[lax.div(asked[i], each), :, 0, pl.ds(start, block_rows)],
            target.at[i % CROSS],
            sems.at[i],
        )

    for i in range(2 * CROSS):
        copy(i).start()
    for i in range(2 * CROSS):
        copy(i).wait()


def pick(message, asked, block_rows):
    _, chunk_heads, _, _, lanes = message.shape
    picked = jax.ShapeDtypeStruct((CROSS, chunk_heads, block_rows, lanes), message.dtype)
    return pl.pallas_call(
        functools.partial(pick_kernel, block_rows=block_rows),
        in_specs=[
            pl.BlockSpec(memory_space=pltpu.SMEM),
            pl.BlockSpec(memory_space=pl.ANY),
        ],
        out_specs=[pl.BlockSpec(memory_space=pl.ANY)] * 2,
        out_shape=[picked, picked],
        scratch_shapes=[pltpu.SemaphoreType.DMA((2 * CROSS,))],
        name="pick",
    )(asked, message)


def attend_kernel(
    lists,
    message,
    came_prev,
    came_next,
    back,
    own,
    to_prev,
    to_next,
    table,
    turned,
    sums,
    both_even,
    both_odd,
    low_even,
    low_odd,
    *,
    block_rows,
    head_dim,
    per_list,
):
    peers, heads, _, rows, lanes = message.shape
    each = rows // block_rows
    blocks = peers * each
    window = blocks + 2 * CROSS
    units = heads * blocks
    keys = per_list * block_rows
    scaling = head_dim ** (-0.5)
    exponent = scaling * math.log2(math.e)
    both = (both_even, both_odd)
    low = (low_even, low_odd)
    step_rows = 64

    for head in range(heads):
        for i in range(CROSS):
            table[head, i] = came_prev[i, head]
            table[head, CROSS + blocks + i] = came_next[i, head]

        def fill(peer, carry):
            for i in range(each):
                table[head, CROSS + peer * each + i] = message[
                    peer, head, 0, i * block_rows : (i + 1) * block_rows
                ]
            return carry

        lax.fori_loop(0, peers, fill, 0)

        def turn(i, carry):
            turned[head, i] = table[head, i].T
            sums[head, i] = jnp.zeros(sums.shape[2:], sums.dtype)
            return carry

        lax.fori_loop(0, window, turn, 0)

    left = lax.broadcasted_iota(jnp.int32, (block_rows, lanes), 1) < head_dim

    def locate(unit):
        head = lax.div(unit, blocks)
        block = lax.rem(unit, blocks)
        ids = [lists[head, block, j] for j in range(per_list)]
        peer = lax.div(block, each)
        start = pl.multiple_of(lax.rem(block, each) * block_rows, block_rows)
        return head, ids, peer, pl.ds(start, block_rows)

    def apart_of(head, peer, here):
        query_grad = message[peer, head, 1, here]
        nothing = jnp.zeros_like(query_grad)
        return jnp.concatenate(
            [jnp.where(left, query_grad, nothing), jnp.where(left, nothing, query_grad)],
            axis=0,
        )

    def score(unit, slot):
        head, ids, peer, here = locate(unit)
        key_value = jnp.concatenate([table[head, i] for i in ids], axis=0)
        both[slot][...] = lax.dot_general(
            key_value,
            apart_of(head, peer, here),
            (((1,), (1,)), ((), ())),
            preferred_element_type=jnp.float32,
        )

    def soften(slot):
        source, target = both[slot], low[slot]
        parts = [slice(i, i + step_rows) for i in range(0, keys, step_rows)]
        top = source[parts[0], :block_rows]
        for part in parts[1:]:
            top = jnp.maximum(top, source[part, :block_rows])
        top = jnp.max(top, axis=0, keepdims=True)
        total = jnp.zeros((step_rows, block_rows), jnp.float32)
        mixed = jnp.zeros((step_rows, block_rows), jnp.float32)
        for part in parts:
            raised = jnp.exp2((source[part, :block_rows] - top) * exponent)
            source[part, :block_rows] = raised
            total += raised
            mixed += raised * source[part, block_rows:]
        inverse = 1.0 / jnp.sum(total, axis=0, keepdims=True)
        correction = jnp.sum(mixed, axis=0, keepdims=True) * inverse
        for part in parts:
            weights = source[part, :block_rows] * inverse
            target[part, block_rows:] = weights.astype(jnp.bfloat16)
            target[part, :block_rows] = (
                weights * (source[part, block_rows:] - correction)
            ).astype(jnp.bfloat16)

    def combine(unit, slot):
        head, ids, peer, here = locate(unit)
        products = low[slot][...]
        terms = jnp.dot(
            products, apart_of(head, peer, here), preferred_element_type=jnp.float32
        )
        for j, i in enumerate(ids):
            sums[head, i] += terms[j * block_rows : (j + 1) * block_rows]
        key_value = jnp.concatenate([turned[head, i] for i in ids], axis=1)
        out = jnp.dot(key_value, products, preferred_element_type=jnp.float32)
        out = jnp.concatenate(
            [out[:head_dim, :block_rows] * scaling, out[head_dim:, block_rows:]], axis=0
        )
        back[peer, head, 1, here] = out.T.astype(back.dtype)

    score(0, 0)
    score(1, 1)
    soften(0)

    def step(i, carry):
        for slot in range(2):
            unit = 2 * i + slot
            combine(unit - 2, slot)
            score(unit, slot)
            soften(1 - slot)
        return carry

    lax.fori_loop(1, units // 2, step, 0)
    combine(units - 2, 0)
    soften(1)
    combine(units - 1, 1)

    factor = jnp.where(left, scaling, 1.0)
    for head in range(heads):
        for i in range(CROSS):
            to_prev[i, head] = (sums[head, i] * factor).astype(to_prev.dtype)
            to_next[i, head] = (sums[head, CROSS + blocks + i] * factor).astype(to_next.dtype)

        def finish(i, carry):
            own[head, i] = sums[head, CROSS + i] * factor
            return carry

        lax.fori_loop(0, blocks, finish, 0)


def attend(message, came_prev, came_next, lists, block_rows):
    peers, chunk_heads, _, rows, lanes = message.shape
    per_list = lists.shape[-1]
    keys = per_list * block_rows
    blocks = peers * rows // block_rows
    window = blocks + 2 * CROSS
    inside = pl.BlockSpec(memory_space=pltpu.VMEM)
    cross_shape = jax.ShapeDtypeStruct(came_prev.shape, message.dtype)
    return pl.pallas_call(
        functools.partial(
            attend_kernel, block_rows=block_rows, head_dim=lanes // 2, per_list=per_list
        ),
        in_specs=[pl.BlockSpec(memory_space=pltpu.SMEM), inside, inside, inside],
        out_specs=[inside] * 4,
        out_shape=[
            jax.ShapeDtypeStruct(message.shape, message.dtype),
            jax.ShapeDtypeStruct((chunk_heads, blocks, block_rows, lanes), jnp.float32),
            cross_shape,
            cross_shape,
        ],
        scratch_shapes=[
            pltpu.VMEM((chunk_heads, window, block_rows, lanes), message.dtype),
            pltpu.VMEM((chunk_heads, window, lanes, block_rows), message.dtype),
            pltpu.VMEM((chunk_heads, window, block_rows, lanes), jnp.float32),
            pltpu.VMEM((keys, 2 * block_rows), jnp.float32),
            pltpu.VMEM((keys, 2 * block_rows), jnp.float32),
            pltpu.VMEM((keys, 2 * block_rows), message.dtype),
            pltpu.VMEM((keys, 2 * block_rows), message.dtype),
        ],
        compiler_params=pltpu.CompilerParams(vmem_limit_bytes=LARGE_VMEM),
        name="attend",
    )(lists, message, came_prev, came_next)


def finish_kernel(asked, own, later, earlier, back_in, back, sums, *, block_rows):
    del back_in
    peers, _, _, rows, _ = back.shape
    each = rows // block_rows
    sums[...] = own[0]
    for i in range(CROSS):
        sums[asked[i]] += later[i, 0].astype(jnp.float32)
    for i in range(CROSS):
        sums[asked[CROSS + i]] += earlier[i, 0].astype(jnp.float32)
    for peer in range(peers):
        for i in range(each):
            back[peer, 0, 0, i * block_rows : (i + 1) * block_rows] = sums[
                peer * each + i
            ].astype(back.dtype)


def finish(back, own, later, earlier, asked):
    peers, chunk_heads, _, rows, lanes = back.shape
    _, blocks, block_rows, _ = own.shape
    cross_spec = pl.BlockSpec(
        (CROSS, 1, block_rows, lanes), lambda head, ids: (0, head, 0, 0)
    )
    return pl.pallas_call(
        functools.partial(finish_kernel, block_rows=block_rows),
        grid_spec=pltpu.PrefetchScalarGridSpec(
            num_scalar_prefetch=1,
            grid=(chunk_heads,),
            in_specs=[
                pl.BlockSpec(
                    (1, blocks, block_rows, lanes), lambda head, ids: (head, 0, 0, 0)
                ),
                cross_spec,
                cross_spec,
                pl.BlockSpec(memory_space=pl.ANY),
            ],
            out_specs=pl.BlockSpec(
                (peers, 1, 1, rows, lanes), lambda head, ids: (0, head, 0, 0, 0)
            ),
            scratch_shapes=[pltpu.VMEM((blocks, block_rows, lanes), jnp.float32)],
        ),
        out_shape=jax.ShapeDtypeStruct(back.shape, back.dtype),
        input_output_aliases={4: 0},
        compiler_params=pltpu.CompilerParams(vmem_limit_bytes=SMALL_VMEM),
        name="finish",
    )(asked, own, later, earlier, back)


def exchange(message):
    return lax.all_to_all(message, "seq", split_axis=0, concat_axis=0, tiled=True)


def local(query, key, value, d_out, pattern):
    heads_here, blocks, _ = pattern.shape
    peers = lax.axis_size("seq")
    rows, columns = query.shape
    head_dim = columns // (peers * heads_here)
    block_rows = rows * peers // blocks
    chunks = min(CHUNKS, heads_here)
    starts = [-(-heads_here * i // chunks) for i in range(chunks)]
    sizes = [end - start for start, end in zip(starts, starts[1:] + [heads_here])]
    arrays = (query, key, value, d_out)

    own_base = lax.axis_index("slab") * blocks
    block_ids = jnp.arange(blocks, dtype=jnp.int32)
    flat_lists = pattern.reshape(-1)
    reverse_rank = blocks - 1 - block_ids
    hits_prev = jnp.any(flat_lists[:, None] == (own_base - blocks + block_ids)[None, :], axis=0)
    hits_next = jnp.any(flat_lists[:, None] == (own_base + blocks + block_ids)[None, :], axis=0)
    need_prev = lax.top_k(hits_prev.astype(jnp.int32) * blocks + reverse_rank, CROSS)[1]
    need_next = lax.top_k(hits_next.astype(jnp.int32) * blocks + reverse_rank, CROSS)[1]
    asked_next = from_behind(need_prev, "slab", -1)
    asked_prev = from_behind(need_next, "slab", 1)
    asked = jnp.concatenate([asked_next, asked_prev])
    rank_ids = jnp.arange(CROSS, dtype=jnp.int32)
    prev_global = own_base - blocks + need_prev
    next_global = own_base + blocks + need_next
    pos_prev = jnp.sum(jnp.where(pattern[..., None] == prev_global, rank_ids, 0), axis=-1)
    pos_next = jnp.sum(jnp.where(pattern[..., None] == next_global, rank_ids, 0), axis=-1)
    in_own = (pattern >= own_base) & (pattern < own_base + blocks)
    local_ids = jnp.where(
        in_own,
        CROSS + pattern - own_base,
        jnp.where(pattern < own_base, pos_prev, CROSS + blocks + pos_next),
    )

    came = [
        exchange(pack(arrays, start, size, heads_here, peers, head_dim))
        for start, size in zip(starts, sizes)
    ]
    received = []
    outs = ()
    for message, start, size in zip(came, starts, sizes):
        for_next, for_prev = pick(message, asked, block_rows)
        came_prev = from_behind(for_next, "slab", 1)
        came_next = from_behind(for_prev, "slab", -1)
        back, own, to_prev, to_next = attend(
            message, came_prev, came_next, local_ids[start : start + size], block_rows
        )
        later = from_behind(to_prev, "slab", -1)
        earlier = from_behind(to_next, "slab", 1)
        received.append(exchange(finish(back, own, later, earlier, asked)))
        outs = unpack(received, starts, heads_here, outs)
    return tuple(outs)


def solution(mesh):
    tokens = P(("slab", "seq"), None)
    return jax.shard_map(
        local,
        mesh=mesh,
        in_specs=(tokens, tokens, tokens, tokens, P("seq", "slab", None)),
        out_specs=(tokens, tokens, tokens, tokens),
        check_vma=False,
    )
```

```python
import functools
import math

import jax
import jax.numpy as jnp
from jax import lax
from jax.experimental import pallas as pl
from jax.experimental.pallas import tpu as pltpu
from jax.sharding import PartitionSpec as P

CROSS = 4
CHUNKS = 2
LANES = 128
SMALL_VMEM = 24 * 1024 * 1024
LARGE_VMEM = 40 * 1024 * 1024


def in_hbm(x):
    return pltpu.with_memory_space_constraint(x, pltpu.HBM)


def from_behind(x, axis, by):
    count = lax.axis_size(axis)
    pairs = [(i, i + by) for i in range(count) if 0 <= i + by < count]
    return lax.ppermute(x, axis, pairs)


def pack_kernel(query, key, value, d_out, *refs, spans):
    message, stage, ready, in_sems, out_sems = refs[-5:]
    sources = (key, value, query, d_out)
    head_dim = ready.shape[-1] // 2

    def fetch(peer, i):
        _, low, high = spans[peer]
        width = high - low
        return pltpu.make_async_copy(
            sources[i].at[:, pl.ds(low, width)],
            stage.at[i, peer, :, pl.ds(0, width)],
            in_sems.at[i, peer],
        )

    def send(peer):
        return pltpu.make_async_copy(ready.at[peer], message.at[peer], out_sems.at[peer])

    for peer in range(len(spans)):
        for i in range(4):
            fetch(peer, i).start()
    for peer, (first, low, _) in enumerate(spans):
        for i in range(4):
            fetch(peer, i).wait()
        for head in range(ready.shape[1]):
            at = first + head * head_dim - low
            for kind in range(2):
                ready[peer, head, kind] = jnp.concatenate(
                    [
                        stage[2 * kind, peer, :, at : at + head_dim],
                        stage[2 * kind + 1, peer, :, at : at + head_dim],
                    ],
                    axis=1,
                )
        send(peer).start()
    for peer in range(len(spans)):
        send(peer).wait()


def pack(arrays, start, chunk_heads, heads_here, peers, head_dim, after):
    rows = arrays[0].shape[0]
    shape = (peers, chunk_heads, 2, rows, 2 * head_dim)
    spans = []
    for peer in range(peers):
        first = (peer * heads_here + start) * head_dim
        last = first + chunk_heads * head_dim
        spans.append((first, first // LANES * LANES, -(-last // LANES) * LANES))
    width = max(high - low for _, low, high in spans)
    dtype = arrays[0].dtype
    anywhere = pl.BlockSpec(memory_space=pltpu.HBM)
    return pl.pallas_call(
        functools.partial(pack_kernel, spans=spans),
        in_specs=[anywhere] * 4 + [pl.BlockSpec(memory_space=pl.ANY)] * len(after),
        out_specs=anywhere,
        out_shape=pltpu.HBM(shape, dtype),
        scratch_shapes=[
            pltpu.VMEM((4, peers, rows, width), dtype),
            pltpu.VMEM(shape, dtype),
            pltpu.SemaphoreType.DMA((4, peers)),
            pltpu.SemaphoreType.DMA((peers,)),
        ],
        compiler_params=pltpu.CompilerParams(vmem_limit_bytes=SMALL_VMEM),
        name="pack",
    )(*[in_hbm(x) for x in arrays], *after)


def unpack_kernel(*refs, chunk, chunks_before, jobs):
    messages = refs[: chunk + 1]
    outs = refs[chunk + 1 + 4 * chunks_before :][:4]
    stages = refs[-2 - chunk - 1 : -2]
    ready, sems = refs[-2], refs[-1]
    in_sems, out_sems = sems.at[0], sems.at[1]
    head_dim = ready.shape[-1] // 2
    needed = sorted({place for job in jobs for place in job[1:]})
    slots = {place: i for i, place in enumerate(needed)}

    def fetch(place):
        which, peer, head = place
        return pltpu.make_async_copy(
            messages[which].at[peer, head],
            stages[which].at[peer, head],
            in_sems.at[slots[place]],
        )

    def send(job, i):
        tile = jobs[job][0]
        return pltpu.make_async_copy(
            ready.at[i, job],
            outs[i].at[:, pl.ds(tile * LANES, LANES)],
            out_sems.at[4 * job + i],
        )

    for place in needed:
        fetch(place).start()
    waited = set()
    for job, (tile, left, right) in enumerate(jobs):
        for place in (left, right):
            if place not in waited:
                fetch(place).wait()
                waited.add(place)
        sides = [stages[which][peer, head] for which, peer, head in (left, right)]
        for i, (kind, at) in enumerate(((1, head_dim), (1, 0), (0, 0), (0, head_dim))):
            ready[i, job] = jnp.concatenate(
                [side[kind, :, at : at + head_dim] for side in sides], axis=1
            )
            send(job, i).start()
    for job in range(len(jobs)):
        for i in range(4):
            send(job, i).wait()


def unpack(messages, starts, heads_here, earlier):
    chunk = len(messages) - 1
    peers, _, _, rows, pair_dim = messages[0].shape
    head_dim = pair_dim // 2
    columns = peers * heads_here * head_dim
    dtype = messages[0].dtype

    def place_of(head):
        peer, local_head = divmod(head, heads_here)
        which = max(c for c, start in enumerate(starts) if start <= local_head)
        return which, peer, local_head - starts[which]

    jobs = []
    for tile in range(columns // LANES):
        left, right = place_of(2 * tile), place_of(2 * tile + 1)
        if max(left[0], right[0]) == chunk:
            jobs.append((tile, left, right))
    if not jobs:
        return earlier
    copies = max(2 * len(jobs), 4 * len(jobs))
    return pl.pallas_call(
        functools.partial(
            unpack_kernel,
            chunk=chunk,
            chunks_before=1 if earlier else 0,
            jobs=jobs,
        ),
        in_specs=[pl.BlockSpec(memory_space=pltpu.HBM)] * (chunk + 1 + len(earlier)),
        out_specs=[pl.BlockSpec(memory_space=pltpu.HBM)] * 4,
        out_shape=[pltpu.HBM((rows, columns), dtype)] * 4,
        input_output_aliases={chunk + 1 + i: i for i in range(len(earlier))},
        scratch_shapes=[pltpu.VMEM(m.shape, dtype) for m in messages]
        + [
            pltpu.VMEM((4, len(jobs), rows, LANES), dtype),
            pltpu.SemaphoreType.DMA((2, copies)),
        ],
        compiler_params=pltpu.CompilerParams(vmem_limit_bytes=SMALL_VMEM),
        name="unpack",
    )(*[in_hbm(x) for x in (*messages, *earlier)])


def pick_kernel(asked, message, for_next, for_prev, sems, *, block_rows):
    each = message.shape[3] // block_rows

    def copy(i):
        target = for_next if i < CROSS else for_prev
        start = pl.multiple_of(lax.rem(asked[i], each) * block_rows, block_rows)
        return pltpu.make_async_copy(
            message.at[lax.div(asked[i], each), :, 0, pl.ds(start, block_rows)],
            target.at[i % CROSS],
            sems.at[i],
        )

    for i in range(2 * CROSS):
        copy(i).start()
    for i in range(2 * CROSS):
        copy(i).wait()


def pick(message, asked, block_rows):
    _, chunk_heads, _, _, lanes = message.shape
    picked = jax.ShapeDtypeStruct((CROSS, chunk_heads, block_rows, lanes), message.dtype)
    return pl.pallas_call(
        functools.partial(pick_kernel, block_rows=block_rows),
        in_specs=[
            pl.BlockSpec(memory_space=pltpu.SMEM),
            pl.BlockSpec(memory_space=pltpu.HBM),
        ],
        out_specs=[pl.BlockSpec(memory_space=pltpu.VMEM)] * 2,
        out_shape=[picked, picked],
        scratch_shapes=[pltpu.SemaphoreType.DMA((2 * CROSS,))],
        name="pick",
    )(asked, in_hbm(message))


def attend_kernel(
    lists,
    message,
    came_prev,
    came_next,
    back,
    own,
    to_prev,
    to_next,
    table,
    turned,
    sums,
    both_even,
    both_odd,
    low_even,
    low_odd,
    *,
    block_rows,
    head_dim,
    per_list,
):
    peers, heads, _, rows, lanes = message.shape
    each = rows // block_rows
    blocks = peers * each
    window = blocks + 2 * CROSS
    units = heads * blocks
    keys = per_list * block_rows
    scaling = head_dim ** (-0.5)
    exponent = scaling * math.log2(math.e)
    both = (both_even, both_odd)
    low = (low_even, low_odd)
    step_rows = 64

    for head in range(heads):
        for i in range(CROSS):
            table[head, i] = came_prev[i, head]
            table[head, CROSS + blocks + i] = came_next[i, head]

        def fill(peer, carry):
            for i in range(each):
                table[head, CROSS + peer * each + i] = message[
                    peer, head, 0, i * block_rows : (i + 1) * block_rows
                ]
            return carry

        lax.fori_loop(0, peers, fill, 0)

        def turn(i, carry):
            turned[head, i] = table[head, i].T
            sums[head, i] = jnp.zeros(sums.shape[2:], sums.dtype)
            return carry

        lax.fori_loop(0, window, turn, 0)

    left = lax.broadcasted_iota(jnp.int32, (block_rows, lanes), 1) < head_dim

    def locate(unit):
        head = lax.div(unit, blocks)
        block = lax.rem(unit, blocks)
        ids = [lists[head, block, j] for j in range(per_list)]
        peer = lax.div(block, each)
        start = pl.multiple_of(lax.rem(block, each) * block_rows, block_rows)
        return head, ids, peer, pl.ds(start, block_rows)

    def apart_of(head, peer, here):
        query_grad = message[peer, head, 1, here]
        nothing = jnp.zeros_like(query_grad)
        return jnp.concatenate(
            [jnp.where(left, query_grad, nothing), jnp.where(left, nothing, query_grad)],
            axis=0,
        )

    def score(unit, slot):
        head, ids, peer, here = locate(unit)
        key_value = jnp.concatenate([table[head, i] for i in ids], axis=0)
        both[slot][...] = lax.dot_general(
            key_value,
            apart_of(head, peer, here),
            (((1,), (1,)), ((), ())),
            preferred_element_type=jnp.float32,
        )

    def soften(slot):
        source, target = both[slot], low[slot]
        parts = [slice(i, i + step_rows) for i in range(0, keys, step_rows)]
        top = source[parts[0], :block_rows]
        for part in parts[1:]:
            top = jnp.maximum(top, source[part, :block_rows])
        top = jnp.max(top, axis=0, keepdims=True)
        total = jnp.zeros((step_rows, block_rows), jnp.float32)
        mixed = jnp.zeros((step_rows, block_rows), jnp.float32)
        for part in parts:
            raised = jnp.exp2((source[part, :block_rows] - top) * exponent)
            source[part, :block_rows] = raised
            total += raised
            mixed += raised * source[part, block_rows:]
        inverse = 1.0 / jnp.sum(total, axis=0, keepdims=True)
        correction = jnp.sum(mixed, axis=0, keepdims=True) * inverse
        for part in parts:
            weights = source[part, :block_rows] * inverse
            target[part, block_rows:] = weights.astype(jnp.bfloat16)
            target[part, :block_rows] = (
                weights * (source[part, block_rows:] - correction)
            ).astype(jnp.bfloat16)

    def combine(unit, slot):
        head, ids, peer, here = locate(unit)
        products = low[slot][...]
        terms = jnp.dot(
            products, apart_of(head, peer, here), preferred_element_type=jnp.float32
        )
        for j, i in enumerate(ids):
            sums[head, i] += terms[j * block_rows : (j + 1) * block_rows]
        key_value = jnp.concatenate([turned[head, i] for i in ids], axis=1)
        out = jnp.dot(key_value, products, preferred_element_type=jnp.float32)
        out = jnp.concatenate(
            [out[:head_dim, :block_rows] * scaling, out[head_dim:, block_rows:]], axis=0
        )
        back[peer, head, 1, here] = out.T.astype(back.dtype)

    score(0, 0)
    score(1, 1)
    soften(0)

    def step(i, carry):
        for slot in range(2):
            unit = 2 * i + slot
            combine(unit - 2, slot)
            score(unit, slot)
            soften(1 - slot)
        return carry

    lax.fori_loop(1, units // 2, step, 0)
    combine(units - 2, 0)
    soften(1)
    combine(units - 1, 1)

    factor = jnp.where(left, scaling, 1.0)
    for head in range(heads):
        for i in range(CROSS):
            to_prev[i, head] = (sums[head, i] * factor).astype(to_prev.dtype)
            to_next[i, head] = (sums[head, CROSS + blocks + i] * factor).astype(to_next.dtype)

        def finish(i, carry):
            own[head, i] = sums[head, CROSS + i] * factor
            return carry

        lax.fori_loop(0, blocks, finish, 0)


def attend(message, came_prev, came_next, lists, block_rows):
    peers, chunk_heads, _, rows, lanes = message.shape
    per_list = lists.shape[-1]
    keys = per_list * block_rows
    blocks = peers * rows // block_rows
    window = blocks + 2 * CROSS
    inside = pl.BlockSpec(memory_space=pltpu.VMEM)
    cross_shape = jax.ShapeDtypeStruct(came_prev.shape, message.dtype)
    return pl.pallas_call(
        functools.partial(
            attend_kernel, block_rows=block_rows, head_dim=lanes // 2, per_list=per_list
        ),
        in_specs=[pl.BlockSpec(memory_space=pltpu.SMEM), inside, inside, inside],
        out_specs=[inside] * 4,
        out_shape=[
            pltpu.HBM(message.shape, message.dtype),
            jax.ShapeDtypeStruct((chunk_heads, blocks, block_rows, lanes), jnp.float32),
            cross_shape,
            cross_shape,
        ],
        scratch_shapes=[
            pltpu.VMEM((chunk_heads, window, block_rows, lanes), message.dtype),
            pltpu.VMEM((chunk_heads, window, lanes, block_rows), message.dtype),
            pltpu.VMEM((chunk_heads, window, block_rows, lanes), jnp.float32),
            pltpu.VMEM((keys, 2 * block_rows), jnp.float32),
            pltpu.VMEM((keys, 2 * block_rows), jnp.float32),
            pltpu.VMEM((keys, 2 * block_rows), message.dtype),
            pltpu.VMEM((keys, 2 * block_rows), message.dtype),
        ],
        compiler_params=pltpu.CompilerParams(vmem_limit_bytes=LARGE_VMEM),
        name="attend",
    )(lists, in_hbm(message), came_prev, came_next)


def finish_kernel(asked, own, later, earlier, back_in, back, sums, *, block_rows):
    del back_in
    peers, _, _, rows, _ = back.shape
    each = rows // block_rows
    sums[...] = own[0]
    for i in range(CROSS):
        sums[asked[i]] += later[i, 0].astype(jnp.float32)
    for i in range(CROSS):
        sums[asked[CROSS + i]] += earlier[i, 0].astype(jnp.float32)
    for peer in range(peers):
        for i in range(each):
            back[peer, 0, 0, i * block_rows : (i + 1) * block_rows] = sums[
                peer * each + i
            ].astype(back.dtype)


def finish(back, own, later, earlier, asked):
    peers, chunk_heads, _, rows, lanes = back.shape
    _, blocks, block_rows, _ = own.shape
    cross_spec = pl.BlockSpec(
        (CROSS, 1, block_rows, lanes), lambda head, ids: (0, head, 0, 0)
    )
    return pl.pallas_call(
        functools.partial(finish_kernel, block_rows=block_rows),
        grid_spec=pltpu.PrefetchScalarGridSpec(
            num_scalar_prefetch=1,
            grid=(chunk_heads,),
            in_specs=[
                pl.BlockSpec(
                    (1, blocks, block_rows, lanes), lambda head, ids: (head, 0, 0, 0)
                ),
                cross_spec,
                cross_spec,
                pl.BlockSpec(memory_space=pltpu.HBM),
            ],
            out_specs=pl.BlockSpec(
                (peers, 1, 1, rows, lanes), lambda head, ids: (0, head, 0, 0, 0)
            ),
            scratch_shapes=[pltpu.VMEM((blocks, block_rows, lanes), jnp.float32)],
        ),
        out_shape=pltpu.HBM(back.shape, back.dtype),
        input_output_aliases={4: 0},
        compiler_params=pltpu.CompilerParams(vmem_limit_bytes=SMALL_VMEM),
        name="finish",
    )(asked, own, later, earlier, in_hbm(back))


def exchange(message):
    return lax.all_to_all(message, "seq", split_axis=0, concat_axis=0, tiled=True)


def local(query, key, value, d_out, pattern):
    heads_here, blocks, _ = pattern.shape
    peers = lax.axis_size("seq")
    rows, columns = query.shape
    head_dim = columns // (peers * heads_here)
    block_rows = rows * peers // blocks
    chunks = min(CHUNKS, heads_here)
    starts = [-(-heads_here * i // chunks) for i in range(chunks)]
    sizes = [end - start for start, end in zip(starts, starts[1:] + [heads_here])]
    arrays = (query, key, value, d_out)

    own_base = lax.axis_index("slab") * blocks
    block_ids = jnp.arange(blocks, dtype=jnp.int32)
    flat_lists = pattern.reshape(-1)
    reverse_rank = blocks - 1 - block_ids
    hits_prev = jnp.any(flat_lists[:, None] == (own_base - blocks + block_ids)[None, :], axis=0)
    hits_next = jnp.any(flat_lists[:, None] == (own_base + blocks + block_ids)[None, :], axis=0)
    need_prev = lax.top_k(hits_prev.astype(jnp.int32) * blocks + reverse_rank, CROSS)[1]
    need_next = lax.top_k(hits_next.astype(jnp.int32) * blocks + reverse_rank, CROSS)[1]
    asked_next = from_behind(need_prev, "slab", -1)
    asked_prev = from_behind(need_next, "slab", 1)
    asked = jnp.concatenate([asked_next, asked_prev])
    rank_ids = jnp.arange(CROSS, dtype=jnp.int32)
    prev_global = own_base - blocks + need_prev
    next_global = own_base + blocks + need_next
    pos_prev = jnp.sum(jnp.where(pattern[..., None] == prev_global, rank_ids, 0), axis=-1)
    pos_next = jnp.sum(jnp.where(pattern[..., None] == next_global, rank_ids, 0), axis=-1)
    in_own = (pattern >= own_base) & (pattern < own_base + blocks)
    local_ids = jnp.where(
        in_own,
        CROSS + pattern - own_base,
        jnp.where(pattern < own_base, pos_prev, CROSS + blocks + pos_next),
    )

    came = []
    for start, size in zip(starts, sizes):
        after = (asked, local_ids) if came else ()
        came.append(exchange(pack(arrays, start, size, heads_here, peers, head_dim, after)))
    received = []
    outs = ()
    for message, start, size in zip(came, starts, sizes):
        for_next, for_prev = pick(message, asked, block_rows)
        came_prev = from_behind(for_next, "slab", 1)
        came_next = from_behind(for_prev, "slab", -1)
        back, own, to_prev, to_next = attend(
            message, came_prev, came_next, local_ids[start : start + size], block_rows
        )
        later = from_behind(to_prev, "slab", -1)
        earlier = from_behind(to_next, "slab", 1)
        received.append(exchange(finish(back, own, later, earlier, asked)))
        outs = unpack(received, starts, heads_here, outs)
    return tuple(outs)


def solution(mesh):
    tokens = P(("slab", "seq"), None)
    return jax.shard_map(
        local,
        mesh=mesh,
        in_specs=(tokens, tokens, tokens, tokens, P("seq", "slab", None)),
        out_specs=(tokens, tokens, tokens, tokens),
        check_vma=False,
    )
```

```python
import functools
import math

import jax
import jax.numpy as jnp
from jax import lax
from jax.experimental import pallas as pl
from jax.experimental.pallas import tpu as pltpu
from jax.sharding import PartitionSpec as P

CROSS = 4
CHUNKS = 2
LANES = 128
SMALL_VMEM = 24 * 1024 * 1024
LARGE_VMEM = 40 * 1024 * 1024


def in_hbm(x):
    return pltpu.with_memory_space_constraint(x, pltpu.HBM)


def from_behind(x, axis, by):
    count = lax.axis_size(axis)
    pairs = [(i, i + by) for i in range(count) if 0 <= i + by < count]
    return lax.ppermute(x, axis, pairs)


def hold_kernel(*refs):
    del refs


def hold(arrays, after):
    count = len(arrays)
    anywhere = pl.BlockSpec(memory_space=pltpu.HBM)
    return pl.pallas_call(
        hold_kernel,
        in_specs=[anywhere] * (count + len(after)),
        out_specs=[anywhere] * count,
        out_shape=[pltpu.HBM(x.shape, x.dtype) for x in arrays],
        input_output_aliases={i: i for i in range(count)},
        name="hold",
    )(*[in_hbm(x) for x in (*arrays, *after)])


def exchange(messages, before=None):
    count = len(messages)
    half = count // 2
    messages = list(messages)
    if before is not None:
        messages[1:half] = hold(messages[1:half], before[1:half])
        messages[half:] = hold(messages[half:], before[-1:])
    received = list(messages)
    for k in range(count - 1, 0, -1):
        pairs = [(i, i ^ k) for i in range(count)]
        received[k] = lax.ppermute(messages[k], "seq", pairs)
    return received


def pack_kernel(me, query, key, value, d_out, *refs, first, heads, peers, per_peer, head_dim):
    messages = refs[-4 - peers : -4]
    stage, ready, in_sems, out_sems = refs[-4:]
    sources = (key, value, query, d_out)
    aligned = per_peer % LANES == 0
    order = range(peers - 1, -1, -1)

    def span(item):
        if aligned:
            base, begin = pl.multiple_of((me[0] ^ item) * per_peer, LANES), first
        else:
            base, begin = 0, item * per_peer + first
        low = begin // LANES * LANES
        high = -(-(begin + heads * head_dim) // LANES) * LANES
        return base + low, high - low, begin - low

    def fetch(item, i):
        low, width, _ = span(item)
        return pltpu.make_async_copy(
            sources[i].at[:, pl.ds(low, width)],
            stage.at[i, item, :, pl.ds(0, width)],
            in_sems.at[i, item],
        )

    def send(item):
        slot = item if aligned else me[0] ^ item
        return pltpu.make_async_copy(ready.at[slot], messages[item], out_sems.at[item])

    for item in order:
        for i in range(4):
            fetch(item, i).start()
    for item in order:
        for i in range(4):
            fetch(item, i).wait()
        at = span(item)[2]
        for head in range(heads):
            lanes = slice(at + head * head_dim, at + (head + 1) * head_dim)
            for kind in range(2):
                ready[item, head, kind] = jnp.concatenate(
                    [stage[2 * kind, item, :, lanes], stage[2 * kind + 1, item, :, lanes]],
                    axis=1,
                )
        if aligned:
            send(item).start()
    if not aligned:
        for item in order:
            send(item).start()
    for item in order:
        send(item).wait()


def pack(me, arrays, start, heads, heads_here, peers, head_dim, after):
    rows = arrays[0].shape[0]
    dtype = arrays[0].dtype
    shape = (heads, 2, rows, 2 * head_dim)
    width = (-(-heads * head_dim // LANES) + 1) * LANES
    anywhere = pl.BlockSpec(memory_space=pltpu.HBM)
    return pl.pallas_call(
        functools.partial(
            pack_kernel,
            first=start * head_dim,
            heads=heads,
            peers=peers,
            per_peer=heads_here * head_dim,
            head_dim=head_dim,
        ),
        in_specs=[pl.BlockSpec(memory_space=pltpu.SMEM)]
        + [anywhere] * 4
        + [pl.BlockSpec(memory_space=pl.ANY)] * len(after),
        out_specs=[anywhere] * peers,
        out_shape=[pltpu.HBM(shape, dtype)] * peers,
        scratch_shapes=[
            pltpu.VMEM((4, peers, rows, width), dtype),
            pltpu.VMEM((peers,) + shape, dtype),
            pltpu.SemaphoreType.DMA((4, peers)),
            pltpu.SemaphoreType.DMA((peers,)),
        ],
        compiler_params=pltpu.CompilerParams(vmem_limit_bytes=SMALL_VMEM),
        name="pack",
    )(me, *[in_hbm(x) for x in arrays], *after)


def unpack_kernel(me, *refs, chunk, peers, earlier, jobs):
    groups = [refs[c * peers : (c + 1) * peers] for c in range(chunk + 1)]
    outs = refs[(chunk + 1) * peers + earlier :][:4]
    stages = refs[-3 - chunk - 1 : -3]
    ready, in_sems, out_sems = refs[-3:]
    head_dim = ready.shape[-1] // 2
    used = sorted({(which, peer) for job in jobs for which, peer, _ in job[1:]})
    chunks_used = sorted({which for which, _ in used})
    heads_used = {
        c: sorted({head for job in jobs for which, _, head in job[1:] if which == c})
        for c in chunks_used
    }

    def fetch(which, item, slot):
        heads = heads_used[which]
        some = pl.ds(heads[0], heads[-1] - heads[0] + 1)
        return pltpu.make_async_copy(
            groups[which][item].at[some],
            stages[which].at[slot, some],
            in_sems.at[which, slot],
        )

    def send(job, i):
        tile = jobs[job][0]
        return pltpu.make_async_copy(
            ready.at[i, job],
            outs[i].at[:, pl.ds(tile * LANES, LANES)],
            out_sems.at[4 * job + i],
        )

    for item in range(peers):
        for which in chunks_used:
            fetch(which, item, me[0] ^ item).start()
    waited = set()

    def wait_for(which, peer):
        if (which, peer) not in waited:
            fetch(which, 0, peer).wait()
            waited.add((which, peer))

    for job, (tile, left, right) in enumerate(jobs):
        for which, peer, _ in (left, right):
            wait_for(which, peer)
        sides = [stages[which][peer, head] for which, peer, head in (left, right)]
        for i, (kind, at) in enumerate(((1, head_dim), (1, 0), (0, 0), (0, head_dim))):
            ready[i, job] = jnp.concatenate(
                [side[kind, :, at : at + head_dim] for side in sides], axis=1
            )
            send(job, i).start()
    for which in chunks_used:
        for peer in range(peers):
            wait_for(which, peer)
    for job in range(len(jobs)):
        for i in range(4):
            send(job, i).wait()


def unpack(me, messages, starts, heads_here, earlier):
    chunk = len(messages) - 1
    peers = len(messages[0])
    _, _, rows, pair_dim = messages[0][0].shape
    head_dim = pair_dim // 2
    columns = peers * heads_here * head_dim
    dtype = messages[0][0].dtype

    def place_of(head):
        peer, local_head = divmod(head, heads_here)
        which = max(c for c, start in enumerate(starts) if start <= local_head)
        return which, peer, local_head - starts[which]

    jobs = []
    for tile in range(columns // LANES):
        left, right = place_of(2 * tile), place_of(2 * tile + 1)
        if max(left[0], right[0]) == chunk:
            jobs.append((tile, left, right))
    if not jobs:
        return earlier
    flat = [x for group in messages for x in group]
    anywhere = pl.BlockSpec(memory_space=pltpu.HBM)
    return pl.pallas_call(
        functools.partial(
            unpack_kernel, chunk=chunk, peers=peers, earlier=len(earlier), jobs=jobs
        ),
        in_specs=[pl.BlockSpec(memory_space=pltpu.SMEM)]
        + [anywhere] * (len(flat) + len(earlier)),
        out_specs=[anywhere] * 4,
        out_shape=[pltpu.HBM((rows, columns), dtype)] * 4,
        input_output_aliases={1 + len(flat) + i: i for i in range(len(earlier))},
        scratch_shapes=[pltpu.VMEM((peers,) + m[0].shape, dtype) for m in messages]
        + [
            pltpu.VMEM((4, len(jobs), rows, LANES), dtype),
            pltpu.SemaphoreType.DMA((chunk + 1, peers)),
            pltpu.SemaphoreType.DMA((4 * len(jobs),)),
        ],
        compiler_params=pltpu.CompilerParams(vmem_limit_bytes=SMALL_VMEM),
        name="unpack",
    )(me, *[in_hbm(x) for x in (*flat, *earlier)])


def pick_kernel(me, asked, *refs, block_rows):
    peers = len(refs) - 4
    for_next, for_prev, stage, sems = refs[peers:]
    rows = stage.shape[2]
    each = rows // block_rows

    def fetch(item):
        slot = me[0] ^ item
        return pltpu.make_async_copy(refs[item].at[:, 0], stage.at[slot], sems.at[item])

    for item in range(peers):
        fetch(item).start()
    for item in range(peers):
        fetch(item).wait()
    for i in range(2 * CROSS):
        target = for_next if i < CROSS else for_prev
        peer = lax.div(asked[i], each)
        start = pl.multiple_of(lax.rem(asked[i], each) * block_rows, block_rows)
        target[i % CROSS] = stage[peer, :, pl.ds(start, block_rows)]


def pick(me, messages, asked, block_rows):
    heads, _, rows, lanes = messages[0].shape
    dtype = messages[0].dtype
    peers = len(messages)
    picked = jax.ShapeDtypeStruct((CROSS, heads, block_rows, lanes), dtype)
    return pl.pallas_call(
        functools.partial(pick_kernel, block_rows=block_rows),
        in_specs=[pl.BlockSpec(memory_space=pltpu.SMEM)] * 2
        + [pl.BlockSpec(memory_space=pltpu.HBM)] * peers,
        out_specs=[pl.BlockSpec(memory_space=pltpu.VMEM)] * 2,
        out_shape=[picked, picked],
        scratch_shapes=[
            pltpu.VMEM((peers, heads, rows, lanes), dtype),
            pltpu.SemaphoreType.DMA((peers,)),
        ],
        compiler_params=pltpu.CompilerParams(vmem_limit_bytes=SMALL_VMEM),
        name="pick",
    )(me, asked, *[in_hbm(x) for x in messages])


def attend_kernel(me, lists, came_prev, came_next, *refs, block_rows, head_dim, per_list):
    peers = len(refs) - 13
    messages = refs[:peers]
    back, own, to_prev, to_next = refs[peers : peers + 4]
    message, table, turned, sums, both_even, both_odd, low_even, low_odd, sems = refs[peers + 4 :]
    _, heads, _, rows, lanes = message.shape
    each = rows // block_rows
    blocks = peers * each
    window = blocks + 2 * CROSS
    units = heads * blocks
    keys = per_list * block_rows
    scaling = head_dim ** (-0.5)
    exponent = scaling * math.log2(math.e)
    both = (both_even, both_odd)
    low = (low_even, low_odd)
    step_rows = 64

    def fetch(item):
        slot = me[0] ^ item
        return pltpu.make_async_copy(messages[item], message.at[slot], sems.at[item])

    for item in range(peers):
        fetch(item).start()
    for item in range(peers):
        fetch(item).wait()
    for head in range(heads):
        for i in range(CROSS):
            table[head, i] = came_prev[i, head]
            table[head, CROSS + blocks + i] = came_next[i, head]

        def fill(peer, carry):
            for i in range(each):
                table[head, CROSS + peer * each + i] = message[
                    peer, head, 0, i * block_rows : (i + 1) * block_rows
                ]
            return carry

        lax.fori_loop(0, peers, fill, 0)

        def turn(i, carry):
            turned[head, i] = table[head, i].T
            sums[head, i] = jnp.zeros(sums.shape[2:], sums.dtype)
            return carry

        lax.fori_loop(0, window, turn, 0)

    left = lax.broadcasted_iota(jnp.int32, (block_rows, lanes), 1) < head_dim

    def locate(unit):
        head = lax.div(unit, blocks)
        block = lax.rem(unit, blocks)
        ids = [lists[head, block, j] for j in range(per_list)]
        peer = lax.div(block, each)
        start = pl.multiple_of(lax.rem(block, each) * block_rows, block_rows)
        return head, ids, peer, pl.ds(start, block_rows)

    def apart_of(head, peer, here):
        query_grad = message[peer, head, 1, here]
        nothing = jnp.zeros_like(query_grad)
        return jnp.concatenate(
            [jnp.where(left, query_grad, nothing), jnp.where(left, nothing, query_grad)],
            axis=0,
        )

    def score(unit, slot):
        head, ids, peer, here = locate(unit)
        key_value = jnp.concatenate([table[head, i] for i in ids], axis=0)
        both[slot][...] = lax.dot_general(
            key_value,
            apart_of(head, peer, here),
            (((1,), (1,)), ((), ())),
            preferred_element_type=jnp.float32,
        )

    def soften(slot):
        source, target = both[slot], low[slot]
        parts = [slice(i, i + step_rows) for i in range(0, keys, step_rows)]
        top = source[parts[0], :block_rows]
        for part in parts[1:]:
            top = jnp.maximum(top, source[part, :block_rows])
        top = jnp.max(top, axis=0, keepdims=True)
        total = jnp.zeros((step_rows, block_rows), jnp.float32)
        mixed = jnp.zeros((step_rows, block_rows), jnp.float32)
        for part in parts:
            raised = jnp.exp2((source[part, :block_rows] - top) * exponent)
            source[part, :block_rows] = raised
            total += raised
            mixed += raised * source[part, block_rows:]
        inverse = 1.0 / jnp.sum(total, axis=0, keepdims=True)
        correction = jnp.sum(mixed, axis=0, keepdims=True) * inverse
        for part in parts:
            weights = source[part, :block_rows] * inverse
            target[part, block_rows:] = weights.astype(jnp.bfloat16)
            target[part, :block_rows] = (
                weights * (source[part, block_rows:] - correction)
            ).astype(jnp.bfloat16)

    def combine(unit, slot):
        head, ids, peer, here = locate(unit)
        products = low[slot][...]
        terms = jnp.dot(
            products, apart_of(head, peer, here), preferred_element_type=jnp.float32
        )
        for j, i in enumerate(ids):
            sums[head, i] += terms[j * block_rows : (j + 1) * block_rows]
        key_value = jnp.concatenate([turned[head, i] for i in ids], axis=1)
        out = jnp.dot(key_value, products, preferred_element_type=jnp.float32)
        out = jnp.concatenate(
            [out[:head_dim, :block_rows] * scaling, out[head_dim:, block_rows:]], axis=0
        )
        back[peer, head, here] = out.T.astype(back.dtype)

    score(0, 0)
    score(1, 1)
    soften(0)

    def step(i, carry):
        for slot in range(2):
            unit = 2 * i + slot
            combine(unit - 2, slot)
            score(unit, slot)
            soften(1 - slot)
        return carry

    lax.fori_loop(1, units // 2, step, 0)
    combine(units - 2, 0)
    soften(1)
    combine(units - 1, 1)

    factor = jnp.where(left, scaling, 1.0)
    for head in range(heads):
        for i in range(CROSS):
            to_prev[i, head] = (sums[head, i] * factor).astype(to_prev.dtype)
            to_next[i, head] = (sums[head, CROSS + blocks + i] * factor).astype(to_next.dtype)

        def finish(i, carry):
            own[head, i] = sums[head, CROSS + i] * factor
            return carry

        lax.fori_loop(0, blocks, finish, 0)


def attend(me, messages, came_prev, came_next, lists, block_rows):
    heads, _, rows, lanes = messages[0].shape
    dtype = messages[0].dtype
    peers = len(messages)
    per_list = lists.shape[-1]
    keys = per_list * block_rows
    blocks = peers * rows // block_rows
    window = blocks + 2 * CROSS
    inside = pl.BlockSpec(memory_space=pltpu.VMEM)
    scalars = pl.BlockSpec(memory_space=pltpu.SMEM)
    cross_shape = jax.ShapeDtypeStruct(came_prev.shape, dtype)
    return pl.pallas_call(
        functools.partial(
            attend_kernel, block_rows=block_rows, head_dim=lanes // 2, per_list=per_list
        ),
        in_specs=[scalars, scalars, inside, inside]
        + [pl.BlockSpec(memory_space=pltpu.HBM)] * peers,
        out_specs=[inside] * 4,
        out_shape=[
            pltpu.VMEM((peers, heads, rows, lanes), dtype),
            pltpu.VMEM((heads, blocks, block_rows, lanes), jnp.float32),
            cross_shape,
            cross_shape,
        ],
        scratch_shapes=[
            pltpu.VMEM((peers,) + messages[0].shape, dtype),
            pltpu.VMEM((heads, window, block_rows, lanes), dtype),
            pltpu.VMEM((heads, window, lanes, block_rows), dtype),
            pltpu.VMEM((heads, window, block_rows, lanes), jnp.float32),
            pltpu.VMEM((keys, 2 * block_rows), jnp.float32),
            pltpu.VMEM((keys, 2 * block_rows), jnp.float32),
            pltpu.VMEM((keys, 2 * block_rows), dtype),
            pltpu.VMEM((keys, 2 * block_rows), dtype),
            pltpu.SemaphoreType.DMA((peers,)),
        ],
        compiler_params=pltpu.CompilerParams(vmem_limit_bytes=LARGE_VMEM),
        name="attend",
    )(me, lists, came_prev, came_next, *[in_hbm(x) for x in messages])


def finish_kernel(me, asked, back, own, later, earlier, *refs, block_rows):
    peers = len(refs) - 3
    messages = refs[:peers]
    sums, ready, sems = refs[peers:]
    _, heads, _, rows, _ = ready.shape
    each = rows // block_rows

    def send(item, head):
        return pltpu.make_async_copy(
            ready.at[me[0] ^ item, head], messages[item].at[head], sems.at[item, head]
        )

    for head in range(heads):
        sums[...] = own[head]
        for i in range(CROSS):
            sums[asked[i]] += later[i, head].astype(jnp.float32)
        for i in range(CROSS):
            sums[asked[CROSS + i]] += earlier[i, head].astype(jnp.float32)
        for peer in range(peers):
            ready[peer, head, 1] = back[peer, head]
            for i in range(each):
                ready[peer, head, 0, i * block_rows : (i + 1) * block_rows] = sums[
                    peer * each + i
                ].astype(ready.dtype)
        for item in range(peers - 1, -1, -1):
            send(item, head).start()
    for head in range(heads):
        for item in range(peers):
            send(item, head).wait()


def finish(me, back, own, later, earlier, asked):
    peers, heads, rows, lanes = back.shape
    _, blocks, block_rows, _ = own.shape
    inside = pl.BlockSpec(memory_space=pltpu.VMEM)
    scalars = pl.BlockSpec(memory_space=pltpu.SMEM)
    shape = (heads, 2, rows, lanes)
    return pl.pallas_call(
        functools.partial(finish_kernel, block_rows=block_rows),
        in_specs=[scalars, scalars] + [inside] * 4,
        out_specs=[pl.BlockSpec(memory_space=pltpu.HBM)] * peers,
        out_shape=[pltpu.HBM(shape, back.dtype)] * peers,
        scratch_shapes=[
            pltpu.VMEM((blocks, block_rows, lanes), jnp.float32),
            pltpu.VMEM((peers,) + shape, back.dtype),
            pltpu.SemaphoreType.DMA((peers, heads)),
        ],
        compiler_params=pltpu.CompilerParams(vmem_limit_bytes=SMALL_VMEM),
        name="finish",
    )(
        me,
        asked,
        pltpu.with_memory_space_constraint(back, pltpu.VMEM),
        pltpu.with_memory_space_constraint(own, pltpu.VMEM),
        later,
        earlier,
    )


def local(query, key, value, d_out, pattern):
    heads_here, blocks, _ = pattern.shape
    peers = lax.axis_size("seq")
    rows, columns = query.shape
    head_dim = columns // (peers * heads_here)
    block_rows = rows * peers // blocks
    chunks = min(CHUNKS, heads_here)
    starts = [-(-heads_here * i // chunks) for i in range(chunks)]
    sizes = [end - start for start, end in zip(starts, starts[1:] + [heads_here])]
    arrays = (query, key, value, d_out)

    own_base = lax.axis_index("slab") * blocks
    block_ids = jnp.arange(blocks, dtype=jnp.int32)
    flat_lists = pattern.reshape(-1)
    reverse_rank = blocks - 1 - block_ids
    hits_prev = jnp.any(flat_lists[:, None] == (own_base - blocks + block_ids)[None, :], axis=0)
    hits_next = jnp.any(flat_lists[:, None] == (own_base + blocks + block_ids)[None, :], axis=0)
    need_prev = lax.top_k(hits_prev.astype(jnp.int32) * blocks + reverse_rank, CROSS)[1]
    need_next = lax.top_k(hits_next.astype(jnp.int32) * blocks + reverse_rank, CROSS)[1]
    asked_next = from_behind(need_prev, "slab", -1)
    asked_prev = from_behind(need_next, "slab", 1)
    asked = jnp.concatenate([asked_next, asked_prev])
    rank_ids = jnp.arange(CROSS, dtype=jnp.int32)
    prev_global = own_base - blocks + need_prev
    next_global = own_base + blocks + need_next
    pos_prev = jnp.sum(jnp.where(pattern[..., None] == prev_global, rank_ids, 0), axis=-1)
    pos_next = jnp.sum(jnp.where(pattern[..., None] == next_global, rank_ids, 0), axis=-1)
    in_own = (pattern >= own_base) & (pattern < own_base + blocks)
    local_ids = jnp.where(
        in_own,
        CROSS + pattern - own_base,
        jnp.where(pattern < own_base, pos_prev, CROSS + blocks + pos_next),
    )

    me = lax.axis_index("seq").astype(jnp.int32).reshape(1)
    came = []
    for start, size in zip(starts, sizes):
        after = (asked, local_ids) if came else ()
        packed = pack(me, arrays, start, size, heads_here, peers, head_dim, after)
        came.append(exchange(packed, came[-1] if came else None))
    received = []
    outs = ()
    for messages, start, size in zip(came, starts, sizes):
        for_next, for_prev = pick(me, messages, asked, block_rows)
        came_prev = from_behind(for_next, "slab", 1)
        came_next = from_behind(for_prev, "slab", -1)
        back, own, to_prev, to_next = attend(
            me, messages, came_prev, came_next, local_ids[start : start + size], block_rows
        )
        later = from_behind(to_prev, "slab", -1)
        earlier = from_behind(to_next, "slab", 1)
        received.append(exchange(finish(me, back, own, later, earlier, asked)))
        outs = unpack(me, received, starts, heads_here, outs)
    return tuple(outs)


def solution(mesh):
    tokens = P(("slab", "seq"), None)
    return jax.shard_map(
        local,
        mesh=mesh,
        in_specs=(tokens, tokens, tokens, tokens, P("seq", "slab", None)),
        out_specs=(tokens, tokens, tokens, tokens),
        check_vma=False,
    )
```

```python
import functools
import math

import jax
import jax.numpy as jnp
from jax import lax
from jax.experimental import pallas as pl
from jax.experimental.pallas import tpu as pltpu
from jax.sharding import PartitionSpec as P

CROSS = 4
CHUNKS = 2
LANES = 128
SMALL_VMEM = 24 * 1024 * 1024
LARGE_VMEM = 40 * 1024 * 1024


def in_hbm(x):
    return pltpu.with_memory_space_constraint(x, pltpu.HBM)


def from_behind(x, axis, by):
    count = lax.axis_size(axis)
    pairs = [(i, i + by) for i in range(count) if 0 <= i + by < count]
    return lax.ppermute(x, axis, pairs)


def part_of(messages, me, item):
    if len(messages) == 1:
        return messages[0].at[item], item
    return messages[item], me[0] ^ item


def message_shape(messages):
    return messages[0].shape[-4:]


def message_outs(peers, shape, dtype, apart):
    if apart:
        return [pltpu.HBM(shape, dtype)] * peers
    return [pltpu.HBM((peers,) + shape, dtype)]


def hold_kernel(*refs):
    del refs


def hold(arrays, after):
    count = len(arrays)
    anywhere = pl.BlockSpec(memory_space=pltpu.HBM)
    return pl.pallas_call(
        hold_kernel,
        in_specs=[anywhere] * (count + len(after)),
        out_specs=[anywhere] * count,
        out_shape=[pltpu.HBM(x.shape, x.dtype) for x in arrays],
        input_output_aliases={i: i for i in range(count)},
        name="hold",
    )(*[in_hbm(x) for x in (*arrays, *after)])


def exchange(messages):
    if len(messages) == 1:
        return [lax.all_to_all(messages[0], "seq", split_axis=0, concat_axis=0, tiled=True)]
    count = len(messages)
    received = list(messages)
    for k in range(count - 1, 0, -1):
        pairs = [(i, i ^ k) for i in range(count)]
        received[k] = lax.ppermute(messages[k], "seq", pairs)
    return received


def pack_kernel(
    me, query, key, value, d_out, *refs, first, heads, peers, apart, per_peer, head_dim
):
    messages = refs[-4 - (peers if apart else 1) : -4]
    stage, ready, in_sems, out_sems = refs[-4:]
    sources = (key, value, query, d_out)
    aligned = apart and per_peer % LANES == 0
    at_once = aligned or not apart
    order = range(peers - 1, -1, -1)

    def span(item):
        if aligned:
            base, begin = pl.multiple_of((me[0] ^ item) * per_peer, LANES), first
        else:
            base, begin = 0, item * per_peer + first
        low = begin // LANES * LANES
        high = -(-(begin + heads * head_dim) // LANES) * LANES
        return base + low, high - low, begin - low

    def fetch(item, i):
        low, width, _ = span(item)
        return pltpu.make_async_copy(
            sources[i].at[:, pl.ds(low, width)],
            stage.at[i, item, :, pl.ds(0, width)],
            in_sems.at[i, item],
        )

    def send(item):
        target, peer = part_of(messages, me, item)
        return pltpu.make_async_copy(
            ready.at[item if aligned else peer], target, out_sems.at[item]
        )

    for item in order:
        for i in range(4):
            fetch(item, i).start()
    for item in order:
        for i in range(4):
            fetch(item, i).wait()
        at = span(item)[2]
        for head in range(heads):
            lanes = slice(at + head * head_dim, at + (head + 1) * head_dim)
            for kind in range(2):
                ready[item, head, kind] = jnp.concatenate(
                    [stage[2 * kind, item, :, lanes], stage[2 * kind + 1, item, :, lanes]],
                    axis=1,
                )
        if at_once:
            send(item).start()
    if not at_once:
        for item in order:
            send(item).start()
    for item in order:
        send(item).wait()


def pack(me, arrays, start, heads, heads_here, peers, head_dim, apart, after):
    rows = arrays[0].shape[0]
    dtype = arrays[0].dtype
    shape = (heads, 2, rows, 2 * head_dim)
    width = (-(-heads * head_dim // LANES) + 1) * LANES
    anywhere = pl.BlockSpec(memory_space=pltpu.HBM)
    outs = message_outs(peers, shape, dtype, apart)
    return pl.pallas_call(
        functools.partial(
            pack_kernel,
            first=start * head_dim,
            heads=heads,
            peers=peers,
            apart=apart,
            per_peer=heads_here * head_dim,
            head_dim=head_dim,
        ),
        in_specs=[pl.BlockSpec(memory_space=pltpu.SMEM)]
        + [anywhere] * 4
        + [pl.BlockSpec(memory_space=pl.ANY)] * len(after),
        out_specs=[anywhere] * len(outs),
        out_shape=outs,
        scratch_shapes=[
            pltpu.VMEM((4, peers, rows, width), dtype),
            pltpu.VMEM((peers,) + shape, dtype),
            pltpu.SemaphoreType.DMA((4, peers)),
            pltpu.SemaphoreType.DMA((peers,)),
        ],
        compiler_params=pltpu.CompilerParams(vmem_limit_bytes=SMALL_VMEM),
        name="pack",
    )(me, *[in_hbm(x) for x in arrays], *after)


def unpack_kernel(me, *refs, chunk, peers, counts, earlier, jobs):
    ends = [sum(counts[: c + 1]) for c in range(chunk + 1)]
    groups = [refs[end - count : end] for end, count in zip(ends, counts)]
    outs = refs[ends[-1] + earlier :][:4]
    stages = refs[-3 - chunk - 1 : -3]
    ready, in_sems, out_sems = refs[-3:]
    head_dim = ready.shape[-1] // 2
    used = sorted({(which, peer) for job in jobs for which, peer, _ in job[1:]})
    chunks_used = sorted({which for which, _ in used})
    heads_used = {
        c: sorted({head for job in jobs for which, _, head in job[1:] if which == c})
        for c in chunks_used
    }

    def fetch(which, item, slot=None):
        heads = heads_used[which]
        some = pl.ds(heads[0], heads[-1] - heads[0] + 1)
        source, peer = part_of(groups[which], me, item)
        slot = peer if slot is None else slot
        return pltpu.make_async_copy(
            source.at[some], stages[which].at[slot, some], in_sems.at[which, slot]
        )

    def send(job, i):
        tile = jobs[job][0]
        return pltpu.make_async_copy(
            ready.at[i, job],
            outs[i].at[:, pl.ds(tile * LANES, LANES)],
            out_sems.at[4 * job + i],
        )

    for item in range(peers):
        for which in chunks_used:
            fetch(which, item).start()
    waited = set()

    def wait_for(which, peer):
        if (which, peer) not in waited:
            fetch(which, 0, peer).wait()
            waited.add((which, peer))

    for job, (tile, left, right) in enumerate(jobs):
        for which, peer, _ in (left, right):
            wait_for(which, peer)
        sides = [stages[which][peer, head] for which, peer, head in (left, right)]
        for i, (kind, at) in enumerate(((1, head_dim), (1, 0), (0, 0), (0, head_dim))):
            ready[i, job] = jnp.concatenate(
                [side[kind, :, at : at + head_dim] for side in sides], axis=1
            )
            send(job, i).start()
    for which in chunks_used:
        for peer in range(peers):
            wait_for(which, peer)
    for job in range(len(jobs)):
        for i in range(4):
            send(job, i).wait()


def unpack(me, messages, starts, heads_here, earlier):
    chunk = len(messages) - 1
    peers = lax.axis_size("seq")
    _, _, rows, pair_dim = message_shape(messages[0])
    head_dim = pair_dim // 2
    columns = peers * heads_here * head_dim
    dtype = messages[0][0].dtype

    def place_of(head):
        peer, local_head = divmod(head, heads_here)
        which = max(c for c, start in enumerate(starts) if start <= local_head)
        return which, peer, local_head - starts[which]

    jobs = []
    for tile in range(columns // LANES):
        left, right = place_of(2 * tile), place_of(2 * tile + 1)
        if max(left[0], right[0]) == chunk:
            jobs.append((tile, left, right))
    if not jobs:
        return earlier
    flat = [x for group in messages for x in group]
    anywhere = pl.BlockSpec(memory_space=pltpu.HBM)
    return pl.pallas_call(
        functools.partial(
            unpack_kernel,
            chunk=chunk,
            peers=peers,
            counts=[len(group) for group in messages],
            earlier=len(earlier),
            jobs=jobs,
        ),
        in_specs=[pl.BlockSpec(memory_space=pltpu.SMEM)]
        + [anywhere] * (len(flat) + len(earlier)),
        out_specs=[anywhere] * 4,
        out_shape=[pltpu.HBM((rows, columns), dtype)] * 4,
        input_output_aliases={1 + len(flat) + i: i for i in range(len(earlier))},
        scratch_shapes=[pltpu.VMEM((peers,) + message_shape(m), dtype) for m in messages]
        + [
            pltpu.VMEM((4, len(jobs), rows, LANES), dtype),
            pltpu.SemaphoreType.DMA((chunk + 1, peers)),
            pltpu.SemaphoreType.DMA((4 * len(jobs),)),
        ],
        compiler_params=pltpu.CompilerParams(vmem_limit_bytes=SMALL_VMEM),
        name="unpack",
    )(me, *[in_hbm(x) for x in (*flat, *earlier)])


def pick_kernel(me, asked, *refs, count, block_rows):
    for_next, for_prev, stage, sems = refs[-4:]
    peers, _, rows, _ = stage.shape
    each = rows // block_rows

    def fetch(item):
        source, peer = part_of(refs[:count], me, item)
        return pltpu.make_async_copy(source.at[:, 0], stage.at[peer], sems.at[item])

    for item in range(peers):
        fetch(item).start()
    for item in range(peers):
        fetch(item).wait()
    for i in range(2 * CROSS):
        target = for_next if i < CROSS else for_prev
        peer = lax.div(asked[i], each)
        start = pl.multiple_of(lax.rem(asked[i], each) * block_rows, block_rows)
        target[i % CROSS] = stage[peer, :, pl.ds(start, block_rows)]


def pick(me, messages, asked, block_rows, after):
    heads, _, rows, lanes = message_shape(messages)
    dtype = messages[0].dtype
    peers = lax.axis_size("seq")
    picked = jax.ShapeDtypeStruct((CROSS, heads, block_rows, lanes), dtype)
    return pl.pallas_call(
        functools.partial(pick_kernel, count=len(messages), block_rows=block_rows),
        in_specs=[pl.BlockSpec(memory_space=pltpu.SMEM)] * 2
        + [pl.BlockSpec(memory_space=pltpu.HBM)] * (len(messages) + len(after)),
        out_specs=[pl.BlockSpec(memory_space=pltpu.VMEM)] * 2,
        out_shape=[picked, picked],
        scratch_shapes=[
            pltpu.VMEM((peers, heads, rows, lanes), dtype),
            pltpu.SemaphoreType.DMA((peers,)),
        ],
        compiler_params=pltpu.CompilerParams(vmem_limit_bytes=SMALL_VMEM),
        name="pick",
    )(me, asked, *[in_hbm(x) for x in (*messages, *after)])


def attend_kernel(me, lists, came_prev, came_next, *refs, block_rows, head_dim, per_list):
    messages = refs[:-13]
    back, own, to_prev, to_next = refs[-13:-9]
    message, table, turned, sums, both_even, both_odd, low_even, low_odd, sems = refs[-9:]
    peers, heads, _, rows, lanes = message.shape
    each = rows // block_rows
    blocks = peers * each
    window = blocks + 2 * CROSS
    units = heads * blocks
    keys = per_list * block_rows
    scaling = head_dim ** (-0.5)
    exponent = scaling * math.log2(math.e)
    both = (both_even, both_odd)
    low = (low_even, low_odd)
    step_rows = 64

    def fetch(item):
        source, peer = part_of(messages, me, item)
        return pltpu.make_async_copy(source, message.at[peer], sems.at[item])

    for item in range(peers):
        fetch(item).start()
    for item in range(peers):
        fetch(item).wait()
    for head in range(heads):
        for i in range(CROSS):
            table[head, i] = came_prev[i, head]
            table[head, CROSS + blocks + i] = came_next[i, head]

        def fill(peer, carry):
            for i in range(each):
                table[head, CROSS + peer * each + i] = message[
                    peer, head, 0, i * block_rows : (i + 1) * block_rows
                ]
            return carry

        lax.fori_loop(0, peers, fill, 0)

        def turn(i, carry):
            turned[head, i] = table[head, i].T
            sums[head, i] = jnp.zeros(sums.shape[2:], sums.dtype)
            return carry

        lax.fori_loop(0, window, turn, 0)

    left = lax.broadcasted_iota(jnp.int32, (block_rows, lanes), 1) < head_dim

    def locate(unit):
        head = lax.div(unit, blocks)
        block = lax.rem(unit, blocks)
        ids = [lists[head, block, j] for j in range(per_list)]
        peer = lax.div(block, each)
        start = pl.multiple_of(lax.rem(block, each) * block_rows, block_rows)
        return head, ids, peer, pl.ds(start, block_rows)

    def apart_of(head, peer, here):
        query_grad = message[peer, head, 1, here]
        nothing = jnp.zeros_like(query_grad)
        return jnp.concatenate(
            [jnp.where(left, query_grad, nothing), jnp.where(left, nothing, query_grad)],
            axis=0,
        )

    def score(unit, slot):
        head, ids, peer, here = locate(unit)
        key_value = jnp.concatenate([table[head, i] for i in ids], axis=0)
        both[slot][...] = lax.dot_general(
            key_value,
            apart_of(head, peer, here),
            (((1,), (1,)), ((), ())),
            preferred_element_type=jnp.float32,
        )

    def soften(slot):
        source, target = both[slot], low[slot]
        parts = [slice(i, i + step_rows) for i in range(0, keys, step_rows)]
        top = source[parts[0], :block_rows]
        for part in parts[1:]:
            top = jnp.maximum(top, source[part, :block_rows])
        top = jnp.max(top, axis=0, keepdims=True)
        total = jnp.zeros((step_rows, block_rows), jnp.float32)
        mixed = jnp.zeros((step_rows, block_rows), jnp.float32)
        for part in parts:
            raised = jnp.exp2((source[part, :block_rows] - top) * exponent)
            source[part, :block_rows] = raised
            total += raised
            mixed += raised * source[part, block_rows:]
        inverse = 1.0 / jnp.sum(total, axis=0, keepdims=True)
        correction = jnp.sum(mixed, axis=0, keepdims=True) * inverse
        for part in parts:
            weights = source[part, :block_rows] * inverse
            target[part, block_rows:] = weights.astype(jnp.bfloat16)
            target[part, :block_rows] = (
                weights * (source[part, block_rows:] - correction)
            ).astype(jnp.bfloat16)

    def combine(unit, slot):
        head, ids, peer, here = locate(unit)
        products = low[slot][...]
        terms = jnp.dot(
            products, apart_of(head, peer, here), preferred_element_type=jnp.float32
        )
        for j, i in enumerate(ids):
            sums[head, i] += terms[j * block_rows : (j + 1) * block_rows]
        key_value = jnp.concatenate([turned[head, i] for i in ids], axis=1)
        out = jnp.dot(key_value, products, preferred_element_type=jnp.float32)
        out = jnp.concatenate(
            [out[:head_dim, :block_rows] * scaling, out[head_dim:, block_rows:]], axis=0
        )
        back[peer, head, here] = out.T.astype(back.dtype)

    score(0, 0)
    score(1, 1)
    soften(0)

    def step(i, carry):
        for slot in range(2):
            unit = 2 * i + slot
            combine(unit - 2, slot)
            score(unit, slot)
            soften(1 - slot)
        return carry

    lax.fori_loop(1, units // 2, step, 0)
    combine(units - 2, 0)
    soften(1)
    combine(units - 1, 1)

    factor = jnp.where(left, scaling, 1.0)
    for head in range(heads):
        for i in range(CROSS):
            to_prev[i, head] = (sums[head, i] * factor).astype(to_prev.dtype)
            to_next[i, head] = (sums[head, CROSS + blocks + i] * factor).astype(to_next.dtype)

        def finish(i, carry):
            own[head, i] = sums[head, CROSS + i] * factor
            return carry

        lax.fori_loop(0, blocks, finish, 0)


def attend(me, messages, came_prev, came_next, lists, block_rows):
    shape = message_shape(messages)
    heads, _, rows, lanes = shape
    dtype = messages[0].dtype
    peers = lax.axis_size("seq")
    per_list = lists.shape[-1]
    keys = per_list * block_rows
    blocks = peers * rows // block_rows
    window = blocks + 2 * CROSS
    inside = pl.BlockSpec(memory_space=pltpu.VMEM)
    scalars = pl.BlockSpec(memory_space=pltpu.SMEM)
    cross_shape = jax.ShapeDtypeStruct(came_prev.shape, dtype)
    return pl.pallas_call(
        functools.partial(
            attend_kernel, block_rows=block_rows, head_dim=lanes // 2, per_list=per_list
        ),
        in_specs=[scalars, scalars, inside, inside]
        + [pl.BlockSpec(memory_space=pltpu.HBM)] * len(messages),
        out_specs=[inside] * 4,
        out_shape=[
            pltpu.VMEM((peers, heads, rows, lanes), dtype),
            pltpu.VMEM((heads, blocks, block_rows, lanes), jnp.float32),
            cross_shape,
            cross_shape,
        ],
        scratch_shapes=[
            pltpu.VMEM((peers,) + shape, dtype),
            pltpu.VMEM((heads, window, block_rows, lanes), dtype),
            pltpu.VMEM((heads, window, lanes, block_rows), dtype),
            pltpu.VMEM((heads, window, block_rows, lanes), jnp.float32),
            pltpu.VMEM((keys, 2 * block_rows), jnp.float32),
            pltpu.VMEM((keys, 2 * block_rows), jnp.float32),
            pltpu.VMEM((keys, 2 * block_rows), dtype),
            pltpu.VMEM((keys, 2 * block_rows), dtype),
            pltpu.SemaphoreType.DMA((peers,)),
        ],
        compiler_params=pltpu.CompilerParams(vmem_limit_bytes=LARGE_VMEM),
        name="attend",
    )(me, lists, came_prev, came_next, *[in_hbm(x) for x in messages])


def finish_kernel(me, asked, back, own, later, earlier, *refs, block_rows):
    messages = refs[:-3]
    sums, ready, sems = refs[-3:]
    peers, heads, _, rows, _ = ready.shape
    each = rows // block_rows

    def send(item, head):
        target, peer = part_of(messages, me, item)
        return pltpu.make_async_copy(
            ready.at[peer, head], target.at[head], sems.at[item, head]
        )

    for head in range(heads):
        sums[...] = own[head]
        for i in range(CROSS):
            sums[asked[i]] += later[i, head].astype(jnp.float32)
        for i in range(CROSS):
            sums[asked[CROSS + i]] += earlier[i, head].astype(jnp.float32)
        for peer in range(peers):
            ready[peer, head, 1] = back[peer, head]
            for i in range(each):
                ready[peer, head, 0, i * block_rows : (i + 1) * block_rows] = sums[
                    peer * each + i
                ].astype(ready.dtype)
        for item in range(peers - 1, -1, -1):
            send(item, head).start()
    for head in range(heads):
        for item in range(peers):
            send(item, head).wait()


def finish(me, back, own, later, earlier, asked, apart):
    peers, heads, rows, lanes = back.shape
    _, blocks, block_rows, _ = own.shape
    inside = pl.BlockSpec(memory_space=pltpu.VMEM)
    scalars = pl.BlockSpec(memory_space=pltpu.SMEM)
    shape = (heads, 2, rows, lanes)
    outs = message_outs(peers, shape, back.dtype, apart)
    return pl.pallas_call(
        functools.partial(finish_kernel, block_rows=block_rows),
        in_specs=[scalars, scalars] + [inside] * 4,
        out_specs=[pl.BlockSpec(memory_space=pltpu.HBM)] * len(outs),
        out_shape=outs,
        scratch_shapes=[
            pltpu.VMEM((blocks, block_rows, lanes), jnp.float32),
            pltpu.VMEM((peers,) + shape, back.dtype),
            pltpu.SemaphoreType.DMA((peers, heads)),
        ],
        compiler_params=pltpu.CompilerParams(vmem_limit_bytes=SMALL_VMEM),
        name="finish",
    )(
        me,
        asked,
        pltpu.with_memory_space_constraint(back, pltpu.VMEM),
        pltpu.with_memory_space_constraint(own, pltpu.VMEM),
        later,
        earlier,
    )


def local(query, key, value, d_out, pattern):
    heads_here, blocks, _ = pattern.shape
    peers = lax.axis_size("seq")
    rows, columns = query.shape
    head_dim = columns // (peers * heads_here)
    block_rows = rows * peers // blocks
    chunks = min(CHUNKS, heads_here)
    starts = [-(-heads_here * i // chunks) for i in range(chunks)]
    sizes = [end - start for start, end in zip(starts, starts[1:] + [heads_here])]
    arrays = (query, key, value, d_out)

    own_base = lax.axis_index("slab") * blocks
    block_ids = jnp.arange(blocks, dtype=jnp.int32)
    flat_lists = pattern.reshape(-1)
    reverse_rank = blocks - 1 - block_ids
    hits_prev = jnp.any(flat_lists[:, None] == (own_base - blocks + block_ids)[None, :], axis=0)
    hits_next = jnp.any(flat_lists[:, None] == (own_base + blocks + block_ids)[None, :], axis=0)
    need_prev = lax.top_k(hits_prev.astype(jnp.int32) * blocks + reverse_rank, CROSS)[1]
    need_next = lax.top_k(hits_next.astype(jnp.int32) * blocks + reverse_rank, CROSS)[1]
    asked_next = from_behind(need_prev, "slab", -1)
    asked_prev = from_behind(need_next, "slab", 1)
    asked = jnp.concatenate([asked_next, asked_prev])
    rank_ids = jnp.arange(CROSS, dtype=jnp.int32)
    prev_global = own_base - blocks + need_prev
    next_global = own_base + blocks + need_next
    pos_prev = jnp.sum(jnp.where(pattern[..., None] == prev_global, rank_ids, 0), axis=-1)
    pos_next = jnp.sum(jnp.where(pattern[..., None] == next_global, rank_ids, 0), axis=-1)
    in_own = (pattern >= own_base) & (pattern < own_base + blocks)
    local_ids = jnp.where(
        in_own,
        CROSS + pattern - own_base,
        jnp.where(pattern < own_base, pos_prev, CROSS + blocks + pos_next),
    )

    me = lax.axis_index("seq").astype(jnp.int32).reshape(1)
    me = lax.axis_index("seq").astype(jnp.int32).reshape(1)
    last = chunks - 1
    came = []
    for chunk, (start, size) in enumerate(zip(starts, sizes)):
        after = (asked, local_ids) if came else ()
        packed = pack(
            me, arrays, start, size, heads_here, peers, head_dim, chunk == 0, after
        )
        if chunk == 1:
            packed = hold(packed, came[0][peers // 2 :])
        came.append(exchange(packed))
    received = []
    outs = finished = ()
    for chunk, (messages, start, size) in enumerate(zip(came, starts, sizes)):
        for_next, for_prev = pick(me, messages, asked, block_rows, finished[:1])
        came_prev = from_behind(for_next, "slab", 1)
        came_next = from_behind(for_prev, "slab", -1)
        back, own, to_prev, to_next = attend(
            me, messages, came_prev, came_next, local_ids[start : start + size], block_rows
        )
        later = from_behind(to_prev, "slab", -1)
        earlier = from_behind(to_next, "slab", 1)
        finished = finish(me, back, own, later, earlier, asked, chunk == last)
        received.append(exchange(finished))
        outs = unpack(me, received, starts, heads_here, outs)
    return tuple(outs)


def solution(mesh):
    tokens = P(("slab", "seq"), None)
    return jax.shard_map(
        local,
        mesh=mesh,
        in_specs=(tokens, tokens, tokens, tokens, P("seq", "slab", None)),
        out_specs=(tokens, tokens, tokens, tokens),
        check_vma=False,
    )
```

```python
import functools
import math

import jax
import jax.numpy as jnp
from jax import lax
from jax.experimental import pallas as pl
from jax.experimental.pallas import tpu as pltpu
from jax.sharding import PartitionSpec as P

CROSS = 4
CHUNKS = 2
LANES = 128
SMALL_VMEM = 24 * 1024 * 1024
LARGE_VMEM = 40 * 1024 * 1024


def in_hbm(x):
    return pltpu.with_memory_space_constraint(x, pltpu.HBM)


def from_behind(x, axis, by):
    count = lax.axis_size(axis)
    pairs = [(i, i + by) for i in range(count) if 0 <= i + by < count]
    return lax.ppermute(x, axis, pairs)


def part_of(messages, me, item):
    if len(messages) == 1:
        return messages[0].at[item], item
    return messages[item], me[0] ^ item


def message_shape(messages):
    return messages[0].shape[-4:]


def message_outs(peers, shape, dtype, apart):
    if apart:
        return [pltpu.HBM(shape, dtype)] * peers
    return [pltpu.HBM((peers,) + shape, dtype)]


def hold_kernel(*refs):
    del refs


def hold(arrays, after):
    count = len(arrays)
    anywhere = pl.BlockSpec(memory_space=pltpu.HBM)
    return pl.pallas_call(
        hold_kernel,
        in_specs=[anywhere] * (count + len(after)),
        out_specs=[anywhere] * count,
        out_shape=[pltpu.HBM(x.shape, x.dtype) for x in arrays],
        input_output_aliases={i: i for i in range(count)},
        name="hold",
    )(*[in_hbm(x) for x in (*arrays, *after)])


def exchange(messages):
    if len(messages) == 1:
        return [lax.all_to_all(messages[0], "seq", split_axis=0, concat_axis=0, tiled=True)]
    count = len(messages)
    received = list(messages)
    for k in range(count - 1, 0, -1):
        pairs = [(i, i ^ k) for i in range(count)]
        received[k] = lax.ppermute(messages[k], "seq", pairs)
    return received


def pack_kernel(
    me, query, key, value, d_out, *refs, first, heads, peers, apart, per_peer, head_dim
):
    messages = refs[-4 - (peers if apart else 1) : -4]
    stage, ready, in_sems, out_sems = refs[-4:]
    sources = (key, value, query, d_out)
    aligned = apart and per_peer % LANES == 0
    at_once = aligned or not apart
    order = range(peers - 1, -1, -1)

    def span(item):
        if aligned:
            base, begin = pl.multiple_of((me[0] ^ item) * per_peer, LANES), first
        else:
            base, begin = 0, item * per_peer + first
        low = begin // LANES * LANES
        high = -(-(begin + heads * head_dim) // LANES) * LANES
        return base + low, high - low, begin - low

    def fetch(item, i):
        low, width, _ = span(item)
        return pltpu.make_async_copy(
            sources[i].at[:, pl.ds(low, width)],
            stage.at[i, item, :, pl.ds(0, width)],
            in_sems.at[i, item],
        )

    def send(item):
        target, peer = part_of(messages, me, item)
        return pltpu.make_async_copy(
            ready.at[item if aligned else peer], target, out_sems.at[item]
        )

    for item in order:
        for i in range(4):
            fetch(item, i).start()
    for item in order:
        for i in range(4):
            fetch(item, i).wait()
        at = span(item)[2]
        for head in range(heads):
            lanes = slice(at + head * head_dim, at + (head + 1) * head_dim)
            for kind in range(2):
                ready[item, head, kind] = jnp.concatenate(
                    [stage[2 * kind, item, :, lanes], stage[2 * kind + 1, item, :, lanes]],
                    axis=1,
                )
        if at_once:
            send(item).start()
    if not at_once:
        for item in order:
            send(item).start()
    for item in order:
        send(item).wait()


def pack(me, arrays, start, heads, heads_here, peers, head_dim, apart, after):
    rows = arrays[0].shape[0]
    dtype = arrays[0].dtype
    shape = (heads, 2, rows, 2 * head_dim)
    width = (-(-heads * head_dim // LANES) + 1) * LANES
    anywhere = pl.BlockSpec(memory_space=pltpu.HBM)
    outs = message_outs(peers, shape, dtype, apart)
    return pl.pallas_call(
        functools.partial(
            pack_kernel,
            first=start * head_dim,
            heads=heads,
            peers=peers,
            apart=apart,
            per_peer=heads_here * head_dim,
            head_dim=head_dim,
        ),
        in_specs=[pl.BlockSpec(memory_space=pltpu.SMEM)]
        + [anywhere] * 4
        + [pl.BlockSpec(memory_space=pl.ANY)] * len(after),
        out_specs=[anywhere] * len(outs),
        out_shape=outs,
        scratch_shapes=[
            pltpu.VMEM((4, peers, rows, width), dtype),
            pltpu.VMEM((peers,) + shape, dtype),
            pltpu.SemaphoreType.DMA((4, peers)),
            pltpu.SemaphoreType.DMA((peers,)),
        ],
        compiler_params=pltpu.CompilerParams(vmem_limit_bytes=SMALL_VMEM),
        name="pack",
    )(me, *[in_hbm(x) for x in arrays], *after)


def unpack_kernel(me, *refs, chunk, peers, counts, earlier, jobs):
    ends = [sum(counts[: c + 1]) for c in range(chunk + 1)]
    groups = [refs[end - count : end] for end, count in zip(ends, counts)]
    outs = refs[ends[-1] + earlier :][:4]
    stages = refs[-3 - chunk - 1 : -3]
    ready, in_sems, out_sems = refs[-3:]
    head_dim = ready.shape[-1] // 2
    used = sorted({(which, peer) for job in jobs for which, peer, _ in job[1:]})
    chunks_used = sorted({which for which, _ in used})
    heads_used = {
        c: sorted({head for job in jobs for which, _, head in job[1:] if which == c})
        for c in chunks_used
    }

    def fetch(which, item, slot=None):
        heads = heads_used[which]
        some = pl.ds(heads[0], heads[-1] - heads[0] + 1)
        source, peer = part_of(groups[which], me, item)
        slot = peer if slot is None else slot
        return pltpu.make_async_copy(
            source.at[some], stages[which].at[slot, some], in_sems.at[which, slot]
        )

    def send(job, i):
        tile = jobs[job][0]
        return pltpu.make_async_copy(
            ready.at[i, job],
            outs[i].at[:, pl.ds(tile * LANES, LANES)],
            out_sems.at[4 * job + i],
        )

    for item in range(peers):
        for which in chunks_used:
            fetch(which, item).start()
    waited = set()

    def wait_for(which, peer):
        if (which, peer) not in waited:
            fetch(which, 0, peer).wait()
            waited.add((which, peer))

    for job, (tile, left, right) in enumerate(jobs):
        for which, peer, _ in (left, right):
            wait_for(which, peer)
        sides = [stages[which][peer, head] for which, peer, head in (left, right)]
        for i, (kind, at) in enumerate(((1, head_dim), (1, 0), (0, 0), (0, head_dim))):
            ready[i, job] = jnp.concatenate(
                [side[kind, :, at : at + head_dim] for side in sides], axis=1
            )
            send(job, i).start()
    for which in chunks_used:
        for peer in range(peers):
            wait_for(which, peer)
    for job in range(len(jobs)):
        for i in range(4):
            send(job, i).wait()


def unpack(me, messages, starts, heads_here, earlier):
    chunk = len(messages) - 1
    peers = lax.axis_size("seq")
    _, _, rows, pair_dim = message_shape(messages[0])
    head_dim = pair_dim // 2
    columns = peers * heads_here * head_dim
    dtype = messages[0][0].dtype

    def place_of(head):
        peer, local_head = divmod(head, heads_here)
        which = max(c for c, start in enumerate(starts) if start <= local_head)
        return which, peer, local_head - starts[which]

    jobs = []
    for tile in range(columns // LANES):
        left, right = place_of(2 * tile), place_of(2 * tile + 1)
        if max(left[0], right[0]) == chunk:
            jobs.append((tile, left, right))
    if not jobs:
        return earlier
    flat = [x for group in messages for x in group]
    anywhere = pl.BlockSpec(memory_space=pltpu.HBM)
    return pl.pallas_call(
        functools.partial(
            unpack_kernel,
            chunk=chunk,
            peers=peers,
            counts=[len(group) for group in messages],
            earlier=len(earlier),
            jobs=jobs,
        ),
        in_specs=[pl.BlockSpec(memory_space=pltpu.SMEM)]
        + [anywhere] * (len(flat) + len(earlier)),
        out_specs=[anywhere] * 4,
        out_shape=[pltpu.HBM((rows, columns), dtype)] * 4,
        input_output_aliases={1 + len(flat) + i: i for i in range(len(earlier))},
        scratch_shapes=[pltpu.VMEM((peers,) + message_shape(m), dtype) for m in messages]
        + [
            pltpu.VMEM((4, len(jobs), rows, LANES), dtype),
            pltpu.SemaphoreType.DMA((chunk + 1, peers)),
            pltpu.SemaphoreType.DMA((4 * len(jobs),)),
        ],
        compiler_params=pltpu.CompilerParams(vmem_limit_bytes=SMALL_VMEM),
        name="unpack",
    )(me, *[in_hbm(x) for x in (*flat, *earlier)])


def pick_kernel(me, asked, *refs, count, block_rows):
    for_next, for_prev, stage, sems = refs[-4:]
    peers, _, rows, _ = stage.shape
    each = rows // block_rows

    def fetch(item):
        source, peer = part_of(refs[:count], me, item)
        return pltpu.make_async_copy(source.at[:, 0], stage.at[peer], sems.at[item])

    for item in range(peers):
        fetch(item).start()
    for item in range(peers):
        fetch(item).wait()
    for i in range(2 * CROSS):
        target = for_next if i < CROSS else for_prev
        peer = lax.div(asked[i], each)
        start = pl.multiple_of(lax.rem(asked[i], each) * block_rows, block_rows)
        target[i % CROSS] = stage[peer, :, pl.ds(start, block_rows)]


def pick(me, messages, asked, block_rows, after):
    heads, _, rows, lanes = message_shape(messages)
    dtype = messages[0].dtype
    peers = lax.axis_size("seq")
    picked = jax.ShapeDtypeStruct((CROSS, heads, block_rows, lanes), dtype)
    return pl.pallas_call(
        functools.partial(pick_kernel, count=len(messages), block_rows=block_rows),
        in_specs=[pl.BlockSpec(memory_space=pltpu.SMEM)] * 2
        + [pl.BlockSpec(memory_space=pltpu.HBM)] * (len(messages) + len(after)),
        out_specs=[pl.BlockSpec(memory_space=pltpu.VMEM)] * 2,
        out_shape=[picked, picked],
        scratch_shapes=[
            pltpu.VMEM((peers, heads, rows, lanes), dtype),
            pltpu.SemaphoreType.DMA((peers,)),
        ],
        compiler_params=pltpu.CompilerParams(vmem_limit_bytes=SMALL_VMEM),
        name="pick",
    )(me, asked, *[in_hbm(x) for x in (*messages, *after)])


def attend_kernel(me, lists, came_prev, came_next, *refs, block_rows, head_dim, per_list):
    messages = refs[:-13]
    back, own, to_prev, to_next = refs[-13:-9]
    message, table, turned, sums, both_even, both_odd, low_even, low_odd, sems = refs[-9:]
    peers, heads, _, rows, lanes = message.shape
    each = rows // block_rows
    blocks = peers * each
    window = blocks + 2 * CROSS
    units = heads * blocks
    keys = per_list * block_rows
    scaling = head_dim ** (-0.5)
    exponent = scaling * math.log2(math.e)
    both = (both_even, both_odd)
    low = (low_even, low_odd)
    step_rows = 64

    def fetch(item):
        source, peer = part_of(messages, me, item)
        return pltpu.make_async_copy(source, message.at[peer], sems.at[item])

    for item in range(peers):
        fetch(item).start()
    for item in range(peers):
        fetch(item).wait()
    for head in range(heads):
        for i in range(CROSS):
            table[head, i] = came_prev[i, head]
            table[head, CROSS + blocks + i] = came_next[i, head]

        def fill(peer, carry):
            for i in range(each):
                table[head, CROSS + peer * each + i] = message[
                    peer, head, 0, i * block_rows : (i + 1) * block_rows
                ]
            return carry

        lax.fori_loop(0, peers, fill, 0)

        def turn(i, carry):
            turned[head, i] = table[head, i].T
            sums[head, i] = jnp.zeros(sums.shape[2:], sums.dtype)
            return carry

        lax.fori_loop(0, window, turn, 0)

    left = lax.broadcasted_iota(jnp.int32, (block_rows, lanes), 1) < head_dim

    def locate(unit):
        head = lax.div(unit, blocks)
        block = lax.rem(unit, blocks)
        ids = [lists[head, block, j] for j in range(per_list)]
        peer = lax.div(block, each)
        start = pl.multiple_of(lax.rem(block, each) * block_rows, block_rows)
        return head, ids, peer, pl.ds(start, block_rows)

    def apart_of(head, peer, here):
        query_grad = message[peer, head, 1, here]
        nothing = jnp.zeros_like(query_grad)
        return jnp.concatenate(
            [jnp.where(left, query_grad, nothing), jnp.where(left, nothing, query_grad)],
            axis=0,
        )

    def score(unit, slot):
        head, ids, peer, here = locate(unit)
        key_value = jnp.concatenate([table[head, i] for i in ids], axis=0)
        both[slot][...] = lax.dot_general(
            key_value,
            apart_of(head, peer, here),
            (((1,), (1,)), ((), ())),
            preferred_element_type=jnp.float32,
        )

    def soften(slot):
        source, target = both[slot], low[slot]
        parts = [slice(i, i + step_rows) for i in range(0, keys, step_rows)]
        top = source[parts[0], :block_rows]
        for part in parts[1:]:
            top = jnp.maximum(top, source[part, :block_rows])
        top = jnp.max(top, axis=0, keepdims=True)
        total = jnp.zeros((step_rows, block_rows), jnp.float32)
        mixed = jnp.zeros((step_rows, block_rows), jnp.float32)
        for part in parts:
            raised = jnp.exp2((source[part, :block_rows] - top) * exponent)
            source[part, :block_rows] = raised
            total += raised
            mixed += raised * source[part, block_rows:]
        inverse = 1.0 / jnp.sum(total, axis=0, keepdims=True)
        correction = jnp.sum(mixed, axis=0, keepdims=True) * inverse
        for part in parts:
            weights = source[part, :block_rows] * inverse
            target[part, block_rows:] = weights.astype(jnp.bfloat16)
            target[part, :block_rows] = (
                weights * (source[part, block_rows:] - correction)
            ).astype(jnp.bfloat16)

    def combine(unit, slot):
        head, ids, peer, here = locate(unit)
        products = low[slot][...]
        terms = jnp.dot(
            products, apart_of(head, peer, here), preferred_element_type=jnp.float32
        )
        for j, i in enumerate(ids):
            sums[head, i] += terms[j * block_rows : (j + 1) * block_rows]
        key_value = jnp.concatenate([turned[head, i] for i in ids], axis=1)
        out = jnp.dot(key_value, products, preferred_element_type=jnp.float32)
        out = jnp.concatenate(
            [out[:head_dim, :block_rows] * scaling, out[head_dim:, block_rows:]], axis=0
        )
        back[peer, head, here] = out.T.astype(back.dtype)

    score(0, 0)
    score(1, 1)
    soften(0)

    def step(i, carry):
        for slot in range(2):
            unit = 2 * i + slot
            combine(unit - 2, slot)
            score(unit, slot)
            soften(1 - slot)
        return carry

    lax.fori_loop(1, units // 2, step, 0)
    combine(units - 2, 0)
    soften(1)
    combine(units - 1, 1)

    factor = jnp.where(left, scaling, 1.0)
    for head in range(heads):
        for i in range(CROSS):
            to_prev[i, head] = (sums[head, i] * factor).astype(to_prev.dtype)
            to_next[i, head] = (sums[head, CROSS + blocks + i] * factor).astype(to_next.dtype)

        def finish(i, carry):
            own[head, i] = sums[head, CROSS + i] * factor
            return carry

        lax.fori_loop(0, blocks, finish, 0)


def attend(me, messages, came_prev, came_next, lists, block_rows):
    shape = message_shape(messages)
    heads, _, rows, lanes = shape
    dtype = messages[0].dtype
    peers = lax.axis_size("seq")
    per_list = lists.shape[-1]
    keys = per_list * block_rows
    blocks = peers * rows // block_rows
    window = blocks + 2 * CROSS
    inside = pl.BlockSpec(memory_space=pltpu.VMEM)
    scalars = pl.BlockSpec(memory_space=pltpu.SMEM)
    cross_shape = jax.ShapeDtypeStruct(came_prev.shape, dtype)
    return pl.pallas_call(
        functools.partial(
            attend_kernel, block_rows=block_rows, head_dim=lanes // 2, per_list=per_list
        ),
        in_specs=[scalars, scalars, inside, inside]
        + [pl.BlockSpec(memory_space=pltpu.HBM)] * len(messages),
        out_specs=[inside] * 4,
        out_shape=[
            pltpu.VMEM((peers, heads, rows, lanes), dtype),
            pltpu.VMEM((heads, blocks, block_rows, lanes), jnp.float32),
            cross_shape,
            cross_shape,
        ],
        scratch_shapes=[
            pltpu.VMEM((peers,) + shape, dtype),
            pltpu.VMEM((heads, window, block_rows, lanes), dtype),
            pltpu.VMEM((heads, window, lanes, block_rows), dtype),
            pltpu.VMEM((heads, window, block_rows, lanes), jnp.float32),
            pltpu.VMEM((keys, 2 * block_rows), jnp.float32),
            pltpu.VMEM((keys, 2 * block_rows), jnp.float32),
            pltpu.VMEM((keys, 2 * block_rows), dtype),
            pltpu.VMEM((keys, 2 * block_rows), dtype),
            pltpu.SemaphoreType.DMA((peers,)),
        ],
        compiler_params=pltpu.CompilerParams(vmem_limit_bytes=LARGE_VMEM),
        name="attend",
    )(me, lists, came_prev, came_next, *[in_hbm(x) for x in messages])


def finish_kernel(me, asked, back, own, later, earlier, *refs, block_rows):
    messages = refs[:-3]
    sums, ready, sems = refs[-3:]
    peers, heads, _, rows, _ = ready.shape
    each = rows // block_rows

    def send(item, head):
        target, peer = part_of(messages, me, item)
        return pltpu.make_async_copy(
            ready.at[peer, head], target.at[head], sems.at[item, head]
        )

    for head in range(heads):
        sums[...] = own[head]
        for i in range(CROSS):
            sums[asked[i]] += later[i, head].astype(jnp.float32)
        for i in range(CROSS):
            sums[asked[CROSS + i]] += earlier[i, head].astype(jnp.float32)
        for peer in range(peers):
            ready[peer, head, 1] = back[peer, head]
            for i in range(each):
                ready[peer, head, 0, i * block_rows : (i + 1) * block_rows] = sums[
                    peer * each + i
                ].astype(ready.dtype)
        for item in range(peers - 1, -1, -1):
            send(item, head).start()
    for head in range(heads):
        for item in range(peers):
            send(item, head).wait()


def finish(me, back, own, later, earlier, asked, apart):
    peers, heads, rows, lanes = back.shape
    _, blocks, block_rows, _ = own.shape
    inside = pl.BlockSpec(memory_space=pltpu.VMEM)
    scalars = pl.BlockSpec(memory_space=pltpu.SMEM)
    shape = (heads, 2, rows, lanes)
    outs = message_outs(peers, shape, back.dtype, apart)
    return pl.pallas_call(
        functools.partial(finish_kernel, block_rows=block_rows),
        in_specs=[scalars, scalars] + [inside] * 4,
        out_specs=[pl.BlockSpec(memory_space=pltpu.HBM)] * len(outs),
        out_shape=outs,
        scratch_shapes=[
            pltpu.VMEM((blocks, block_rows, lanes), jnp.float32),
            pltpu.VMEM((peers,) + shape, back.dtype),
            pltpu.SemaphoreType.DMA((peers, heads)),
        ],
        compiler_params=pltpu.CompilerParams(vmem_limit_bytes=SMALL_VMEM),
        name="finish",
    )(
        me,
        asked,
        pltpu.with_memory_space_constraint(back, pltpu.VMEM),
        pltpu.with_memory_space_constraint(own, pltpu.VMEM),
        later,
        earlier,
    )


def local(query, key, value, d_out, pattern):
    heads_here, blocks, _ = pattern.shape
    peers = lax.axis_size("seq")
    rows, columns = query.shape
    head_dim = columns // (peers * heads_here)
    block_rows = rows * peers // blocks
    chunks = min(CHUNKS, heads_here)
    starts = [-(-heads_here * i // chunks) for i in range(chunks)]
    sizes = [end - start for start, end in zip(starts, starts[1:] + [heads_here])]
    arrays = (query, key, value, d_out)

    own_base = lax.axis_index("slab") * blocks
    block_ids = jnp.arange(blocks, dtype=jnp.int32)
    flat_lists = pattern.reshape(-1)
    reverse_rank = blocks - 1 - block_ids
    hits_prev = jnp.any(flat_lists[:, None] == (own_base - blocks + block_ids)[None, :], axis=0)
    hits_next = jnp.any(flat_lists[:, None] == (own_base + blocks + block_ids)[None, :], axis=0)
    need_prev = lax.top_k(hits_prev.astype(jnp.int32) * blocks + reverse_rank, CROSS)[1]
    need_next = lax.top_k(hits_next.astype(jnp.int32) * blocks + reverse_rank, CROSS)[1]
    asked_next = from_behind(need_prev, "slab", -1)
    asked_prev = from_behind(need_next, "slab", 1)
    asked = jnp.concatenate([asked_next, asked_prev])
    rank_ids = jnp.arange(CROSS, dtype=jnp.int32)
    prev_global = own_base - blocks + need_prev
    next_global = own_base + blocks + need_next
    pos_prev = jnp.sum(jnp.where(pattern[..., None] == prev_global, rank_ids, 0), axis=-1)
    pos_next = jnp.sum(jnp.where(pattern[..., None] == next_global, rank_ids, 0), axis=-1)
    in_own = (pattern >= own_base) & (pattern < own_base + blocks)
    local_ids = jnp.where(
        in_own,
        CROSS + pattern - own_base,
        jnp.where(pattern < own_base, pos_prev, CROSS + blocks + pos_next),
    )

    me = lax.axis_index("seq").astype(jnp.int32).reshape(1)
    me = lax.axis_index("seq").astype(jnp.int32).reshape(1)
    last = chunks - 1
    came = []
    for chunk, (start, size) in enumerate(zip(starts, sizes)):
        after = (asked, local_ids) if came else ()
        packed = pack(
            me, arrays, start, size, heads_here, peers, head_dim, chunk == 0, after
        )
        if chunk == 1:
            packed = hold(packed, came[0][1:])
        came.append(exchange(packed))
    received = []
    outs = finished = ()
    for chunk, (messages, start, size) in enumerate(zip(came, starts, sizes)):
        for_next, for_prev = pick(me, messages, asked, block_rows, finished[:1])
        came_prev = from_behind(for_next, "slab", 1)
        came_next = from_behind(for_prev, "slab", -1)
        back, own, to_prev, to_next = attend(
            me, messages, came_prev, came_next, local_ids[start : start + size], block_rows
        )
        later = from_behind(to_prev, "slab", -1)
        earlier = from_behind(to_next, "slab", 1)
        finished = finish(me, back, own, later, earlier, asked, chunk == last)
        received.append(exchange(finished))
        outs = unpack(me, received, starts, heads_here, outs)
    return tuple(outs)


def solution(mesh):
    tokens = P(("slab", "seq"), None)
    return jax.shard_map(
        local,
        mesh=mesh,
        in_specs=(tokens, tokens, tokens, tokens, P("seq", "slab", None)),
        out_specs=(tokens, tokens, tokens, tokens),
        check_vma=False,
    )
```

```python
import functools
import math

import jax
import jax.numpy as jnp
from jax import lax
from jax.experimental import pallas as pl
from jax.experimental.pallas import tpu as pltpu
from jax.sharding import PartitionSpec as P

CROSS = 4
CHUNKS = 2
LANES = 128
SMALL_VMEM = 24 * 1024 * 1024
LARGE_VMEM = 40 * 1024 * 1024


def in_hbm(x):
    return pltpu.with_memory_space_constraint(x, pltpu.HBM)


def from_behind(x, axis, by):
    count = lax.axis_size(axis)
    pairs = [(i, i + by) for i in range(count) if 0 <= i + by < count]
    return lax.ppermute(x, axis, pairs)


def part_of(messages, me, item):
    if len(messages) == 1:
        return messages[0].at[item], item
    return messages[item], me[0] ^ item


def message_shape(messages):
    return messages[0].shape[-4:]


def message_outs(peers, shape, dtype, apart):
    if apart:
        return [pltpu.HBM(shape, dtype)] * peers
    return [pltpu.HBM((peers,) + shape, dtype)]


def hold_kernel(*refs):
    del refs


def hold(arrays, after):
    count = len(arrays)
    anywhere = pl.BlockSpec(memory_space=pltpu.HBM)
    return pl.pallas_call(
        hold_kernel,
        in_specs=[anywhere] * (count + len(after)),
        out_specs=[anywhere] * count,
        out_shape=[pltpu.HBM(x.shape, x.dtype) for x in arrays],
        input_output_aliases={i: i for i in range(count)},
        name="hold",
    )(*[in_hbm(x) for x in (*arrays, *after)])


def exchange(messages):
    if len(messages) == 1:
        return [lax.all_to_all(messages[0], "seq", split_axis=0, concat_axis=0, tiled=True)]
    count = len(messages)
    received = list(messages)
    for k in range(1, count):
        pairs = [(i, i ^ k) for i in range(count)]
        received[k] = lax.ppermute(messages[k], "seq", pairs)
    return received


def pack_kernel(
    me, query, key, value, d_out, *refs, first, heads, peers, apart, per_peer, head_dim
):
    messages = refs[-4 - (peers if apart else 1) : -4]
    stage, ready, in_sems, out_sems = refs[-4:]
    sources = (key, value, query, d_out)
    aligned = apart and per_peer % LANES == 0
    at_once = aligned or not apart
    order = range(peers - 1, -1, -1)

    def span(item):
        if aligned:
            base, begin = pl.multiple_of((me[0] ^ item) * per_peer, LANES), first
        else:
            base, begin = 0, item * per_peer + first
        low = begin // LANES * LANES
        high = -(-(begin + heads * head_dim) // LANES) * LANES
        return base + low, high - low, begin - low

    def fetch(item, i):
        low, width, _ = span(item)
        return pltpu.make_async_copy(
            sources[i].at[:, pl.ds(low, width)],
            stage.at[i, item, :, pl.ds(0, width)],
            in_sems.at[i, item],
        )

    def send(item):
        target, peer = part_of(messages, me, item)
        return pltpu.make_async_copy(
            ready.at[item if aligned else peer], target, out_sems.at[item]
        )

    for item in order:
        for i in range(4):
            fetch(item, i).start()
    for item in order:
        for i in range(4):
            fetch(item, i).wait()
        at = span(item)[2]
        for head in range(heads):
            lanes = slice(at + head * head_dim, at + (head + 1) * head_dim)
            for kind in range(2):
                ready[item, head, kind] = jnp.concatenate(
                    [stage[2 * kind, item, :, lanes], stage[2 * kind + 1, item, :, lanes]],
                    axis=1,
                )
        if at_once:
            send(item).start()
    if not at_once:
        for item in order:
            send(item).start()
    for item in order:
        send(item).wait()


def pack(me, arrays, start, heads, heads_here, peers, head_dim, apart, after):
    rows = arrays[0].shape[0]
    dtype = arrays[0].dtype
    shape = (heads, 2, rows, 2 * head_dim)
    width = (-(-heads * head_dim // LANES) + 1) * LANES
    anywhere = pl.BlockSpec(memory_space=pltpu.HBM)
    outs = message_outs(peers, shape, dtype, apart)
    return pl.pallas_call(
        functools.partial(
            pack_kernel,
            first=start * head_dim,
            heads=heads,
            peers=peers,
            apart=apart,
            per_peer=heads_here * head_dim,
            head_dim=head_dim,
        ),
        in_specs=[pl.BlockSpec(memory_space=pltpu.SMEM)]
        + [anywhere] * 4
        + [pl.BlockSpec(memory_space=pl.ANY)] * len(after),
        out_specs=[anywhere] * len(outs),
        out_shape=outs,
        scratch_shapes=[
            pltpu.VMEM((4, peers, rows, width), dtype),
            pltpu.VMEM((peers,) + shape, dtype),
            pltpu.SemaphoreType.DMA((4, peers)),
            pltpu.SemaphoreType.DMA((peers,)),
        ],
        compiler_params=pltpu.CompilerParams(vmem_limit_bytes=SMALL_VMEM),
        name="pack",
    )(me, *[in_hbm(x) for x in arrays], *after)


def unpack_kernel(me, *refs, chunk, peers, counts, earlier, jobs):
    ends = [sum(counts[: c + 1]) for c in range(chunk + 1)]
    groups = [refs[end - count : end] for end, count in zip(ends, counts)]
    outs = refs[ends[-1] + earlier :][:4]
    stages = refs[-3 - chunk - 1 : -3]
    ready, in_sems, out_sems = refs[-3:]
    head_dim = ready.shape[-1] // 2
    used = sorted({(which, peer) for job in jobs for which, peer, _ in job[1:]})
    chunks_used = sorted({which for which, _ in used})
    heads_used = {
        c: sorted({head for job in jobs for which, _, head in job[1:] if which == c})
        for c in chunks_used
    }

    def fetch(which, item, slot=None):
        heads = heads_used[which]
        some = pl.ds(heads[0], heads[-1] - heads[0] + 1)
        source, peer = part_of(groups[which], me, item)
        slot = peer if slot is None else slot
        return pltpu.make_async_copy(
            source.at[some], stages[which].at[slot, some], in_sems.at[which, slot]
        )

    def send(job, i):
        tile = jobs[job][0]
        return pltpu.make_async_copy(
            ready.at[i, job],
            outs[i].at[:, pl.ds(tile * LANES, LANES)],
            out_sems.at[4 * job + i],
        )

    for item in range(peers):
        for which in chunks_used:
            fetch(which, item).start()
    waited = set()

    def wait_for(which, peer):
        if (which, peer) not in waited:
            fetch(which, 0, peer).wait()
            waited.add((which, peer))

    for job, (tile, left, right) in enumerate(jobs):
        for which, peer, _ in (left, right):
            wait_for(which, peer)
        sides = [stages[which][peer, head] for which, peer, head in (left, right)]
        for i, (kind, at) in enumerate(((1, head_dim), (1, 0), (0, 0), (0, head_dim))):
            ready[i, job] = jnp.concatenate(
                [side[kind, :, at : at + head_dim] for side in sides], axis=1
            )
            send(job, i).start()
    for which in chunks_used:
        for peer in range(peers):
            wait_for(which, peer)
    for job in range(len(jobs)):
        for i in range(4):
            send(job, i).wait()


def unpack(me, messages, starts, heads_here, earlier):
    chunk = len(messages) - 1
    peers = lax.axis_size("seq")
    _, _, rows, pair_dim = message_shape(messages[0])
    head_dim = pair_dim // 2
    columns = peers * heads_here * head_dim
    dtype = messages[0][0].dtype

    def place_of(head):
        peer, local_head = divmod(head, heads_here)
        which = max(c for c, start in enumerate(starts) if start <= local_head)
        return which, peer, local_head - starts[which]

    jobs = []
    for tile in range(columns // LANES):
        left, right = place_of(2 * tile), place_of(2 * tile + 1)
        if max(left[0], right[0]) == chunk:
            jobs.append((tile, left, right))
    if not jobs:
        return earlier
    flat = [x for group in messages for x in group]
    anywhere = pl.BlockSpec(memory_space=pltpu.HBM)
    return pl.pallas_call(
        functools.partial(
            unpack_kernel,
            chunk=chunk,
            peers=peers,
            counts=[len(group) for group in messages],
            earlier=len(earlier),
            jobs=jobs,
        ),
        in_specs=[pl.BlockSpec(memory_space=pltpu.SMEM)]
        + [anywhere] * (len(flat) + len(earlier)),
        out_specs=[anywhere] * 4,
        out_shape=[pltpu.HBM((rows, columns), dtype)] * 4,
        input_output_aliases={1 + len(flat) + i: i for i in range(len(earlier))},
        scratch_shapes=[pltpu.VMEM((peers,) + message_shape(m), dtype) for m in messages]
        + [
            pltpu.VMEM((4, len(jobs), rows, LANES), dtype),
            pltpu.SemaphoreType.DMA((chunk + 1, peers)),
            pltpu.SemaphoreType.DMA((4 * len(jobs),)),
        ],
        compiler_params=pltpu.CompilerParams(vmem_limit_bytes=SMALL_VMEM),
        name="unpack",
    )(me, *[in_hbm(x) for x in (*flat, *earlier)])


def pick_kernel(me, asked, *refs, count, block_rows):
    for_next, for_prev, stage, sems = refs[-4:]
    peers, _, rows, _ = stage.shape
    each = rows // block_rows

    def fetch(item):
        source, peer = part_of(refs[:count], me, item)
        return pltpu.make_async_copy(source.at[:, 0], stage.at[peer], sems.at[item])

    for item in range(peers):
        fetch(item).start()
    for item in range(peers):
        fetch(item).wait()
    for i in range(2 * CROSS):
        target = for_next if i < CROSS else for_prev
        peer = lax.div(asked[i], each)
        start = pl.multiple_of(lax.rem(asked[i], each) * block_rows, block_rows)
        target[i % CROSS] = stage[peer, :, pl.ds(start, block_rows)]


def pick(me, messages, asked, block_rows, after):
    heads, _, rows, lanes = message_shape(messages)
    dtype = messages[0].dtype
    peers = lax.axis_size("seq")
    picked = jax.ShapeDtypeStruct((CROSS, heads, block_rows, lanes), dtype)
    return pl.pallas_call(
        functools.partial(pick_kernel, count=len(messages), block_rows=block_rows),
        in_specs=[pl.BlockSpec(memory_space=pltpu.SMEM)] * 2
        + [pl.BlockSpec(memory_space=pltpu.HBM)] * (len(messages) + len(after)),
        out_specs=[pl.BlockSpec(memory_space=pltpu.VMEM)] * 2,
        out_shape=[picked, picked],
        scratch_shapes=[
            pltpu.VMEM((peers, heads, rows, lanes), dtype),
            pltpu.SemaphoreType.DMA((peers,)),
        ],
        compiler_params=pltpu.CompilerParams(vmem_limit_bytes=SMALL_VMEM),
        name="pick",
    )(me, asked, *[in_hbm(x) for x in (*messages, *after)])


def attend_kernel(me, lists, came_prev, came_next, *refs, block_rows, head_dim, per_list):
    messages = refs[:-13]
    back, own, to_prev, to_next = refs[-13:-9]
    message, table, turned, sums, both_even, both_odd, low_even, low_odd, sems = refs[-9:]
    peers, heads, _, rows, lanes = message.shape
    each = rows // block_rows
    blocks = peers * each
    window = blocks + 2 * CROSS
    units = heads * blocks
    keys = per_list * block_rows
    scaling = head_dim ** (-0.5)
    exponent = scaling * math.log2(math.e)
    both = (both_even, both_odd)
    low = (low_even, low_odd)
    step_rows = 64

    def fetch(item):
        source, peer = part_of(messages, me, item)
        return pltpu.make_async_copy(source, message.at[peer], sems.at[item])

    for item in range(peers):
        fetch(item).start()
    for item in range(peers):
        fetch(item).wait()
    for head in range(heads):
        for i in range(CROSS):
            table[head, i] = came_prev[i, head]
            table[head, CROSS + blocks + i] = came_next[i, head]

        def fill(peer, carry):
            for i in range(each):
                table[head, CROSS + peer * each + i] = message[
                    peer, head, 0, i * block_rows : (i + 1) * block_rows
                ]
            return carry

        lax.fori_loop(0, peers, fill, 0)

        def turn(i, carry):
            turned[head, i] = table[head, i].T
            sums[head, i] = jnp.zeros(sums.shape[2:], sums.dtype)
            return carry

        lax.fori_loop(0, window, turn, 0)

    left = lax.broadcasted_iota(jnp.int32, (block_rows, lanes), 1) < head_dim

    def locate(unit):
        head = lax.div(unit, blocks)
        block = lax.rem(unit, blocks)
        ids = [lists[head, block, j] for j in range(per_list)]
        peer = lax.div(block, each)
        start = pl.multiple_of(lax.rem(block, each) * block_rows, block_rows)
        return head, ids, peer, pl.ds(start, block_rows)

    def apart_of(head, peer, here):
        query_grad = message[peer, head, 1, here]
        nothing = jnp.zeros_like(query_grad)
        return jnp.concatenate(
            [jnp.where(left, query_grad, nothing), jnp.where(left, nothing, query_grad)],
            axis=0,
        )

    def score(unit, slot):
        head, ids, peer, here = locate(unit)
        key_value = jnp.concatenate([table[head, i] for i in ids], axis=0)
        both[slot][...] = lax.dot_general(
            key_value,
            apart_of(head, peer, here),
            (((1,), (1,)), ((), ())),
            preferred_element_type=jnp.float32,
        )

    def soften(slot):
        source, target = both[slot], low[slot]
        parts = [slice(i, i + step_rows) for i in range(0, keys, step_rows)]
        top = source[parts[0], :block_rows]
        for part in parts[1:]:
            top = jnp.maximum(top, source[part, :block_rows])
        top = jnp.max(top, axis=0, keepdims=True)
        total = jnp.zeros((step_rows, block_rows), jnp.float32)
        mixed = jnp.zeros((step_rows, block_rows), jnp.float32)
        for part in parts:
            raised = jnp.exp2((source[part, :block_rows] - top) * exponent)
            source[part, :block_rows] = raised
            total += raised
            mixed += raised * source[part, block_rows:]
        inverse = 1.0 / jnp.sum(total, axis=0, keepdims=True)
        correction = jnp.sum(mixed, axis=0, keepdims=True) * inverse
        for part in parts:
            weights = source[part, :block_rows] * inverse
            target[part, block_rows:] = weights.astype(jnp.bfloat16)
            target[part, :block_rows] = (
                weights * (source[part, block_rows:] - correction)
            ).astype(jnp.bfloat16)

    def combine(unit, slot):
        head, ids, peer, here = locate(unit)
        products = low[slot][...]
        terms = jnp.dot(
            products, apart_of(head, peer, here), preferred_element_type=jnp.float32
        )
        for j, i in enumerate(ids):
            sums[head, i] += terms[j * block_rows : (j + 1) * block_rows]
        key_value = jnp.concatenate([turned[head, i] for i in ids], axis=1)
        out = jnp.dot(key_value, products, preferred_element_type=jnp.float32)
        out = jnp.concatenate(
            [out[:head_dim, :block_rows] * scaling, out[head_dim:, block_rows:]], axis=0
        )
        back[peer, head, here] = out.T.astype(back.dtype)

    score(0, 0)
    score(1, 1)
    soften(0)

    def step(i, carry):
        for slot in range(2):
            unit = 2 * i + slot
            combine(unit - 2, slot)
            score(unit, slot)
            soften(1 - slot)
        return carry

    lax.fori_loop(1, units // 2, step, 0)
    combine(units - 2, 0)
    soften(1)
    combine(units - 1, 1)

    factor = jnp.where(left, scaling, 1.0)
    for head in range(heads):
        for i in range(CROSS):
            to_prev[i, head] = (sums[head, i] * factor).astype(to_prev.dtype)
            to_next[i, head] = (sums[head, CROSS + blocks + i] * factor).astype(to_next.dtype)

        def finish(i, carry):
            own[head, i] = sums[head, CROSS + i] * factor
            return carry

        lax.fori_loop(0, blocks, finish, 0)


def attend(me, messages, came_prev, came_next, lists, block_rows):
    shape = message_shape(messages)
    heads, _, rows, lanes = shape
    dtype = messages[0].dtype
    peers = lax.axis_size("seq")
    per_list = lists.shape[-1]
    keys = per_list * block_rows
    blocks = peers * rows // block_rows
    window = blocks + 2 * CROSS
    inside = pl.BlockSpec(memory_space=pltpu.VMEM)
    scalars = pl.BlockSpec(memory_space=pltpu.SMEM)
    cross_shape = jax.ShapeDtypeStruct(came_prev.shape, dtype)
    return pl.pallas_call(
        functools.partial(
            attend_kernel, block_rows=block_rows, head_dim=lanes // 2, per_list=per_list
        ),
        in_specs=[scalars, scalars, inside, inside]
        + [pl.BlockSpec(memory_space=pltpu.HBM)] * len(messages),
        out_specs=[inside] * 4,
        out_shape=[
            pltpu.VMEM((peers, heads, rows, lanes), dtype),
            pltpu.VMEM((heads, blocks, block_rows, lanes), jnp.float32),
            cross_shape,
            cross_shape,
        ],
        scratch_shapes=[
            pltpu.VMEM((peers,) + shape, dtype),
            pltpu.VMEM((heads, window, block_rows, lanes), dtype),
            pltpu.VMEM((heads, window, lanes, block_rows), dtype),
            pltpu.VMEM((heads, window, block_rows, lanes), jnp.float32),
            pltpu.VMEM((keys, 2 * block_rows), jnp.float32),
            pltpu.VMEM((keys, 2 * block_rows), jnp.float32),
            pltpu.VMEM((keys, 2 * block_rows), dtype),
            pltpu.VMEM((keys, 2 * block_rows), dtype),
            pltpu.SemaphoreType.DMA((peers,)),
        ],
        compiler_params=pltpu.CompilerParams(vmem_limit_bytes=LARGE_VMEM),
        name="attend",
    )(me, lists, came_prev, came_next, *[in_hbm(x) for x in messages])


def finish_kernel(me, asked, back, own, later, earlier, *refs, block_rows):
    messages = refs[:-3]
    sums, ready, sems = refs[-3:]
    peers, heads, _, rows, _ = ready.shape
    each = rows // block_rows

    def send(item, head):
        target, peer = part_of(messages, me, item)
        return pltpu.make_async_copy(
            ready.at[peer, head], target.at[head], sems.at[item, head]
        )

    for head in range(heads):
        sums[...] = own[head]
        for i in range(CROSS):
            sums[asked[i]] += later[i, head].astype(jnp.float32)
        for i in range(CROSS):
            sums[asked[CROSS + i]] += earlier[i, head].astype(jnp.float32)
        for peer in range(peers):
            ready[peer, head, 1] = back[peer, head]
            for i in range(each):
                ready[peer, head, 0, i * block_rows : (i + 1) * block_rows] = sums[
                    peer * each + i
                ].astype(ready.dtype)
        for item in range(peers - 1, -1, -1):
            send(item, head).start()
    for head in range(heads):
        for item in range(peers):
            send(item, head).wait()


def finish(me, back, own, later, earlier, asked, apart):
    peers, heads, rows, lanes = back.shape
    _, blocks, block_rows, _ = own.shape
    inside = pl.BlockSpec(memory_space=pltpu.VMEM)
    scalars = pl.BlockSpec(memory_space=pltpu.SMEM)
    shape = (heads, 2, rows, lanes)
    outs = message_outs(peers, shape, back.dtype, apart)
    return pl.pallas_call(
        functools.partial(finish_kernel, block_rows=block_rows),
        in_specs=[scalars, scalars] + [inside] * 4,
        out_specs=[pl.BlockSpec(memory_space=pltpu.HBM)] * len(outs),
        out_shape=outs,
        scratch_shapes=[
            pltpu.VMEM((blocks, block_rows, lanes), jnp.float32),
            pltpu.VMEM((peers,) + shape, back.dtype),
            pltpu.SemaphoreType.DMA((peers, heads)),
        ],
        compiler_params=pltpu.CompilerParams(vmem_limit_bytes=SMALL_VMEM),
        name="finish",
    )(
        me,
        asked,
        pltpu.with_memory_space_constraint(back, pltpu.VMEM),
        pltpu.with_memory_space_constraint(own, pltpu.VMEM),
        later,
        earlier,
    )


def local(query, key, value, d_out, pattern):
    heads_here, blocks, _ = pattern.shape
    peers = lax.axis_size("seq")
    rows, columns = query.shape
    head_dim = columns // (peers * heads_here)
    block_rows = rows * peers // blocks
    chunks = min(CHUNKS, heads_here)
    starts = [-(-heads_here * i // chunks) for i in range(chunks)]
    sizes = [end - start for start, end in zip(starts, starts[1:] + [heads_here])]
    arrays = (query, key, value, d_out)

    own_base = lax.axis_index("slab") * blocks
    block_ids = jnp.arange(blocks, dtype=jnp.int32)
    flat_lists = pattern.reshape(-1)
    reverse_rank = blocks - 1 - block_ids
    hits_prev = jnp.any(flat_lists[:, None] == (own_base - blocks + block_ids)[None, :], axis=0)
    hits_next = jnp.any(flat_lists[:, None] == (own_base + blocks + block_ids)[None, :], axis=0)
    need_prev = lax.top_k(hits_prev.astype(jnp.int32) * blocks + reverse_rank, CROSS)[1]
    need_next = lax.top_k(hits_next.astype(jnp.int32) * blocks + reverse_rank, CROSS)[1]
    asked_next = from_behind(need_prev, "slab", -1)
    asked_prev = from_behind(need_next, "slab", 1)
    asked = jnp.concatenate([asked_next, asked_prev])
    rank_ids = jnp.arange(CROSS, dtype=jnp.int32)
    prev_global = own_base - blocks + need_prev
    next_global = own_base + blocks + need_next
    pos_prev = jnp.sum(jnp.where(pattern[..., None] == prev_global, rank_ids, 0), axis=-1)
    pos_next = jnp.sum(jnp.where(pattern[..., None] == next_global, rank_ids, 0), axis=-1)
    in_own = (pattern >= own_base) & (pattern < own_base + blocks)
    local_ids = jnp.where(
        in_own,
        CROSS + pattern - own_base,
        jnp.where(pattern < own_base, pos_prev, CROSS + blocks + pos_next),
    )

    me = lax.axis_index("seq").astype(jnp.int32).reshape(1)
    me = lax.axis_index("seq").astype(jnp.int32).reshape(1)
    last = chunks - 1
    came = []
    for chunk, (start, size) in enumerate(zip(starts, sizes)):
        after = (asked, local_ids) if came else ()
        packed = pack(
            me, arrays, start, size, heads_here, peers, head_dim, chunk == 0, after
        )
        if chunk == 1:
            packed = hold(packed, came[0][1:])
        came.append(exchange(packed))
    received = []
    outs = finished = ()
    for chunk, (messages, start, size) in enumerate(zip(came, starts, sizes)):
        for_next, for_prev = pick(me, messages, asked, block_rows, finished[:1])
        came_prev = from_behind(for_next, "slab", 1)
        came_next = from_behind(for_prev, "slab", -1)
        back, own, to_prev, to_next = attend(
            me, messages, came_prev, came_next, local_ids[start : start + size], block_rows
        )
        later = from_behind(to_prev, "slab", -1)
        earlier = from_behind(to_next, "slab", 1)
        finished = finish(me, back, own, later, earlier, asked, chunk == last)
        received.append(exchange(finished))
        outs = unpack(me, received, starts, heads_here, outs)
    return tuple(outs)


def solution(mesh):
    tokens = P(("slab", "seq"), None)
    return jax.shard_map(
        local,
        mesh=mesh,
        in_specs=(tokens, tokens, tokens, tokens, P("seq", "slab", None)),
        out_specs=(tokens, tokens, tokens, tokens),
        check_vma=False,
    )
```

```python
import functools
import math

import jax
import jax.numpy as jnp
from jax import lax
from jax.experimental import pallas as pl
from jax.experimental.pallas import tpu as pltpu
from jax.sharding import PartitionSpec as P

CROSS = 4
CHUNKS = 2
LANES = 128
SMALL_VMEM = 24 * 1024 * 1024
LARGE_VMEM = 40 * 1024 * 1024


def in_hbm(x):
    return pltpu.with_memory_space_constraint(x, pltpu.HBM)


def from_behind(x, axis, by):
    count = lax.axis_size(axis)
    pairs = [(i, i + by) for i in range(count) if 0 <= i + by < count]
    return lax.ppermute(x, axis, pairs)


def part_of(messages, me, item):
    if len(messages) == 1:
        return messages[0].at[item], item
    return messages[item], me[0] ^ (len(messages) - 1 - item)


def message_shape(messages):
    return messages[0].shape[-4:]


def message_outs(peers, shape, dtype, apart):
    if apart:
        return [pltpu.HBM(shape, dtype)] * peers
    return [pltpu.HBM((peers,) + shape, dtype)]


def hold_kernel(*refs):
    del refs


def hold(arrays, after):
    count = len(arrays)
    anywhere = pl.BlockSpec(memory_space=pltpu.HBM)
    return pl.pallas_call(
        hold_kernel,
        in_specs=[anywhere] * (count + len(after)),
        out_specs=[anywhere] * count,
        out_shape=[pltpu.HBM(x.shape, x.dtype) for x in arrays],
        input_output_aliases={i: i for i in range(count)},
        name="hold",
    )(*[in_hbm(x) for x in (*arrays, *after)])


def exchange(messages):
    if len(messages) == 1:
        return [lax.all_to_all(messages[0], "seq", split_axis=0, concat_axis=0, tiled=True)]
    count = len(messages)
    received = list(messages)
    for item in range(count - 1):
        pairs = [(i, i ^ (count - 1 - item)) for i in range(count)]
        received[item] = lax.ppermute(messages[item], "seq", pairs)
    return received


def pack_kernel(
    me, query, key, value, d_out, *refs, first, heads, peers, apart, per_peer, head_dim
):
    messages = refs[-4 - (peers if apart else 1) : -4]
    stage, ready, in_sems, out_sems = refs[-4:]
    sources = (key, value, query, d_out)
    aligned = apart and per_peer % LANES == 0
    at_once = aligned or not apart
    order = range(peers)

    def span(item):
        if aligned:
            base, begin = pl.multiple_of(part_of(messages, me, item)[1] * per_peer, LANES), first
        else:
            base, begin = 0, item * per_peer + first
        low = begin // LANES * LANES
        high = -(-(begin + heads * head_dim) // LANES) * LANES
        return base + low, high - low, begin - low

    def fetch(item, i):
        low, width, _ = span(item)
        return pltpu.make_async_copy(
            sources[i].at[:, pl.ds(low, width)],
            stage.at[i, item, :, pl.ds(0, width)],
            in_sems.at[i, item],
        )

    def send(item):
        target, peer = part_of(messages, me, item)
        return pltpu.make_async_copy(
            ready.at[item if aligned else peer], target, out_sems.at[item]
        )

    for item in order:
        for i in range(4):
            fetch(item, i).start()
    for item in order:
        for i in range(4):
            fetch(item, i).wait()
        at = span(item)[2]
        for head in range(heads):
            lanes = slice(at + head * head_dim, at + (head + 1) * head_dim)
            for kind in range(2):
                ready[item, head, kind] = jnp.concatenate(
                    [stage[2 * kind, item, :, lanes], stage[2 * kind + 1, item, :, lanes]],
                    axis=1,
                )
        if at_once:
            send(item).start()
    if not at_once:
        for item in order:
            send(item).start()
    for item in order:
        send(item).wait()


def pack(me, arrays, start, heads, heads_here, peers, head_dim, apart, after):
    rows = arrays[0].shape[0]
    dtype = arrays[0].dtype
    shape = (heads, 2, rows, 2 * head_dim)
    width = (-(-heads * head_dim // LANES) + 1) * LANES
    anywhere = pl.BlockSpec(memory_space=pltpu.HBM)
    outs = message_outs(peers, shape, dtype, apart)
    return pl.pallas_call(
        functools.partial(
            pack_kernel,
            first=start * head_dim,
            heads=heads,
            peers=peers,
            apart=apart,
            per_peer=heads_here * head_dim,
            head_dim=head_dim,
        ),
        in_specs=[pl.BlockSpec(memory_space=pltpu.SMEM)]
        + [anywhere] * 4
        + [pl.BlockSpec(memory_space=pl.ANY)] * len(after),
        out_specs=[anywhere] * len(outs),
        out_shape=outs,
        scratch_shapes=[
            pltpu.VMEM((4, peers, rows, width), dtype),
            pltpu.VMEM((peers,) + shape, dtype),
            pltpu.SemaphoreType.DMA((4, peers)),
            pltpu.SemaphoreType.DMA((peers,)),
        ],
        compiler_params=pltpu.CompilerParams(vmem_limit_bytes=SMALL_VMEM),
        name="pack",
    )(me, *[in_hbm(x) for x in arrays], *after)


def unpack_kernel(me, *refs, chunk, peers, counts, earlier, jobs):
    ends = [sum(counts[: c + 1]) for c in range(chunk + 1)]
    groups = [refs[end - count : end] for end, count in zip(ends, counts)]
    outs = refs[ends[-1] + earlier :][:4]
    stages = refs[-3 - chunk - 1 : -3]
    ready, in_sems, out_sems = refs[-3:]
    head_dim = ready.shape[-1] // 2
    used = sorted({(which, peer) for job in jobs for which, peer, _ in job[1:]})
    chunks_used = sorted({which for which, _ in used})
    heads_used = {
        c: sorted({head for job in jobs for which, _, head in job[1:] if which == c})
        for c in chunks_used
    }

    def fetch(which, item, slot=None):
        heads = heads_used[which]
        some = pl.ds(heads[0], heads[-1] - heads[0] + 1)
        source, peer = part_of(groups[which], me, item)
        slot = peer if slot is None else slot
        return pltpu.make_async_copy(
            source.at[some], stages[which].at[slot, some], in_sems.at[which, slot]
        )

    def send(job, i):
        tile = jobs[job][0]
        return pltpu.make_async_copy(
            ready.at[i, job],
            outs[i].at[:, pl.ds(tile * LANES, LANES)],
            out_sems.at[4 * job + i],
        )

    for item in range(peers):
        for which in chunks_used:
            fetch(which, item).start()
    waited = set()

    def wait_for(which, peer):
        if (which, peer) not in waited:
            fetch(which, 0, peer).wait()
            waited.add((which, peer))

    for job, (tile, left, right) in enumerate(jobs):
        for which, peer, _ in (left, right):
            wait_for(which, peer)
        sides = [stages[which][peer, head] for which, peer, head in (left, right)]
        for i, (kind, at) in enumerate(((1, head_dim), (1, 0), (0, 0), (0, head_dim))):
            ready[i, job] = jnp.concatenate(
                [side[kind, :, at : at + head_dim] for side in sides], axis=1
            )
            send(job, i).start()
    for which in chunks_used:
        for peer in range(peers):
            wait_for(which, peer)
    for job in range(len(jobs)):
        for i in range(4):
            send(job, i).wait()


def unpack(me, messages, starts, heads_here, earlier):
    chunk = len(messages) - 1
    peers = lax.axis_size("seq")
    _, _, rows, pair_dim = message_shape(messages[0])
    head_dim = pair_dim // 2
    columns = peers * heads_here * head_dim
    dtype = messages[0][0].dtype

    def place_of(head):
        peer, local_head = divmod(head, heads_here)
        which = max(c for c, start in enumerate(starts) if start <= local_head)
        return which, peer, local_head - starts[which]

    jobs = []
    for tile in range(columns // LANES):
        left, right = place_of(2 * tile), place_of(2 * tile + 1)
        if max(left[0], right[0]) == chunk:
            jobs.append((tile, left, right))
    if not jobs:
        return earlier
    flat = [x for group in messages for x in group]
    anywhere = pl.BlockSpec(memory_space=pltpu.HBM)
    return pl.pallas_call(
        functools.partial(
            unpack_kernel,
            chunk=chunk,
            peers=peers,
            counts=[len(group) for group in messages],
            earlier=len(earlier),
            jobs=jobs,
        ),
        in_specs=[pl.BlockSpec(memory_space=pltpu.SMEM)]
        + [anywhere] * (len(flat) + len(earlier)),
        out_specs=[anywhere] * 4,
        out_shape=[pltpu.HBM((rows, columns), dtype)] * 4,
        input_output_aliases={1 + len(flat) + i: i for i in range(len(earlier))},
        scratch_shapes=[pltpu.VMEM((peers,) + message_shape(m), dtype) for m in messages]
        + [
            pltpu.VMEM((4, len(jobs), rows, LANES), dtype),
            pltpu.SemaphoreType.DMA((chunk + 1, peers)),
            pltpu.SemaphoreType.DMA((4 * len(jobs),)),
        ],
        compiler_params=pltpu.CompilerParams(vmem_limit_bytes=SMALL_VMEM),
        name="unpack",
    )(me, *[in_hbm(x) for x in (*flat, *earlier)])


def pick_kernel(me, asked, *refs, count, block_rows):
    for_next, for_prev, stage, sems = refs[-4:]
    peers, _, rows, _ = stage.shape
    each = rows // block_rows

    def fetch(item):
        source, peer = part_of(refs[:count], me, item)
        return pltpu.make_async_copy(source.at[:, 0], stage.at[peer], sems.at[item])

    for item in range(peers):
        fetch(item).start()
    for item in range(peers):
        fetch(item).wait()
    for i in range(2 * CROSS):
        target = for_next if i < CROSS else for_prev
        peer = lax.div(asked[i], each)
        start = pl.multiple_of(lax.rem(asked[i], each) * block_rows, block_rows)
        target[i % CROSS] = stage[peer, :, pl.ds(start, block_rows)]


def pick(me, messages, asked, block_rows, after):
    heads, _, rows, lanes = message_shape(messages)
    dtype = messages[0].dtype
    peers = lax.axis_size("seq")
    picked = jax.ShapeDtypeStruct((CROSS, heads, block_rows, lanes), dtype)
    return pl.pallas_call(
        functools.partial(pick_kernel, count=len(messages), block_rows=block_rows),
        in_specs=[pl.BlockSpec(memory_space=pltpu.SMEM)] * 2
        + [pl.BlockSpec(memory_space=pltpu.HBM)] * (len(messages) + len(after)),
        out_specs=[pl.BlockSpec(memory_space=pltpu.VMEM)] * 2,
        out_shape=[picked, picked],
        scratch_shapes=[
            pltpu.VMEM((peers, heads, rows, lanes), dtype),
            pltpu.SemaphoreType.DMA((peers,)),
        ],
        compiler_params=pltpu.CompilerParams(vmem_limit_bytes=SMALL_VMEM),
        name="pick",
    )(me, asked, *[in_hbm(x) for x in (*messages, *after)])


def attend_kernel(me, lists, came_prev, came_next, *refs, block_rows, head_dim, per_list):
    messages = refs[:-13]
    back, own, to_prev, to_next = refs[-13:-9]
    message, table, turned, sums, both_even, both_odd, low_even, low_odd, sems = refs[-9:]
    peers, heads, _, rows, lanes = message.shape
    each = rows // block_rows
    blocks = peers * each
    window = blocks + 2 * CROSS
    units = heads * blocks
    keys = per_list * block_rows
    scaling = head_dim ** (-0.5)
    exponent = scaling * math.log2(math.e)
    both = (both_even, both_odd)
    low = (low_even, low_odd)
    step_rows = 64

    def fetch(item):
        source, peer = part_of(messages, me, item)
        return pltpu.make_async_copy(source, message.at[peer], sems.at[item])

    for item in range(peers):
        fetch(item).start()
    for item in range(peers):
        fetch(item).wait()
    for head in range(heads):
        for i in range(CROSS):
            table[head, i] = came_prev[i, head]
            table[head, CROSS + blocks + i] = came_next[i, head]

        def fill(peer, carry):
            for i in range(each):
                table[head, CROSS + peer * each + i] = message[
                    peer, head, 0, i * block_rows : (i + 1) * block_rows
                ]
            return carry

        lax.fori_loop(0, peers, fill, 0)

        def turn(i, carry):
            turned[head, i] = table[head, i].T
            sums[head, i] = jnp.zeros(sums.shape[2:], sums.dtype)
            return carry

        lax.fori_loop(0, window, turn, 0)

    left = lax.broadcasted_iota(jnp.int32, (block_rows, lanes), 1) < head_dim

    def locate(unit):
        head = lax.div(unit, blocks)
        block = lax.rem(unit, blocks)
        ids = [lists[head, block, j] for j in range(per_list)]
        peer = lax.div(block, each)
        start = pl.multiple_of(lax.rem(block, each) * block_rows, block_rows)
        return head, ids, peer, pl.ds(start, block_rows)

    def apart_of(head, peer, here):
        query_grad = message[peer, head, 1, here]
        nothing = jnp.zeros_like(query_grad)
        return jnp.concatenate(
            [jnp.where(left, query_grad, nothing), jnp.where(left, nothing, query_grad)],
            axis=0,
        )

    def score(unit, slot):
        head, ids, peer, here = locate(unit)
        key_value = jnp.concatenate([table[head, i] for i in ids], axis=0)
        both[slot][...] = lax.dot_general(
            key_value,
            apart_of(head, peer, here),
            (((1,), (1,)), ((), ())),
            preferred_element_type=jnp.float32,
        )

    def soften(slot):
        source, target = both[slot], low[slot]
        parts = [slice(i, i + step_rows) for i in range(0, keys, step_rows)]
        top = source[parts[0], :block_rows]
        for part in parts[1:]:
            top = jnp.maximum(top, source[part, :block_rows])
        top = jnp.max(top, axis=0, keepdims=True)
        total = jnp.zeros((step_rows, block_rows), jnp.float32)
        mixed = jnp.zeros((step_rows, block_rows), jnp.float32)
        for part in parts:
            raised = jnp.exp2((source[part, :block_rows] - top) * exponent)
            source[part, :block_rows] = raised
            total += raised
            mixed += raised * source[part, block_rows:]
        inverse = 1.0 / jnp.sum(total, axis=0, keepdims=True)
        correction = jnp.sum(mixed, axis=0, keepdims=True) * inverse
        for part in parts:
            weights = source[part, :block_rows] * inverse
            target[part, block_rows:] = weights.astype(jnp.bfloat16)
            target[part, :block_rows] = (
                weights * (source[part, block_rows:] - correction)
            ).astype(jnp.bfloat16)

    def combine(unit, slot):
        head, ids, peer, here = locate(unit)
        products = low[slot][...]
        terms = jnp.dot(
            products, apart_of(head, peer, here), preferred_element_type=jnp.float32
        )
        for j, i in enumerate(ids):
            sums[head, i] += terms[j * block_rows : (j + 1) * block_rows]
        key_value = jnp.concatenate([turned[head, i] for i in ids], axis=1)
        out = jnp.dot(key_value, products, preferred_element_type=jnp.float32)
        out = jnp.concatenate(
            [out[:head_dim, :block_rows] * scaling, out[head_dim:, block_rows:]], axis=0
        )
        back[peer, head, here] = out.T.astype(back.dtype)

    score(0, 0)
    score(1, 1)
    soften(0)

    def step(i, carry):
        for slot in range(2):
            unit = 2 * i + slot
            combine(unit - 2, slot)
            score(unit, slot)
            soften(1 - slot)
        return carry

    lax.fori_loop(1, units // 2, step, 0)
    combine(units - 2, 0)
    soften(1)
    combine(units - 1, 1)

    factor = jnp.where(left, scaling, 1.0)
    for head in range(heads):
        for i in range(CROSS):
            to_prev[i, head] = (sums[head, i] * factor).astype(to_prev.dtype)
            to_next[i, head] = (sums[head, CROSS + blocks + i] * factor).astype(to_next.dtype)

        def finish(i, carry):
            own[head, i] = sums[head, CROSS + i] * factor
            return carry

        lax.fori_loop(0, blocks, finish, 0)


def attend(me, messages, came_prev, came_next, lists, block_rows):
    shape = message_shape(messages)
    heads, _, rows, lanes = shape
    dtype = messages[0].dtype
    peers = lax.axis_size("seq")
    per_list = lists.shape[-1]
    keys = per_list * block_rows
    blocks = peers * rows // block_rows
    window = blocks + 2 * CROSS
    inside = pl.BlockSpec(memory_space=pltpu.VMEM)
    scalars = pl.BlockSpec(memory_space=pltpu.SMEM)
    cross_shape = jax.ShapeDtypeStruct(came_prev.shape, dtype)
    return pl.pallas_call(
        functools.partial(
            attend_kernel, block_rows=block_rows, head_dim=lanes // 2, per_list=per_list
        ),
        in_specs=[scalars, scalars, inside, inside]
        + [pl.BlockSpec(memory_space=pltpu.HBM)] * len(messages),
        out_specs=[inside] * 4,
        out_shape=[
            pltpu.VMEM((peers, heads, rows, lanes), dtype),
            pltpu.VMEM((heads, blocks, block_rows, lanes), jnp.float32),
            cross_shape,
            cross_shape,
        ],
        scratch_shapes=[
            pltpu.VMEM((peers,) + shape, dtype),
            pltpu.VMEM((heads, window, block_rows, lanes), dtype),
            pltpu.VMEM((heads, window, lanes, block_rows), dtype),
            pltpu.VMEM((heads, window, block_rows, lanes), jnp.float32),
            pltpu.VMEM((keys, 2 * block_rows), jnp.float32),
            pltpu.VMEM((keys, 2 * block_rows), jnp.float32),
            pltpu.VMEM((keys, 2 * block_rows), dtype),
            pltpu.VMEM((keys, 2 * block_rows), dtype),
            pltpu.SemaphoreType.DMA((peers,)),
        ],
        compiler_params=pltpu.CompilerParams(vmem_limit_bytes=LARGE_VMEM),
        name="attend",
    )(me, lists, came_prev, came_next, *[in_hbm(x) for x in messages])


def finish_kernel(me, asked, back, own, later, earlier, *refs, block_rows):
    messages = refs[:-3]
    sums, ready, sems = refs[-3:]
    peers, heads, _, rows, _ = ready.shape
    each = rows // block_rows

    def send(item, head):
        target, peer = part_of(messages, me, item)
        return pltpu.make_async_copy(
            ready.at[peer, head], target.at[head], sems.at[item, head]
        )

    for head in range(heads):
        sums[...] = own[head]
        for i in range(CROSS):
            sums[asked[i]] += later[i, head].astype(jnp.float32)
        for i in range(CROSS):
            sums[asked[CROSS + i]] += earlier[i, head].astype(jnp.float32)
        for peer in range(peers):
            ready[peer, head, 1] = back[peer, head]
            for i in range(each):
                ready[peer, head, 0, i * block_rows : (i + 1) * block_rows] = sums[
                    peer * each + i
                ].astype(ready.dtype)
        for item in range(peers):
            send(item, head).start()
    for head in range(heads):
        for item in range(peers):
            send(item, head).wait()


def finish(me, back, own, later, earlier, asked, apart):
    peers, heads, rows, lanes = back.shape
    _, blocks, block_rows, _ = own.shape
    inside = pl.BlockSpec(memory_space=pltpu.VMEM)
    scalars = pl.BlockSpec(memory_space=pltpu.SMEM)
    shape = (heads, 2, rows, lanes)
    outs = message_outs(peers, shape, back.dtype, apart)
    return pl.pallas_call(
        functools.partial(finish_kernel, block_rows=block_rows),
        in_specs=[scalars, scalars] + [inside] * 4,
        out_specs=[pl.BlockSpec(memory_space=pltpu.HBM)] * len(outs),
        out_shape=outs,
        scratch_shapes=[
            pltpu.VMEM((blocks, block_rows, lanes), jnp.float32),
            pltpu.VMEM((peers,) + shape, back.dtype),
            pltpu.SemaphoreType.DMA((peers, heads)),
        ],
        compiler_params=pltpu.CompilerParams(vmem_limit_bytes=SMALL_VMEM),
        name="finish",
    )(
        me,
        asked,
        pltpu.with_memory_space_constraint(back, pltpu.VMEM),
        pltpu.with_memory_space_constraint(own, pltpu.VMEM),
        later,
        earlier,
    )


def local(query, key, value, d_out, pattern):
    heads_here, blocks, _ = pattern.shape
    peers = lax.axis_size("seq")
    rows, columns = query.shape
    head_dim = columns // (peers * heads_here)
    block_rows = rows * peers // blocks
    chunks = min(CHUNKS, heads_here)
    starts = [-(-heads_here * i // chunks) for i in range(chunks)]
    sizes = [end - start for start, end in zip(starts, starts[1:] + [heads_here])]
    arrays = (query, key, value, d_out)

    own_base = lax.axis_index("slab") * blocks
    block_ids = jnp.arange(blocks, dtype=jnp.int32)
    flat_lists = pattern.reshape(-1)
    reverse_rank = blocks - 1 - block_ids
    hits_prev = jnp.any(flat_lists[:, None] == (own_base - blocks + block_ids)[None, :], axis=0)
    hits_next = jnp.any(flat_lists[:, None] == (own_base + blocks + block_ids)[None, :], axis=0)
    need_prev = lax.top_k(hits_prev.astype(jnp.int32) * blocks + reverse_rank, CROSS)[1]
    need_next = lax.top_k(hits_next.astype(jnp.int32) * blocks + reverse_rank, CROSS)[1]
    asked_next = from_behind(need_prev, "slab", -1)
    asked_prev = from_behind(need_next, "slab", 1)
    asked = jnp.concatenate([asked_next, asked_prev])
    rank_ids = jnp.arange(CROSS, dtype=jnp.int32)
    prev_global = own_base - blocks + need_prev
    next_global = own_base + blocks + need_next
    pos_prev = jnp.sum(jnp.where(pattern[..., None] == prev_global, rank_ids, 0), axis=-1)
    pos_next = jnp.sum(jnp.where(pattern[..., None] == next_global, rank_ids, 0), axis=-1)
    in_own = (pattern >= own_base) & (pattern < own_base + blocks)
    local_ids = jnp.where(
        in_own,
        CROSS + pattern - own_base,
        jnp.where(pattern < own_base, pos_prev, CROSS + blocks + pos_next),
    )

    me = lax.axis_index("seq").astype(jnp.int32).reshape(1)
    me = lax.axis_index("seq").astype(jnp.int32).reshape(1)
    last = chunks - 1
    came = []
    for chunk, (start, size) in enumerate(zip(starts, sizes)):
        after = (asked, local_ids) if came else ()
        packed = pack(
            me, arrays, start, size, heads_here, peers, head_dim, chunk == 0, after
        )
        if chunk == 1:
            packed = hold(packed, came[0][:-1])
        came.append(exchange(packed))
    received = []
    outs = finished = ()
    for chunk, (messages, start, size) in enumerate(zip(came, starts, sizes)):
        for_next, for_prev = pick(me, messages, asked, block_rows, finished[:1])
        came_prev = from_behind(for_next, "slab", 1)
        came_next = from_behind(for_prev, "slab", -1)
        back, own, to_prev, to_next = attend(
            me, messages, came_prev, came_next, local_ids[start : start + size], block_rows
        )
        later = from_behind(to_prev, "slab", -1)
        earlier = from_behind(to_next, "slab", 1)
        finished = finish(me, back, own, later, earlier, asked, chunk == last)
        received.append(exchange(finished))
        outs = unpack(me, received, starts, heads_here, outs)
    return tuple(outs)


def solution(mesh):
    tokens = P(("slab", "seq"), None)
    return jax.shard_map(
        local,
        mesh=mesh,
        in_specs=(tokens, tokens, tokens, tokens, P("seq", "slab", None)),
        out_specs=(tokens, tokens, tokens, tokens),
        check_vma=False,
    )
```

```python
import functools
import math

import jax
import jax.numpy as jnp
from jax import lax
from jax.experimental import pallas as pl
from jax.experimental.pallas import tpu as pltpu
from jax.sharding import PartitionSpec as P

CROSS = 4
CHUNKS = 2
LANES = 128
SMALL_VMEM = 24 * 1024 * 1024
LARGE_VMEM = 40 * 1024 * 1024


def in_hbm(x):
    return pltpu.with_memory_space_constraint(x, pltpu.HBM)


def from_behind(x, axis, by):
    count = lax.axis_size(axis)
    pairs = [(i, i + by) for i in range(count) if 0 <= i + by < count]
    return lax.ppermute(x, axis, pairs)


def part_of(messages, me, item):
    far = len(messages) - 1
    if far == 0:
        return messages[0].at[item], item
    if item < far:
        return messages[item], me[0] ^ (2 * far - 1 - item)
    return messages[far].at[item - far], lax.div(me[0], far) * far + item - far


def message_shape(messages):
    return messages[0].shape[-4:]


def message_outs(peers, shape, dtype, apart):
    if apart:
        far = peers // 2
        return [pltpu.HBM(shape, dtype)] * far + [pltpu.HBM((far,) + shape, dtype)]
    return [pltpu.HBM((peers,) + shape, dtype)]


def hold_kernel(*refs):
    del refs


def hold(arrays, after):
    count = len(arrays)
    anywhere = pl.BlockSpec(memory_space=pltpu.HBM)
    return pl.pallas_call(
        hold_kernel,
        in_specs=[anywhere] * (count + len(after)),
        out_specs=[anywhere] * count,
        out_shape=[pltpu.HBM(x.shape, x.dtype) for x in arrays],
        input_output_aliases={i: i for i in range(count)},
        name="hold",
    )(*[in_hbm(x) for x in (*arrays, *after)])


def exchange(messages):
    far = len(messages) - 1
    if far == 0:
        return [lax.all_to_all(messages[0], "seq", split_axis=0, concat_axis=0, tiled=True)]
    peers = range(2 * far)
    received = [
        lax.ppermute(messages[item], "seq", [(i, i ^ (2 * far - 1 - item)) for i in peers])
        for item in range(far)
    ]
    halves = [list(peers[:far]), list(peers[far:])]
    near = lax.all_to_all(
        messages[far],
        "seq",
        split_axis=0,
        concat_axis=0,
        axis_index_groups=halves,
        tiled=True,
    )
    return received + [near]


def pack_kernel(
    me, query, key, value, d_out, *refs, first, heads, peers, apart, per_peer, head_dim
):
    messages = refs[-4 - (peers // 2 + 1 if apart else 1) : -4]
    stage, ready, in_sems, out_sems = refs[-4:]
    sources = (key, value, query, d_out)
    aligned = apart and per_peer % LANES == 0
    at_once = aligned or not apart
    order = range(peers)

    def span(item):
        if aligned:
            base, begin = pl.multiple_of(part_of(messages, me, item)[1] * per_peer, LANES), first
        else:
            base, begin = 0, item * per_peer + first
        low = begin // LANES * LANES
        high = -(-(begin + heads * head_dim) // LANES) * LANES
        return base + low, high - low, begin - low

    def fetch(item, i):
        low, width, _ = span(item)
        return pltpu.make_async_copy(
            sources[i].at[:, pl.ds(low, width)],
            stage.at[i, item, :, pl.ds(0, width)],
            in_sems.at[i, item],
        )

    def send(item):
        target, peer = part_of(messages, me, item)
        return pltpu.make_async_copy(
            ready.at[item if aligned else peer], target, out_sems.at[item]
        )

    for item in order:
        for i in range(4):
            fetch(item, i).start()
    for item in order:
        for i in range(4):
            fetch(item, i).wait()
        at = span(item)[2]
        for head in range(heads):
            lanes = slice(at + head * head_dim, at + (head + 1) * head_dim)
            for kind in range(2):
                ready[item, head, kind] = jnp.concatenate(
                    [stage[2 * kind, item, :, lanes], stage[2 * kind + 1, item, :, lanes]],
                    axis=1,
                )
        if at_once:
            send(item).start()
    if not at_once:
        for item in order:
            send(item).start()
    for item in order:
        send(item).wait()


def pack(me, arrays, start, heads, heads_here, peers, head_dim, apart, after):
    rows = arrays[0].shape[0]
    dtype = arrays[0].dtype
    shape = (heads, 2, rows, 2 * head_dim)
    width = (-(-heads * head_dim // LANES) + 1) * LANES
    anywhere = pl.BlockSpec(memory_space=pltpu.HBM)
    outs = message_outs(peers, shape, dtype, apart)
    return pl.pallas_call(
        functools.partial(
            pack_kernel,
            first=start * head_dim,
            heads=heads,
            peers=peers,
            apart=apart,
            per_peer=heads_here * head_dim,
            head_dim=head_dim,
        ),
        in_specs=[pl.BlockSpec(memory_space=pltpu.SMEM)]
        + [anywhere] * 4
        + [pl.BlockSpec(memory_space=pl.ANY)] * len(after),
        out_specs=[anywhere] * len(outs),
        out_shape=outs,
        scratch_shapes=[
            pltpu.VMEM((4, peers, rows, width), dtype),
            pltpu.VMEM((peers,) + shape, dtype),
            pltpu.SemaphoreType.DMA((4, peers)),
            pltpu.SemaphoreType.DMA((peers,)),
        ],
        compiler_params=pltpu.CompilerParams(vmem_limit_bytes=SMALL_VMEM),
        name="pack",
    )(me, *[in_hbm(x) for x in arrays], *after)


def unpack_kernel(me, *refs, chunk, peers, counts, earlier, jobs):
    ends = [sum(counts[: c + 1]) for c in range(chunk + 1)]
    groups = [refs[end - count : end] for end, count in zip(ends, counts)]
    outs = refs[ends[-1] + earlier :][:4]
    stages = refs[-3 - chunk - 1 : -3]
    ready, in_sems, out_sems = refs[-3:]
    head_dim = ready.shape[-1] // 2
    used = sorted({(which, peer) for job in jobs for which, peer, _ in job[1:]})
    chunks_used = sorted({which for which, _ in used})
    heads_used = {
        c: sorted({head for job in jobs for which, _, head in job[1:] if which == c})
        for c in chunks_used
    }

    def fetch(which, item, slot=None):
        heads = heads_used[which]
        some = pl.ds(heads[0], heads[-1] - heads[0] + 1)
        source, peer = part_of(groups[which], me, item)
        slot = peer if slot is None else slot
        return pltpu.make_async_copy(
            source.at[some], stages[which].at[slot, some], in_sems.at[which, slot]
        )

    def send(job, i):
        tile = jobs[job][0]
        return pltpu.make_async_copy(
            ready.at[i, job],
            outs[i].at[:, pl.ds(tile * LANES, LANES)],
            out_sems.at[4 * job + i],
        )

    for item in range(peers):
        for which in chunks_used:
            fetch(which, item).start()
    waited = set()

    def wait_for(which, peer):
        if (which, peer) not in waited:
            fetch(which, 0, peer).wait()
            waited.add((which, peer))

    for job, (tile, left, right) in enumerate(jobs):
        for which, peer, _ in (left, right):
            wait_for(which, peer)
        sides = [stages[which][peer, head] for which, peer, head in (left, right)]
        for i, (kind, at) in enumerate(((1, head_dim), (1, 0), (0, 0), (0, head_dim))):
            ready[i, job] = jnp.concatenate(
                [side[kind, :, at : at + head_dim] for side in sides], axis=1
            )
            send(job, i).start()
    for which in chunks_used:
        for peer in range(peers):
            wait_for(which, peer)
    for job in range(len(jobs)):
        for i in range(4):
            send(job, i).wait()


def unpack(me, messages, starts, heads_here, earlier):
    chunk = len(messages) - 1
    peers = lax.axis_size("seq")
    _, _, rows, pair_dim = message_shape(messages[0])
    head_dim = pair_dim // 2
    columns = peers * heads_here * head_dim
    dtype = messages[0][0].dtype

    def place_of(head):
        peer, local_head = divmod(head, heads_here)
        which = max(c for c, start in enumerate(starts) if start <= local_head)
        return which, peer, local_head - starts[which]

    jobs = []
    for tile in range(columns // LANES):
        left, right = place_of(2 * tile), place_of(2 * tile + 1)
        if max(left[0], right[0]) == chunk:
            jobs.append((tile, left, right))
    if not jobs:
        return earlier
    flat = [x for group in messages for x in group]
    anywhere = pl.BlockSpec(memory_space=pltpu.HBM)
    return pl.pallas_call(
        functools.partial(
            unpack_kernel,
            chunk=chunk,
            peers=peers,
            counts=[len(group) for group in messages],
            earlier=len(earlier),
            jobs=jobs,
        ),
        in_specs=[pl.BlockSpec(memory_space=pltpu.SMEM)]
        + [anywhere] * (len(flat) + len(earlier)),
        out_specs=[anywhere] * 4,
        out_shape=[pltpu.HBM((rows, columns), dtype)] * 4,
        input_output_aliases={1 + len(flat) + i: i for i in range(len(earlier))},
        scratch_shapes=[pltpu.VMEM((peers,) + message_shape(m), dtype) for m in messages]
        + [
            pltpu.VMEM((4, len(jobs), rows, LANES), dtype),
            pltpu.SemaphoreType.DMA((chunk + 1, peers)),
            pltpu.SemaphoreType.DMA((4 * len(jobs),)),
        ],
        compiler_params=pltpu.CompilerParams(vmem_limit_bytes=SMALL_VMEM),
        name="unpack",
    )(me, *[in_hbm(x) for x in (*flat, *earlier)])


def pick_kernel(me, asked, *refs, count, block_rows):
    for_next, for_prev, stage, sems = refs[-4:]
    peers, _, rows, _ = stage.shape
    each = rows // block_rows

    def fetch(item):
        source, peer = part_of(refs[:count], me, item)
        return pltpu.make_async_copy(source.at[:, 0], stage.at[peer], sems.at[item])

    for item in range(peers):
        fetch(item).start()
    for item in range(peers):
        fetch(item).wait()
    for i in range(2 * CROSS):
        target = for_next if i < CROSS else for_prev
        peer = lax.div(asked[i], each)
        start = pl.multiple_of(lax.rem(asked[i], each) * block_rows, block_rows)
        target[i % CROSS] = stage[peer, :, pl.ds(start, block_rows)]


def pick(me, messages, asked, block_rows, after):
    heads, _, rows, lanes = message_shape(messages)
    dtype = messages[0].dtype
    peers = lax.axis_size("seq")
    picked = jax.ShapeDtypeStruct((CROSS, heads, block_rows, lanes), dtype)
    return pl.pallas_call(
        functools.partial(pick_kernel, count=len(messages), block_rows=block_rows),
        in_specs=[pl.BlockSpec(memory_space=pltpu.SMEM)] * 2
        + [pl.BlockSpec(memory_space=pltpu.HBM)] * (len(messages) + len(after)),
        out_specs=[pl.BlockSpec(memory_space=pltpu.VMEM)] * 2,
        out_shape=[picked, picked],
        scratch_shapes=[
            pltpu.VMEM((peers, heads, rows, lanes), dtype),
            pltpu.SemaphoreType.DMA((peers,)),
        ],
        compiler_params=pltpu.CompilerParams(vmem_limit_bytes=SMALL_VMEM),
        name="pick",
    )(me, asked, *[in_hbm(x) for x in (*messages, *after)])


def attend_kernel(me, lists, came_prev, came_next, *refs, block_rows, head_dim, per_list):
    messages = refs[:-13]
    back, own, to_prev, to_next = refs[-13:-9]
    message, table, turned, sums, both_even, both_odd, low_even, low_odd, sems = refs[-9:]
    peers, heads, _, rows, lanes = message.shape
    each = rows // block_rows
    blocks = peers * each
    window = blocks + 2 * CROSS
    units = heads * blocks
    keys = per_list * block_rows
    scaling = head_dim ** (-0.5)
    exponent = scaling * math.log2(math.e)
    both = (both_even, both_odd)
    low = (low_even, low_odd)
    step_rows = 64

    def fetch(item):
        source, peer = part_of(messages, me, item)
        return pltpu.make_async_copy(source, message.at[peer], sems.at[item])

    for item in range(peers):
        fetch(item).start()
    for item in range(peers):
        fetch(item).wait()
    for head in range(heads):
        for i in range(CROSS):
            table[head, i] = came_prev[i, head]
            table[head, CROSS + blocks + i] = came_next[i, head]

        def fill(peer, carry):
            for i in range(each):
                table[head, CROSS + peer * each + i] = message[
                    peer, head, 0, i * block_rows : (i + 1) * block_rows
                ]
            return carry

        lax.fori_loop(0, peers, fill, 0)

        def turn(i, carry):
            turned[head, i] = table[head, i].T
            sums[head, i] = jnp.zeros(sums.shape[2:], sums.dtype)
            return carry

        lax.fori_loop(0, window, turn, 0)

    left = lax.broadcasted_iota(jnp.int32, (block_rows, lanes), 1) < head_dim

    def locate(unit):
        head = lax.div(unit, blocks)
        block = lax.rem(unit, blocks)
        ids = [lists[head, block, j] for j in range(per_list)]
        peer = lax.div(block, each)
        start = pl.multiple_of(lax.rem(block, each) * block_rows, block_rows)
        return head, ids, peer, pl.ds(start, block_rows)

    def apart_of(head, peer, here):
        query_grad = message[peer, head, 1, here]
        nothing = jnp.zeros_like(query_grad)
        return jnp.concatenate(
            [jnp.where(left, query_grad, nothing), jnp.where(left, nothing, query_grad)],
            axis=0,
        )

    def score(unit, slot):
        head, ids, peer, here = locate(unit)
        key_value = jnp.concatenate([table[head, i] for i in ids], axis=0)
        both[slot][...] = lax.dot_general(
            key_value,
            apart_of(head, peer, here),
            (((1,), (1,)), ((), ())),
            preferred_element_type=jnp.float32,
        )

    def soften(slot):
        source, target = both[slot], low[slot]
        parts = [slice(i, i + step_rows) for i in range(0, keys, step_rows)]
        top = source[parts[0], :block_rows]
        for part in parts[1:]:
            top = jnp.maximum(top, source[part, :block_rows])
        top = jnp.max(top, axis=0, keepdims=True)
        total = jnp.zeros((step_rows, block_rows), jnp.float32)
        mixed = jnp.zeros((step_rows, block_rows), jnp.float32)
        for part in parts:
            raised = jnp.exp2((source[part, :block_rows] - top) * exponent)
            source[part, :block_rows] = raised
            total += raised
            mixed += raised * source[part, block_rows:]
        inverse = 1.0 / jnp.sum(total, axis=0, keepdims=True)
        correction = jnp.sum(mixed, axis=0, keepdims=True) * inverse
        for part in parts:
            weights = source[part, :block_rows] * inverse
            target[part, block_rows:] = weights.astype(jnp.bfloat16)
            target[part, :block_rows] = (
                weights * (source[part, block_rows:] - correction)
            ).astype(jnp.bfloat16)

    def combine(unit, slot):
        head, ids, peer, here = locate(unit)
        products = low[slot][...]
        terms = jnp.dot(
            products, apart_of(head, peer, here), preferred_element_type=jnp.float32
        )
        for j, i in enumerate(ids):
            sums[head, i] += terms[j * block_rows : (j + 1) * block_rows]
        key_value = jnp.concatenate([turned[head, i] for i in ids], axis=1)
        out = jnp.dot(key_value, products, preferred_element_type=jnp.float32)
        out = jnp.concatenate(
            [out[:head_dim, :block_rows] * scaling, out[head_dim:, block_rows:]], axis=0
        )
        back[peer, head, here] = out.T.astype(back.dtype)

    score(0, 0)
    score(1, 1)
    soften(0)

    def step(i, carry):
        for slot in range(2):
            unit = 2 * i + slot
            combine(unit - 2, slot)
            score(unit, slot)
            soften(1 - slot)
        return carry

    lax.fori_loop(1, units // 2, step, 0)
    combine(units - 2, 0)
    soften(1)
    combine(units - 1, 1)

    factor = jnp.where(left, scaling, 1.0)
    for head in range(heads):
        for i in range(CROSS):
            to_prev[i, head] = (sums[head, i] * factor).astype(to_prev.dtype)
            to_next[i, head] = (sums[head, CROSS + blocks + i] * factor).astype(to_next.dtype)

        def finish(i, carry):
            own[head, i] = sums[head, CROSS + i] * factor
            return carry

        lax.fori_loop(0, blocks, finish, 0)


def attend(me, messages, came_prev, came_next, lists, block_rows):
    shape = message_shape(messages)
    heads, _, rows, lanes = shape
    dtype = messages[0].dtype
    peers = lax.axis_size("seq")
    per_list = lists.shape[-1]
    keys = per_list * block_rows
    blocks = peers * rows // block_rows
    window = blocks + 2 * CROSS
    inside = pl.BlockSpec(memory_space=pltpu.VMEM)
    scalars = pl.BlockSpec(memory_space=pltpu.SMEM)
    cross_shape = jax.ShapeDtypeStruct(came_prev.shape, dtype)
    return pl.pallas_call(
        functools.partial(
            attend_kernel, block_rows=block_rows, head_dim=lanes // 2, per_list=per_list
        ),
        in_specs=[scalars, scalars, inside, inside]
        + [pl.BlockSpec(memory_space=pltpu.HBM)] * len(messages),
        out_specs=[inside] * 4,
        out_shape=[
            pltpu.VMEM((peers, heads, rows, lanes), dtype),
            pltpu.VMEM((heads, blocks, block_rows, lanes), jnp.float32),
            cross_shape,
            cross_shape,
        ],
        scratch_shapes=[
            pltpu.VMEM((peers,) + shape, dtype),
            pltpu.VMEM((heads, window, block_rows, lanes), dtype),
            pltpu.VMEM((heads, window, lanes, block_rows), dtype),
            pltpu.VMEM((heads, window, block_rows, lanes), jnp.float32),
            pltpu.VMEM((keys, 2 * block_rows), jnp.float32),
            pltpu.VMEM((keys, 2 * block_rows), jnp.float32),
            pltpu.VMEM((keys, 2 * block_rows), dtype),
            pltpu.VMEM((keys, 2 * block_rows), dtype),
            pltpu.SemaphoreType.DMA((peers,)),
        ],
        compiler_params=pltpu.CompilerParams(vmem_limit_bytes=LARGE_VMEM),
        name="attend",
    )(me, lists, came_prev, came_next, *[in_hbm(x) for x in messages])


def finish_kernel(me, asked, back, own, later, earlier, *refs, block_rows):
    messages = refs[:-3]
    sums, ready, sems = refs[-3:]
    peers, heads, _, rows, _ = ready.shape
    each = rows // block_rows

    def send(item, head):
        target, peer = part_of(messages, me, item)
        return pltpu.make_async_copy(
            ready.at[peer, head], target.at[head], sems.at[item, head]
        )

    for head in range(heads):
        sums[...] = own[head]
        for i in range(CROSS):
            sums[asked[i]] += later[i, head].astype(jnp.float32)
        for i in range(CROSS):
            sums[asked[CROSS + i]] += earlier[i, head].astype(jnp.float32)
        for peer in range(peers):
            ready[peer, head, 1] = back[peer, head]
            for i in range(each):
                ready[peer, head, 0, i * block_rows : (i + 1) * block_rows] = sums[
                    peer * each + i
                ].astype(ready.dtype)
        for item in range(peers):
            send(item, head).start()
    for head in range(heads):
        for item in range(peers):
            send(item, head).wait()


def finish(me, back, own, later, earlier, asked, apart):
    peers, heads, rows, lanes = back.shape
    _, blocks, block_rows, _ = own.shape
    inside = pl.BlockSpec(memory_space=pltpu.VMEM)
    scalars = pl.BlockSpec(memory_space=pltpu.SMEM)
    shape = (heads, 2, rows, lanes)
    outs = message_outs(peers, shape, back.dtype, apart)
    return pl.pallas_call(
        functools.partial(finish_kernel, block_rows=block_rows),
        in_specs=[scalars, scalars] + [inside] * 4,
        out_specs=[pl.BlockSpec(memory_space=pltpu.HBM)] * len(outs),
        out_shape=outs,
        scratch_shapes=[
            pltpu.VMEM((blocks, block_rows, lanes), jnp.float32),
            pltpu.VMEM((peers,) + shape, back.dtype),
            pltpu.SemaphoreType.DMA((peers, heads)),
        ],
        compiler_params=pltpu.CompilerParams(vmem_limit_bytes=SMALL_VMEM),
        name="finish",
    )(
        me,
        asked,
        pltpu.with_memory_space_constraint(back, pltpu.VMEM),
        pltpu.with_memory_space_constraint(own, pltpu.VMEM),
        later,
        earlier,
    )


def local(query, key, value, d_out, pattern):
    heads_here, blocks, _ = pattern.shape
    peers = lax.axis_size("seq")
    rows, columns = query.shape
    head_dim = columns // (peers * heads_here)
    block_rows = rows * peers // blocks
    chunks = min(CHUNKS, heads_here)
    starts = [-(-heads_here * i // chunks) for i in range(chunks)]
    sizes = [end - start for start, end in zip(starts, starts[1:] + [heads_here])]
    arrays = (query, key, value, d_out)

    own_base = lax.axis_index("slab") * blocks
    block_ids = jnp.arange(blocks, dtype=jnp.int32)
    flat_lists = pattern.reshape(-1)
    reverse_rank = blocks - 1 - block_ids
    hits_prev = jnp.any(flat_lists[:, None] == (own_base - blocks + block_ids)[None, :], axis=0)
    hits_next = jnp.any(flat_lists[:, None] == (own_base + blocks + block_ids)[None, :], axis=0)
    need_prev = lax.top_k(hits_prev.astype(jnp.int32) * blocks + reverse_rank, CROSS)[1]
    need_next = lax.top_k(hits_next.astype(jnp.int32) * blocks + reverse_rank, CROSS)[1]
    asked_next = from_behind(need_prev, "slab", -1)
    asked_prev = from_behind(need_next, "slab", 1)
    asked = jnp.concatenate([asked_next, asked_prev])
    rank_ids = jnp.arange(CROSS, dtype=jnp.int32)
    prev_global = own_base - blocks + need_prev
    next_global = own_base + blocks + need_next
    pos_prev = jnp.sum(jnp.where(pattern[..., None] == prev_global, rank_ids, 0), axis=-1)
    pos_next = jnp.sum(jnp.where(pattern[..., None] == next_global, rank_ids, 0), axis=-1)
    in_own = (pattern >= own_base) & (pattern < own_base + blocks)
    local_ids = jnp.where(
        in_own,
        CROSS + pattern - own_base,
        jnp.where(pattern < own_base, pos_prev, CROSS + blocks + pos_next),
    )

    me = lax.axis_index("seq").astype(jnp.int32).reshape(1)
    me = lax.axis_index("seq").astype(jnp.int32).reshape(1)
    last = chunks - 1
    came = []
    for chunk, (start, size) in enumerate(zip(starts, sizes)):
        after = (asked, local_ids) if came else ()
        packed = pack(
            me, arrays, start, size, heads_here, peers, head_dim, chunk == 0, after
        )
        if chunk == 1:
            packed = hold(packed, came[0][: peers // 4])
        came.append(exchange(packed))
    received = []
    outs = finished = ()
    for chunk, (messages, start, size) in enumerate(zip(came, starts, sizes)):
        for_next, for_prev = pick(me, messages, asked, block_rows, finished[:1])
        came_prev = from_behind(for_next, "slab", 1)
        came_next = from_behind(for_prev, "slab", -1)
        back, own, to_prev, to_next = attend(
            me, messages, came_prev, came_next, local_ids[start : start + size], block_rows
        )
        later = from_behind(to_prev, "slab", -1)
        earlier = from_behind(to_next, "slab", 1)
        finished = finish(me, back, own, later, earlier, asked, chunk == last)
        received.append(exchange(finished))
        outs = unpack(me, received, starts, heads_here, outs)
    return tuple(outs)


def solution(mesh):
    tokens = P(("slab", "seq"), None)
    return jax.shard_map(
        local,
        mesh=mesh,
        in_specs=(tokens, tokens, tokens, tokens, P("seq", "slab", None)),
        out_specs=(tokens, tokens, tokens, tokens),
        check_vma=False,
    )
```

```python
import functools
import math

import jax
import jax.numpy as jnp
from jax import lax
from jax.experimental import pallas as pl
from jax.experimental.pallas import tpu as pltpu
from jax.sharding import PartitionSpec as P

CROSS = 4
CHUNKS = 2
LANES = 128
SMALL_VMEM = 24 * 1024 * 1024
LARGE_VMEM = 40 * 1024 * 1024


def in_hbm(x):
    return pltpu.with_memory_space_constraint(x, pltpu.HBM)


def in_vmem(x):
    return pltpu.with_memory_space_constraint(x, pltpu.VMEM)


def from_behind(x, axis, by):
    count = lax.axis_size(axis)
    pairs = [(i, i + by) for i in range(count) if 0 <= i + by < count]
    return lax.ppermute(x, axis, pairs)


def part_of(messages, me, item):
    if len(messages) == 1:
        return messages[0].at[item], item
    return messages[item], me[0] ^ (len(messages) - 1 - item)


def message_shape(messages):
    return messages[0].shape[-4:]


def message_outs(peers, shape, dtype, apart):
    if apart:
        return [pltpu.HBM(shape, dtype)] * peers
    return [pltpu.HBM((peers,) + shape, dtype)]


def hold_kernel(*refs):
    del refs


def hold(arrays, after):
    count = len(arrays)
    anywhere = pl.BlockSpec(memory_space=pltpu.HBM)
    return pl.pallas_call(
        hold_kernel,
        in_specs=[anywhere] * (count + len(after)),
        out_specs=[anywhere] * count,
        out_shape=[pltpu.HBM(x.shape, x.dtype) for x in arrays],
        input_output_aliases={i: i for i in range(count)},
        name="hold",
    )(*[in_hbm(x) for x in (*arrays, *after)])


def exchange(messages):
    if len(messages) == 1:
        return [lax.all_to_all(messages[0], "seq", split_axis=0, concat_axis=0, tiled=True)]
    count = len(messages)
    received = list(messages)
    for item in range(count - 1):
        pairs = [(i, i ^ (count - 1 - item)) for i in range(count)]
        received[item] = lax.ppermute(messages[item], "seq", pairs)
    return received


def pack_kernel(
    me, query, key, value, d_out, *refs, first, heads, items, apart, per_peer, head_dim
):
    messages = refs[-4 - (len(items) if apart else 1) : -4]
    stage, ready, in_sems, out_sems = refs[-4:]
    sources = (key, value, query, d_out)
    aligned = apart and per_peer % LANES == 0
    at_once = aligned or not apart
    peers = stage.shape[1]

    def place_of(item):
        if apart:
            return messages[item - items[0]], me[0] ^ (peers - 1 - item)
        return messages[0].at[item], item

    def span(item):
        if aligned:
            base, begin = pl.multiple_of(place_of(item)[1] * per_peer, LANES), first
        else:
            base, begin = 0, item * per_peer + first
        low = begin // LANES * LANES
        high = -(-(begin + heads * head_dim) // LANES) * LANES
        return base + low, high - low, begin - low

    def fetch(item, i):
        low, width, _ = span(item)
        return pltpu.make_async_copy(
            sources[i].at[:, pl.ds(low, width)],
            stage.at[i, item, :, pl.ds(0, width)],
            in_sems.at[i, item],
        )

    def send(item):
        target, peer = place_of(item)
        return pltpu.make_async_copy(
            ready.at[item if aligned else peer], target, out_sems.at[item]
        )

    made = items if at_once else range(peers)
    for item in made:
        for i in range(4):
            fetch(item, i).start()
    for item in made:
        for i in range(4):
            fetch(item, i).wait()
        at = span(item)[2]
        for head in range(heads):
            lanes = slice(at + head * head_dim, at + (head + 1) * head_dim)
            for kind in range(2):
                ready[item, head, kind] = jnp.concatenate(
                    [stage[2 * kind, item, :, lanes], stage[2 * kind + 1, item, :, lanes]],
                    axis=1,
                )
        if at_once:
            send(item).start()
    if not at_once:
        for item in items:
            send(item).start()
    for item in items:
        send(item).wait()


def pack(me, arrays, start, heads, heads_here, peers, head_dim, apart, after):
    rows = arrays[0].shape[0]
    dtype = arrays[0].dtype
    shape = (heads, 2, rows, 2 * head_dim)
    width = (-(-heads * head_dim // LANES) + 1) * LANES
    anywhere = pl.BlockSpec(memory_space=pltpu.HBM)
    outs = message_outs(peers, shape, dtype, apart)
    return pl.pallas_call(
        functools.partial(
            pack_kernel,
            first=start * head_dim,
            heads=heads,
            items=range(peers),
            apart=apart,
            per_peer=heads_here * head_dim,
            head_dim=head_dim,
        ),
        in_specs=[pl.BlockSpec(memory_space=pltpu.SMEM)]
        + [anywhere] * 4
        + [pl.BlockSpec(memory_space=pl.ANY)] * len(after),
        out_specs=[anywhere] * len(outs),
        out_shape=outs,
        scratch_shapes=[
            pltpu.VMEM((4, peers, rows, width), dtype),
            pltpu.VMEM((peers,) + shape, dtype),
            pltpu.SemaphoreType.DMA((4, peers)),
            pltpu.SemaphoreType.DMA((peers,)),
        ],
        compiler_params=pltpu.CompilerParams(vmem_limit_bytes=SMALL_VMEM),
        name="pack",
    )(me, *[in_hbm(x) for x in arrays], *after)


def unpack_kernel(me, *refs, chunk, peers, counts, earlier, jobs):
    ends = [sum(counts[: c + 1]) for c in range(chunk + 1)]
    groups = [refs[end - count : end] for end, count in zip(ends, counts)]
    outs = refs[ends[-1] + earlier :][:4]
    stages = refs[-3 - chunk - 1 : -3]
    ready, in_sems, out_sems = refs[-3:]
    head_dim = ready.shape[-1] // 2
    used = sorted({(which, peer) for job in jobs for which, peer, _ in job[1:]})
    chunks_used = sorted({which for which, _ in used})
    heads_used = {
        c: sorted({head for job in jobs for which, _, head in job[1:] if which == c})
        for c in chunks_used
    }

    def fetch(which, item, slot=None):
        heads = heads_used[which]
        some = pl.ds(heads[0], heads[-1] - heads[0] + 1)
        source, peer = part_of(groups[which], me, item)
        slot = peer if slot is None else slot
        return pltpu.make_async_copy(
            source.at[some], stages[which].at[slot, some], in_sems.at[which, slot]
        )

    def send(job, i):
        tile = jobs[job][0]
        return pltpu.make_async_copy(
            ready.at[i, job],
            outs[i].at[:, pl.ds(tile * LANES, LANES)],
            out_sems.at[4 * job + i],
        )

    for item in range(peers):
        for which in chunks_used:
            fetch(which, item).start()
    waited = set()

    def wait_for(which, peer):
        if (which, peer) not in waited:
            fetch(which, 0, peer).wait()
            waited.add((which, peer))

    for job, (tile, left, right) in enumerate(jobs):
        for which, peer, _ in (left, right):
            wait_for(which, peer)
        sides = [stages[which][peer, head] for which, peer, head in (left, right)]
        for i, (kind, at) in enumerate(((1, head_dim), (1, 0), (0, 0), (0, head_dim))):
            ready[i, job] = jnp.concatenate(
                [side[kind, :, at : at + head_dim] for side in sides], axis=1
            )
            send(job, i).start()
    for which in chunks_used:
        for peer in range(peers):
            wait_for(which, peer)
    for job in range(len(jobs)):
        for i in range(4):
            send(job, i).wait()


def unpack(me, messages, starts, heads_here, earlier):
    chunk = len(messages) - 1
    peers = lax.axis_size("seq")
    _, _, rows, pair_dim = message_shape(messages[0])
    head_dim = pair_dim // 2
    columns = peers * heads_here * head_dim
    dtype = messages[0][0].dtype

    def place_of(head):
        peer, local_head = divmod(head, heads_here)
        which = max(c for c, start in enumerate(starts) if start <= local_head)
        return which, peer, local_head - starts[which]

    jobs = []
    for tile in range(columns // LANES):
        left, right = place_of(2 * tile), place_of(2 * tile + 1)
        if max(left[0], right[0]) == chunk:
            jobs.append((tile, left, right))
    if not jobs:
        return earlier
    flat = [x for group in messages for x in group]
    anywhere = pl.BlockSpec(memory_space=pltpu.HBM)
    return pl.pallas_call(
        functools.partial(
            unpack_kernel,
            chunk=chunk,
            peers=peers,
            counts=[len(group) for group in messages],
            earlier=len(earlier),
            jobs=jobs,
        ),
        in_specs=[pl.BlockSpec(memory_space=pltpu.SMEM)]
        + [anywhere] * (len(flat) + len(earlier)),
        out_specs=[anywhere] * 4,
        out_shape=[pltpu.HBM((rows, columns), dtype)] * 4,
        input_output_aliases={1 + len(flat) + i: i for i in range(len(earlier))},
        scratch_shapes=[pltpu.VMEM((peers,) + message_shape(m), dtype) for m in messages]
        + [
            pltpu.VMEM((4, len(jobs), rows, LANES), dtype),
            pltpu.SemaphoreType.DMA((chunk + 1, peers)),
            pltpu.SemaphoreType.DMA((4 * len(jobs),)),
        ],
        compiler_params=pltpu.CompilerParams(vmem_limit_bytes=SMALL_VMEM),
        name="unpack",
    )(me, *[in_hbm(x) for x in (*flat, *earlier)])


def pick_kernel(me, asked, *refs, count):
    for_next, for_prev, table, sems = refs[-4:]
    heads, window, block_rows, _ = table.shape
    peers, each = sems.shape

    def fetch(item, i):
        source, peer = part_of(refs[:count], me, item)
        rows = pl.ds(i * block_rows, block_rows)
        return pltpu.make_async_copy(
            source.at[:, 0, rows], table.at[:, CROSS + peer * each + i], sems.at[item, i]
        )

    for item in range(peers):
        for i in range(each):
            fetch(item, i).start()
    for item in range(peers):
        for i in range(each):
            fetch(item, i).wait()
    for i in range(CROSS):
        for_next[i] = table[:, CROSS + asked[i]]
        for_prev[i] = table[:, CROSS + asked[CROSS + i]]


def pick(me, messages, asked, block_rows, after):
    heads, _, rows, lanes = message_shape(messages)
    dtype = messages[0].dtype
    peers = lax.axis_size("seq")
    each = rows // block_rows
    window = peers * each + 2 * CROSS
    picked = jax.ShapeDtypeStruct((CROSS, heads, block_rows, lanes), dtype)
    return pl.pallas_call(
        functools.partial(pick_kernel, count=len(messages)),
        in_specs=[pl.BlockSpec(memory_space=pltpu.SMEM)] * 2
        + [pl.BlockSpec(memory_space=pltpu.HBM)] * (len(messages) + len(after)),
        out_specs=[pl.BlockSpec(memory_space=pltpu.VMEM)] * 3,
        out_shape=[picked, picked, pltpu.VMEM((heads, window, block_rows, lanes), dtype)],
        scratch_shapes=[pltpu.SemaphoreType.DMA((peers, each))],
        compiler_params=pltpu.CompilerParams(vmem_limit_bytes=SMALL_VMEM),
        name="pick",
    )(me, asked, *[in_hbm(x) for x in (*messages, *after)])


def prepare_kernel(me, table, *refs, peers):
    messages = refs[:-4]
    turned, pairs, sums, sems = refs[-4:]
    heads, window, _, _ = table.shape

    def fetch(item):
        source, peer = part_of(messages, me, item)
        return pltpu.make_async_copy(source.at[:, 1], pairs.at[peer], sems.at[item])

    for item in range(peers):
        fetch(item).start()
    for head in range(heads):

        def clear(i, carry):
            sums[head, i] = jnp.zeros(sums.shape[2:], sums.dtype)
            return carry

        def turn(i, carry):
            turned[head, i] = table[head, i].T
            return carry

        lax.fori_loop(0, window, clear, 0)
        lax.fori_loop(CROSS, window - CROSS, turn, 0)
    for item in range(peers):
        fetch(item).wait()


def prepare(me, messages, table):
    heads, _, rows, lanes = message_shape(messages)
    _, window, block_rows, _ = table.shape
    dtype = messages[0].dtype
    peers = lax.axis_size("seq")
    inside = pl.BlockSpec(memory_space=pltpu.VMEM)
    return pl.pallas_call(
        functools.partial(prepare_kernel, peers=peers),
        in_specs=[pl.BlockSpec(memory_space=pltpu.SMEM), inside]
        + [pl.BlockSpec(memory_space=pltpu.HBM)] * len(messages),
        out_specs=[inside] * 3,
        out_shape=[
            pltpu.VMEM((heads, window, lanes, block_rows), dtype),
            pltpu.VMEM((peers, heads, rows, lanes), dtype),
            pltpu.VMEM((heads, window, block_rows, lanes), jnp.float32),
        ],
        scratch_shapes=[pltpu.SemaphoreType.DMA((peers,))],
        compiler_params=pltpu.CompilerParams(vmem_limit_bytes=SMALL_VMEM),
        name="prepare",
    )(me, in_vmem(table), *[in_hbm(x) for x in messages])


def attend_kernel(
    lists,
    came_prev,
    came_next,
    pairs,
    table_in,
    turned_in,
    sums_in,
    back,
    to_prev,
    to_next,
    table,
    turned,
    sums,
    both_even,
    both_odd,
    low_even,
    low_odd,
    *,
    head_dim,
    per_list,
):
    del table_in, turned_in, sums_in
    peers, heads, rows, lanes = pairs.shape
    _, window, block_rows, _ = table.shape
    each = rows // block_rows
    blocks = peers * each
    units = heads * blocks
    keys = per_list * block_rows
    scaling = head_dim ** (-0.5)
    exponent = scaling * math.log2(math.e)
    both = (both_even, both_odd)
    low = (low_even, low_odd)
    step_rows = 64

    for head in range(heads):
        for i in range(CROSS):
            table[head, i] = came_prev[i, head]
            table[head, CROSS + blocks + i] = came_next[i, head]
            turned[head, i] = came_prev[i, head].T
            turned[head, CROSS + blocks + i] = came_next[i, head].T

    left = lax.broadcasted_iota(jnp.int32, (block_rows, lanes), 1) < head_dim

    def locate(unit):
        head = lax.div(unit, blocks)
        block = lax.rem(unit, blocks)
        ids = [lists[head, block, j] for j in range(per_list)]
        peer = lax.div(block, each)
        start = pl.multiple_of(lax.rem(block, each) * block_rows, block_rows)
        return head, ids, peer, pl.ds(start, block_rows)

    def apart_of(head, peer, here):
        query_grad = pairs[peer, head, here]
        nothing = jnp.zeros_like(query_grad)
        return jnp.concatenate(
            [jnp.where(left, query_grad, nothing), jnp.where(left, nothing, query_grad)],
            axis=0,
        )

    def score(unit, slot):
        head, ids, peer, here = locate(unit)
        key_value = jnp.concatenate([table[head, i] for i in ids], axis=0)
        both[slot][...] = lax.dot_general(
            key_value,
            apart_of(head, peer, here),
            (((1,), (1,)), ((), ())),
            preferred_element_type=jnp.float32,
        )

    def soften(slot):
        source, target = both[slot], low[slot]
        parts = [slice(i, i + step_rows) for i in range(0, keys, step_rows)]
        top = source[parts[0], :block_rows]
        for part in parts[1:]:
            top = jnp.maximum(top, source[part, :block_rows])
        top = jnp.max(top, axis=0, keepdims=True)
        total = jnp.zeros((step_rows, block_rows), jnp.float32)
        mixed = jnp.zeros((step_rows, block_rows), jnp.float32)
        for part in parts:
            raised = jnp.exp2((source[part, :block_rows] - top) * exponent)
            source[part, :block_rows] = raised
            total += raised
            mixed += raised * source[part, block_rows:]
        inverse = 1.0 / jnp.sum(total, axis=0, keepdims=True)
        correction = jnp.sum(mixed, axis=0, keepdims=True) * inverse
        for part in parts:
            weights = source[part, :block_rows] * inverse
            target[part, block_rows:] = weights.astype(jnp.bfloat16)
            target[part, :block_rows] = (
                weights * (source[part, block_rows:] - correction)
            ).astype(jnp.bfloat16)

    def combine(unit, slot):
        head, ids, peer, here = locate(unit)
        products = low[slot][...]
        terms = jnp.dot(
            products, apart_of(head, peer, here), preferred_element_type=jnp.float32
        )
        for j, i in enumerate(ids):
            sums[head, i] += terms[j * block_rows : (j + 1) * block_rows]
        key_value = jnp.concatenate([turned[head, i] for i in ids], axis=1)
        out = jnp.dot(key_value, products, preferred_element_type=jnp.float32)
        out = jnp.concatenate(
            [out[:head_dim, :block_rows] * scaling, out[head_dim:, block_rows:]], axis=0
        )
        back[peer, head, here] = out.T.astype(back.dtype)

    score(0, 0)
    score(1, 1)
    soften(0)

    def step(i, carry):
        for slot in range(2):
            unit = 2 * i + slot
            combine(unit - 2, slot)
            score(unit, slot)
            soften(1 - slot)
        return carry

    lax.fori_loop(1, units // 2, step, 0)
    combine(units - 2, 0)
    soften(1)
    combine(units - 1, 1)

    factor = jnp.where(left, scaling, 1.0)
    for head in range(heads):
        for i in range(CROSS):
            to_prev[i, head] = (sums[head, i] * factor).astype(to_prev.dtype)
            to_next[i, head] = (sums[head, CROSS + blocks + i] * factor).astype(to_next.dtype)


def attend(lists, came_prev, came_next, pairs, table, turned, sums):
    _, _, block_rows, lanes = came_prev.shape
    dtype = pairs.dtype
    per_list = lists.shape[-1]
    keys = per_list * block_rows
    inside = pl.BlockSpec(memory_space=pltpu.VMEM)
    cross_shape = jax.ShapeDtypeStruct(came_prev.shape, dtype)
    kept = (table, turned, sums)
    return pl.pallas_call(
        functools.partial(attend_kernel, head_dim=lanes // 2, per_list=per_list),
        in_specs=[pl.BlockSpec(memory_space=pltpu.SMEM)] + [inside] * 6,
        out_specs=[inside] * 6,
        out_shape=[pltpu.VMEM(pairs.shape, dtype), cross_shape, cross_shape]
        + [pltpu.VMEM(x.shape, x.dtype) for x in kept],
        input_output_aliases={4: 3, 5: 4, 6: 5},
        scratch_shapes=[
            pltpu.VMEM((keys, 2 * block_rows), jnp.float32),
            pltpu.VMEM((keys, 2 * block_rows), jnp.float32),
            pltpu.VMEM((keys, 2 * block_rows), dtype),
            pltpu.VMEM((keys, 2 * block_rows), dtype),
        ],
        compiler_params=pltpu.CompilerParams(vmem_limit_bytes=SMALL_VMEM),
        name="attend",
    )(lists, came_prev, came_next, *[in_vmem(x) for x in (pairs, *kept)])


def finish_kernel(me, asked, back, kept, later, earlier, *refs, block_rows):
    messages = refs[:-3]
    sums, ready, sems = refs[-3:]
    peers, heads, _, rows, lanes = ready.shape
    each = rows // block_rows
    blocks = peers * each
    head_dim = lanes // 2
    left = lax.broadcasted_iota(jnp.int32, (block_rows, lanes), 1) < head_dim
    factor = jnp.where(left, head_dim ** (-0.5), 1.0)

    def send(item, head):
        target, peer = part_of(messages, me, item)
        return pltpu.make_async_copy(
            ready.at[peer, head], target.at[head], sems.at[item, head]
        )

    for head in range(heads):
        sums[...] = kept[head, CROSS : CROSS + blocks] * factor
        for i in range(CROSS):
            sums[asked[i]] += later[i, head].astype(jnp.float32)
        for i in range(CROSS):
            sums[asked[CROSS + i]] += earlier[i, head].astype(jnp.float32)
        for peer in range(peers):
            ready[peer, head, 1] = back[peer, head]
            for i in range(each):
                ready[peer, head, 0, i * block_rows : (i + 1) * block_rows] = sums[
                    peer * each + i
                ].astype(ready.dtype)
        for item in range(peers):
            send(item, head).start()
    for head in range(heads):
        for item in range(peers):
            send(item, head).wait()


def finish(me, back, kept, later, earlier, asked, apart):
    peers, heads, rows, lanes = back.shape
    _, window, block_rows, _ = kept.shape
    blocks = window - 2 * CROSS
    inside = pl.BlockSpec(memory_space=pltpu.VMEM)
    scalars = pl.BlockSpec(memory_space=pltpu.SMEM)
    shape = (heads, 2, rows, lanes)
    outs = message_outs(peers, shape, back.dtype, apart)
    return pl.pallas_call(
        functools.partial(finish_kernel, block_rows=block_rows),
        in_specs=[scalars, scalars] + [inside] * 4,
        out_specs=[pl.BlockSpec(memory_space=pltpu.HBM)] * len(outs),
        out_shape=outs,
        scratch_shapes=[
            pltpu.VMEM((blocks, block_rows, lanes), jnp.float32),
            pltpu.VMEM((peers,) + shape, back.dtype),
            pltpu.SemaphoreType.DMA((peers, heads)),
        ],
        compiler_params=pltpu.CompilerParams(vmem_limit_bytes=SMALL_VMEM),
        name="finish",
    )(
        me,
        asked,
        in_vmem(back),
        in_vmem(kept),
        later,
        earlier,
    )


def local(query, key, value, d_out, pattern):
    heads_here, blocks, _ = pattern.shape
    peers = lax.axis_size("seq")
    rows, columns = query.shape
    head_dim = columns // (peers * heads_here)
    block_rows = rows * peers // blocks
    chunks = min(CHUNKS, heads_here)
    starts = [-(-heads_here * i // chunks) for i in range(chunks)]
    sizes = [end - start for start, end in zip(starts, starts[1:] + [heads_here])]
    arrays = (query, key, value, d_out)

    own_base = lax.axis_index("slab") * blocks
    block_ids = jnp.arange(blocks, dtype=jnp.int32)
    flat_lists = pattern.reshape(-1)
    reverse_rank = blocks - 1 - block_ids
    hits_prev = jnp.any(flat_lists[:, None] == (own_base - blocks + block_ids)[None, :], axis=0)
    hits_next = jnp.any(flat_lists[:, None] == (own_base + blocks + block_ids)[None, :], axis=0)
    need_prev = lax.top_k(hits_prev.astype(jnp.int32) * blocks + reverse_rank, CROSS)[1]
    need_next = lax.top_k(hits_next.astype(jnp.int32) * blocks + reverse_rank, CROSS)[1]
    asked_next = from_behind(need_prev, "slab", -1)
    asked_prev = from_behind(need_next, "slab", 1)
    asked = jnp.concatenate([asked_next, asked_prev])
    rank_ids = jnp.arange(CROSS, dtype=jnp.int32)
    prev_global = own_base - blocks + need_prev
    next_global = own_base + blocks + need_next
    pos_prev = jnp.sum(jnp.where(pattern[..., None] == prev_global, rank_ids, 0), axis=-1)
    pos_next = jnp.sum(jnp.where(pattern[..., None] == next_global, rank_ids, 0), axis=-1)
    in_own = (pattern >= own_base) & (pattern < own_base + blocks)
    local_ids = jnp.where(
        in_own,
        CROSS + pattern - own_base,
        jnp.where(pattern < own_base, pos_prev, CROSS + blocks + pos_next),
    )

    me = lax.axis_index("seq").astype(jnp.int32).reshape(1)
    me = lax.axis_index("seq").astype(jnp.int32).reshape(1)
    last = chunks - 1
    came = []
    for chunk, (start, size) in enumerate(zip(starts, sizes)):
        after = (asked, local_ids) if came else ()
        packed = pack(
            me, arrays, start, size, heads_here, peers, head_dim, chunk == 0, after
        )
        if chunk == 1:
            packed = hold(packed, came[0][:-1])
        came.append(exchange(packed))
    received = []
    outs = finished = ()
    for chunk, (messages, start, size) in enumerate(zip(came, starts, sizes)):
        for_next, for_prev, table = pick(me, messages, asked, block_rows, finished[:1])
        came_prev = from_behind(for_next, "slab", 1)
        came_next = from_behind(for_prev, "slab", -1)
        turned, pairs, sums = prepare(me, messages, table)
        lists = local_ids[start : start + size]
        back, to_prev, to_next, _, _, kept = attend(
            lists, came_prev, came_next, pairs, table, turned, sums
        )
        later = from_behind(to_prev, "slab", -1)
        earlier = from_behind(to_next, "slab", 1)
        finished = finish(me, back, kept, later, earlier, asked, chunk == last)
        received.append(exchange(finished))
        outs = unpack(me, received, starts, heads_here, outs)
    return tuple(outs)


def solution(mesh):
    tokens = P(("slab", "seq"), None)
    return jax.shard_map(
        local,
        mesh=mesh,
        in_specs=(tokens, tokens, tokens, tokens, P("seq", "slab", None)),
        out_specs=(tokens, tokens, tokens, tokens),
        check_vma=False,
    )
```

```python
import functools
import math

import jax
import jax.numpy as jnp
from jax import lax
from jax.experimental import pallas as pl
from jax.experimental.pallas import tpu as pltpu
from jax.sharding import PartitionSpec as P

CROSS = 4
CHUNKS = 2
LANES = 128
SMALL_VMEM = 24 * 1024 * 1024
LARGE_VMEM = 40 * 1024 * 1024


def in_hbm(x):
    return pltpu.with_memory_space_constraint(x, pltpu.HBM)


def in_vmem(x):
    return pltpu.with_memory_space_constraint(x, pltpu.VMEM)


def from_behind(x, axis, by):
    count = lax.axis_size(axis)
    pairs = [(i, i + by) for i in range(count) if 0 <= i + by < count]
    return lax.ppermute(x, axis, pairs)


def part_of(messages, me, item):
    if len(messages) == 1:
        return messages[0].at[item], item
    return messages[item], me[0] ^ (len(messages) - 1 - item)


def message_shape(messages):
    return messages[0].shape[-4:]


def message_outs(peers, shape, dtype, apart):
    if apart:
        return [pltpu.HBM(shape, dtype)] * peers
    return [pltpu.HBM((peers,) + shape, dtype)]


def hold_kernel(*refs):
    del refs


def hold(arrays, after):
    count = len(arrays)
    anywhere = pl.BlockSpec(memory_space=pltpu.HBM)
    return pl.pallas_call(
        hold_kernel,
        in_specs=[anywhere] * (count + len(after)),
        out_specs=[anywhere] * count,
        out_shape=[pltpu.HBM(x.shape, x.dtype) for x in arrays],
        input_output_aliases={i: i for i in range(count)},
        name="hold",
    )(*[in_hbm(x) for x in (*arrays, *after)])


def exchange(messages):
    if len(messages) == 1:
        return [lax.all_to_all(messages[0], "seq", split_axis=0, concat_axis=0, tiled=True)]
    count = len(messages)
    received = list(messages)
    for item in range(count - 1):
        pairs = [(i, i ^ (count - 1 - item)) for i in range(count)]
        received[item] = lax.ppermute(messages[item], "seq", pairs)
    return received


def pack_kernel(
    me, query, key, value, d_out, *refs, first, heads, items, apart, per_peer, head_dim
):
    messages = refs[-4 - (len(items) if apart else 1) : -4]
    stage, ready, in_sems, out_sems = refs[-4:]
    sources = (key, value, query, d_out)
    aligned = apart and per_peer % LANES == 0
    at_once = aligned or not apart
    peers = stage.shape[1]

    def place_of(item):
        if apart:
            return messages[item - items[0]], me[0] ^ (peers - 1 - item)
        return messages[0].at[item], item

    def span(item):
        if aligned:
            base, begin = pl.multiple_of(place_of(item)[1] * per_peer, LANES), first
        else:
            base, begin = 0, item * per_peer + first
        low = begin // LANES * LANES
        high = -(-(begin + heads * head_dim) // LANES) * LANES
        return base + low, high - low, begin - low

    def fetch(item, i):
        low, width, _ = span(item)
        return pltpu.make_async_copy(
            sources[i].at[:, pl.ds(low, width)],
            stage.at[i, item, :, pl.ds(0, width)],
            in_sems.at[i, item],
        )

    def send(item):
        target, peer = place_of(item)
        return pltpu.make_async_copy(
            ready.at[item if aligned else peer], target, out_sems.at[item]
        )

    made = items if at_once else range(peers)
    for item in made:
        for i in range(4):
            fetch(item, i).start()
    for item in made:
        for i in range(4):
            fetch(item, i).wait()
        at = span(item)[2]
        for head in range(heads):
            lanes = slice(at + head * head_dim, at + (head + 1) * head_dim)
            for kind in range(2):
                ready[item, head, kind] = jnp.concatenate(
                    [stage[2 * kind, item, :, lanes], stage[2 * kind + 1, item, :, lanes]],
                    axis=1,
                )
        if at_once:
            send(item).start()
    if not at_once:
        for item in items:
            send(item).start()
    for item in items:
        send(item).wait()


def pack(me, arrays, start, heads, heads_here, peers, head_dim, apart, after):
    rows = arrays[0].shape[0]
    dtype = arrays[0].dtype
    shape = (heads, 2, rows, 2 * head_dim)
    width = (-(-heads * head_dim // LANES) + 1) * LANES
    anywhere = pl.BlockSpec(memory_space=pltpu.HBM)
    outs = message_outs(peers, shape, dtype, apart)
    return pl.pallas_call(
        functools.partial(
            pack_kernel,
            first=start * head_dim,
            heads=heads,
            items=range(peers),
            apart=apart,
            per_peer=heads_here * head_dim,
            head_dim=head_dim,
        ),
        in_specs=[pl.BlockSpec(memory_space=pltpu.SMEM)]
        + [anywhere] * 4
        + [pl.BlockSpec(memory_space=pl.ANY)] * len(after),
        out_specs=[anywhere] * len(outs),
        out_shape=outs,
        scratch_shapes=[
            pltpu.VMEM((4, peers, rows, width), dtype),
            pltpu.VMEM((peers,) + shape, dtype),
            pltpu.SemaphoreType.DMA((4, peers)),
            pltpu.SemaphoreType.DMA((peers,)),
        ],
        compiler_params=pltpu.CompilerParams(vmem_limit_bytes=SMALL_VMEM),
        name="pack",
    )(me, *[in_hbm(x) for x in arrays], *after)


def unpack_kernel(me, *refs, chunk, peers, counts, earlier, jobs):
    ends = [sum(counts[: c + 1]) for c in range(chunk + 1)]
    groups = [refs[end - count : end] for end, count in zip(ends, counts)]
    outs = refs[ends[-1] + earlier :][:4]
    stages = refs[-3 - chunk - 1 : -3]
    ready, in_sems, out_sems = refs[-3:]
    head_dim = ready.shape[-1] // 2
    used = sorted({(which, peer) for job in jobs for which, peer, _ in job[1:]})
    chunks_used = sorted({which for which, _ in used})
    heads_used = {
        c: sorted({head for job in jobs for which, _, head in job[1:] if which == c})
        for c in chunks_used
    }

    def fetch(which, item, slot=None):
        heads = heads_used[which]
        some = pl.ds(heads[0], heads[-1] - heads[0] + 1)
        source, peer = part_of(groups[which], me, item)
        slot = peer if slot is None else slot
        return pltpu.make_async_copy(
            source.at[some], stages[which].at[slot, some], in_sems.at[which, slot]
        )

    def send(job, i):
        tile = jobs[job][0]
        return pltpu.make_async_copy(
            ready.at[i, job],
            outs[i].at[:, pl.ds(tile * LANES, LANES)],
            out_sems.at[4 * job + i],
        )

    for item in range(peers):
        for which in chunks_used:
            fetch(which, item).start()
    waited = set()

    def wait_for(which, peer):
        if (which, peer) not in waited:
            fetch(which, 0, peer).wait()
            waited.add((which, peer))

    for job, (tile, left, right) in enumerate(jobs):
        for which, peer, _ in (left, right):
            wait_for(which, peer)
        sides = [stages[which][peer, head] for which, peer, head in (left, right)]
        for i, (kind, at) in enumerate(((1, head_dim), (1, 0), (0, 0), (0, head_dim))):
            ready[i, job] = jnp.concatenate(
                [side[kind, :, at : at + head_dim] for side in sides], axis=1
            )
            send(job, i).start()
    for which in chunks_used:
        for peer in range(peers):
            wait_for(which, peer)
    for job in range(len(jobs)):
        for i in range(4):
            send(job, i).wait()


def unpack(me, messages, starts, heads_here, earlier):
    chunk = len(messages) - 1
    peers = lax.axis_size("seq")
    _, _, rows, pair_dim = message_shape(messages[0])
    head_dim = pair_dim // 2
    columns = peers * heads_here * head_dim
    dtype = messages[0][0].dtype

    def place_of(head):
        peer, local_head = divmod(head, heads_here)
        which = max(c for c, start in enumerate(starts) if start <= local_head)
        return which, peer, local_head - starts[which]

    jobs = []
    for tile in range(columns // LANES):
        left, right = place_of(2 * tile), place_of(2 * tile + 1)
        if max(left[0], right[0]) == chunk:
            jobs.append((tile, left, right))
    if not jobs:
        return earlier
    flat = [x for group in messages for x in group]
    anywhere = pl.BlockSpec(memory_space=pltpu.HBM)
    return pl.pallas_call(
        functools.partial(
            unpack_kernel,
            chunk=chunk,
            peers=peers,
            counts=[len(group) for group in messages],
            earlier=len(earlier),
            jobs=jobs,
        ),
        in_specs=[pl.BlockSpec(memory_space=pltpu.SMEM)]
        + [anywhere] * (len(flat) + len(earlier)),
        out_specs=[anywhere] * 4,
        out_shape=[pltpu.HBM((rows, columns), dtype)] * 4,
        input_output_aliases={1 + len(flat) + i: i for i in range(len(earlier))},
        scratch_shapes=[pltpu.VMEM((peers,) + message_shape(m), dtype) for m in messages]
        + [
            pltpu.VMEM((4, len(jobs), rows, LANES), dtype),
            pltpu.SemaphoreType.DMA((chunk + 1, peers)),
            pltpu.SemaphoreType.DMA((4 * len(jobs),)),
        ],
        compiler_params=pltpu.CompilerParams(vmem_limit_bytes=SMALL_VMEM),
        name="unpack",
    )(me, *[in_hbm(x) for x in (*flat, *earlier)])


def unpack_items_kernel(me, *refs, items, peers, counts, joint, earlier, jobs, per_peer):
    ends = [sum(counts[: c + 1]) for c in range(len(counts))]
    groups = [refs[end - count : end] for end, count in zip(ends, counts)]
    outs = refs[ends[-1] + earlier :][:4]
    stages = refs[-3 - len(counts) : -3]
    ready, in_sems, out_sems = refs[-3:]
    head_dim = ready.shape[-1] // 2
    used = [
        sorted({head for job in jobs for which, head in job[1:] if which == c})
        for c in range(len(counts))
    ]

    def peer_of(j):
        return me[0] ^ (peers - 1 - items[j])

    def fetch(which, j):
        group = groups[which]
        source = group[0].at[peer_of(j)] if joint[which] else group[j]
        some = pl.ds(used[which][0], used[which][-1] - used[which][0] + 1)
        return pltpu.make_async_copy(
            source.at[some], stages[which].at[j, some], in_sems.at[which, j]
        )

    def send(j, job, i):
        first = pl.multiple_of(peer_of(j) * per_peer, LANES) + jobs[job][0] * LANES
        return pltpu.make_async_copy(
            ready.at[j, i, job], outs[i].at[:, pl.ds(first, LANES)], out_sems.at[j, i, job]
        )

    steps = [(j, which) for j in range(len(items)) for which in range(len(counts))]
    steps = [(j, which) for j, which in steps if used[which]]
    for j, which in steps:
        fetch(which, j).start()
    for j in range(len(items)):
        for at, which in steps:
            if at == j:
                fetch(which, j).wait()
        for job, (_, left, right) in enumerate(jobs):
            sides = [stages[which][j, head] for which, head in (left, right)]
            for i, (kind, at) in enumerate(((1, head_dim), (1, 0), (0, 0), (0, head_dim))):
                ready[j, i, job] = jnp.concatenate(
                    [side[kind, :, at : at + head_dim] for side in sides], axis=1
                )
                send(j, job, i).start()
    for j in range(len(items)):
        for job in range(len(jobs)):
            for i in range(4):
                send(j, job, i).wait()


def unpack_items(me, messages, starts, heads_here, items, earlier):
    chunk = len(messages) - 1
    peers = lax.axis_size("seq")
    _, _, rows, pair_dim = message_shape(messages[0])
    head_dim = pair_dim // 2
    per_peer = heads_here * head_dim
    dtype = messages[0][0].dtype

    def place_of(head):
        which = max(c for c, start in enumerate(starts) if start <= head)
        return which, head - starts[which]

    jobs = []
    for tile in range(per_peer // LANES):
        left, right = place_of(2 * tile), place_of(2 * tile + 1)
        if max(left[0], right[0]) == chunk:
            jobs.append((tile, left, right))
    groups = [
        list(group) if len(group) == 1 else [group[item] for item in items]
        for group in messages
    ]
    flat = [x for group in groups for x in group]
    anywhere = pl.BlockSpec(memory_space=pltpu.HBM)
    return pl.pallas_call(
        functools.partial(
            unpack_items_kernel,
            items=items,
            peers=peers,
            counts=[len(group) for group in groups],
            joint=[len(group) == 1 for group in messages],
            earlier=len(earlier),
            jobs=jobs,
            per_peer=per_peer,
        ),
        in_specs=[pl.BlockSpec(memory_space=pltpu.SMEM)]
        + [anywhere] * (len(flat) + len(earlier)),
        out_specs=[anywhere] * 4,
        out_shape=[pltpu.HBM((rows, peers * per_peer), dtype)] * 4,
        input_output_aliases={1 + len(flat) + i: i for i in range(len(earlier))},
        scratch_shapes=[
            pltpu.VMEM((len(items),) + message_shape(m), dtype) for m in messages
        ]
        + [
            pltpu.VMEM((len(items), 4, len(jobs), rows, LANES), dtype),
            pltpu.SemaphoreType.DMA((chunk + 1, len(items))),
            pltpu.SemaphoreType.DMA((len(items), 4, len(jobs))),
        ],
        compiler_params=pltpu.CompilerParams(vmem_limit_bytes=SMALL_VMEM),
        name="unpack_items",
    )(me, *[in_hbm(x) for x in (*flat, *earlier)])


def pick_kernel(me, asked, *refs, count):
    for_next, for_prev, table, sems = refs[-4:]
    heads, window, block_rows, _ = table.shape
    peers, each = sems.shape

    def fetch(item, i):
        source, peer = part_of(refs[:count], me, item)
        rows = pl.ds(i * block_rows, block_rows)
        return pltpu.make_async_copy(
            source.at[:, 0, rows], table.at[:, CROSS + peer * each + i], sems.at[item, i]
        )

    for item in range(peers):
        for i in range(each):
            fetch(item, i).start()
    for item in range(peers):
        for i in range(each):
            fetch(item, i).wait()
    for i in range(CROSS):
        for_next[i] = table[:, CROSS + asked[i]]
        for_prev[i] = table[:, CROSS + asked[CROSS + i]]


def pick(me, messages, asked, block_rows, after):
    heads, _, rows, lanes = message_shape(messages)
    dtype = messages[0].dtype
    peers = lax.axis_size("seq")
    each = rows // block_rows
    window = peers * each + 2 * CROSS
    picked = jax.ShapeDtypeStruct((CROSS, heads, block_rows, lanes), dtype)
    return pl.pallas_call(
        functools.partial(pick_kernel, count=len(messages)),
        in_specs=[pl.BlockSpec(memory_space=pltpu.SMEM)] * 2
        + [pl.BlockSpec(memory_space=pltpu.HBM)] * (len(messages) + len(after)),
        out_specs=[pl.BlockSpec(memory_space=pltpu.VMEM)] * 3,
        out_shape=[picked, picked, pltpu.VMEM((heads, window, block_rows, lanes), dtype)],
        scratch_shapes=[pltpu.SemaphoreType.DMA((peers, each))],
        compiler_params=pltpu.CompilerParams(vmem_limit_bytes=SMALL_VMEM),
        name="pick",
    )(me, asked, *[in_hbm(x) for x in (*messages, *after)])


def prepare_kernel(me, table, *refs, peers):
    messages = refs[:-4]
    turned, pairs, sums, sems = refs[-4:]
    heads, window, _, _ = table.shape

    def fetch(item):
        source, peer = part_of(messages, me, item)
        return pltpu.make_async_copy(source.at[:, 1], pairs.at[peer], sems.at[item])

    for item in range(peers):
        fetch(item).start()
    for head in range(heads):

        def clear(i, carry):
            sums[head, i] = jnp.zeros(sums.shape[2:], sums.dtype)
            return carry

        def turn(i, carry):
            turned[head, i] = table[head, i].T
            return carry

        lax.fori_loop(0, window, clear, 0)
        lax.fori_loop(CROSS, window - CROSS, turn, 0)
    for item in range(peers):
        fetch(item).wait()


def prepare(me, messages, table):
    heads, _, rows, lanes = message_shape(messages)
    _, window, block_rows, _ = table.shape
    dtype = messages[0].dtype
    peers = lax.axis_size("seq")
    inside = pl.BlockSpec(memory_space=pltpu.VMEM)
    return pl.pallas_call(
        functools.partial(prepare_kernel, peers=peers),
        in_specs=[pl.BlockSpec(memory_space=pltpu.SMEM), inside]
        + [pl.BlockSpec(memory_space=pltpu.HBM)] * len(messages),
        out_specs=[inside] * 3,
        out_shape=[
            pltpu.VMEM((heads, window, lanes, block_rows), dtype),
            pltpu.VMEM((peers, heads, rows, lanes), dtype),
            pltpu.VMEM((heads, window, block_rows, lanes), jnp.float32),
        ],
        scratch_shapes=[pltpu.SemaphoreType.DMA((peers,))],
        compiler_params=pltpu.CompilerParams(vmem_limit_bytes=SMALL_VMEM),
        name="prepare",
    )(me, in_vmem(table), *[in_hbm(x) for x in messages])


def attend_kernel(
    lists,
    came_prev,
    came_next,
    pairs,
    table_in,
    turned_in,
    sums_in,
    back,
    to_prev,
    to_next,
    table,
    turned,
    sums,
    both_even,
    both_odd,
    low_even,
    low_odd,
    *,
    head_dim,
    per_list,
):
    del table_in, turned_in, sums_in
    peers, heads, rows, lanes = pairs.shape
    _, window, block_rows, _ = table.shape
    each = rows // block_rows
    blocks = peers * each
    units = heads * blocks
    keys = per_list * block_rows
    scaling = head_dim ** (-0.5)
    exponent = scaling * math.log2(math.e)
    both = (both_even, both_odd)
    low = (low_even, low_odd)
    step_rows = 64

    for head in range(heads):
        for i in range(CROSS):
            table[head, i] = came_prev[i, head]
            table[head, CROSS + blocks + i] = came_next[i, head]
            turned[head, i] = came_prev[i, head].T
            turned[head, CROSS + blocks + i] = came_next[i, head].T

    left = lax.broadcasted_iota(jnp.int32, (block_rows, lanes), 1) < head_dim

    def locate(unit):
        head = lax.div(unit, blocks)
        block = lax.rem(unit, blocks)
        ids = [lists[head, block, j] for j in range(per_list)]
        peer = lax.div(block, each)
        start = pl.multiple_of(lax.rem(block, each) * block_rows, block_rows)
        return head, ids, peer, pl.ds(start, block_rows)

    def apart_of(head, peer, here):
        query_grad = pairs[peer, head, here]
        nothing = jnp.zeros_like(query_grad)
        return jnp.concatenate(
            [jnp.where(left, query_grad, nothing), jnp.where(left, nothing, query_grad)],
            axis=0,
        )

    def score(unit, slot):
        head, ids, peer, here = locate(unit)
        key_value = jnp.concatenate([table[head, i] for i in ids], axis=0)
        both[slot][...] = lax.dot_general(
            key_value,
            apart_of(head, peer, here),
            (((1,), (1,)), ((), ())),
            preferred_element_type=jnp.float32,
        )

    def soften(slot):
        source, target = both[slot], low[slot]
        parts = [slice(i, i + step_rows) for i in range(0, keys, step_rows)]
        top = source[parts[0], :block_rows]
        for part in parts[1:]:
            top = jnp.maximum(top, source[part, :block_rows])
        top = jnp.max(top, axis=0, keepdims=True)
        total = jnp.zeros((step_rows, block_rows), jnp.float32)
        mixed = jnp.zeros((step_rows, block_rows), jnp.float32)
        for part in parts:
            raised = jnp.exp2((source[part, :block_rows] - top) * exponent)
            source[part, :block_rows] = raised
            total += raised
            mixed += raised * source[part, block_rows:]
        inverse = 1.0 / jnp.sum(total, axis=0, keepdims=True)
        correction = jnp.sum(mixed, axis=0, keepdims=True) * inverse
        for part in parts:
            weights = source[part, :block_rows] * inverse
            target[part, block_rows:] = weights.astype(jnp.bfloat16)
            target[part, :block_rows] = (
                weights * (source[part, block_rows:] - correction)
            ).astype(jnp.bfloat16)

    def combine(unit, slot):
        head, ids, peer, here = locate(unit)
        products = low[slot][...]
        terms = jnp.dot(
            products, apart_of(head, peer, here), preferred_element_type=jnp.float32
        )
        for j, i in enumerate(ids):
            sums[head, i] += terms[j * block_rows : (j + 1) * block_rows]
        key_value = jnp.concatenate([turned[head, i] for i in ids], axis=1)
        out = jnp.dot(key_value, products, preferred_element_type=jnp.float32)
        out = jnp.concatenate(
            [out[:head_dim, :block_rows] * scaling, out[head_dim:, block_rows:]], axis=0
        )
        back[peer, head, here] = out.T.astype(back.dtype)

    score(0, 0)
    score(1, 1)
    soften(0)

    def step(i, carry):
        for slot in range(2):
            unit = 2 * i + slot
            combine(unit - 2, slot)
            score(unit, slot)
            soften(1 - slot)
        return carry

    lax.fori_loop(1, units // 2, step, 0)
    combine(units - 2, 0)
    soften(1)
    combine(units - 1, 1)

    factor = jnp.where(left, scaling, 1.0)
    for head in range(heads):
        for i in range(CROSS):
            to_prev[i, head] = (sums[head, i] * factor).astype(to_prev.dtype)
            to_next[i, head] = (sums[head, CROSS + blocks + i] * factor).astype(to_next.dtype)


def attend(lists, came_prev, came_next, pairs, table, turned, sums):
    _, _, block_rows, lanes = came_prev.shape
    dtype = pairs.dtype
    per_list = lists.shape[-1]
    keys = per_list * block_rows
    inside = pl.BlockSpec(memory_space=pltpu.VMEM)
    cross_shape = jax.ShapeDtypeStruct(came_prev.shape, dtype)
    kept = (table, turned, sums)
    return pl.pallas_call(
        functools.partial(attend_kernel, head_dim=lanes // 2, per_list=per_list),
        in_specs=[pl.BlockSpec(memory_space=pltpu.SMEM)] + [inside] * 6,
        out_specs=[inside] * 6,
        out_shape=[pltpu.VMEM(pairs.shape, dtype), cross_shape, cross_shape]
        + [pltpu.VMEM(x.shape, x.dtype) for x in kept],
        input_output_aliases={4: 3, 5: 4, 6: 5},
        scratch_shapes=[
            pltpu.VMEM((keys, 2 * block_rows), jnp.float32),
            pltpu.VMEM((keys, 2 * block_rows), jnp.float32),
            pltpu.VMEM((keys, 2 * block_rows), dtype),
            pltpu.VMEM((keys, 2 * block_rows), dtype),
        ],
        compiler_params=pltpu.CompilerParams(vmem_limit_bytes=SMALL_VMEM),
        name="attend",
    )(lists, came_prev, came_next, *[in_vmem(x) for x in (pairs, *kept)])


def finish_kernel(me, asked, back, kept, later, earlier, *refs, block_rows):
    messages = refs[:-3]
    sums, ready, sems = refs[-3:]
    peers, heads, _, rows, lanes = ready.shape
    each = rows // block_rows
    blocks = peers * each
    head_dim = lanes // 2
    left = lax.broadcasted_iota(jnp.int32, (block_rows, lanes), 1) < head_dim
    factor = jnp.where(left, head_dim ** (-0.5), 1.0)

    def send(item, head):
        target, peer = part_of(messages, me, item)
        return pltpu.make_async_copy(
            ready.at[peer, head], target.at[head], sems.at[item, head]
        )

    for head in range(heads):
        sums[...] = kept[head, CROSS : CROSS + blocks] * factor
        for i in range(CROSS):
            sums[asked[i]] += later[i, head].astype(jnp.float32)
        for i in range(CROSS):
            sums[asked[CROSS + i]] += earlier[i, head].astype(jnp.float32)
        for peer in range(peers):
            ready[peer, head, 1] = back[peer, head]
            for i in range(each):
                ready[peer, head, 0, i * block_rows : (i + 1) * block_rows] = sums[
                    peer * each + i
                ].astype(ready.dtype)
        for item in range(peers):
            send(item, head).start()
    for head in range(heads):
        for item in range(peers):
            send(item, head).wait()


def finish(me, back, kept, later, earlier, asked, apart):
    peers, heads, rows, lanes = back.shape
    _, window, block_rows, _ = kept.shape
    blocks = window - 2 * CROSS
    inside = pl.BlockSpec(memory_space=pltpu.VMEM)
    scalars = pl.BlockSpec(memory_space=pltpu.SMEM)
    shape = (heads, 2, rows, lanes)
    outs = message_outs(peers, shape, back.dtype, apart)
    return pl.pallas_call(
        functools.partial(finish_kernel, block_rows=block_rows),
        in_specs=[scalars, scalars] + [inside] * 4,
        out_specs=[pl.BlockSpec(memory_space=pltpu.HBM)] * len(outs),
        out_shape=outs,
        scratch_shapes=[
            pltpu.VMEM((blocks, block_rows, lanes), jnp.float32),
            pltpu.VMEM((peers,) + shape, back.dtype),
            pltpu.SemaphoreType.DMA((peers, heads)),
        ],
        compiler_params=pltpu.CompilerParams(vmem_limit_bytes=SMALL_VMEM),
        name="finish",
    )(
        me,
        asked,
        in_vmem(back),
        in_vmem(kept),
        later,
        earlier,
    )


def local(query, key, value, d_out, pattern):
    heads_here, blocks, _ = pattern.shape
    peers = lax.axis_size("seq")
    rows, columns = query.shape
    head_dim = columns // (peers * heads_here)
    block_rows = rows * peers // blocks
    chunks = min(CHUNKS, heads_here)
    starts = [-(-heads_here * i // chunks) for i in range(chunks)]
    sizes = [end - start for start, end in zip(starts, starts[1:] + [heads_here])]
    arrays = (query, key, value, d_out)

    own_base = lax.axis_index("slab") * blocks
    block_ids = jnp.arange(blocks, dtype=jnp.int32)
    flat_lists = pattern.reshape(-1)
    reverse_rank = blocks - 1 - block_ids
    hits_prev = jnp.any(flat_lists[:, None] == (own_base - blocks + block_ids)[None, :], axis=0)
    hits_next = jnp.any(flat_lists[:, None] == (own_base + blocks + block_ids)[None, :], axis=0)
    need_prev = lax.top_k(hits_prev.astype(jnp.int32) * blocks + reverse_rank, CROSS)[1]
    need_next = lax.top_k(hits_next.astype(jnp.int32) * blocks + reverse_rank, CROSS)[1]
    asked_next = from_behind(need_prev, "slab", -1)
    asked_prev = from_behind(need_next, "slab", 1)
    asked = jnp.concatenate([asked_next, asked_prev])
    rank_ids = jnp.arange(CROSS, dtype=jnp.int32)
    prev_global = own_base - blocks + need_prev
    next_global = own_base + blocks + need_next
    pos_prev = jnp.sum(jnp.where(pattern[..., None] == prev_global, rank_ids, 0), axis=-1)
    pos_next = jnp.sum(jnp.where(pattern[..., None] == next_global, rank_ids, 0), axis=-1)
    in_own = (pattern >= own_base) & (pattern < own_base + blocks)
    local_ids = jnp.where(
        in_own,
        CROSS + pattern - own_base,
        jnp.where(pattern < own_base, pos_prev, CROSS + blocks + pos_next),
    )

    me = lax.axis_index("seq").astype(jnp.int32).reshape(1)
    me = lax.axis_index("seq").astype(jnp.int32).reshape(1)
    last = chunks - 1
    came = []
    for chunk, (start, size) in enumerate(zip(starts, sizes)):
        after = (asked, local_ids) if came else ()
        packed = pack(
            me, arrays, start, size, heads_here, peers, head_dim, chunk == 0, after
        )
        if chunk == 1:
            packed = hold(packed, came[0][:-1])
        came.append(exchange(packed))
    received = []
    outs = finished = ()
    for chunk, (messages, start, size) in enumerate(zip(came, starts, sizes)):
        for_next, for_prev, table = pick(me, messages, asked, block_rows, finished[:1])
        came_prev = from_behind(for_next, "slab", 1)
        came_next = from_behind(for_prev, "slab", -1)
        turned, pairs, sums = prepare(me, messages, table)
        lists = local_ids[start : start + size]
        back, to_prev, to_next, _, _, kept = attend(
            lists, came_prev, came_next, pairs, table, turned, sums
        )
        later = from_behind(to_prev, "slab", -1)
        earlier = from_behind(to_next, "slab", 1)
        finished = finish(me, back, kept, later, earlier, asked, chunk == last)
        received.append(exchange(finished))
        if chunk == last and heads_here * head_dim % LANES == 0:
            half = peers // 2
            parts = (
                [peers - 1, *range(half // 2)],
                [*range(half // 2, half - 1), *range(half, peers - 1)],
                [half - 1],
            )
            for items in parts:
                outs = unpack_items(me, received, starts, heads_here, items, outs)
        else:
            outs = unpack(me, received, starts, heads_here, outs)
    return tuple(outs)


def solution(mesh):
    tokens = P(("slab", "seq"), None)
    return jax.shard_map(
        local,
        mesh=mesh,
        in_specs=(tokens, tokens, tokens, tokens, P("seq", "slab", None)),
        out_specs=(tokens, tokens, tokens, tokens),
        check_vma=False,
    )
```

```python
import functools
import math

import jax
import jax.numpy as jnp
from jax import lax
from jax.experimental import pallas as pl
from jax.experimental.pallas import tpu as pltpu
from jax.sharding import PartitionSpec as P

CROSS = 4
CHUNKS = 2
LANES = 128
SMALL_VMEM = 24 * 1024 * 1024
LARGE_VMEM = 40 * 1024 * 1024


def in_hbm(x):
    return pltpu.with_memory_space_constraint(x, pltpu.HBM)


def in_vmem(x):
    return pltpu.with_memory_space_constraint(x, pltpu.VMEM)


def from_behind(x, axis, by):
    count = lax.axis_size(axis)
    pairs = [(i, i + by) for i in range(count) if 0 <= i + by < count]
    return lax.ppermute(x, axis, pairs)


def part_of(messages, me, item):
    if len(messages) == 1:
        return messages[0].at[item], item
    return messages[item], me[0] ^ (len(messages) - 1 - item)


def message_shape(messages):
    return messages[0].shape[-4:]


def message_outs(peers, shape, dtype, apart):
    if apart:
        return [pltpu.HBM(shape, dtype)] * peers
    return [pltpu.HBM((peers,) + shape, dtype)]


def exchange(messages):
    if len(messages) == 1:
        return [lax.all_to_all(messages[0], "seq", split_axis=0, concat_axis=0, tiled=True)]
    count = len(messages)
    received = list(messages)
    for item in range(count - 1):
        pairs = [(i, i ^ (count - 1 - item)) for i in range(count)]
        received[item] = lax.ppermute(messages[item], "seq", pairs)
    return received


def pack_kernel(query, key, value, d_out, *refs, first, heads, per_peer, head_dim):
    message, stage, ready, in_sems, out_sems = refs[-5:]
    sources = (key, value, query, d_out)
    peers = message.shape[0]

    def span(peer):
        begin = peer * per_peer + first
        low = begin // LANES * LANES
        high = -(-(begin + heads * head_dim) // LANES) * LANES
        return low, high - low, begin - low

    def fetch(peer, i):
        low, width, _ = span(peer)
        return pltpu.make_async_copy(
            sources[i].at[:, pl.ds(low, width)],
            stage.at[i, peer, :, pl.ds(0, width)],
            in_sems.at[i, peer],
        )

    def send(peer):
        return pltpu.make_async_copy(ready.at[peer], message.at[peer], out_sems.at[peer])

    for peer in range(peers):
        for i in range(4):
            fetch(peer, i).start()
    for peer in range(peers):
        for i in range(4):
            fetch(peer, i).wait()
        at = span(peer)[2]
        for head in range(heads):
            lanes = slice(at + head * head_dim, at + (head + 1) * head_dim)
            for kind in range(2):
                ready[peer, head, kind] = jnp.concatenate(
                    [stage[2 * kind, peer, :, lanes], stage[2 * kind + 1, peer, :, lanes]],
                    axis=1,
                )
        send(peer).start()
    for peer in range(peers):
        send(peer).wait()


def pack(arrays, start, heads, heads_here, peers, head_dim, after):
    rows = arrays[0].shape[0]
    dtype = arrays[0].dtype
    shape = (peers, heads, 2, rows, 2 * head_dim)
    width = (-(-heads * head_dim // LANES) + 1) * LANES
    anywhere = pl.BlockSpec(memory_space=pltpu.HBM)
    return pl.pallas_call(
        functools.partial(
            pack_kernel,
            first=start * head_dim,
            heads=heads,
            per_peer=heads_here * head_dim,
            head_dim=head_dim,
        ),
        in_specs=[anywhere] * 4 + [pl.BlockSpec(memory_space=pl.ANY)] * len(after),
        out_specs=[anywhere],
        out_shape=[pltpu.HBM(shape, dtype)],
        scratch_shapes=[
            pltpu.VMEM((4, peers, rows, width), dtype),
            pltpu.VMEM(shape, dtype),
            pltpu.SemaphoreType.DMA((4, peers)),
            pltpu.SemaphoreType.DMA((peers,)),
        ],
        compiler_params=pltpu.CompilerParams(vmem_limit_bytes=SMALL_VMEM),
        name="pack",
    )(*[in_hbm(x) for x in arrays], *after)


def unpack_kernel(me, *refs, chunk, peers, counts, earlier, jobs):
    ends = [sum(counts[: c + 1]) for c in range(chunk + 1)]
    groups = [refs[end - count : end] for end, count in zip(ends, counts)]
    outs = refs[ends[-1] + earlier :][:4]
    stages = refs[-3 - chunk - 1 : -3]
    ready, in_sems, out_sems = refs[-3:]
    head_dim = ready.shape[-1] // 2
    used = sorted({(which, peer) for job in jobs for which, peer, _ in job[1:]})
    chunks_used = sorted({which for which, _ in used})
    heads_used = {
        c: sorted({head for job in jobs for which, _, head in job[1:] if which == c})
        for c in chunks_used
    }

    def fetch(which, item, slot=None):
        heads = heads_used[which]
        some = pl.ds(heads[0], heads[-1] - heads[0] + 1)
        source, peer = part_of(groups[which], me, item)
        slot = peer if slot is None else slot
        return pltpu.make_async_copy(
            source.at[some], stages[which].at[slot, some], in_sems.at[which, slot]
        )

    def send(job, i):
        tile = jobs[job][0]
        return pltpu.make_async_copy(
            ready.at[i, job],
            outs[i].at[:, pl.ds(tile * LANES, LANES)],
            out_sems.at[4 * job + i],
        )

    for item in range(peers):
        for which in chunks_used:
            fetch(which, item).start()
    waited = set()

    def wait_for(which, peer):
        if (which, peer) not in waited:
            fetch(which, 0, peer).wait()
            waited.add((which, peer))

    for job, (tile, left, right) in enumerate(jobs):
        for which, peer, _ in (left, right):
            wait_for(which, peer)
        sides = [stages[which][peer, head] for which, peer, head in (left, right)]
        for i, (kind, at) in enumerate(((1, head_dim), (1, 0), (0, 0), (0, head_dim))):
            ready[i, job] = jnp.concatenate(
                [side[kind, :, at : at + head_dim] for side in sides], axis=1
            )
            send(job, i).start()
    for which in chunks_used:
        for peer in range(peers):
            wait_for(which, peer)
    for job in range(len(jobs)):
        for i in range(4):
            send(job, i).wait()


def unpack(me, messages, starts, heads_here, earlier):
    chunk = len(messages) - 1
    peers = lax.axis_size("seq")
    _, _, rows, pair_dim = message_shape(messages[0])
    head_dim = pair_dim // 2
    columns = peers * heads_here * head_dim
    dtype = messages[0][0].dtype

    def place_of(head):
        peer, local_head = divmod(head, heads_here)
        which = max(c for c, start in enumerate(starts) if start <= local_head)
        return which, peer, local_head - starts[which]

    jobs = []
    for tile in range(columns // LANES):
        left, right = place_of(2 * tile), place_of(2 * tile + 1)
        if max(left[0], right[0]) == chunk:
            jobs.append((tile, left, right))
    if not jobs:
        return earlier
    flat = [x for group in messages for x in group]
    anywhere = pl.BlockSpec(memory_space=pltpu.HBM)
    return pl.pallas_call(
        functools.partial(
            unpack_kernel,
            chunk=chunk,
            peers=peers,
            counts=[len(group) for group in messages],
            earlier=len(earlier),
            jobs=jobs,
        ),
        in_specs=[pl.BlockSpec(memory_space=pltpu.SMEM)]
        + [anywhere] * (len(flat) + len(earlier)),
        out_specs=[anywhere] * 4,
        out_shape=[pltpu.HBM((rows, columns), dtype)] * 4,
        input_output_aliases={1 + len(flat) + i: i for i in range(len(earlier))},
        scratch_shapes=[pltpu.VMEM((peers,) + message_shape(m), dtype) for m in messages]
        + [
            pltpu.VMEM((4, len(jobs), rows, LANES), dtype),
            pltpu.SemaphoreType.DMA((chunk + 1, peers)),
            pltpu.SemaphoreType.DMA((4 * len(jobs),)),
        ],
        compiler_params=pltpu.CompilerParams(vmem_limit_bytes=SMALL_VMEM),
        name="unpack",
    )(me, *[in_hbm(x) for x in (*flat, *earlier)])


def unpack_items_kernel(me, *refs, items, peers, counts, joint, earlier, jobs, per_peer):
    ends = [sum(counts[: c + 1]) for c in range(len(counts))]
    groups = [refs[end - count : end] for end, count in zip(ends, counts)]
    outs = refs[ends[-1] + earlier :][:4]
    stages = refs[-3 - len(counts) : -3]
    ready, in_sems, out_sems = refs[-3:]
    head_dim = ready.shape[-1] // 2
    used = [
        sorted({head for job in jobs for which, head in job[1:] if which == c})
        for c in range(len(counts))
    ]

    def peer_of(j):
        return me[0] ^ (peers - 1 - items[j])

    def fetch(which, j):
        group = groups[which]
        source = group[0].at[peer_of(j)] if joint[which] else group[j]
        some = pl.ds(used[which][0], used[which][-1] - used[which][0] + 1)
        return pltpu.make_async_copy(
            source.at[some], stages[which].at[j, some], in_sems.at[which, j]
        )

    def send(j, job, i):
        first = pl.multiple_of(peer_of(j) * per_peer, LANES) + jobs[job][0] * LANES
        return pltpu.make_async_copy(
            ready.at[j, i, job], outs[i].at[:, pl.ds(first, LANES)], out_sems.at[j, i, job]
        )

    steps = [(j, which) for j in range(len(items)) for which in range(len(counts))]
    steps = [(j, which) for j, which in steps if used[which]]
    for j, which in steps:
        fetch(which, j).start()
    for j in range(len(items)):
        for at, which in steps:
            if at == j:
                fetch(which, j).wait()
        for job, (_, left, right) in enumerate(jobs):
            sides = [stages[which][j, head] for which, head in (left, right)]
            for i, (kind, at) in enumerate(((1, head_dim), (1, 0), (0, 0), (0, head_dim))):
                ready[j, i, job] = jnp.concatenate(
                    [side[kind, :, at : at + head_dim] for side in sides], axis=1
                )
                send(j, job, i).start()
    for j in range(len(items)):
        for job in range(len(jobs)):
            for i in range(4):
                send(j, job, i).wait()


def unpack_items(me, messages, starts, heads_here, items, earlier):
    chunk = len(messages) - 1
    peers = lax.axis_size("seq")
    _, _, rows, pair_dim = message_shape(messages[0])
    head_dim = pair_dim // 2
    per_peer = heads_here * head_dim
    dtype = messages[0][0].dtype

    def place_of(head):
        which = max(c for c, start in enumerate(starts) if start <= head)
        return which, head - starts[which]

    jobs = []
    for tile in range(per_peer // LANES):
        left, right = place_of(2 * tile), place_of(2 * tile + 1)
        if max(left[0], right[0]) == chunk:
            jobs.append((tile, left, right))
    groups = [
        list(group) if len(group) == 1 else [group[item] for item in items]
        for group in messages
    ]
    flat = [x for group in groups for x in group]
    anywhere = pl.BlockSpec(memory_space=pltpu.HBM)
    return pl.pallas_call(
        functools.partial(
            unpack_items_kernel,
            items=items,
            peers=peers,
            counts=[len(group) for group in groups],
            joint=[len(group) == 1 for group in messages],
            earlier=len(earlier),
            jobs=jobs,
            per_peer=per_peer,
        ),
        in_specs=[pl.BlockSpec(memory_space=pltpu.SMEM)]
        + [anywhere] * (len(flat) + len(earlier)),
        out_specs=[anywhere] * 4,
        out_shape=[pltpu.HBM((rows, peers * per_peer), dtype)] * 4,
        input_output_aliases={1 + len(flat) + i: i for i in range(len(earlier))},
        scratch_shapes=[
            pltpu.VMEM((len(items),) + message_shape(m), dtype) for m in messages
        ]
        + [
            pltpu.VMEM((len(items), 4, len(jobs), rows, LANES), dtype),
            pltpu.SemaphoreType.DMA((chunk + 1, len(items))),
            pltpu.SemaphoreType.DMA((len(items), 4, len(jobs))),
        ],
        compiler_params=pltpu.CompilerParams(vmem_limit_bytes=SMALL_VMEM),
        name="unpack_items",
    )(me, *[in_hbm(x) for x in (*flat, *earlier)])


def pick_kernel(me, asked, *refs, count):
    for_next, for_prev, table, sems = refs[-4:]
    heads, window, block_rows, _ = table.shape
    peers, each = sems.shape

    def fetch(item, i):
        source, peer = part_of(refs[:count], me, item)
        rows = pl.ds(i * block_rows, block_rows)
        return pltpu.make_async_copy(
            source.at[:, 0, rows], table.at[:, CROSS + peer * each + i], sems.at[item, i]
        )

    for item in range(peers):
        for i in range(each):
            fetch(item, i).start()
    for item in range(peers):
        for i in range(each):
            fetch(item, i).wait()
    for i in range(CROSS):
        for_next[i] = table[:, CROSS + asked[i]]
        for_prev[i] = table[:, CROSS + asked[CROSS + i]]


def pick(me, messages, asked, block_rows, after):
    heads, _, rows, lanes = message_shape(messages)
    dtype = messages[0].dtype
    peers = lax.axis_size("seq")
    each = rows // block_rows
    window = peers * each + 2 * CROSS
    picked = jax.ShapeDtypeStruct((CROSS, heads, block_rows, lanes), dtype)
    return pl.pallas_call(
        functools.partial(pick_kernel, count=len(messages)),
        in_specs=[pl.BlockSpec(memory_space=pltpu.SMEM)] * 2
        + [pl.BlockSpec(memory_space=pltpu.HBM)] * (len(messages) + len(after)),
        out_specs=[pl.BlockSpec(memory_space=pltpu.VMEM)] * 3,
        out_shape=[picked, picked, pltpu.VMEM((heads, window, block_rows, lanes), dtype)],
        scratch_shapes=[pltpu.SemaphoreType.DMA((peers, each))],
        compiler_params=pltpu.CompilerParams(vmem_limit_bytes=SMALL_VMEM),
        name="pick",
    )(me, asked, *[in_hbm(x) for x in (*messages, *after)])


def prepare_kernel(me, table, *refs, peers):
    messages = refs[:-4]
    turned, pairs, sums, sems = refs[-4:]
    heads, window, _, _ = table.shape

    def fetch(item):
        source, peer = part_of(messages, me, item)
        return pltpu.make_async_copy(source.at[:, 1], pairs.at[peer], sems.at[item])

    for item in range(peers):
        fetch(item).start()
    for head in range(heads):

        def clear(i, carry):
            sums[head, i] = jnp.zeros(sums.shape[2:], sums.dtype)
            return carry

        def turn(i, carry):
            turned[head, i] = table[head, i].T
            return carry

        lax.fori_loop(0, window, clear, 0)
        lax.fori_loop(CROSS, window - CROSS, turn, 0)
    for item in range(peers):
        fetch(item).wait()


def prepare(me, messages, table):
    heads, _, rows, lanes = message_shape(messages)
    _, window, block_rows, _ = table.shape
    dtype = messages[0].dtype
    peers = lax.axis_size("seq")
    inside = pl.BlockSpec(memory_space=pltpu.VMEM)
    return pl.pallas_call(
        functools.partial(prepare_kernel, peers=peers),
        in_specs=[pl.BlockSpec(memory_space=pltpu.SMEM), inside]
        + [pl.BlockSpec(memory_space=pltpu.HBM)] * len(messages),
        out_specs=[inside] * 3,
        out_shape=[
            pltpu.VMEM((heads, window, lanes, block_rows), dtype),
            pltpu.VMEM((peers, heads, rows, lanes), dtype),
            pltpu.VMEM((heads, window, block_rows, lanes), jnp.float32),
        ],
        scratch_shapes=[pltpu.SemaphoreType.DMA((peers,))],
        compiler_params=pltpu.CompilerParams(vmem_limit_bytes=SMALL_VMEM),
        name="prepare",
    )(me, in_vmem(table), *[in_hbm(x) for x in messages])


def attend_kernel(
    lists,
    came_prev,
    came_next,
    pairs,
    table_in,
    turned_in,
    sums_in,
    back,
    to_prev,
    to_next,
    table,
    turned,
    sums,
    both_even,
    both_odd,
    low_even,
    low_odd,
    *,
    head_dim,
    per_list,
):
    del table_in, turned_in, sums_in
    peers, heads, rows, lanes = pairs.shape
    _, window, block_rows, _ = table.shape
    each = rows // block_rows
    blocks = peers * each
    units = heads * blocks
    keys = per_list * block_rows
    scaling = head_dim ** (-0.5)
    exponent = scaling * math.log2(math.e)
    both = (both_even, both_odd)
    low = (low_even, low_odd)
    step_rows = 64

    for head in range(heads):
        for i in range(CROSS):
            table[head, i] = came_prev[i, head]
            table[head, CROSS + blocks + i] = came_next[i, head]
            turned[head, i] = came_prev[i, head].T
            turned[head, CROSS + blocks + i] = came_next[i, head].T

    left = lax.broadcasted_iota(jnp.int32, (block_rows, lanes), 1) < head_dim

    def locate(unit):
        head = lax.div(unit, blocks)
        block = lax.rem(unit, blocks)
        ids = [lists[head, block, j] for j in range(per_list)]
        peer = lax.div(block, each)
        start = pl.multiple_of(lax.rem(block, each) * block_rows, block_rows)
        return head, ids, peer, pl.ds(start, block_rows)

    def apart_of(head, peer, here):
        query_grad = pairs[peer, head, here]
        nothing = jnp.zeros_like(query_grad)
        return jnp.concatenate(
            [jnp.where(left, query_grad, nothing), jnp.where(left, nothing, query_grad)],
            axis=0,
        )

    def score(unit, slot):
        head, ids, peer, here = locate(unit)
        key_value = jnp.concatenate([table[head, i] for i in ids], axis=0)
        both[slot][...] = lax.dot_general(
            key_value,
            apart_of(head, peer, here),
            (((1,), (1,)), ((), ())),
            preferred_element_type=jnp.float32,
        )

    def soften(slot):
        source, target = both[slot], low[slot]
        parts = [slice(i, i + step_rows) for i in range(0, keys, step_rows)]
        top = source[parts[0], :block_rows]
        for part in parts[1:]:
            top = jnp.maximum(top, source[part, :block_rows])
        top = jnp.max(top, axis=0, keepdims=True)
        total = jnp.zeros((step_rows, block_rows), jnp.float32)
        mixed = jnp.zeros((step_rows, block_rows), jnp.float32)
        for part in parts:
            raised = jnp.exp2((source[part, :block_rows] - top) * exponent)
            source[part, :block_rows] = raised
            total += raised
            mixed += raised * source[part, block_rows:]
        inverse = 1.0 / jnp.sum(total, axis=0, keepdims=True)
        correction = jnp.sum(mixed, axis=0, keepdims=True) * inverse
        for part in parts:
            weights = source[part, :block_rows] * inverse
            target[part, block_rows:] = weights.astype(jnp.bfloat16)
            target[part, :block_rows] = (
                weights * (source[part, block_rows:] - correction)
            ).astype(jnp.bfloat16)

    def combine(unit, slot):
        head, ids, peer, here = locate(unit)
        products = low[slot][...]
        terms = jnp.dot(
            products, apart_of(head, peer, here), preferred_element_type=jnp.float32
        )
        for j, i in enumerate(ids):
            sums[head, i] += terms[j * block_rows : (j + 1) * block_rows]
        key_value = jnp.concatenate([turned[head, i] for i in ids], axis=1)
        out = jnp.dot(key_value, products, preferred_element_type=jnp.float32)
        out = jnp.concatenate(
            [out[:head_dim, :block_rows] * scaling, out[head_dim:, block_rows:]], axis=0
        )
        back[peer, head, here] = out.T.astype(back.dtype)

    score(0, 0)
    score(1, 1)
    soften(0)

    def step(i, carry):
        for slot in range(2):
            unit = 2 * i + slot
            combine(unit - 2, slot)
            score(unit, slot)
            soften(1 - slot)
        return carry

    lax.fori_loop(1, units // 2, step, 0)
    combine(units - 2, 0)
    soften(1)
    combine(units - 1, 1)

    factor = jnp.where(left, scaling, 1.0)
    for head in range(heads):
        for i in range(CROSS):
            to_prev[i, head] = (sums[head, i] * factor).astype(to_prev.dtype)
            to_next[i, head] = (sums[head, CROSS + blocks + i] * factor).astype(to_next.dtype)


def attend(lists, came_prev, came_next, pairs, table, turned, sums):
    _, _, block_rows, lanes = came_prev.shape
    dtype = pairs.dtype
    per_list = lists.shape[-1]
    keys = per_list * block_rows
    inside = pl.BlockSpec(memory_space=pltpu.VMEM)
    cross_shape = jax.ShapeDtypeStruct(came_prev.shape, dtype)
    kept = (table, turned, sums)
    return pl.pallas_call(
        functools.partial(attend_kernel, head_dim=lanes // 2, per_list=per_list),
        in_specs=[pl.BlockSpec(memory_space=pltpu.SMEM)] + [inside] * 6,
        out_specs=[inside] * 6,
        out_shape=[pltpu.VMEM(pairs.shape, dtype), cross_shape, cross_shape]
        + [pltpu.VMEM(x.shape, x.dtype) for x in kept],
        input_output_aliases={4: 3, 5: 4, 6: 5},
        scratch_shapes=[
            pltpu.VMEM((keys, 2 * block_rows), jnp.float32),
            pltpu.VMEM((keys, 2 * block_rows), jnp.float32),
            pltpu.VMEM((keys, 2 * block_rows), dtype),
            pltpu.VMEM((keys, 2 * block_rows), dtype),
        ],
        compiler_params=pltpu.CompilerParams(vmem_limit_bytes=SMALL_VMEM),
        name="attend",
    )(lists, came_prev, came_next, *[in_vmem(x) for x in (pairs, *kept)])


def finish_kernel(me, asked, back, kept, later, earlier, *refs, block_rows):
    messages = refs[:-3]
    sums, ready, sems = refs[-3:]
    peers, heads, _, rows, lanes = ready.shape
    each = rows // block_rows
    blocks = peers * each
    head_dim = lanes // 2
    left = lax.broadcasted_iota(jnp.int32, (block_rows, lanes), 1) < head_dim
    factor = jnp.where(left, head_dim ** (-0.5), 1.0)

    def send(item, head):
        target, peer = part_of(messages, me, item)
        return pltpu.make_async_copy(
            ready.at[peer, head], target.at[head], sems.at[item, head]
        )

    for head in range(heads):
        sums[...] = kept[head, CROSS : CROSS + blocks] * factor
        for i in range(CROSS):
            sums[asked[i]] += later[i, head].astype(jnp.float32)
        for i in range(CROSS):
            sums[asked[CROSS + i]] += earlier[i, head].astype(jnp.float32)
        for peer in range(peers):
            ready[peer, head, 1] = back[peer, head]
            for i in range(each):
                ready[peer, head, 0, i * block_rows : (i + 1) * block_rows] = sums[
                    peer * each + i
                ].astype(ready.dtype)
        for item in range(peers):
            send(item, head).start()
    for head in range(heads):
        for item in range(peers):
            send(item, head).wait()


def finish(me, back, kept, later, earlier, asked, apart):
    peers, heads, rows, lanes = back.shape
    _, window, block_rows, _ = kept.shape
    blocks = window - 2 * CROSS
    inside = pl.BlockSpec(memory_space=pltpu.VMEM)
    scalars = pl.BlockSpec(memory_space=pltpu.SMEM)
    shape = (heads, 2, rows, lanes)
    outs = message_outs(peers, shape, back.dtype, apart)
    return pl.pallas_call(
        functools.partial(finish_kernel, block_rows=block_rows),
        in_specs=[scalars, scalars] + [inside] * 4,
        out_specs=[pl.BlockSpec(memory_space=pltpu.HBM)] * len(outs),
        out_shape=outs,
        scratch_shapes=[
            pltpu.VMEM((blocks, block_rows, lanes), jnp.float32),
            pltpu.VMEM((peers,) + shape, back.dtype),
            pltpu.SemaphoreType.DMA((peers, heads)),
        ],
        compiler_params=pltpu.CompilerParams(vmem_limit_bytes=SMALL_VMEM),
        name="finish",
    )(
        me,
        asked,
        in_vmem(back),
        in_vmem(kept),
        later,
        earlier,
    )


def local(query, key, value, d_out, pattern):
    heads_here, blocks, _ = pattern.shape
    peers = lax.axis_size("seq")
    rows, columns = query.shape
    head_dim = columns // (peers * heads_here)
    block_rows = rows * peers // blocks
    chunks = min(CHUNKS, heads_here)
    starts = [-(-heads_here * i // chunks) for i in range(chunks)]
    sizes = [end - start for start, end in zip(starts, starts[1:] + [heads_here])]
    arrays = (query, key, value, d_out)

    own_base = lax.axis_index("slab") * blocks
    block_ids = jnp.arange(blocks, dtype=jnp.int32)
    flat_lists = pattern.reshape(-1)
    reverse_rank = blocks - 1 - block_ids
    hits_prev = jnp.any(flat_lists[:, None] == (own_base - blocks + block_ids)[None, :], axis=0)
    hits_next = jnp.any(flat_lists[:, None] == (own_base + blocks + block_ids)[None, :], axis=0)
    need_prev = lax.top_k(hits_prev.astype(jnp.int32) * blocks + reverse_rank, CROSS)[1]
    need_next = lax.top_k(hits_next.astype(jnp.int32) * blocks + reverse_rank, CROSS)[1]
    asked_next = from_behind(need_prev, "slab", -1)
    asked_prev = from_behind(need_next, "slab", 1)
    asked = jnp.concatenate([asked_next, asked_prev])
    rank_ids = jnp.arange(CROSS, dtype=jnp.int32)
    prev_global = own_base - blocks + need_prev
    next_global = own_base + blocks + need_next
    pos_prev = jnp.sum(jnp.where(pattern[..., None] == prev_global, rank_ids, 0), axis=-1)
    pos_next = jnp.sum(jnp.where(pattern[..., None] == next_global, rank_ids, 0), axis=-1)
    in_own = (pattern >= own_base) & (pattern < own_base + blocks)
    local_ids = jnp.where(
        in_own,
        CROSS + pattern - own_base,
        jnp.where(pattern < own_base, pos_prev, CROSS + blocks + pos_next),
    )

    me = lax.axis_index("seq").astype(jnp.int32).reshape(1)
    me = lax.axis_index("seq").astype(jnp.int32).reshape(1)
    last = chunks - 1
    came = []
    for chunk, (start, size) in enumerate(zip(starts, sizes)):
        after = (asked, local_ids) if came else ()
        packed = pack(arrays, start, size, heads_here, peers, head_dim, after)
        came.append(exchange(packed))
    received = []
    outs = finished = ()
    for chunk, (messages, start, size) in enumerate(zip(came, starts, sizes)):
        for_next, for_prev, table = pick(me, messages, asked, block_rows, finished[:1])
        came_prev = from_behind(for_next, "slab", 1)
        came_next = from_behind(for_prev, "slab", -1)
        turned, pairs, sums = prepare(me, messages, table)
        lists = local_ids[start : start + size]
        back, to_prev, to_next, _, _, kept = attend(
            lists, came_prev, came_next, pairs, table, turned, sums
        )
        later = from_behind(to_prev, "slab", -1)
        earlier = from_behind(to_next, "slab", 1)
        finished = finish(me, back, kept, later, earlier, asked, chunk == last)
        received.append(exchange(finished))
        if chunk == last and heads_here * head_dim % LANES == 0:
            half = peers // 2
            parts = (
                [peers - 1, *range(half // 2)],
                list(range(half // 2, half)),
                list(range(half, peers - 1)),
            )
            for items in parts:
                outs = unpack_items(me, received, starts, heads_here, items, outs)
        else:
            outs = unpack(me, received, starts, heads_here, outs)
    return tuple(outs)


def solution(mesh):
    tokens = P(("slab", "seq"), None)
    return jax.shard_map(
        local,
        mesh=mesh,
        in_specs=(tokens, tokens, tokens, tokens, P("seq", "slab", None)),
        out_specs=(tokens, tokens, tokens, tokens),
        check_vma=False,
    )
```

```python
import functools
import math

import jax
import jax.numpy as jnp
from jax import lax
from jax.experimental import pallas as pl
from jax.experimental.pallas import tpu as pltpu
from jax.sharding import PartitionSpec as P

CROSS = 4
CHUNKS = 2
LANES = 128
SMALL_VMEM = 24 * 1024 * 1024
LARGE_VMEM = 40 * 1024 * 1024


def in_hbm(x):
    return pltpu.with_memory_space_constraint(x, pltpu.HBM)


def in_vmem(x):
    return pltpu.with_memory_space_constraint(x, pltpu.VMEM)


def from_behind(x, axis, by):
    count = lax.axis_size(axis)
    pairs = [(i, i + by) for i in range(count) if 0 <= i + by < count]
    return lax.ppermute(x, axis, pairs)


def part_of(messages, me, item):
    if len(messages) == 1:
        return messages[0].at[item], item
    return messages[item], me[0] ^ (len(messages) - 1 - item)


def message_shape(messages):
    return messages[0].shape[-4:]


def message_outs(peers, shape, dtype, apart):
    if apart:
        return [pltpu.HBM(shape, dtype)] * peers
    return [pltpu.HBM((peers,) + shape, dtype)]


def exchange(messages):
    if len(messages) == 1:
        return [lax.all_to_all(messages[0], "seq", split_axis=0, concat_axis=0, tiled=True)]
    count = len(messages)
    received = list(messages)
    for item in range(count - 1):
        pairs = [(i, i ^ (count - 1 - item)) for i in range(count)]
        received[item] = lax.ppermute(messages[item], "seq", pairs)
    return received


def pack_kernel(query, key, value, d_out, *refs, first, heads, per_peer, head_dim):
    message, stage, ready, in_sems, out_sems = refs[-5:]
    sources = (key, value, query, d_out)
    peers = message.shape[0]

    def span(peer):
        begin = peer * per_peer + first
        low = begin // LANES * LANES
        high = -(-(begin + heads * head_dim) // LANES) * LANES
        return low, high - low, begin - low

    def fetch(peer, i):
        low, width, _ = span(peer)
        return pltpu.make_async_copy(
            sources[i].at[:, pl.ds(low, width)],
            stage.at[i, peer, :, pl.ds(0, width)],
            in_sems.at[i, peer],
        )

    def send(peer):
        return pltpu.make_async_copy(ready.at[peer], message.at[peer], out_sems.at[peer])

    for peer in range(peers):
        for i in range(4):
            fetch(peer, i).start()
    for peer in range(peers):
        for i in range(4):
            fetch(peer, i).wait()
        at = span(peer)[2]
        for head in range(heads):
            lanes = slice(at + head * head_dim, at + (head + 1) * head_dim)
            for kind in range(2):
                ready[peer, head, kind] = jnp.concatenate(
                    [stage[2 * kind, peer, :, lanes], stage[2 * kind + 1, peer, :, lanes]],
                    axis=1,
                )
        send(peer).start()
    for peer in range(peers):
        send(peer).wait()


def pack(arrays, start, heads, heads_here, peers, head_dim, after):
    rows = arrays[0].shape[0]
    dtype = arrays[0].dtype
    shape = (peers, heads, 2, rows, 2 * head_dim)
    width = (-(-heads * head_dim // LANES) + 1) * LANES
    anywhere = pl.BlockSpec(memory_space=pltpu.HBM)
    return pl.pallas_call(
        functools.partial(
            pack_kernel,
            first=start * head_dim,
            heads=heads,
            per_peer=heads_here * head_dim,
            head_dim=head_dim,
        ),
        in_specs=[anywhere] * 4 + [pl.BlockSpec(memory_space=pl.ANY)] * len(after),
        out_specs=[anywhere],
        out_shape=[pltpu.HBM(shape, dtype)],
        scratch_shapes=[
            pltpu.VMEM((4, peers, rows, width), dtype),
            pltpu.VMEM(shape, dtype),
            pltpu.SemaphoreType.DMA((4, peers)),
            pltpu.SemaphoreType.DMA((peers,)),
        ],
        compiler_params=pltpu.CompilerParams(vmem_limit_bytes=SMALL_VMEM),
        name="pack",
    )(*[in_hbm(x) for x in arrays], *after)


def unpack_kernel(me, *refs, chunk, peers, counts, earlier, jobs):
    ends = [sum(counts[: c + 1]) for c in range(chunk + 1)]
    groups = [refs[end - count : end] for end, count in zip(ends, counts)]
    outs = refs[ends[-1] + earlier :][:4]
    stages = refs[-3 - chunk - 1 : -3]
    ready, in_sems, out_sems = refs[-3:]
    head_dim = ready.shape[-1] // 2
    used = sorted({(which, peer) for job in jobs for which, peer, _ in job[1:]})
    chunks_used = sorted({which for which, _ in used})
    heads_used = {
        c: sorted({head for job in jobs for which, _, head in job[1:] if which == c})
        for c in chunks_used
    }

    def fetch(which, item, slot=None):
        heads = heads_used[which]
        some = pl.ds(heads[0], heads[-1] - heads[0] + 1)
        source, peer = part_of(groups[which], me, item)
        slot = peer if slot is None else slot
        return pltpu.make_async_copy(
            source.at[some], stages[which].at[slot, some], in_sems.at[which, slot]
        )

    def send(job, i):
        tile = jobs[job][0]
        return pltpu.make_async_copy(
            ready.at[i, job],
            outs[i].at[:, pl.ds(tile * LANES, LANES)],
            out_sems.at[4 * job + i],
        )

    for item in range(peers):
        for which in chunks_used:
            fetch(which, item).start()
    waited = set()

    def wait_for(which, peer):
        if (which, peer) not in waited:
            fetch(which, 0, peer).wait()
            waited.add((which, peer))

    for job, (tile, left, right) in enumerate(jobs):
        for which, peer, _ in (left, right):
            wait_for(which, peer)
        sides = [stages[which][peer, head] for which, peer, head in (left, right)]
        for i, (kind, at) in enumerate(((1, head_dim), (1, 0), (0, 0), (0, head_dim))):
            ready[i, job] = jnp.concatenate(
                [side[kind, :, at : at + head_dim] for side in sides], axis=1
            )
            send(job, i).start()
    for which in chunks_used:
        for peer in range(peers):
            wait_for(which, peer)
    for job in range(len(jobs)):
        for i in range(4):
            send(job, i).wait()


def unpack(me, messages, starts, heads_here, earlier):
    chunk = len(messages) - 1
    peers = lax.axis_size("seq")
    _, _, rows, pair_dim = message_shape(messages[0])
    head_dim = pair_dim // 2
    columns = peers * heads_here * head_dim
    dtype = messages[0][0].dtype

    def place_of(head):
        peer, local_head = divmod(head, heads_here)
        which = max(c for c, start in enumerate(starts) if start <= local_head)
        return which, peer, local_head - starts[which]

    jobs = []
    for tile in range(columns // LANES):
        left, right = place_of(2 * tile), place_of(2 * tile + 1)
        if max(left[0], right[0]) == chunk:
            jobs.append((tile, left, right))
    if not jobs:
        return earlier
    flat = [x for group in messages for x in group]
    anywhere = pl.BlockSpec(memory_space=pltpu.HBM)
    return pl.pallas_call(
        functools.partial(
            unpack_kernel,
            chunk=chunk,
            peers=peers,
            counts=[len(group) for group in messages],
            earlier=len(earlier),
            jobs=jobs,
        ),
        in_specs=[pl.BlockSpec(memory_space=pltpu.SMEM)]
        + [pl.BlockSpec(memory_space=pl.ANY)] * len(flat)
        + [anywhere] * len(earlier),
        out_specs=[anywhere] * 4,
        out_shape=[pltpu.HBM((rows, columns), dtype)] * 4,
        input_output_aliases={1 + len(flat) + i: i for i in range(len(earlier))},
        scratch_shapes=[pltpu.VMEM((peers,) + message_shape(m), dtype) for m in messages]
        + [
            pltpu.VMEM((4, len(jobs), rows, LANES), dtype),
            pltpu.SemaphoreType.DMA((chunk + 1, peers)),
            pltpu.SemaphoreType.DMA((4 * len(jobs),)),
        ],
        compiler_params=pltpu.CompilerParams(vmem_limit_bytes=SMALL_VMEM),
        name="unpack",
    )(me, *flat, *[in_hbm(x) for x in earlier])


def unpack_items_kernel(me, *refs, items, peers, counts, joint, earlier, jobs, per_peer):
    ends = [sum(counts[: c + 1]) for c in range(len(counts))]
    groups = [refs[end - count : end] for end, count in zip(ends, counts)]
    outs = refs[ends[-1] + earlier :][:4]
    stages = refs[-3 - len(counts) : -3]
    ready, in_sems, out_sems = refs[-3:]
    head_dim = ready.shape[-1] // 2
    used = [
        sorted({head for job in jobs for which, head in job[1:] if which == c})
        for c in range(len(counts))
    ]

    def peer_of(j):
        return me[0] ^ (peers - 1 - items[j])

    def fetch(which, j):
        group = groups[which]
        source = group[0].at[peer_of(j)] if joint[which] else group[j]
        some = pl.ds(used[which][0], used[which][-1] - used[which][0] + 1)
        return pltpu.make_async_copy(
            source.at[some], stages[which].at[j, some], in_sems.at[which, j]
        )

    def send(j, job, i):
        first = pl.multiple_of(peer_of(j) * per_peer, LANES) + jobs[job][0] * LANES
        return pltpu.make_async_copy(
            ready.at[j, i, job], outs[i].at[:, pl.ds(first, LANES)], out_sems.at[j, i, job]
        )

    steps = [(j, which) for j in range(len(items)) for which in range(len(counts))]
    steps = [(j, which) for j, which in steps if used[which]]
    for j, which in steps:
        fetch(which, j).start()
    for j in range(len(items)):
        for at, which in steps:
            if at == j:
                fetch(which, j).wait()
        for job, (_, left, right) in enumerate(jobs):
            sides = [stages[which][j, head] for which, head in (left, right)]
            for i, (kind, at) in enumerate(((1, head_dim), (1, 0), (0, 0), (0, head_dim))):
                ready[j, i, job] = jnp.concatenate(
                    [side[kind, :, at : at + head_dim] for side in sides], axis=1
                )
                send(j, job, i).start()
    for j in range(len(items)):
        for job in range(len(jobs)):
            for i in range(4):
                send(j, job, i).wait()


def unpack_items(me, messages, starts, heads_here, items, earlier):
    chunk = len(messages) - 1
    peers = lax.axis_size("seq")
    _, _, rows, pair_dim = message_shape(messages[0])
    head_dim = pair_dim // 2
    per_peer = heads_here * head_dim
    dtype = messages[0][0].dtype

    def place_of(head):
        which = max(c for c, start in enumerate(starts) if start <= head)
        return which, head - starts[which]

    jobs = []
    for tile in range(per_peer // LANES):
        left, right = place_of(2 * tile), place_of(2 * tile + 1)
        if max(left[0], right[0]) == chunk:
            jobs.append((tile, left, right))
    groups = [
        list(group) if len(group) == 1 else [group[item] for item in items]
        for group in messages
    ]
    flat = [x for group in groups for x in group]
    anywhere = pl.BlockSpec(memory_space=pltpu.HBM)
    return pl.pallas_call(
        functools.partial(
            unpack_items_kernel,
            items=items,
            peers=peers,
            counts=[len(group) for group in groups],
            joint=[len(group) == 1 for group in messages],
            earlier=len(earlier),
            jobs=jobs,
            per_peer=per_peer,
        ),
        in_specs=[pl.BlockSpec(memory_space=pltpu.SMEM)]
        + [pl.BlockSpec(memory_space=pl.ANY)] * len(flat)
        + [anywhere] * len(earlier),
        out_specs=[anywhere] * 4,
        out_shape=[pltpu.HBM((rows, peers * per_peer), dtype)] * 4,
        input_output_aliases={1 + len(flat) + i: i for i in range(len(earlier))},
        scratch_shapes=[
            pltpu.VMEM((len(items),) + message_shape(m), dtype) for m in messages
        ]
        + [
            pltpu.VMEM((len(items), 4, len(jobs), rows, LANES), dtype),
            pltpu.SemaphoreType.DMA((chunk + 1, len(items))),
            pltpu.SemaphoreType.DMA((len(items), 4, len(jobs))),
        ],
        compiler_params=pltpu.CompilerParams(vmem_limit_bytes=SMALL_VMEM),
        name="unpack_items",
    )(me, *flat, *[in_hbm(x) for x in earlier])


def pick_kernel(me, asked, *refs, count):
    for_next, for_prev, table, sems = refs[-4:]
    heads, window, block_rows, _ = table.shape
    peers, each = sems.shape

    def fetch(item, i):
        source, peer = part_of(refs[:count], me, item)
        rows = pl.ds(i * block_rows, block_rows)
        return pltpu.make_async_copy(
            source.at[:, 0, rows], table.at[:, CROSS + peer * each + i], sems.at[item, i]
        )

    for item in range(peers):
        for i in range(each):
            fetch(item, i).start()
    for item in range(peers):
        for i in range(each):
            fetch(item, i).wait()
    for i in range(CROSS):
        for_next[i] = table[:, CROSS + asked[i]]
        for_prev[i] = table[:, CROSS + asked[CROSS + i]]


def pick(me, messages, asked, block_rows, after):
    heads, _, rows, lanes = message_shape(messages)
    dtype = messages[0].dtype
    peers = lax.axis_size("seq")
    each = rows // block_rows
    window = peers * each + 2 * CROSS
    picked = jax.ShapeDtypeStruct((CROSS, heads, block_rows, lanes), dtype)
    return pl.pallas_call(
        functools.partial(pick_kernel, count=len(messages)),
        in_specs=[pl.BlockSpec(memory_space=pltpu.SMEM)] * 2
        + [pl.BlockSpec(memory_space=pl.ANY)] * (len(messages) + len(after)),
        out_specs=[pl.BlockSpec(memory_space=pltpu.VMEM)] * 3,
        out_shape=[picked, picked, pltpu.VMEM((heads, window, block_rows, lanes), dtype)],
        scratch_shapes=[pltpu.SemaphoreType.DMA((peers, each))],
        compiler_params=pltpu.CompilerParams(vmem_limit_bytes=SMALL_VMEM),
        name="pick",
    )(me, asked, *messages, *[in_hbm(x) for x in after])


def prepare_kernel(me, table, *refs, peers):
    messages = refs[:-4]
    turned, pairs, sums, sems = refs[-4:]
    heads, window, _, _ = table.shape

    def fetch(item):
        source, peer = part_of(messages, me, item)
        return pltpu.make_async_copy(source.at[:, 1], pairs.at[peer], sems.at[item])

    for item in range(peers):
        fetch(item).start()
    for head in range(heads):

        def clear(i, carry):
            sums[head, i] = jnp.zeros(sums.shape[2:], sums.dtype)
            return carry

        def turn(i, carry):
            turned[head, i] = table[head, i].T
            return carry

        lax.fori_loop(0, window, clear, 0)
        lax.fori_loop(CROSS, window - CROSS, turn, 0)
    for item in range(peers):
        fetch(item).wait()


def prepare(me, messages, table):
    heads, _, rows, lanes = message_shape(messages)
    _, window, block_rows, _ = table.shape
    dtype = messages[0].dtype
    peers = lax.axis_size("seq")
    inside = pl.BlockSpec(memory_space=pltpu.VMEM)
    return pl.pallas_call(
        functools.partial(prepare_kernel, peers=peers),
        in_specs=[pl.BlockSpec(memory_space=pltpu.SMEM), inside]
        + [pl.BlockSpec(memory_space=pl.ANY)] * len(messages),
        out_specs=[inside] * 3,
        out_shape=[
            pltpu.VMEM((heads, window, lanes, block_rows), dtype),
            pltpu.VMEM((peers, heads, rows, lanes), dtype),
            pltpu.VMEM((heads, window, block_rows, lanes), jnp.float32),
        ],
        scratch_shapes=[pltpu.SemaphoreType.DMA((peers,))],
        compiler_params=pltpu.CompilerParams(vmem_limit_bytes=SMALL_VMEM),
        name="prepare",
    )(me, in_vmem(table), *messages)


def attend_kernel(
    lists,
    came_prev,
    came_next,
    pairs,
    table_in,
    turned_in,
    sums_in,
    back,
    to_prev,
    to_next,
    table,
    turned,
    sums,
    both_even,
    both_odd,
    low_even,
    low_odd,
    *,
    head_dim,
    per_list,
):
    del table_in, turned_in, sums_in
    peers, heads, rows, lanes = pairs.shape
    _, window, block_rows, _ = table.shape
    each = rows // block_rows
    blocks = peers * each
    units = heads * blocks
    keys = per_list * block_rows
    scaling = head_dim ** (-0.5)
    exponent = scaling * math.log2(math.e)
    both = (both_even, both_odd)
    low = (low_even, low_odd)
    step_rows = 64

    for head in range(heads):
        for i in range(CROSS):
            table[head, i] = came_prev[i, head]
            table[head, CROSS + blocks + i] = came_next[i, head]
            turned[head, i] = came_prev[i, head].T
            turned[head, CROSS + blocks + i] = came_next[i, head].T

    left = lax.broadcasted_iota(jnp.int32, (block_rows, lanes), 1) < head_dim

    def locate(unit):
        head = lax.div(unit, blocks)
        block = lax.rem(unit, blocks)
        ids = [lists[head, block, j] for j in range(per_list)]
        peer = lax.div(block, each)
        start = pl.multiple_of(lax.rem(block, each) * block_rows, block_rows)
        return head, ids, peer, pl.ds(start, block_rows)

    def apart_of(head, peer, here):
        query_grad = pairs[peer, head, here]
        nothing = jnp.zeros_like(query_grad)
        return jnp.concatenate(
            [jnp.where(left, query_grad, nothing), jnp.where(left, nothing, query_grad)],
            axis=0,
        )

    def score(unit, slot):
        head, ids, peer, here = locate(unit)
        key_value = jnp.concatenate([table[head, i] for i in ids], axis=0)
        both[slot][...] = lax.dot_general(
            key_value,
            apart_of(head, peer, here),
            (((1,), (1,)), ((), ())),
            preferred_element_type=jnp.float32,
        )

    def soften(slot):
        source, target = both[slot], low[slot]
        parts = [slice(i, i + step_rows) for i in range(0, keys, step_rows)]
        top = source[parts[0], :block_rows]
        for part in parts[1:]:
            top = jnp.maximum(top, source[part, :block_rows])
        top = jnp.max(top, axis=0, keepdims=True)
        total = jnp.zeros((step_rows, block_rows), jnp.float32)
        mixed = jnp.zeros((step_rows, block_rows), jnp.float32)
        for part in parts:
            raised = jnp.exp2((source[part, :block_rows] - top) * exponent)
            source[part, :block_rows] = raised
            total += raised
            mixed += raised * source[part, block_rows:]
        inverse = 1.0 / jnp.sum(total, axis=0, keepdims=True)
        correction = jnp.sum(mixed, axis=0, keepdims=True) * inverse
        for part in parts:
            weights = source[part, :block_rows] * inverse
            target[part, block_rows:] = weights.astype(jnp.bfloat16)
            target[part, :block_rows] = (
                weights * (source[part, block_rows:] - correction)
            ).astype(jnp.bfloat16)

    def combine(unit, slot):
        head, ids, peer, here = locate(unit)
        products = low[slot][...]
        terms = jnp.dot(
            products, apart_of(head, peer, here), preferred_element_type=jnp.float32
        )
        for j, i in enumerate(ids):
            sums[head, i] += terms[j * block_rows : (j + 1) * block_rows]
        key_value = jnp.concatenate([turned[head, i] for i in ids], axis=1)
        out = jnp.dot(key_value, products, preferred_element_type=jnp.float32)
        out = jnp.concatenate(
            [out[:head_dim, :block_rows] * scaling, out[head_dim:, block_rows:]], axis=0
        )
        back[peer, head, here] = out.T.astype(back.dtype)

    score(0, 0)
    score(1, 1)
    soften(0)

    def step(i, carry):
        for slot in range(2):
            unit = 2 * i + slot
            combine(unit - 2, slot)
            score(unit, slot)
            soften(1 - slot)
        return carry

    lax.fori_loop(1, units // 2, step, 0)
    combine(units - 2, 0)
    soften(1)
    combine(units - 1, 1)

    factor = jnp.where(left, scaling, 1.0)
    for head in range(heads):
        for i in range(CROSS):
            to_prev[i, head] = (sums[head, i] * factor).astype(to_prev.dtype)
            to_next[i, head] = (sums[head, CROSS + blocks + i] * factor).astype(to_next.dtype)


def attend(lists, came_prev, came_next, pairs, table, turned, sums):
    _, _, block_rows, lanes = came_prev.shape
    dtype = pairs.dtype
    per_list = lists.shape[-1]
    keys = per_list * block_rows
    inside = pl.BlockSpec(memory_space=pltpu.VMEM)
    cross_shape = jax.ShapeDtypeStruct(came_prev.shape, dtype)
    kept = (table, turned, sums)
    return pl.pallas_call(
        functools.partial(attend_kernel, head_dim=lanes // 2, per_list=per_list),
        in_specs=[pl.BlockSpec(memory_space=pltpu.SMEM)] + [inside] * 6,
        out_specs=[inside] * 6,
        out_shape=[pltpu.VMEM(pairs.shape, dtype), cross_shape, cross_shape]
        + [pltpu.VMEM(x.shape, x.dtype) for x in kept],
        input_output_aliases={4: 3, 5: 4, 6: 5},
        scratch_shapes=[
            pltpu.VMEM((keys, 2 * block_rows), jnp.float32),
            pltpu.VMEM((keys, 2 * block_rows), jnp.float32),
            pltpu.VMEM((keys, 2 * block_rows), dtype),
            pltpu.VMEM((keys, 2 * block_rows), dtype),
        ],
        compiler_params=pltpu.CompilerParams(vmem_limit_bytes=SMALL_VMEM),
        name="attend",
    )(lists, came_prev, came_next, *[in_vmem(x) for x in (pairs, *kept)])


def finish_kernel(me, asked, back, kept, later, earlier, *refs, block_rows):
    messages = refs[:-3]
    sums, ready, sems = refs[-3:]
    peers, heads, _, rows, lanes = ready.shape
    each = rows // block_rows
    blocks = peers * each
    head_dim = lanes // 2
    left = lax.broadcasted_iota(jnp.int32, (block_rows, lanes), 1) < head_dim
    factor = jnp.where(left, head_dim ** (-0.5), 1.0)

    def send(item, head):
        target, peer = part_of(messages, me, item)
        return pltpu.make_async_copy(
            ready.at[peer, head], target.at[head], sems.at[item, head]
        )

    for head in range(heads):
        sums[...] = kept[head, CROSS : CROSS + blocks] * factor
        for i in range(CROSS):
            sums[asked[i]] += later[i, head].astype(jnp.float32)
        for i in range(CROSS):
            sums[asked[CROSS + i]] += earlier[i, head].astype(jnp.float32)
        for peer in range(peers):
            ready[peer, head, 1] = back[peer, head]
            for i in range(each):
                ready[peer, head, 0, i * block_rows : (i + 1) * block_rows] = sums[
                    peer * each + i
                ].astype(ready.dtype)
        for item in range(peers):
            send(item, head).start()
    for head in range(heads):
        for item in range(peers):
            send(item, head).wait()


def finish(me, back, kept, later, earlier, asked, apart):
    peers, heads, rows, lanes = back.shape
    _, window, block_rows, _ = kept.shape
    blocks = window - 2 * CROSS
    inside = pl.BlockSpec(memory_space=pltpu.VMEM)
    scalars = pl.BlockSpec(memory_space=pltpu.SMEM)
    shape = (heads, 2, rows, lanes)
    outs = message_outs(peers, shape, back.dtype, apart)
    return pl.pallas_call(
        functools.partial(finish_kernel, block_rows=block_rows),
        in_specs=[scalars, scalars] + [inside] * 4,
        out_specs=[pl.BlockSpec(memory_space=pltpu.HBM)] * len(outs),
        out_shape=outs,
        scratch_shapes=[
            pltpu.VMEM((blocks, block_rows, lanes), jnp.float32),
            pltpu.VMEM((peers,) + shape, back.dtype),
            pltpu.SemaphoreType.DMA((peers, heads)),
        ],
        compiler_params=pltpu.CompilerParams(vmem_limit_bytes=SMALL_VMEM),
        name="finish",
    )(
        me,
        asked,
        in_vmem(back),
        in_vmem(kept),
        later,
        earlier,
    )


def local(query, key, value, d_out, pattern):
    heads_here, blocks, _ = pattern.shape
    peers = lax.axis_size("seq")
    rows, columns = query.shape
    head_dim = columns // (peers * heads_here)
    block_rows = rows * peers // blocks
    chunks = min(CHUNKS, heads_here)
    starts = [-(-heads_here * i // chunks) for i in range(chunks)]
    sizes = [end - start for start, end in zip(starts, starts[1:] + [heads_here])]
    arrays = (query, key, value, d_out)

    own_base = lax.axis_index("slab") * blocks
    block_ids = jnp.arange(blocks, dtype=jnp.int32)
    flat_lists = pattern.reshape(-1)
    reverse_rank = blocks - 1 - block_ids
    hits_prev = jnp.any(flat_lists[:, None] == (own_base - blocks + block_ids)[None, :], axis=0)
    hits_next = jnp.any(flat_lists[:, None] == (own_base + blocks + block_ids)[None, :], axis=0)
    need_prev = lax.top_k(hits_prev.astype(jnp.int32) * blocks + reverse_rank, CROSS)[1]
    need_next = lax.top_k(hits_next.astype(jnp.int32) * blocks + reverse_rank, CROSS)[1]
    asked_next = from_behind(need_prev, "slab", -1)
    asked_prev = from_behind(need_next, "slab", 1)
    asked = jnp.concatenate([asked_next, asked_prev])
    rank_ids = jnp.arange(CROSS, dtype=jnp.int32)
    prev_global = own_base - blocks + need_prev
    next_global = own_base + blocks + need_next
    pos_prev = jnp.sum(jnp.where(pattern[..., None] == prev_global, rank_ids, 0), axis=-1)
    pos_next = jnp.sum(jnp.where(pattern[..., None] == next_global, rank_ids, 0), axis=-1)
    in_own = (pattern >= own_base) & (pattern < own_base + blocks)
    local_ids = jnp.where(
        in_own,
        CROSS + pattern - own_base,
        jnp.where(pattern < own_base, pos_prev, CROSS + blocks + pos_next),
    )

    me = lax.axis_index("seq").astype(jnp.int32).reshape(1)
    last = chunks - 1
    came = []
    for chunk, (start, size) in enumerate(zip(starts, sizes)):
        after = (asked, local_ids) if came else ()
        packed = pack(arrays, start, size, heads_here, peers, head_dim, after)
        came.append(exchange(packed))
    received = []
    outs = finished = ()
    for chunk, (messages, start, size) in enumerate(zip(came, starts, sizes)):
        for_next, for_prev, table = pick(me, messages, asked, block_rows, finished[:1])
        came_prev = from_behind(for_next, "slab", 1)
        came_next = from_behind(for_prev, "slab", -1)
        turned, pairs, sums = prepare(me, messages, table)
        lists = local_ids[start : start + size]
        back, to_prev, to_next, _, _, kept = attend(
            lists, came_prev, came_next, pairs, table, turned, sums
        )
        later = from_behind(to_prev, "slab", -1)
        earlier = from_behind(to_next, "slab", 1)
        finished = finish(me, back, kept, later, earlier, asked, chunk == last)
        received.append(exchange(finished))
        if chunk == last and heads_here * head_dim % LANES == 0:
            half = peers // 2
            parts = (
                [peers - 1, *range(half // 2)],
                list(range(half // 2, half - 1)),
                list(range(half - 1, peers - 1)),
            )
            for items in parts:
                outs = unpack_items(me, received, starts, heads_here, items, outs)
        else:
            outs = unpack(me, received, starts, heads_here, outs)
    return tuple(outs)


def solution(mesh):
    tokens = P(("slab", "seq"), None)
    return jax.shard_map(
        local,
        mesh=mesh,
        in_specs=(tokens, tokens, tokens, tokens, P("seq", "slab", None)),
        out_specs=(tokens, tokens, tokens, tokens),
        check_vma=False,
    )
```

```python
import functools
import math

import jax
import jax.numpy as jnp
from jax import lax
from jax.experimental import pallas as pl
from jax.experimental.pallas import tpu as pltpu
from jax.sharding import PartitionSpec as P

CROSS = 4
CHUNKS = 2
LANES = 128
SMALL_VMEM = 24 * 1024 * 1024
LARGE_VMEM = 40 * 1024 * 1024


def in_hbm(x):
    return pltpu.with_memory_space_constraint(x, pltpu.HBM)


def in_vmem(x):
    return pltpu.with_memory_space_constraint(x, pltpu.VMEM)


def from_behind(x, axis, by):
    count = lax.axis_size(axis)
    pairs = [(i, i + by) for i in range(count) if 0 <= i + by < count]
    return lax.ppermute(x, axis, pairs)


def part_of(messages, me, item):
    if len(messages) == 1:
        return messages[0].at[item], item
    return messages[item], me[0] ^ (len(messages) - 1 - item)


def message_shape(messages):
    return messages[0].shape[-4:]


def message_outs(peers, shape, dtype, apart):
    if apart:
        return [pltpu.HBM(shape, dtype)] * peers
    return [pltpu.HBM((peers,) + shape, dtype)]


def exchange(messages):
    if len(messages) == 1:
        return [lax.all_to_all(messages[0], "seq", split_axis=0, concat_axis=0, tiled=True)]
    count = len(messages)
    received = list(messages)
    for item in range(count - 1):
        pairs = [(i, i ^ (count - 1 - item)) for i in range(count)]
        received[item] = lax.ppermute(messages[item], "seq", pairs)
    return received


def pack_kernel(query, key, value, d_out, *refs, first, heads, per_peer, head_dim):
    message, stage, ready, in_sems, out_sems = refs[-5:]
    sources = (key, value, query, d_out)
    peers = message.shape[0]

    def span(peer):
        begin = peer * per_peer + first
        low = begin // LANES * LANES
        high = -(-(begin + heads * head_dim) // LANES) * LANES
        return low, high - low, begin - low

    def fetch(peer, i):
        low, width, _ = span(peer)
        return pltpu.make_async_copy(
            sources[i].at[:, pl.ds(low, width)],
            stage.at[i, peer, :, pl.ds(0, width)],
            in_sems.at[i, peer],
        )

    def send(peer):
        return pltpu.make_async_copy(ready.at[peer], message.at[peer], out_sems.at[peer])

    for peer in range(peers):
        for i in range(4):
            fetch(peer, i).start()
    for peer in range(peers):
        for i in range(4):
            fetch(peer, i).wait()
        at = span(peer)[2]
        for head in range(heads):
            lanes = slice(at + head * head_dim, at + (head + 1) * head_dim)
            for kind in range(2):
                ready[peer, head, kind] = jnp.concatenate(
                    [stage[2 * kind, peer, :, lanes], stage[2 * kind + 1, peer, :, lanes]],
                    axis=1,
                )
        send(peer).start()
    for peer in range(peers):
        send(peer).wait()


def pack(arrays, start, heads, heads_here, peers, head_dim, after):
    rows = arrays[0].shape[0]
    dtype = arrays[0].dtype
    shape = (peers, heads, 2, rows, 2 * head_dim)
    width = (-(-heads * head_dim // LANES) + 1) * LANES
    anywhere = pl.BlockSpec(memory_space=pltpu.HBM)
    return pl.pallas_call(
        functools.partial(
            pack_kernel,
            first=start * head_dim,
            heads=heads,
            per_peer=heads_here * head_dim,
            head_dim=head_dim,
        ),
        in_specs=[anywhere] * 4 + [pl.BlockSpec(memory_space=pl.ANY)] * len(after),
        out_specs=[anywhere],
        out_shape=[pltpu.HBM(shape, dtype)],
        scratch_shapes=[
            pltpu.VMEM((4, peers, rows, width), dtype),
            pltpu.VMEM(shape, dtype),
            pltpu.SemaphoreType.DMA((4, peers)),
            pltpu.SemaphoreType.DMA((peers,)),
        ],
        compiler_params=pltpu.CompilerParams(vmem_limit_bytes=SMALL_VMEM),
        name="pack",
    )(*[in_hbm(x) for x in arrays], *after)


def unpack_kernel(me, *refs, chunk, peers, counts, earlier, jobs):
    ends = [sum(counts[: c + 1]) for c in range(chunk + 1)]
    groups = [refs[end - count : end] for end, count in zip(ends, counts)]
    outs = refs[ends[-1] + earlier :][:4]
    stages = refs[-3 - chunk - 1 : -3]
    ready, in_sems, out_sems = refs[-3:]
    head_dim = ready.shape[-1] // 2
    used = sorted({(which, peer) for job in jobs for which, peer, _ in job[1:]})
    chunks_used = sorted({which for which, _ in used})
    heads_used = {
        c: sorted({head for job in jobs for which, _, head in job[1:] if which == c})
        for c in chunks_used
    }

    def fetch(which, item, slot=None):
        heads = heads_used[which]
        some = pl.ds(heads[0], heads[-1] - heads[0] + 1)
        source, peer = part_of(groups[which], me, item)
        slot = peer if slot is None else slot
        return pltpu.make_async_copy(
            source.at[some], stages[which].at[slot, some], in_sems.at[which, slot]
        )

    def send(job, i):
        tile = jobs[job][0]
        return pltpu.make_async_copy(
            ready.at[i, job],
            outs[i].at[:, pl.ds(tile * LANES, LANES)],
            out_sems.at[4 * job + i],
        )

    for item in range(peers):
        for which in chunks_used:
            fetch(which, item).start()
    waited = set()

    def wait_for(which, peer):
        if (which, peer) not in waited:
            fetch(which, 0, peer).wait()
            waited.add((which, peer))

    for job, (tile, left, right) in enumerate(jobs):
        for which, peer, _ in (left, right):
            wait_for(which, peer)
        sides = [stages[which][peer, head] for which, peer, head in (left, right)]
        for i, (kind, at) in enumerate(((1, head_dim), (1, 0), (0, 0), (0, head_dim))):
            ready[i, job] = jnp.concatenate(
                [side[kind, :, at : at + head_dim] for side in sides], axis=1
            )
            send(job, i).start()
    for which in chunks_used:
        for peer in range(peers):
            wait_for(which, peer)
    for job in range(len(jobs)):
        for i in range(4):
            send(job, i).wait()


def unpack(me, messages, starts, heads_here, earlier):
    chunk = len(messages) - 1
    peers = lax.axis_size("seq")
    _, _, rows, pair_dim = message_shape(messages[0])
    head_dim = pair_dim // 2
    columns = peers * heads_here * head_dim
    dtype = messages[0][0].dtype

    def place_of(head):
        peer, local_head = divmod(head, heads_here)
        which = max(c for c, start in enumerate(starts) if start <= local_head)
        return which, peer, local_head - starts[which]

    jobs = []
    for tile in range(columns // LANES):
        left, right = place_of(2 * tile), place_of(2 * tile + 1)
        if max(left[0], right[0]) == chunk:
            jobs.append((tile, left, right))
    if not jobs:
        return earlier
    flat = [x for group in messages for x in group]
    anywhere = pl.BlockSpec(memory_space=pltpu.HBM)
    return pl.pallas_call(
        functools.partial(
            unpack_kernel,
            chunk=chunk,
            peers=peers,
            counts=[len(group) for group in messages],
            earlier=len(earlier),
            jobs=jobs,
        ),
        in_specs=[pl.BlockSpec(memory_space=pltpu.SMEM)]
        + [pl.BlockSpec(memory_space=pl.ANY)] * len(flat)
        + [anywhere] * len(earlier),
        out_specs=[anywhere] * 4,
        out_shape=[pltpu.HBM((rows, columns), dtype)] * 4,
        input_output_aliases={1 + len(flat) + i: i for i in range(len(earlier))},
        scratch_shapes=[pltpu.VMEM((peers,) + message_shape(m), dtype) for m in messages]
        + [
            pltpu.VMEM((4, len(jobs), rows, LANES), dtype),
            pltpu.SemaphoreType.DMA((chunk + 1, peers)),
            pltpu.SemaphoreType.DMA((4 * len(jobs),)),
        ],
        compiler_params=pltpu.CompilerParams(vmem_limit_bytes=SMALL_VMEM),
        name="unpack",
    )(me, *flat, *[in_hbm(x) for x in earlier])


def unpack_items_kernel(me, *refs, items, peers, counts, joint, earlier, jobs, per_peer):
    ends = [sum(counts[: c + 1]) for c in range(len(counts))]
    groups = [refs[end - count : end] for end, count in zip(ends, counts)]
    outs = refs[ends[-1] + earlier :][:4]
    stages = refs[-3 - len(counts) : -3]
    ready, in_sems, out_sems = refs[-3:]
    head_dim = ready.shape[-1] // 2
    used = [
        sorted({head for job in jobs for which, head in job[1:] if which == c})
        for c in range(len(counts))
    ]

    def peer_of(j):
        return me[0] ^ (peers - 1 - items[j])

    def fetch(which, j):
        group = groups[which]
        source = group[0].at[peer_of(j)] if joint[which] else group[j]
        some = pl.ds(used[which][0], used[which][-1] - used[which][0] + 1)
        return pltpu.make_async_copy(
            source.at[some], stages[which].at[j, some], in_sems.at[which, j]
        )

    def send(j, job, i):
        first = pl.multiple_of(peer_of(j) * per_peer, LANES) + jobs[job][0] * LANES
        return pltpu.make_async_copy(
            ready.at[j, i, job], outs[i].at[:, pl.ds(first, LANES)], out_sems.at[j, i, job]
        )

    steps = [(j, which) for j in range(len(items)) for which in range(len(counts))]
    steps = [(j, which) for j, which in steps if used[which]]
    for j, which in steps:
        fetch(which, j).start()
    for j in range(len(items)):
        for at, which in steps:
            if at == j:
                fetch(which, j).wait()
        for job, (_, left, right) in enumerate(jobs):
            sides = [stages[which][j, head] for which, head in (left, right)]
            for i, (kind, at) in enumerate(((1, head_dim), (1, 0), (0, 0), (0, head_dim))):
                ready[j, i, job] = jnp.concatenate(
                    [side[kind, :, at : at + head_dim] for side in sides], axis=1
                )
                send(j, job, i).start()
    for j in range(len(items)):
        for job in range(len(jobs)):
            for i in range(4):
                send(j, job, i).wait()


def unpack_items(me, messages, starts, heads_here, items, earlier):
    chunk = len(messages) - 1
    peers = lax.axis_size("seq")
    _, _, rows, pair_dim = message_shape(messages[0])
    head_dim = pair_dim // 2
    per_peer = heads_here * head_dim
    dtype = messages[0][0].dtype

    def place_of(head):
        which = max(c for c, start in enumerate(starts) if start <= head)
        return which, head - starts[which]

    jobs = []
    for tile in range(per_peer // LANES):
        left, right = place_of(2 * tile), place_of(2 * tile + 1)
        if max(left[0], right[0]) == chunk:
            jobs.append((tile, left, right))
    groups = [
        list(group) if len(group) == 1 else [group[item] for item in items]
        for group in messages
    ]
    flat = [x for group in groups for x in group]
    anywhere = pl.BlockSpec(memory_space=pltpu.HBM)
    return pl.pallas_call(
        functools.partial(
            unpack_items_kernel,
            items=items,
            peers=peers,
            counts=[len(group) for group in groups],
            joint=[len(group) == 1 for group in messages],
            earlier=len(earlier),
            jobs=jobs,
            per_peer=per_peer,
        ),
        in_specs=[pl.BlockSpec(memory_space=pltpu.SMEM)]
        + [pl.BlockSpec(memory_space=pl.ANY)] * len(flat)
        + [anywhere] * len(earlier),
        out_specs=[anywhere] * 4,
        out_shape=[pltpu.HBM((rows, peers * per_peer), dtype)] * 4,
        input_output_aliases={1 + len(flat) + i: i for i in range(len(earlier))},
        scratch_shapes=[
            pltpu.VMEM((len(items),) + message_shape(m), dtype) for m in messages
        ]
        + [
            pltpu.VMEM((len(items), 4, len(jobs), rows, LANES), dtype),
            pltpu.SemaphoreType.DMA((chunk + 1, len(items))),
            pltpu.SemaphoreType.DMA((len(items), 4, len(jobs))),
        ],
        compiler_params=pltpu.CompilerParams(vmem_limit_bytes=SMALL_VMEM),
        name="unpack_items",
    )(me, *flat, *[in_hbm(x) for x in earlier])


def pick_kernel(me, asked, *refs, count):
    for_next, for_prev, table, sems = refs[-4:]
    heads, window, block_rows, _ = table.shape
    peers, each = sems.shape

    def fetch(item, i):
        source, peer = part_of(refs[:count], me, item)
        rows = pl.ds(i * block_rows, block_rows)
        return pltpu.make_async_copy(
            source.at[:, 0, rows], table.at[:, CROSS + peer * each + i], sems.at[item, i]
        )

    for item in range(peers):
        for i in range(each):
            fetch(item, i).start()
    for item in range(peers):
        for i in range(each):
            fetch(item, i).wait()
    for i in range(CROSS):
        for_next[i] = table[:, CROSS + asked[i]]
        for_prev[i] = table[:, CROSS + asked[CROSS + i]]


def pick(me, messages, asked, block_rows, after):
    heads, _, rows, lanes = message_shape(messages)
    dtype = messages[0].dtype
    peers = lax.axis_size("seq")
    each = rows // block_rows
    window = peers * each + 2 * CROSS
    picked = jax.ShapeDtypeStruct((CROSS, heads, block_rows, lanes), dtype)
    return pl.pallas_call(
        functools.partial(pick_kernel, count=len(messages)),
        in_specs=[pl.BlockSpec(memory_space=pltpu.SMEM)] * 2
        + [pl.BlockSpec(memory_space=pl.ANY)] * (len(messages) + len(after)),
        out_specs=[pl.BlockSpec(memory_space=pltpu.VMEM)] * 3,
        out_shape=[picked, picked, pltpu.VMEM((heads, window, block_rows, lanes), dtype)],
        scratch_shapes=[pltpu.SemaphoreType.DMA((peers, each))],
        compiler_params=pltpu.CompilerParams(vmem_limit_bytes=SMALL_VMEM),
        name="pick",
    )(me, asked, *messages, *[in_hbm(x) for x in after])


def prepare_kernel(me, table, *refs, peers):
    messages = refs[:-4]
    turned, pairs, sums, sems = refs[-4:]
    heads, window, _, _ = table.shape

    def fetch(item):
        source, peer = part_of(messages, me, item)
        return pltpu.make_async_copy(source.at[:, 1], pairs.at[peer], sems.at[item])

    for item in range(peers):
        fetch(item).start()
    for head in range(heads):

        def clear(i, carry):
            sums[head, i] = jnp.zeros(sums.shape[2:], sums.dtype)
            return carry

        def turn(i, carry):
            turned[head, i] = table[head, i].T
            return carry

        lax.fori_loop(0, window, clear, 0)
        lax.fori_loop(CROSS, window - CROSS, turn, 0)
    for item in range(peers):
        fetch(item).wait()


def prepare(me, messages, table):
    heads, _, rows, lanes = message_shape(messages)
    _, window, block_rows, _ = table.shape
    dtype = messages[0].dtype
    peers = lax.axis_size("seq")
    inside = pl.BlockSpec(memory_space=pltpu.VMEM)
    return pl.pallas_call(
        functools.partial(prepare_kernel, peers=peers),
        in_specs=[pl.BlockSpec(memory_space=pltpu.SMEM), inside]
        + [pl.BlockSpec(memory_space=pl.ANY)] * len(messages),
        out_specs=[inside] * 3,
        out_shape=[
            pltpu.VMEM((heads, window, lanes, block_rows), dtype),
            pltpu.VMEM((peers, heads, rows, lanes), dtype),
            pltpu.VMEM((heads, window, block_rows, lanes), jnp.float32),
        ],
        scratch_shapes=[pltpu.SemaphoreType.DMA((peers,))],
        compiler_params=pltpu.CompilerParams(vmem_limit_bytes=SMALL_VMEM),
        name="prepare",
    )(me, in_vmem(table), *messages)


def attend_kernel(
    lists,
    came_prev,
    came_next,
    pairs,
    table_in,
    turned_in,
    sums_in,
    back,
    to_prev,
    to_next,
    table,
    turned,
    sums,
    both_even,
    both_odd,
    low_even,
    low_odd,
    *,
    head_dim,
    per_list,
):
    del table_in, turned_in, sums_in
    peers, heads, rows, lanes = pairs.shape
    _, window, block_rows, _ = table.shape
    each = rows // block_rows
    blocks = peers * each
    units = heads * blocks
    keys = per_list * block_rows
    scaling = head_dim ** (-0.5)
    exponent = scaling * math.log2(math.e)
    both = (both_even, both_odd)
    low = (low_even, low_odd)
    step_rows = 64

    for head in range(heads):
        for i in range(CROSS):
            table[head, i] = came_prev[i, head]
            table[head, CROSS + blocks + i] = came_next[i, head]
            turned[head, i] = came_prev[i, head].T
            turned[head, CROSS + blocks + i] = came_next[i, head].T

    left = lax.broadcasted_iota(jnp.int32, (block_rows, lanes), 1) < head_dim

    def locate(unit):
        head = lax.div(unit, blocks)
        block = lax.rem(unit, blocks)
        ids = [lists[head, block, j] for j in range(per_list)]
        peer = lax.div(block, each)
        start = pl.multiple_of(lax.rem(block, each) * block_rows, block_rows)
        return head, ids, peer, pl.ds(start, block_rows)

    def apart_of(head, peer, here):
        query_grad = pairs[peer, head, here]
        nothing = jnp.zeros_like(query_grad)
        return jnp.concatenate(
            [jnp.where(left, query_grad, nothing), jnp.where(left, nothing, query_grad)],
            axis=0,
        )

    def score(unit, slot):
        head, ids, peer, here = locate(unit)
        key_value = jnp.concatenate([table[head, i] for i in ids], axis=0)
        both[slot][...] = lax.dot_general(
            key_value,
            apart_of(head, peer, here),
            (((1,), (1,)), ((), ())),
            preferred_element_type=jnp.float32,
        )

    def soften(slot):
        source, target = both[slot], low[slot]
        parts = [slice(i, i + step_rows) for i in range(0, keys, step_rows)]
        top = source[parts[0], :block_rows]
        for part in parts[1:]:
            top = jnp.maximum(top, source[part, :block_rows])
        top = jnp.max(top, axis=0, keepdims=True)
        total = jnp.zeros((step_rows, block_rows), jnp.float32)
        mixed = jnp.zeros((step_rows, block_rows), jnp.float32)
        for part in parts:
            raised = jnp.exp2((source[part, :block_rows] - top) * exponent)
            source[part, :block_rows] = raised
            total += raised
            mixed += raised * source[part, block_rows:]
        inverse = 1.0 / jnp.sum(total, axis=0, keepdims=True)
        correction = jnp.sum(mixed, axis=0, keepdims=True) * inverse
        for part in parts:
            weights = source[part, :block_rows] * inverse
            target[part, block_rows:] = weights.astype(jnp.bfloat16)
            target[part, :block_rows] = (
                weights * (source[part, block_rows:] - correction)
            ).astype(jnp.bfloat16)

    def combine(unit, slot):
        head, ids, peer, here = locate(unit)
        products = low[slot][...]
        terms = jnp.dot(
            products, apart_of(head, peer, here), preferred_element_type=jnp.float32
        )
        for j, i in enumerate(ids):
            sums[head, i] += terms[j * block_rows : (j + 1) * block_rows]
        key_value = jnp.concatenate([turned[head, i] for i in ids], axis=1)
        out = jnp.dot(key_value, products, preferred_element_type=jnp.float32)
        out = jnp.concatenate(
            [out[:head_dim, :block_rows] * scaling, out[head_dim:, block_rows:]], axis=0
        )
        back[peer, head, here] = out.T.astype(back.dtype)

    score(0, 0)
    score(1, 1)
    soften(0)

    def step(i, carry):
        for slot in range(2):
            unit = 2 * i + slot
            combine(unit - 2, slot)
            score(unit, slot)
            soften(1 - slot)
        return carry

    lax.fori_loop(1, units // 2, step, 0)
    combine(units - 2, 0)
    soften(1)
    combine(units - 1, 1)

    factor = jnp.where(left, scaling, 1.0)
    for head in range(heads):
        for i in range(CROSS):
            to_prev[i, head] = (sums[head, i] * factor).astype(to_prev.dtype)
            to_next[i, head] = (sums[head, CROSS + blocks + i] * factor).astype(to_next.dtype)


def attend(lists, came_prev, came_next, pairs, table, turned, sums):
    _, _, block_rows, lanes = came_prev.shape
    dtype = pairs.dtype
    per_list = lists.shape[-1]
    keys = per_list * block_rows
    inside = pl.BlockSpec(memory_space=pltpu.VMEM)
    cross_shape = jax.ShapeDtypeStruct(came_prev.shape, dtype)
    kept = (table, turned, sums)
    return pl.pallas_call(
        functools.partial(attend_kernel, head_dim=lanes // 2, per_list=per_list),
        in_specs=[pl.BlockSpec(memory_space=pltpu.SMEM)] + [inside] * 6,
        out_specs=[inside] * 6,
        out_shape=[pltpu.VMEM(pairs.shape, dtype), cross_shape, cross_shape]
        + [pltpu.VMEM(x.shape, x.dtype) for x in kept],
        input_output_aliases={4: 3, 5: 4, 6: 5},
        scratch_shapes=[
            pltpu.VMEM((keys, 2 * block_rows), jnp.float32),
            pltpu.VMEM((keys, 2 * block_rows), jnp.float32),
            pltpu.VMEM((keys, 2 * block_rows), dtype),
            pltpu.VMEM((keys, 2 * block_rows), dtype),
        ],
        compiler_params=pltpu.CompilerParams(vmem_limit_bytes=SMALL_VMEM),
        name="attend",
    )(lists, came_prev, came_next, *[in_vmem(x) for x in (pairs, *kept)])


def finish_kernel(me, asked, back, kept, later, earlier, *refs, block_rows):
    messages = refs[:-3]
    sums, ready, sems = refs[-3:]
    peers, heads, _, rows, lanes = ready.shape
    each = rows // block_rows
    blocks = peers * each
    head_dim = lanes // 2
    left = lax.broadcasted_iota(jnp.int32, (block_rows, lanes), 1) < head_dim
    factor = jnp.where(left, head_dim ** (-0.5), 1.0)

    def send(item, head):
        target, peer = part_of(messages, me, item)
        return pltpu.make_async_copy(
            ready.at[peer, head], target.at[head], sems.at[item, head]
        )

    for head in range(heads):
        sums[...] = kept[head, CROSS : CROSS + blocks] * factor
        for i in range(CROSS):
            sums[asked[i]] += later[i, head].astype(jnp.float32)
        for i in range(CROSS):
            sums[asked[CROSS + i]] += earlier[i, head].astype(jnp.float32)
        for peer in range(peers):
            ready[peer, head, 1] = back[peer, head]
            for i in range(each):
                ready[peer, head, 0, i * block_rows : (i + 1) * block_rows] = sums[
                    peer * each + i
                ].astype(ready.dtype)
        for item in range(peers):
            send(item, head).start()
    for head in range(heads):
        for item in range(peers):
            send(item, head).wait()


def finish(me, back, kept, later, earlier, asked, apart):
    peers, heads, rows, lanes = back.shape
    _, window, block_rows, _ = kept.shape
    blocks = window - 2 * CROSS
    inside = pl.BlockSpec(memory_space=pltpu.VMEM)
    scalars = pl.BlockSpec(memory_space=pltpu.SMEM)
    shape = (heads, 2, rows, lanes)
    outs = message_outs(peers, shape, back.dtype, apart)
    return pl.pallas_call(
        functools.partial(finish_kernel, block_rows=block_rows),
        in_specs=[scalars, scalars] + [inside] * 4,
        out_specs=[pl.BlockSpec(memory_space=pltpu.HBM)] * len(outs),
        out_shape=outs,
        scratch_shapes=[
            pltpu.VMEM((blocks, block_rows, lanes), jnp.float32),
            pltpu.VMEM((peers,) + shape, back.dtype),
            pltpu.SemaphoreType.DMA((peers, heads)),
        ],
        compiler_params=pltpu.CompilerParams(vmem_limit_bytes=SMALL_VMEM),
        name="finish",
    )(
        me,
        asked,
        in_vmem(back),
        in_vmem(kept),
        later,
        earlier,
    )


def local(query, key, value, d_out, pattern):
    heads_here, blocks, _ = pattern.shape
    peers = lax.axis_size("seq")
    rows, columns = query.shape
    head_dim = columns // (peers * heads_here)
    block_rows = rows * peers // blocks
    chunks = min(CHUNKS, heads_here)
    starts = [-(-heads_here * i // chunks) for i in range(chunks)]
    sizes = [end - start for start, end in zip(starts, starts[1:] + [heads_here])]
    arrays = (query, key, value, d_out)

    own_base = lax.axis_index("slab") * blocks
    block_ids = jnp.arange(blocks, dtype=jnp.int32)
    flat_lists = pattern.reshape(-1)
    reverse_rank = blocks - 1 - block_ids
    hits_prev = jnp.any(flat_lists[:, None] == (own_base - blocks + block_ids)[None, :], axis=0)
    hits_next = jnp.any(flat_lists[:, None] == (own_base + blocks + block_ids)[None, :], axis=0)
    need_prev = lax.top_k(hits_prev.astype(jnp.int32) * blocks + reverse_rank, CROSS)[1]
    need_next = lax.top_k(hits_next.astype(jnp.int32) * blocks + reverse_rank, CROSS)[1]
    asked_next = from_behind(need_prev, "slab", -1)
    asked_prev = from_behind(need_next, "slab", 1)
    asked = jnp.concatenate([asked_next, asked_prev])
    rank_ids = jnp.arange(CROSS, dtype=jnp.int32)
    prev_global = own_base - blocks + need_prev
    next_global = own_base + blocks + need_next
    pos_prev = jnp.sum(jnp.where(pattern[..., None] == prev_global, rank_ids, 0), axis=-1)
    pos_next = jnp.sum(jnp.where(pattern[..., None] == next_global, rank_ids, 0), axis=-1)
    in_own = (pattern >= own_base) & (pattern < own_base + blocks)
    local_ids = jnp.where(
        in_own,
        CROSS + pattern - own_base,
        jnp.where(pattern < own_base, pos_prev, CROSS + blocks + pos_next),
    )

    me = lax.axis_index("seq").astype(jnp.int32).reshape(1)
    last = chunks - 1
    came = []
    for chunk, (start, size) in enumerate(zip(starts, sizes)):
        after = (asked, local_ids) if came else ()
        packed = pack(arrays, start, size, heads_here, peers, head_dim, after)
        came.append(exchange(packed))
    received = []
    outs = finished = ()
    for chunk, (messages, start, size) in enumerate(zip(came, starts, sizes)):
        for_next, for_prev, table = pick(me, messages, asked, block_rows, finished[:1])
        came_prev = from_behind(for_next, "slab", 1)
        came_next = from_behind(for_prev, "slab", -1)
        turned, pairs, sums = prepare(me, messages, table)
        lists = local_ids[start : start + size]
        back, to_prev, to_next, _, _, kept = attend(
            lists, came_prev, came_next, pairs, table, turned, sums
        )
        later = from_behind(to_prev, "slab", -1)
        earlier = from_behind(to_next, "slab", 1)
        finished = finish(me, back, kept, later, earlier, asked, chunk == last)
        received.append(exchange(finished))
        if chunk == last and heads_here * head_dim % LANES == 0:
            half = peers // 2
            near = list(range(peers - 2, half - 1, -1))
            parts = (
                [peers - 1, *near[::2]],
                list(range(half // 2)),
                [*range(half // 2, half), *near[1::2]],
            )
            for items in parts:
                outs = unpack_items(me, received, starts, heads_here, items, outs)
        else:
            outs = unpack(me, received, starts, heads_here, outs)
    return tuple(outs)


def solution(mesh):
    tokens = P(("slab", "seq"), None)
    return jax.shard_map(
        local,
        mesh=mesh,
        in_specs=(tokens, tokens, tokens, tokens, P("seq", "slab", None)),
        out_specs=(tokens, tokens, tokens, tokens),
        check_vma=False,
    )
```

```python
import functools
import math

import jax
import jax.numpy as jnp
from jax import lax
from jax.experimental import pallas as pl
from jax.experimental.pallas import tpu as pltpu
from jax.sharding import PartitionSpec as P

CROSS = 4
CHUNKS = 2
LANES = 128
SMALL_VMEM = 24 * 1024 * 1024
LARGE_VMEM = 40 * 1024 * 1024


def in_hbm(x):
    return pltpu.with_memory_space_constraint(x, pltpu.HBM)


def in_vmem(x):
    return pltpu.with_memory_space_constraint(x, pltpu.VMEM)


def from_behind(x, axis, by):
    count = lax.axis_size(axis)
    pairs = [(i, i + by) for i in range(count) if 0 <= i + by < count]
    return lax.ppermute(x, axis, pairs)


JOINT, APART, PAIRED = "joint", "apart", "paired"


def form_of(messages, peers):
    return {1: JOINT, peers: APART}.get(len(messages), PAIRED)


def part_of(messages, me, item, peers):
    form, half = form_of(messages, peers), peers // 2
    if form == JOINT:
        return messages[0].at[item], item
    if form == PAIRED and item >= half:
        return messages[half].at[item - half], lax.div(me[0], half) * half + item - half
    part = messages[item]
    if len(part.shape) == 5:
        part = part.at[1 - lax.div(me[0], half)]
    return part, me[0] ^ (peers - 1 - item)


def message_shape(messages):
    return messages[0].shape[-4:]


def message_outs(peers, shape, dtype, form):
    if form == JOINT:
        return [pltpu.HBM((peers,) + shape, dtype)]
    if form == APART:
        return [pltpu.HBM(shape, dtype)] * peers
    half = peers // 2
    return [pltpu.HBM(shape, dtype)] * half + [pltpu.HBM((half,) + shape, dtype)]


def exchange(messages):
    peers = lax.axis_size("seq")
    form, half = form_of(messages, peers), peers // 2
    swap = functools.partial(
        lax.all_to_all, axis_name="seq", split_axis=0, concat_axis=0, tiled=True
    )
    if form == JOINT:
        return [swap(messages[0])]
    received = list(messages)
    if form == APART:
        for item in range(peers - 1):
            pairs = [(i, i ^ (peers - 1 - item)) for i in range(peers)]
            received[item] = lax.ppermute(messages[item], "seq", pairs)
        return received
    for item in range(half):
        pairs = [[i, i ^ (peers - 1 - item)] for i in range(half)]
        received[item] = lax.all_gather(messages[item], "seq", axis_index_groups=pairs)
    halves = [list(range(half)), list(range(half, peers))]
    received[half] = swap(messages[half], axis_index_groups=halves)
    return received


def pack_kernel(query, key, value, d_out, *refs, first, heads, per_peer, head_dim):
    message, stage, ready, in_sems, out_sems = refs[-5:]
    sources = (key, value, query, d_out)
    peers = message.shape[0]

    def span(peer):
        begin = peer * per_peer + first
        low = begin // LANES * LANES
        high = -(-(begin + heads * head_dim) // LANES) * LANES
        return low, high - low, begin - low

    def fetch(peer, i):
        low, width, _ = span(peer)
        return pltpu.make_async_copy(
            sources[i].at[:, pl.ds(low, width)],
            stage.at[i, peer, :, pl.ds(0, width)],
            in_sems.at[i, peer],
        )

    def send(peer):
        return pltpu.make_async_copy(ready.at[peer], message.at[peer], out_sems.at[peer])

    for peer in range(peers):
        for i in range(4):
            fetch(peer, i).start()
    for peer in range(peers):
        for i in range(4):
            fetch(peer, i).wait()
        at = span(peer)[2]
        for head in range(heads):
            lanes = slice(at + head * head_dim, at + (head + 1) * head_dim)
            for kind in range(2):
                ready[peer, head, kind] = jnp.concatenate(
                    [stage[2 * kind, peer, :, lanes], stage[2 * kind + 1, peer, :, lanes]],
                    axis=1,
                )
        send(peer).start()
    for peer in range(peers):
        send(peer).wait()


def pack(arrays, start, heads, heads_here, peers, head_dim, after):
    rows = arrays[0].shape[0]
    dtype = arrays[0].dtype
    shape = (peers, heads, 2, rows, 2 * head_dim)
    width = (-(-heads * head_dim // LANES) + 1) * LANES
    anywhere = pl.BlockSpec(memory_space=pltpu.HBM)
    return pl.pallas_call(
        functools.partial(
            pack_kernel,
            first=start * head_dim,
            heads=heads,
            per_peer=heads_here * head_dim,
            head_dim=head_dim,
        ),
        in_specs=[anywhere] * 4 + [pl.BlockSpec(memory_space=pl.ANY)] * len(after),
        out_specs=[anywhere],
        out_shape=[pltpu.HBM(shape, dtype)],
        scratch_shapes=[
            pltpu.VMEM((4, peers, rows, width), dtype),
            pltpu.VMEM(shape, dtype),
            pltpu.SemaphoreType.DMA((4, peers)),
            pltpu.SemaphoreType.DMA((peers,)),
        ],
        compiler_params=pltpu.CompilerParams(vmem_limit_bytes=SMALL_VMEM),
        name="pack",
    )(*[in_hbm(x) for x in arrays], *after)


def unpack_kernel(me, *refs, chunk, peers, counts, earlier, jobs):
    ends = [sum(counts[: c + 1]) for c in range(chunk + 1)]
    groups = [refs[end - count : end] for end, count in zip(ends, counts)]
    outs = refs[ends[-1] + earlier :][:4]
    stages = refs[-3 - chunk - 1 : -3]
    ready, in_sems, out_sems = refs[-3:]
    head_dim = ready.shape[-1] // 2
    used = sorted({(which, peer) for job in jobs for which, peer, _ in job[1:]})
    chunks_used = sorted({which for which, _ in used})
    heads_used = {
        c: sorted({head for job in jobs for which, _, head in job[1:] if which == c})
        for c in chunks_used
    }

    def fetch(which, item, slot=None):
        heads = heads_used[which]
        some = pl.ds(heads[0], heads[-1] - heads[0] + 1)
        source, peer = part_of(groups[which], me, item, peers)
        slot = peer if slot is None else slot
        return pltpu.make_async_copy(
            source.at[some], stages[which].at[slot, some], in_sems.at[which, slot]
        )

    def send(job, i):
        tile = jobs[job][0]
        return pltpu.make_async_copy(
            ready.at[i, job],
            outs[i].at[:, pl.ds(tile * LANES, LANES)],
            out_sems.at[4 * job + i],
        )

    for item in range(peers):
        for which in chunks_used:
            fetch(which, item).start()
    waited = set()

    def wait_for(which, peer):
        if (which, peer) not in waited:
            fetch(which, 0, peer).wait()
            waited.add((which, peer))

    for job, (tile, left, right) in enumerate(jobs):
        for which, peer, _ in (left, right):
            wait_for(which, peer)
        sides = [stages[which][peer, head] for which, peer, head in (left, right)]
        for i, (kind, at) in enumerate(((1, head_dim), (1, 0), (0, 0), (0, head_dim))):
            ready[i, job] = jnp.concatenate(
                [side[kind, :, at : at + head_dim] for side in sides], axis=1
            )
            send(job, i).start()
    for which in chunks_used:
        for peer in range(peers):
            wait_for(which, peer)
    for job in range(len(jobs)):
        for i in range(4):
            send(job, i).wait()


def unpack(me, messages, starts, heads_here, earlier):
    chunk = len(messages) - 1
    peers = lax.axis_size("seq")
    _, _, rows, pair_dim = message_shape(messages[0])
    head_dim = pair_dim // 2
    columns = peers * heads_here * head_dim
    dtype = messages[0][0].dtype

    def place_of(head):
        peer, local_head = divmod(head, heads_here)
        which = max(c for c, start in enumerate(starts) if start <= local_head)
        return which, peer, local_head - starts[which]

    jobs = []
    for tile in range(columns // LANES):
        left, right = place_of(2 * tile), place_of(2 * tile + 1)
        if max(left[0], right[0]) == chunk:
            jobs.append((tile, left, right))
    if not jobs:
        return earlier
    flat = [x for group in messages for x in group]
    anywhere = pl.BlockSpec(memory_space=pltpu.HBM)
    return pl.pallas_call(
        functools.partial(
            unpack_kernel,
            chunk=chunk,
            peers=peers,
            counts=[len(group) for group in messages],
            earlier=len(earlier),
            jobs=jobs,
        ),
        in_specs=[pl.BlockSpec(memory_space=pltpu.SMEM)]
        + [pl.BlockSpec(memory_space=pl.ANY)] * len(flat)
        + [anywhere] * len(earlier),
        out_specs=[anywhere] * 4,
        out_shape=[pltpu.HBM((rows, columns), dtype)] * 4,
        input_output_aliases={1 + len(flat) + i: i for i in range(len(earlier))},
        scratch_shapes=[pltpu.VMEM((peers,) + message_shape(m), dtype) for m in messages]
        + [
            pltpu.VMEM((4, len(jobs), rows, LANES), dtype),
            pltpu.SemaphoreType.DMA((chunk + 1, peers)),
            pltpu.SemaphoreType.DMA((4 * len(jobs),)),
        ],
        compiler_params=pltpu.CompilerParams(vmem_limit_bytes=SMALL_VMEM),
        name="unpack",
    )(me, *flat, *[in_hbm(x) for x in earlier])


def unpack_items_kernel(me, *refs, items, peers, counts, forms, earlier, jobs, per_peer):
    ends = [sum(counts[: c + 1]) for c in range(len(counts))]
    groups = [refs[end - count : end] for end, count in zip(ends, counts)]
    outs = refs[ends[-1] + earlier :][:4]
    stages = refs[-3 - len(counts) : -3]
    ready, in_sems, out_sems = refs[-3:]
    head_dim = ready.shape[-1] // 2
    used = [
        sorted({head for job in jobs for which, head in job[1:] if which == c})
        for c in range(len(counts))
    ]

    def peer_of(j):
        return me[0] ^ (peers - 1 - items[j])

    def source_of(group, form, j):
        half = peers // 2
        if form == JOINT:
            return group[0].at[peer_of(j)]
        if form == APART:
            return group[j]
        if items[j] < half:
            return group[items[j]].at[1 - lax.div(me[0], half)]
        return group[half].at[lax.rem(peer_of(j), half)]

    def fetch(which, j):
        source = source_of(groups[which], forms[which], j)
        some = pl.ds(used[which][0], used[which][-1] - used[which][0] + 1)
        return pltpu.make_async_copy(
            source.at[some], stages[which].at[j, some], in_sems.at[which, j]
        )

    def send(j, job, i):
        first = pl.multiple_of(peer_of(j) * per_peer, LANES) + jobs[job][0] * LANES
        return pltpu.make_async_copy(
            ready.at[j, i, job], outs[i].at[:, pl.ds(first, LANES)], out_sems.at[j, i, job]
        )

    steps = [(j, which) for j in range(len(items)) for which in range(len(counts))]
    steps = [(j, which) for j, which in steps if used[which]]
    for j, which in steps:
        fetch(which, j).start()
    for j in range(len(items)):
        for at, which in steps:
            if at == j:
                fetch(which, j).wait()
        for job, (_, left, right) in enumerate(jobs):
            sides = [stages[which][j, head] for which, head in (left, right)]
            for i, (kind, at) in enumerate(((1, head_dim), (1, 0), (0, 0), (0, head_dim))):
                ready[j, i, job] = jnp.concatenate(
                    [side[kind, :, at : at + head_dim] for side in sides], axis=1
                )
                send(j, job, i).start()
    for j in range(len(items)):
        for job in range(len(jobs)):
            for i in range(4):
                send(j, job, i).wait()


def unpack_items(me, messages, starts, heads_here, items, earlier):
    chunk = len(messages) - 1
    peers = lax.axis_size("seq")
    _, _, rows, pair_dim = message_shape(messages[0])
    head_dim = pair_dim // 2
    per_peer = heads_here * head_dim
    dtype = messages[0][0].dtype

    def place_of(head):
        which = max(c for c, start in enumerate(starts) if start <= head)
        return which, head - starts[which]

    jobs = []
    for tile in range(per_peer // LANES):
        left, right = place_of(2 * tile), place_of(2 * tile + 1)
        if max(left[0], right[0]) == chunk:
            jobs.append((tile, left, right))
    forms = [form_of(group, peers) for group in messages]
    groups = [
        [group[item] for item in items] if form == APART else list(group)
        for group, form in zip(messages, forms)
    ]
    flat = [x for group in groups for x in group]
    anywhere = pl.BlockSpec(memory_space=pltpu.HBM)
    return pl.pallas_call(
        functools.partial(
            unpack_items_kernel,
            items=items,
            peers=peers,
            counts=[len(group) for group in groups],
            forms=forms,
            earlier=len(earlier),
            jobs=jobs,
            per_peer=per_peer,
        ),
        in_specs=[pl.BlockSpec(memory_space=pltpu.SMEM)]
        + [pl.BlockSpec(memory_space=pl.ANY)] * len(flat)
        + [anywhere] * len(earlier),
        out_specs=[anywhere] * 4,
        out_shape=[pltpu.HBM((rows, peers * per_peer), dtype)] * 4,
        input_output_aliases={1 + len(flat) + i: i for i in range(len(earlier))},
        scratch_shapes=[
            pltpu.VMEM((len(items),) + message_shape(m), dtype) for m in messages
        ]
        + [
            pltpu.VMEM((len(items), 4, len(jobs), rows, LANES), dtype),
            pltpu.SemaphoreType.DMA((chunk + 1, len(items))),
            pltpu.SemaphoreType.DMA((len(items), 4, len(jobs))),
        ],
        compiler_params=pltpu.CompilerParams(vmem_limit_bytes=SMALL_VMEM),
        name="unpack_items",
    )(me, *flat, *[in_hbm(x) for x in earlier])


def pick_kernel(me, asked, *refs, count):
    for_next, for_prev, table, sems = refs[-4:]
    heads, window, block_rows, _ = table.shape
    peers, each = sems.shape

    def fetch(item, i):
        source, peer = part_of(refs[:count], me, item, peers)
        rows = pl.ds(i * block_rows, block_rows)
        return pltpu.make_async_copy(
            source.at[:, 0, rows], table.at[:, CROSS + peer * each + i], sems.at[item, i]
        )

    for item in range(peers):
        for i in range(each):
            fetch(item, i).start()
    for item in range(peers):
        for i in range(each):
            fetch(item, i).wait()
    for i in range(CROSS):
        for_next[i] = table[:, CROSS + asked[i]]
        for_prev[i] = table[:, CROSS + asked[CROSS + i]]


def pick(me, messages, asked, block_rows, after):
    heads, _, rows, lanes = message_shape(messages)
    dtype = messages[0].dtype
    peers = lax.axis_size("seq")
    each = rows // block_rows
    window = peers * each + 2 * CROSS
    picked = jax.ShapeDtypeStruct((CROSS, heads, block_rows, lanes), dtype)
    return pl.pallas_call(
        functools.partial(pick_kernel, count=len(messages)),
        in_specs=[pl.BlockSpec(memory_space=pltpu.SMEM)] * 2
        + [pl.BlockSpec(memory_space=pl.ANY)] * (len(messages) + len(after)),
        out_specs=[pl.BlockSpec(memory_space=pltpu.VMEM)] * 3,
        out_shape=[picked, picked, pltpu.VMEM((heads, window, block_rows, lanes), dtype)],
        scratch_shapes=[pltpu.SemaphoreType.DMA((peers, each))],
        compiler_params=pltpu.CompilerParams(vmem_limit_bytes=SMALL_VMEM),
        name="pick",
    )(me, asked, *messages, *[in_hbm(x) for x in after])


def prepare_kernel(me, table, *refs, peers):
    messages = refs[:-4]
    turned, pairs, sums, sems = refs[-4:]
    heads, window, _, _ = table.shape

    def fetch(item):
        source, peer = part_of(messages, me, item, peers)
        return pltpu.make_async_copy(source.at[:, 1], pairs.at[peer], sems.at[item])

    for item in range(peers):
        fetch(item).start()
    for head in range(heads):

        def clear(i, carry):
            sums[head, i] = jnp.zeros(sums.shape[2:], sums.dtype)
            return carry

        def turn(i, carry):
            turned[head, i] = table[head, i].T
            return carry

        lax.fori_loop(0, window, clear, 0)
        lax.fori_loop(CROSS, window - CROSS, turn, 0)
    for item in range(peers):
        fetch(item).wait()


def prepare(me, messages, table):
    heads, _, rows, lanes = message_shape(messages)
    _, window, block_rows, _ = table.shape
    dtype = messages[0].dtype
    peers = lax.axis_size("seq")
    inside = pl.BlockSpec(memory_space=pltpu.VMEM)
    return pl.pallas_call(
        functools.partial(prepare_kernel, peers=peers),
        in_specs=[pl.BlockSpec(memory_space=pltpu.SMEM), inside]
        + [pl.BlockSpec(memory_space=pl.ANY)] * len(messages),
        out_specs=[inside] * 3,
        out_shape=[
            pltpu.VMEM((heads, window, lanes, block_rows), dtype),
            pltpu.VMEM((peers, heads, rows, lanes), dtype),
            pltpu.VMEM((heads, window, block_rows, lanes), jnp.float32),
        ],
        scratch_shapes=[pltpu.SemaphoreType.DMA((peers,))],
        compiler_params=pltpu.CompilerParams(vmem_limit_bytes=SMALL_VMEM),
        name="prepare",
    )(me, in_vmem(table), *messages)


def attend_kernel(
    lists,
    came_prev,
    came_next,
    pairs,
    table_in,
    turned_in,
    sums_in,
    back,
    to_prev,
    to_next,
    table,
    turned,
    sums,
    both_even,
    both_odd,
    low_even,
    low_odd,
    *,
    head_dim,
    per_list,
):
    del table_in, turned_in, sums_in
    peers, heads, rows, lanes = pairs.shape
    _, window, block_rows, _ = table.shape
    each = rows // block_rows
    blocks = peers * each
    units = heads * blocks
    keys = per_list * block_rows
    scaling = head_dim ** (-0.5)
    exponent = scaling * math.log2(math.e)
    both = (both_even, both_odd)
    low = (low_even, low_odd)
    step_rows = 64

    for head in range(heads):
        for i in range(CROSS):
            table[head, i] = came_prev[i, head]
            table[head, CROSS + blocks + i] = came_next[i, head]
            turned[head, i] = came_prev[i, head].T
            turned[head, CROSS + blocks + i] = came_next[i, head].T

    left = lax.broadcasted_iota(jnp.int32, (block_rows, lanes), 1) < head_dim

    def locate(unit):
        head = lax.div(unit, blocks)
        block = lax.rem(unit, blocks)
        ids = [lists[head, block, j] for j in range(per_list)]
        peer = lax.div(block, each)
        start = pl.multiple_of(lax.rem(block, each) * block_rows, block_rows)
        return head, ids, peer, pl.ds(start, block_rows)

    def apart_of(head, peer, here):
        query_grad = pairs[peer, head, here]
        nothing = jnp.zeros_like(query_grad)
        return jnp.concatenate(
            [jnp.where(left, query_grad, nothing), jnp.where(left, nothing, query_grad)],
            axis=0,
        )

    def score(unit, slot):
        head, ids, peer, here = locate(unit)
        key_value = jnp.concatenate([table[head, i] for i in ids], axis=0)
        both[slot][...] = lax.dot_general(
            key_value,
            apart_of(head, peer, here),
            (((1,), (1,)), ((), ())),
            preferred_element_type=jnp.float32,
        )

    def soften(slot):
        source, target = both[slot], low[slot]
        parts = [slice(i, i + step_rows) for i in range(0, keys, step_rows)]
        top = source[parts[0], :block_rows]
        for part in parts[1:]:
            top = jnp.maximum(top, source[part, :block_rows])
        top = jnp.max(top, axis=0, keepdims=True)
        total = jnp.zeros((step_rows, block_rows), jnp.float32)
        mixed = jnp.zeros((step_rows, block_rows), jnp.float32)
        for part in parts:
            raised = jnp.exp2((source[part, :block_rows] - top) * exponent)
            source[part, :block_rows] = raised
            total += raised
            mixed += raised * source[part, block_rows:]
        inverse = 1.0 / jnp.sum(total, axis=0, keepdims=True)
        correction = jnp.sum(mixed, axis=0, keepdims=True) * inverse
        for part in parts:
            weights = source[part, :block_rows] * inverse
            target[part, block_rows:] = weights.astype(jnp.bfloat16)
            target[part, :block_rows] = (
                weights * (source[part, block_rows:] - correction)
            ).astype(jnp.bfloat16)

    def combine(unit, slot):
        head, ids, peer, here = locate(unit)
        products = low[slot][...]
        terms = jnp.dot(
            products, apart_of(head, peer, here), preferred_element_type=jnp.float32
        )
        for j, i in enumerate(ids):
            sums[head, i] += terms[j * block_rows : (j + 1) * block_rows]
        key_value = jnp.concatenate([turned[head, i] for i in ids], axis=1)
        out = jnp.dot(key_value, products, preferred_element_type=jnp.float32)
        out = jnp.concatenate(
            [out[:head_dim, :block_rows] * scaling, out[head_dim:, block_rows:]], axis=0
        )
        back[peer, head, here] = out.T.astype(back.dtype)

    score(0, 0)
    score(1, 1)
    soften(0)

    def step(i, carry):
        for slot in range(2):
            unit = 2 * i + slot
            combine(unit - 2, slot)
            score(unit, slot)
            soften(1 - slot)
        return carry

    lax.fori_loop(1, units // 2, step, 0)
    combine(units - 2, 0)
    soften(1)
    combine(units - 1, 1)

    factor = jnp.where(left, scaling, 1.0)
    for head in range(heads):
        for i in range(CROSS):
            to_prev[i, head] = (sums[head, i] * factor).astype(to_prev.dtype)
            to_next[i, head] = (sums[head, CROSS + blocks + i] * factor).astype(to_next.dtype)


def attend(lists, came_prev, came_next, pairs, table, turned, sums):
    _, _, block_rows, lanes = came_prev.shape
    dtype = pairs.dtype
    per_list = lists.shape[-1]
    keys = per_list * block_rows
    inside = pl.BlockSpec(memory_space=pltpu.VMEM)
    cross_shape = jax.ShapeDtypeStruct(came_prev.shape, dtype)
    kept = (table, turned, sums)
    return pl.pallas_call(
        functools.partial(attend_kernel, head_dim=lanes // 2, per_list=per_list),
        in_specs=[pl.BlockSpec(memory_space=pltpu.SMEM)] + [inside] * 6,
        out_specs=[inside] * 6,
        out_shape=[pltpu.VMEM(pairs.shape, dtype), cross_shape, cross_shape]
        + [pltpu.VMEM(x.shape, x.dtype) for x in kept],
        input_output_aliases={4: 3, 5: 4, 6: 5},
        scratch_shapes=[
            pltpu.VMEM((keys, 2 * block_rows), jnp.float32),
            pltpu.VMEM((keys, 2 * block_rows), jnp.float32),
            pltpu.VMEM((keys, 2 * block_rows), dtype),
            pltpu.VMEM((keys, 2 * block_rows), dtype),
        ],
        compiler_params=pltpu.CompilerParams(vmem_limit_bytes=SMALL_VMEM),
        name="attend",
    )(lists, came_prev, came_next, *[in_vmem(x) for x in (pairs, *kept)])


def finish_kernel(me, asked, back, kept, later, earlier, *refs, block_rows):
    messages = refs[:-3]
    sums, ready, sems = refs[-3:]
    peers, heads, _, rows, lanes = ready.shape
    each = rows // block_rows
    blocks = peers * each
    head_dim = lanes // 2
    left = lax.broadcasted_iota(jnp.int32, (block_rows, lanes), 1) < head_dim
    factor = jnp.where(left, head_dim ** (-0.5), 1.0)

    def send(item, head):
        target, peer = part_of(messages, me, item, peers)
        return pltpu.make_async_copy(
            ready.at[peer, head], target.at[head], sems.at[item, head]
        )

    for head in range(heads):
        sums[...] = kept[head, CROSS : CROSS + blocks] * factor
        for i in range(CROSS):
            sums[asked[i]] += later[i, head].astype(jnp.float32)
        for i in range(CROSS):
            sums[asked[CROSS + i]] += earlier[i, head].astype(jnp.float32)
        for peer in range(peers):
            ready[peer, head, 1] = back[peer, head]
            for i in range(each):
                ready[peer, head, 0, i * block_rows : (i + 1) * block_rows] = sums[
                    peer * each + i
                ].astype(ready.dtype)
        for item in range(peers):
            send(item, head).start()
    for head in range(heads):
        for item in range(peers):
            send(item, head).wait()


def finish(me, back, kept, later, earlier, asked, form):
    peers, heads, rows, lanes = back.shape
    _, window, block_rows, _ = kept.shape
    blocks = window - 2 * CROSS
    inside = pl.BlockSpec(memory_space=pltpu.VMEM)
    scalars = pl.BlockSpec(memory_space=pltpu.SMEM)
    shape = (heads, 2, rows, lanes)
    outs = message_outs(peers, shape, back.dtype, form)
    return pl.pallas_call(
        functools.partial(finish_kernel, block_rows=block_rows),
        in_specs=[scalars, scalars] + [inside] * 4,
        out_specs=[pl.BlockSpec(memory_space=pltpu.HBM)] * len(outs),
        out_shape=outs,
        scratch_shapes=[
            pltpu.VMEM((blocks, block_rows, lanes), jnp.float32),
            pltpu.VMEM((peers,) + shape, back.dtype),
            pltpu.SemaphoreType.DMA((peers, heads)),
        ],
        compiler_params=pltpu.CompilerParams(vmem_limit_bytes=SMALL_VMEM),
        name="finish",
    )(
        me,
        asked,
        in_vmem(back),
        in_vmem(kept),
        later,
        earlier,
    )


def local(query, key, value, d_out, pattern):
    heads_here, blocks, _ = pattern.shape
    peers = lax.axis_size("seq")
    rows, columns = query.shape
    head_dim = columns // (peers * heads_here)
    block_rows = rows * peers // blocks
    chunks = min(CHUNKS, heads_here)
    starts = [-(-heads_here * i // chunks) for i in range(chunks)]
    sizes = [end - start for start, end in zip(starts, starts[1:] + [heads_here])]
    arrays = (query, key, value, d_out)

    own_base = lax.axis_index("slab") * blocks
    block_ids = jnp.arange(blocks, dtype=jnp.int32)
    flat_lists = pattern.reshape(-1)
    reverse_rank = blocks - 1 - block_ids
    hits_prev = jnp.any(flat_lists[:, None] == (own_base - blocks + block_ids)[None, :], axis=0)
    hits_next = jnp.any(flat_lists[:, None] == (own_base + blocks + block_ids)[None, :], axis=0)
    need_prev = lax.top_k(hits_prev.astype(jnp.int32) * blocks + reverse_rank, CROSS)[1]
    need_next = lax.top_k(hits_next.astype(jnp.int32) * blocks + reverse_rank, CROSS)[1]
    asked_next = from_behind(need_prev, "slab", -1)
    asked_prev = from_behind(need_next, "slab", 1)
    asked = jnp.concatenate([asked_next, asked_prev])
    rank_ids = jnp.arange(CROSS, dtype=jnp.int32)
    prev_global = own_base - blocks + need_prev
    next_global = own_base + blocks + need_next
    pos_prev = jnp.sum(jnp.where(pattern[..., None] == prev_global, rank_ids, 0), axis=-1)
    pos_next = jnp.sum(jnp.where(pattern[..., None] == next_global, rank_ids, 0), axis=-1)
    in_own = (pattern >= own_base) & (pattern < own_base + blocks)
    local_ids = jnp.where(
        in_own,
        CROSS + pattern - own_base,
        jnp.where(pattern < own_base, pos_prev, CROSS + blocks + pos_next),
    )

    me = lax.axis_index("seq").astype(jnp.int32).reshape(1)
    last = chunks - 1
    came = []
    for chunk, (start, size) in enumerate(zip(starts, sizes)):
        after = (asked, local_ids) if came else ()
        packed = pack(arrays, start, size, heads_here, peers, head_dim, after)
        came.append(exchange(packed))
    received = []
    outs = finished = ()
    for chunk, (messages, start, size) in enumerate(zip(came, starts, sizes)):
        for_next, for_prev, table = pick(me, messages, asked, block_rows, finished[:1])
        came_prev = from_behind(for_next, "slab", 1)
        came_next = from_behind(for_prev, "slab", -1)
        turned, pairs, sums = prepare(me, messages, table)
        lists = local_ids[start : start + size]
        back, to_prev, to_next, _, _, kept = attend(
            lists, came_prev, came_next, pairs, table, turned, sums
        )
        later = from_behind(to_prev, "slab", -1)
        earlier = from_behind(to_next, "slab", 1)
        form = APART if chunk == last else PAIRED
        finished = finish(me, back, kept, later, earlier, asked, form)
        received.append(exchange(finished))
        if chunk == last and heads_here * head_dim % LANES == 0:
            half = peers // 2
            near = list(range(peers - 2, half - 1, -1))
            parts = (
                [peers - 1, *near[::2]],
                list(range(half // 2)),
                [*range(half // 2, half), *near[1::2]],
            )
            for items in parts:
                outs = unpack_items(me, received, starts, heads_here, items, outs)
        else:
            outs = unpack(me, received, starts, heads_here, outs)
    return tuple(outs)


def solution(mesh):
    tokens = P(("slab", "seq"), None)
    return jax.shard_map(
        local,
        mesh=mesh,
        in_specs=(tokens, tokens, tokens, tokens, P("seq", "slab", None)),
        out_specs=(tokens, tokens, tokens, tokens),
        check_vma=False,
    )
```

```python
import functools
import math

import jax
import jax.numpy as jnp
from jax import lax
from jax.experimental import pallas as pl
from jax.experimental.pallas import tpu as pltpu
from jax.sharding import PartitionSpec as P

CROSS = 4
CHUNKS = 2
LANES = 128
SMALL_VMEM = 24 * 1024 * 1024
LARGE_VMEM = 40 * 1024 * 1024


def in_hbm(x):
    return pltpu.with_memory_space_constraint(x, pltpu.HBM)


def in_vmem(x):
    return pltpu.with_memory_space_constraint(x, pltpu.VMEM)


def from_behind(x, axis, by):
    count = lax.axis_size(axis)
    pairs = [(i, i + by) for i in range(count) if 0 <= i + by < count]
    return lax.ppermute(x, axis, pairs)


def part_of(messages, me, item):
    if len(messages) == 1:
        return messages[0].at[item], item
    return messages[item], me[0] ^ (len(messages) - 1 - item)


def message_shape(messages):
    return messages[0].shape[-4:]


def message_outs(peers, shape, dtype, apart):
    if apart:
        return [pltpu.HBM(shape, dtype)] * peers
    return [pltpu.HBM((peers,) + shape, dtype)]


def hold_kernel(*refs):
    del refs


def hold(arrays, after):
    count = len(arrays)
    anywhere = pl.BlockSpec(memory_space=pl.ANY)
    held = pl.pallas_call(
        hold_kernel,
        in_specs=[anywhere] * (count + len(after)),
        out_specs=[anywhere] * count,
        out_shape=[jax.ShapeDtypeStruct(x.shape, x.dtype) for x in arrays],
        input_output_aliases={i: i for i in range(count)},
        name="hold",
    )(*arrays, *after)
    return list(held)


def swap(messages, first, last):
    count = len(messages)
    return [
        lax.ppermute(
            messages[item], "seq", [(i, i ^ (count - 1 - item)) for i in range(count)]
        )
        for item in range(first, last)
    ]


def exchange(messages):
    if len(messages) == 1:
        return [lax.all_to_all(messages[0], "seq", split_axis=0, concat_axis=0, tiled=True)]
    return swap(messages, 0, len(messages) - 1) + list(messages[-1:])


def pack_kernel(
    me, query, key, value, d_out, *refs, first, heads, items, apart, per_peer, head_dim
):
    messages = refs[-4 - (len(items) if apart else 1) : -4]
    stage, ready, in_sems, out_sems = refs[-4:]
    sources = (key, value, query, d_out)
    aligned = apart and per_peer % LANES == 0
    at_once = aligned or not apart
    peers = stage.shape[1]

    def place_of(item):
        if apart:
            return messages[item - items[0]], me[0] ^ (peers - 1 - item)
        return messages[0].at[item], item

    def span(item):
        if aligned:
            base, begin = pl.multiple_of(place_of(item)[1] * per_peer, LANES), first
        else:
            base, begin = 0, item * per_peer + first
        low = begin // LANES * LANES
        high = -(-(begin + heads * head_dim) // LANES) * LANES
        return base + low, high - low, begin - low

    def fetch(item, i):
        low, width, _ = span(item)
        return pltpu.make_async_copy(
            sources[i].at[:, pl.ds(low, width)],
            stage.at[i, item, :, pl.ds(0, width)],
            in_sems.at[i, item],
        )

    def send(item):
        target, peer = place_of(item)
        return pltpu.make_async_copy(
            ready.at[item if aligned else peer], target, out_sems.at[item]
        )

    made = items if at_once else range(peers)
    for item in made:
        for i in range(4):
            fetch(item, i).start()
    for item in made:
        for i in range(4):
            fetch(item, i).wait()
        at = span(item)[2]
        for head in range(heads):
            lanes = slice(at + head * head_dim, at + (head + 1) * head_dim)
            for kind in range(2):
                ready[item, head, kind] = jnp.concatenate(
                    [stage[2 * kind, item, :, lanes], stage[2 * kind + 1, item, :, lanes]],
                    axis=1,
                )
        if at_once:
            send(item).start()
    if not at_once:
        for item in items:
            send(item).start()
    for item in items:
        send(item).wait()


def pack(me, arrays, start, heads, heads_here, peers, head_dim, apart, after):
    rows = arrays[0].shape[0]
    dtype = arrays[0].dtype
    shape = (heads, 2, rows, 2 * head_dim)
    width = (-(-heads * head_dim // LANES) + 1) * LANES
    anywhere = pl.BlockSpec(memory_space=pltpu.HBM)
    outs = message_outs(peers, shape, dtype, apart)
    return pl.pallas_call(
        functools.partial(
            pack_kernel,
            first=start * head_dim,
            heads=heads,
            items=range(peers),
            apart=apart,
            per_peer=heads_here * head_dim,
            head_dim=head_dim,
        ),
        in_specs=[pl.BlockSpec(memory_space=pltpu.SMEM)]
        + [anywhere] * 4
        + [pl.BlockSpec(memory_space=pl.ANY)] * len(after),
        out_specs=[anywhere] * len(outs),
        out_shape=outs,
        scratch_shapes=[
            pltpu.VMEM((4, peers, rows, width), dtype),
            pltpu.VMEM((peers,) + shape, dtype),
            pltpu.SemaphoreType.DMA((4, peers)),
            pltpu.SemaphoreType.DMA((peers,)),
        ],
        compiler_params=pltpu.CompilerParams(vmem_limit_bytes=SMALL_VMEM),
        name="pack",
    )(me, *[in_hbm(x) for x in arrays], *after)


def unpack_kernel(me, *refs, chunk, peers, counts, earlier, jobs):
    ends = [sum(counts[: c + 1]) for c in range(chunk + 1)]
    groups = [refs[end - count : end] for end, count in zip(ends, counts)]
    outs = refs[ends[-1] + earlier :][:4]
    stages = refs[-3 - chunk - 1 : -3]
    ready, in_sems, out_sems = refs[-3:]
    head_dim = ready.shape[-1] // 2
    used = sorted({(which, peer) for job in jobs for which, peer, _ in job[1:]})
    chunks_used = sorted({which for which, _ in used})
    heads_used = {
        c: sorted({head for job in jobs for which, _, head in job[1:] if which == c})
        for c in chunks_used
    }

    def fetch(which, item, slot=None):
        heads = heads_used[which]
        some = pl.ds(heads[0], heads[-1] - heads[0] + 1)
        source, peer = part_of(groups[which], me, item)
        slot = peer if slot is None else slot
        return pltpu.make_async_copy(
            source.at[some], stages[which].at[slot, some], in_sems.at[which, slot]
        )

    def send(job, i):
        tile = jobs[job][0]
        return pltpu.make_async_copy(
            ready.at[i, job],
            outs[i].at[:, pl.ds(tile * LANES, LANES)],
            out_sems.at[4 * job + i],
        )

    for item in range(peers):
        for which in chunks_used:
            fetch(which, item).start()
    waited = set()

    def wait_for(which, peer):
        if (which, peer) not in waited:
            fetch(which, 0, peer).wait()
            waited.add((which, peer))

    for job, (tile, left, right) in enumerate(jobs):
        for which, peer, _ in (left, right):
            wait_for(which, peer)
        sides = [stages[which][peer, head] for which, peer, head in (left, right)]
        for i, (kind, at) in enumerate(((1, head_dim), (1, 0), (0, 0), (0, head_dim))):
            ready[i, job] = jnp.concatenate(
                [side[kind, :, at : at + head_dim] for side in sides], axis=1
            )
            send(job, i).start()
    for which in chunks_used:
        for peer in range(peers):
            wait_for(which, peer)
    for job in range(len(jobs)):
        for i in range(4):
            send(job, i).wait()


def unpack(me, messages, starts, heads_here, earlier):
    chunk = len(messages) - 1
    peers = lax.axis_size("seq")
    _, _, rows, pair_dim = message_shape(messages[0])
    head_dim = pair_dim // 2
    columns = peers * heads_here * head_dim
    dtype = messages[0][0].dtype

    def place_of(head):
        peer, local_head = divmod(head, heads_here)
        which = max(c for c, start in enumerate(starts) if start <= local_head)
        return which, peer, local_head - starts[which]

    jobs = []
    for tile in range(columns // LANES):
        left, right = place_of(2 * tile), place_of(2 * tile + 1)
        if max(left[0], right[0]) == chunk:
            jobs.append((tile, left, right))
    if not jobs:
        return earlier
    flat = [x for group in messages for x in group]
    anywhere = pl.BlockSpec(memory_space=pltpu.HBM)
    return pl.pallas_call(
        functools.partial(
            unpack_kernel,
            chunk=chunk,
            peers=peers,
            counts=[len(group) for group in messages],
            earlier=len(earlier),
            jobs=jobs,
        ),
        in_specs=[pl.BlockSpec(memory_space=pltpu.SMEM)]
        + [pl.BlockSpec(memory_space=pl.ANY)] * len(flat)
        + [anywhere] * len(earlier),
        out_specs=[anywhere] * 4,
        out_shape=[pltpu.HBM((rows, columns), dtype)] * 4,
        input_output_aliases={1 + len(flat) + i: i for i in range(len(earlier))},
        scratch_shapes=[pltpu.VMEM((peers,) + message_shape(m), dtype) for m in messages]
        + [
            pltpu.VMEM((4, len(jobs), rows, LANES), dtype),
            pltpu.SemaphoreType.DMA((chunk + 1, peers)),
            pltpu.SemaphoreType.DMA((4 * len(jobs),)),
        ],
        compiler_params=pltpu.CompilerParams(vmem_limit_bytes=SMALL_VMEM),
        name="unpack",
    )(me, *flat, *[in_hbm(x) for x in earlier])


def unpack_items_kernel(me, *refs, items, peers, counts, joint, earlier, jobs, per_peer):
    ends = [sum(counts[: c + 1]) for c in range(len(counts))]
    groups = [refs[end - count : end] for end, count in zip(ends, counts)]
    outs = refs[ends[-1] + earlier :][:4]
    stages = refs[-3 - len(counts) : -3]
    ready, in_sems, out_sems = refs[-3:]
    head_dim = ready.shape[-1] // 2
    used = [
        sorted({head for job in jobs for which, head in job[1:] if which == c})
        for c in range(len(counts))
    ]

    def peer_of(j):
        return me[0] ^ (peers - 1 - items[j])

    def fetch(which, j):
        group = groups[which]
        source = group[0].at[peer_of(j)] if joint[which] else group[j]
        some = pl.ds(used[which][0], used[which][-1] - used[which][0] + 1)
        return pltpu.make_async_copy(
            source.at[some], stages[which].at[j, some], in_sems.at[which, j]
        )

    def send(j, job, i):
        first = pl.multiple_of(peer_of(j) * per_peer, LANES) + jobs[job][0] * LANES
        return pltpu.make_async_copy(
            ready.at[j, i, job], outs[i].at[:, pl.ds(first, LANES)], out_sems.at[j, i, job]
        )

    steps = [(j, which) for j in range(len(items)) for which in range(len(counts))]
    steps = [(j, which) for j, which in steps if used[which]]
    for j, which in steps:
        fetch(which, j).start()
    for j in range(len(items)):
        for at, which in steps:
            if at == j:
                fetch(which, j).wait()
        for job, (_, left, right) in enumerate(jobs):
            sides = [stages[which][j, head] for which, head in (left, right)]
            for i, (kind, at) in enumerate(((1, head_dim), (1, 0), (0, 0), (0, head_dim))):
                ready[j, i, job] = jnp.concatenate(
                    [side[kind, :, at : at + head_dim] for side in sides], axis=1
                )
                send(j, job, i).start()
    for j in range(len(items)):
        for job in range(len(jobs)):
            for i in range(4):
                send(j, job, i).wait()


def unpack_items(me, messages, starts, heads_here, items, earlier):
    chunk = len(messages) - 1
    peers = lax.axis_size("seq")
    _, _, rows, pair_dim = message_shape(messages[0])
    head_dim = pair_dim // 2
    per_peer = heads_here * head_dim
    dtype = messages[0][0].dtype

    def place_of(head):
        which = max(c for c, start in enumerate(starts) if start <= head)
        return which, head - starts[which]

    jobs = []
    for tile in range(per_peer // LANES):
        left, right = place_of(2 * tile), place_of(2 * tile + 1)
        if max(left[0], right[0]) == chunk:
            jobs.append((tile, left, right))
    groups = [
        list(group) if len(group) == 1 else [group[item] for item in items]
        for group in messages
    ]
    flat = [x for group in groups for x in group]
    anywhere = pl.BlockSpec(memory_space=pltpu.HBM)
    return pl.pallas_call(
        functools.partial(
            unpack_items_kernel,
            items=items,
            peers=peers,
            counts=[len(group) for group in groups],
            joint=[len(group) == 1 for group in messages],
            earlier=len(earlier),
            jobs=jobs,
            per_peer=per_peer,
        ),
        in_specs=[pl.BlockSpec(memory_space=pltpu.SMEM)]
        + [pl.BlockSpec(memory_space=pl.ANY)] * len(flat)
        + [anywhere] * len(earlier),
        out_specs=[anywhere] * 4,
        out_shape=[pltpu.HBM((rows, peers * per_peer), dtype)] * 4,
        input_output_aliases={1 + len(flat) + i: i for i in range(len(earlier))},
        scratch_shapes=[
            pltpu.VMEM((len(items),) + message_shape(m), dtype) for m in messages
        ]
        + [
            pltpu.VMEM((len(items), 4, len(jobs), rows, LANES), dtype),
            pltpu.SemaphoreType.DMA((chunk + 1, len(items))),
            pltpu.SemaphoreType.DMA((len(items), 4, len(jobs))),
        ],
        compiler_params=pltpu.CompilerParams(vmem_limit_bytes=SMALL_VMEM),
        name="unpack_items",
    )(me, *flat, *[in_hbm(x) for x in earlier])


def pick_kernel(me, asked, *refs, order):
    messages = [refs[order.index(item)] for item in range(len(order))]
    for_next, for_prev, table, sems = refs[-4:]
    heads, window, block_rows, _ = table.shape
    peers, each = sems.shape

    def fetch(item, i):
        source, peer = part_of(messages, me, item)
        rows = pl.ds(i * block_rows, block_rows)
        return pltpu.make_async_copy(
            source.at[:, 0, rows], table.at[:, CROSS + peer * each + i], sems.at[item, i]
        )

    for item in range(peers):
        for i in range(each):
            fetch(item, i).start()
    for item in range(peers):
        for i in range(each):
            fetch(item, i).wait()
    for i in range(CROSS):
        for_next[i] = table[:, CROSS + asked[i]]
        for_prev[i] = table[:, CROSS + asked[CROSS + i]]


def pick(me, messages, asked, block_rows, order, after):
    heads, _, rows, lanes = message_shape(messages)
    dtype = messages[0].dtype
    peers = lax.axis_size("seq")
    each = rows // block_rows
    window = peers * each + 2 * CROSS
    picked = jax.ShapeDtypeStruct((CROSS, heads, block_rows, lanes), dtype)
    return pl.pallas_call(
        functools.partial(pick_kernel, order=order),
        in_specs=[pl.BlockSpec(memory_space=pltpu.SMEM)] * 2
        + [pl.BlockSpec(memory_space=pl.ANY)] * (len(messages) + len(after)),
        out_specs=[pl.BlockSpec(memory_space=pltpu.VMEM)] * 3,
        out_shape=[picked, picked, pltpu.VMEM((heads, window, block_rows, lanes), dtype)],
        scratch_shapes=[pltpu.SemaphoreType.DMA((peers, each))],
        compiler_params=pltpu.CompilerParams(vmem_limit_bytes=SMALL_VMEM),
        name="pick",
    )(me, asked, *[messages[item] for item in order], *[in_hbm(x) for x in after])


def prepare_kernel(me, table, *refs, peers):
    messages = refs[:-4]
    turned, pairs, sums, sems = refs[-4:]
    heads, window, _, _ = table.shape

    def fetch(item):
        source, peer = part_of(messages, me, item)
        return pltpu.make_async_copy(source.at[:, 1], pairs.at[peer], sems.at[item])

    for item in range(peers):
        fetch(item).start()
    for head in range(heads):

        def clear(i, carry):
            sums[head, i] = jnp.zeros(sums.shape[2:], sums.dtype)
            return carry

        def turn(i, carry):
            turned[head, i] = table[head, i].T
            return carry

        lax.fori_loop(0, window, clear, 0)
        lax.fori_loop(CROSS, window - CROSS, turn, 0)
    for item in range(peers):
        fetch(item).wait()


def prepare(me, messages, table):
    heads, _, rows, lanes = message_shape(messages)
    _, window, block_rows, _ = table.shape
    dtype = messages[0].dtype
    peers = lax.axis_size("seq")
    inside = pl.BlockSpec(memory_space=pltpu.VMEM)
    return pl.pallas_call(
        functools.partial(prepare_kernel, peers=peers),
        in_specs=[pl.BlockSpec(memory_space=pltpu.SMEM), inside]
        + [pl.BlockSpec(memory_space=pl.ANY)] * len(messages),
        out_specs=[inside] * 3,
        out_shape=[
            pltpu.VMEM((heads, window, lanes, block_rows), dtype),
            pltpu.VMEM((peers, heads, rows, lanes), dtype),
            pltpu.VMEM((heads, window, block_rows, lanes), jnp.float32),
        ],
        scratch_shapes=[pltpu.SemaphoreType.DMA((peers,))],
        compiler_params=pltpu.CompilerParams(vmem_limit_bytes=SMALL_VMEM),
        name="prepare",
    )(me, in_vmem(table), *messages)


def attend_kernel(
    lists,
    came_prev,
    came_next,
    pairs,
    table_in,
    turned_in,
    sums_in,
    back,
    to_prev,
    to_next,
    table,
    turned,
    sums,
    both_even,
    both_odd,
    low_even,
    low_odd,
    *,
    head_dim,
    per_list,
):
    del table_in, turned_in, sums_in
    peers, heads, rows, lanes = pairs.shape
    _, window, block_rows, _ = table.shape
    each = rows // block_rows
    blocks = peers * each
    units = heads * blocks
    keys = per_list * block_rows
    scaling = head_dim ** (-0.5)
    exponent = scaling * math.log2(math.e)
    both = (both_even, both_odd)
    low = (low_even, low_odd)
    step_rows = 64

    for head in range(heads):
        for i in range(CROSS):
            table[head, i] = came_prev[i, head]
            table[head, CROSS + blocks + i] = came_next[i, head]
            turned[head, i] = came_prev[i, head].T
            turned[head, CROSS + blocks + i] = came_next[i, head].T

    left = lax.broadcasted_iota(jnp.int32, (block_rows, lanes), 1) < head_dim

    def locate(unit):
        head = lax.div(unit, blocks)
        block = lax.rem(unit, blocks)
        ids = [lists[head, block, j] for j in range(per_list)]
        peer = lax.div(block, each)
        start = pl.multiple_of(lax.rem(block, each) * block_rows, block_rows)
        return head, ids, peer, pl.ds(start, block_rows)

    def apart_of(head, peer, here):
        query_grad = pairs[peer, head, here]
        nothing = jnp.zeros_like(query_grad)
        return jnp.concatenate(
            [jnp.where(left, query_grad, nothing), jnp.where(left, nothing, query_grad)],
            axis=0,
        )

    def score(unit, slot):
        head, ids, peer, here = locate(unit)
        key_value = jnp.concatenate([table[head, i] for i in ids], axis=0)
        both[slot][...] = lax.dot_general(
            key_value,
            apart_of(head, peer, here),
            (((1,), (1,)), ((), ())),
            preferred_element_type=jnp.float32,
        )

    def soften(slot):
        source, target = both[slot], low[slot]
        parts = [slice(i, i + step_rows) for i in range(0, keys, step_rows)]
        top = source[parts[0], :block_rows]
        for part in parts[1:]:
            top = jnp.maximum(top, source[part, :block_rows])
        top = jnp.max(top, axis=0, keepdims=True)
        total = jnp.zeros((step_rows, block_rows), jnp.float32)
        mixed = jnp.zeros((step_rows, block_rows), jnp.float32)
        for part in parts:
            raised = jnp.exp2((source[part, :block_rows] - top) * exponent)
            source[part, :block_rows] = raised
            total += raised
            mixed += raised * source[part, block_rows:]
        inverse = 1.0 / jnp.sum(total, axis=0, keepdims=True)
        correction = jnp.sum(mixed, axis=0, keepdims=True) * inverse
        for part in parts:
            weights = source[part, :block_rows] * inverse
            target[part, block_rows:] = weights.astype(jnp.bfloat16)
            target[part, :block_rows] = (
                weights * (source[part, block_rows:] - correction)
            ).astype(jnp.bfloat16)

    def combine(unit, slot):
        head, ids, peer, here = locate(unit)
        products = low[slot][...]
        terms = jnp.dot(
            products, apart_of(head, peer, here), preferred_element_type=jnp.float32
        )
        for j, i in enumerate(ids):
            sums[head, i] += terms[j * block_rows : (j + 1) * block_rows]
        key_value = jnp.concatenate([turned[head, i] for i in ids], axis=1)
        out = jnp.dot(key_value, products, preferred_element_type=jnp.float32)
        out = jnp.concatenate(
            [out[:head_dim, :block_rows] * scaling, out[head_dim:, block_rows:]], axis=0
        )
        back[peer, head, here] = out.T.astype(back.dtype)

    score(0, 0)
    score(1, 1)
    soften(0)

    def step(i, carry):
        for slot in range(2):
            unit = 2 * i + slot
            combine(unit - 2, slot)
            score(unit, slot)
            soften(1 - slot)
        return carry

    lax.fori_loop(1, units // 2, step, 0)
    combine(units - 2, 0)
    soften(1)
    combine(units - 1, 1)

    factor = jnp.where(left, scaling, 1.0)
    for head in range(heads):
        for i in range(CROSS):
            to_prev[i, head] = (sums[head, i] * factor).astype(to_prev.dtype)
            to_next[i, head] = (sums[head, CROSS + blocks + i] * factor).astype(to_next.dtype)


def attend(lists, came_prev, came_next, pairs, table, turned, sums):
    _, _, block_rows, lanes = came_prev.shape
    dtype = pairs.dtype
    per_list = lists.shape[-1]
    keys = per_list * block_rows
    inside = pl.BlockSpec(memory_space=pltpu.VMEM)
    cross_shape = jax.ShapeDtypeStruct(came_prev.shape, dtype)
    kept = (table, turned, sums)
    return pl.pallas_call(
        functools.partial(attend_kernel, head_dim=lanes // 2, per_list=per_list),
        in_specs=[pl.BlockSpec(memory_space=pltpu.SMEM)] + [inside] * 6,
        out_specs=[inside] * 6,
        out_shape=[pltpu.VMEM(pairs.shape, dtype), cross_shape, cross_shape]
        + [pltpu.VMEM(x.shape, x.dtype) for x in kept],
        input_output_aliases={4: 3, 5: 4, 6: 5},
        scratch_shapes=[
            pltpu.VMEM((keys, 2 * block_rows), jnp.float32),
            pltpu.VMEM((keys, 2 * block_rows), jnp.float32),
            pltpu.VMEM((keys, 2 * block_rows), dtype),
            pltpu.VMEM((keys, 2 * block_rows), dtype),
        ],
        compiler_params=pltpu.CompilerParams(vmem_limit_bytes=SMALL_VMEM),
        name="attend",
    )(lists, came_prev, came_next, *[in_vmem(x) for x in (pairs, *kept)])


def finish_kernel(me, asked, back, kept, later, earlier, *refs, block_rows):
    messages = refs[:-3]
    sums, ready, sems = refs[-3:]
    peers, heads, _, rows, lanes = ready.shape
    each = rows // block_rows
    blocks = peers * each
    head_dim = lanes // 2
    left = lax.broadcasted_iota(jnp.int32, (block_rows, lanes), 1) < head_dim
    factor = jnp.where(left, head_dim ** (-0.5), 1.0)

    def send(item, head):
        target, peer = part_of(messages, me, item)
        return pltpu.make_async_copy(
            ready.at[peer, head], target.at[head], sems.at[item, head]
        )

    for head in range(heads):
        sums[...] = kept[head, CROSS : CROSS + blocks] * factor
        for i in range(CROSS):
            sums[asked[i]] += later[i, head].astype(jnp.float32)
        for i in range(CROSS):
            sums[asked[CROSS + i]] += earlier[i, head].astype(jnp.float32)
        for peer in range(peers):
            ready[peer, head, 1] = back[peer, head]
            for i in range(each):
                ready[peer, head, 0, i * block_rows : (i + 1) * block_rows] = sums[
                    peer * each + i
                ].astype(ready.dtype)
        for item in range(peers):
            send(item, head).start()
    for head in range(heads):
        for item in range(peers):
            send(item, head).wait()


def finish(me, back, kept, later, earlier, asked, apart):
    peers, heads, rows, lanes = back.shape
    _, window, block_rows, _ = kept.shape
    blocks = window - 2 * CROSS
    inside = pl.BlockSpec(memory_space=pltpu.VMEM)
    scalars = pl.BlockSpec(memory_space=pltpu.SMEM)
    shape = (heads, 2, rows, lanes)
    outs = message_outs(peers, shape, back.dtype, apart)
    return pl.pallas_call(
        functools.partial(finish_kernel, block_rows=block_rows),
        in_specs=[scalars, scalars] + [inside] * 4,
        out_specs=[pl.BlockSpec(memory_space=pltpu.HBM)] * len(outs),
        out_shape=outs,
        scratch_shapes=[
            pltpu.VMEM((blocks, block_rows, lanes), jnp.float32),
            pltpu.VMEM((peers,) + shape, back.dtype),
            pltpu.SemaphoreType.DMA((peers, heads)),
        ],
        compiler_params=pltpu.CompilerParams(vmem_limit_bytes=SMALL_VMEM),
        name="finish",
    )(
        me,
        asked,
        in_vmem(back),
        in_vmem(kept),
        later,
        earlier,
    )


def local(query, key, value, d_out, pattern):
    heads_here, blocks, _ = pattern.shape
    peers = lax.axis_size("seq")
    rows, columns = query.shape
    head_dim = columns // (peers * heads_here)
    block_rows = rows * peers // blocks
    chunks = min(CHUNKS, heads_here)
    starts = [-(-heads_here * i // chunks) for i in range(chunks)]
    sizes = [end - start for start, end in zip(starts, starts[1:] + [heads_here])]
    arrays = (query, key, value, d_out)

    own_base = lax.axis_index("slab") * blocks
    block_ids = jnp.arange(blocks, dtype=jnp.int32)
    flat_lists = pattern.reshape(-1)
    reverse_rank = blocks - 1 - block_ids
    hits_prev = jnp.any(flat_lists[:, None] == (own_base - blocks + block_ids)[None, :], axis=0)
    hits_next = jnp.any(flat_lists[:, None] == (own_base + blocks + block_ids)[None, :], axis=0)
    need_prev = lax.top_k(hits_prev.astype(jnp.int32) * blocks + reverse_rank, CROSS)[1]
    need_next = lax.top_k(hits_next.astype(jnp.int32) * blocks + reverse_rank, CROSS)[1]
    asked_next = from_behind(need_prev, "slab", -1)
    asked_prev = from_behind(need_next, "slab", 1)
    asked = jnp.concatenate([asked_next, asked_prev])
    rank_ids = jnp.arange(CROSS, dtype=jnp.int32)
    prev_global = own_base - blocks + need_prev
    next_global = own_base + blocks + need_next
    pos_prev = jnp.sum(jnp.where(pattern[..., None] == prev_global, rank_ids, 0), axis=-1)
    pos_next = jnp.sum(jnp.where(pattern[..., None] == next_global, rank_ids, 0), axis=-1)
    in_own = (pattern >= own_base) & (pattern < own_base + blocks)
    local_ids = jnp.where(
        in_own,
        CROSS + pattern - own_base,
        jnp.where(pattern < own_base, pos_prev, CROSS + blocks + pos_next),
    )

    me = lax.axis_index("seq").astype(jnp.int32).reshape(1)
    last = chunks - 1
    half = peers // 2
    near = list(range(peers - 2, half - 1, -1))
    parts = (near[::2], list(range(half // 2)), [*range(half // 2, half), *near[1::2]])
    came = []
    for chunk, (start, size) in enumerate(zip(starts, sizes)):
        after = (asked, local_ids) if came else ()
        packed = list(
            pack(me, arrays, start, size, heads_here, peers, head_dim, chunk == 0, after)
        )
        if chunk == 1:
            packed = hold(packed, [came[0][item] for part in parts for item in part])
        came.append(exchange(packed))
    received = []
    outs = finished = ()
    for chunk, (messages, start, size) in enumerate(zip(came, starts, sizes)):
        order = [item for part in parts for item in part] + [peers - 1]
        order = order if len(messages) > 1 else [0]
        for_next, for_prev, table = pick(
            me, messages, asked, block_rows, order, finished[:1]
        )
        came_prev = from_behind(for_next, "slab", 1)
        came_next = from_behind(for_prev, "slab", -1)
        turned, pairs, sums = prepare(me, messages, table)
        lists = local_ids[start : start + size]
        back, to_prev, to_next, _, _, kept = attend(
            lists, came_prev, came_next, pairs, table, turned, sums
        )
        later = from_behind(to_prev, "slab", -1)
        earlier = from_behind(to_next, "slab", 1)
        finished = finish(me, back, kept, later, earlier, asked, chunk == last)
        received.append(exchange(finished))
        if chunk == last and heads_here * head_dim % LANES == 0:
            for items in ([peers - 1, *parts[0]], *parts[1:]):
                outs = unpack_items(me, received, starts, heads_here, items, outs)
        else:
            outs = unpack(me, received, starts, heads_here, outs)
    return tuple(outs)


def solution(mesh):
    tokens = P(("slab", "seq"), None)
    return jax.shard_map(
        local,
        mesh=mesh,
        in_specs=(tokens, tokens, tokens, tokens, P("seq", "slab", None)),
        out_specs=(tokens, tokens, tokens, tokens),
        check_vma=False,
    )
```

```python
import functools
import math

import jax
import jax.numpy as jnp
from jax import lax
from jax.experimental import pallas as pl
from jax.experimental.pallas import tpu as pltpu
from jax.sharding import PartitionSpec as P

CROSS = 4
CHUNKS = 2
LANES = 128
SMALL_VMEM = 24 * 1024 * 1024
LARGE_VMEM = 40 * 1024 * 1024


def in_hbm(x):
    return pltpu.with_memory_space_constraint(x, pltpu.HBM)


def in_vmem(x):
    return pltpu.with_memory_space_constraint(x, pltpu.VMEM)


def from_behind(x, axis, by):
    count = lax.axis_size(axis)
    pairs = [(i, i + by) for i in range(count) if 0 <= i + by < count]
    return lax.ppermute(x, axis, pairs)


def part_of(messages, me, item):
    if len(messages) == 1:
        return messages[0].at[item], item
    return messages[item], me[0] ^ (len(messages) - 1 - item)


def message_shape(messages):
    return messages[0].shape[-4:]


def message_outs(peers, shape, dtype, apart):
    if apart:
        return [pltpu.HBM(shape, dtype)] * peers
    return [pltpu.HBM((peers,) + shape, dtype)]


def exchange(messages):
    if len(messages) == 1:
        return [lax.all_to_all(messages[0], "seq", split_axis=0, concat_axis=0, tiled=True)]
    count = len(messages)
    received = list(messages)
    for item in range(count - 1):
        pairs = [(i, i ^ (count - 1 - item)) for i in range(count)]
        received[item] = lax.ppermute(messages[item], "seq", pairs)
    return received


def join(left, right, head_dim, half):
    first = lax.broadcasted_iota(jnp.int32, left.shape, 1) < head_dim
    if half == 0:
        return jnp.where(first, left, pltpu.roll(right, head_dim, 1))
    return jnp.where(first, pltpu.roll(left, head_dim, 1), right)


def pack_kernel(query, key, value, d_out, *refs, first, heads, per_peer, head_dim):
    message, stage, ready, in_sems, out_sems = refs[-5:]
    sources = (key, value, query, d_out)
    peers = message.shape[0]

    def span(peer):
        begin = peer * per_peer + first
        low = begin // LANES * LANES
        high = -(-(begin + heads * head_dim) // LANES) * LANES
        return low, high - low, begin - low

    def fetch(peer, i):
        low, width, _ = span(peer)
        return pltpu.make_async_copy(
            sources[i].at[:, pl.ds(low, width)],
            stage.at[i, peer, :, pl.ds(0, width)],
            in_sems.at[i, peer],
        )

    def send(peer):
        return pltpu.make_async_copy(ready.at[peer], message.at[peer], out_sems.at[peer])

    for peer in range(peers):
        for i in range(4):
            fetch(peer, i).start()
    for peer in range(peers):
        for i in range(4):
            fetch(peer, i).wait()
        at = span(peer)[2]
        for head in range(heads):
            tile, inside = divmod(at + head * head_dim, LANES)
            lanes = slice(tile * LANES, (tile + 1) * LANES)
            for kind in range(2):
                ready[peer, head, kind] = join(
                    stage[2 * kind, peer, :, lanes],
                    stage[2 * kind + 1, peer, :, lanes],
                    head_dim,
                    inside // head_dim,
                )
        send(peer).start()
    for peer in range(peers):
        send(peer).wait()


def pack(arrays, start, heads, heads_here, peers, head_dim, after):
    rows = arrays[0].shape[0]
    dtype = arrays[0].dtype
    shape = (peers, heads, 2, rows, 2 * head_dim)
    width = (-(-heads * head_dim // LANES) + 1) * LANES
    anywhere = pl.BlockSpec(memory_space=pltpu.HBM)
    return pl.pallas_call(
        functools.partial(
            pack_kernel,
            first=start * head_dim,
            heads=heads,
            per_peer=heads_here * head_dim,
            head_dim=head_dim,
        ),
        in_specs=[anywhere] * 4 + [pl.BlockSpec(memory_space=pl.ANY)] * len(after),
        out_specs=[anywhere],
        out_shape=[pltpu.HBM(shape, dtype)],
        scratch_shapes=[
            pltpu.VMEM((4, peers, rows, width), dtype),
            pltpu.VMEM(shape, dtype),
            pltpu.SemaphoreType.DMA((4, peers)),
            pltpu.SemaphoreType.DMA((peers,)),
        ],
        compiler_params=pltpu.CompilerParams(vmem_limit_bytes=SMALL_VMEM),
        name="pack",
    )(*[in_hbm(x) for x in arrays], *after)


def unpack_kernel(me, *refs, chunk, peers, counts, earlier, jobs):
    ends = [sum(counts[: c + 1]) for c in range(chunk + 1)]
    groups = [refs[end - count : end] for end, count in zip(ends, counts)]
    outs = refs[ends[-1] + earlier :][:4]
    stages = refs[-3 - chunk - 1 : -3]
    ready, in_sems, out_sems = refs[-3:]
    head_dim = ready.shape[-1] // 2
    used = sorted({(which, peer) for job in jobs for which, peer, _ in job[1:]})
    chunks_used = sorted({which for which, _ in used})
    heads_used = {
        c: sorted({head for job in jobs for which, _, head in job[1:] if which == c})
        for c in chunks_used
    }

    def fetch(which, item, slot=None):
        heads = heads_used[which]
        some = pl.ds(heads[0], heads[-1] - heads[0] + 1)
        source, peer = part_of(groups[which], me, item)
        slot = peer if slot is None else slot
        return pltpu.make_async_copy(
            source.at[some], stages[which].at[slot, some], in_sems.at[which, slot]
        )

    def send(job, i):
        tile = jobs[job][0]
        return pltpu.make_async_copy(
            ready.at[i, job],
            outs[i].at[:, pl.ds(tile * LANES, LANES)],
            out_sems.at[4 * job + i],
        )

    for item in range(peers):
        for which in chunks_used:
            fetch(which, item).start()
    waited = set()

    def wait_for(which, peer):
        if (which, peer) not in waited:
            fetch(which, 0, peer).wait()
            waited.add((which, peer))

    for job, (tile, left, right) in enumerate(jobs):
        for which, peer, _ in (left, right):
            wait_for(which, peer)
        sides = [stages[which][peer, head] for which, peer, head in (left, right)]
        for i, (kind, half) in enumerate(((1, 1), (1, 0), (0, 0), (0, 1))):
            ready[i, job] = join(sides[0][kind], sides[1][kind], head_dim, half)
            send(job, i).start()
    for which in chunks_used:
        for peer in range(peers):
            wait_for(which, peer)
    for job in range(len(jobs)):
        for i in range(4):
            send(job, i).wait()


def unpack(me, messages, starts, heads_here, earlier):
    chunk = len(messages) - 1
    peers = lax.axis_size("seq")
    _, _, rows, pair_dim = message_shape(messages[0])
    head_dim = pair_dim // 2
    columns = peers * heads_here * head_dim
    dtype = messages[0][0].dtype

    def place_of(head):
        peer, local_head = divmod(head, heads_here)
        which = max(c for c, start in enumerate(starts) if start <= local_head)
        return which, peer, local_head - starts[which]

    jobs = []
    for tile in range(columns // LANES):
        left, right = place_of(2 * tile), place_of(2 * tile + 1)
        if max(left[0], right[0]) == chunk:
            jobs.append((tile, left, right))
    if not jobs:
        return earlier
    flat = [x for group in messages for x in group]
    anywhere = pl.BlockSpec(memory_space=pltpu.HBM)
    return pl.pallas_call(
        functools.partial(
            unpack_kernel,
            chunk=chunk,
            peers=peers,
            counts=[len(group) for group in messages],
            earlier=len(earlier),
            jobs=jobs,
        ),
        in_specs=[pl.BlockSpec(memory_space=pltpu.SMEM)]
        + [pl.BlockSpec(memory_space=pl.ANY)] * len(flat)
        + [anywhere] * len(earlier),
        out_specs=[anywhere] * 4,
        out_shape=[pltpu.HBM((rows, columns), dtype)] * 4,
        input_output_aliases={1 + len(flat) + i: i for i in range(len(earlier))},
        scratch_shapes=[pltpu.VMEM((peers,) + message_shape(m), dtype) for m in messages]
        + [
            pltpu.VMEM((4, len(jobs), rows, LANES), dtype),
            pltpu.SemaphoreType.DMA((chunk + 1, peers)),
            pltpu.SemaphoreType.DMA((4 * len(jobs),)),
        ],
        compiler_params=pltpu.CompilerParams(vmem_limit_bytes=SMALL_VMEM),
        name="unpack",
    )(me, *flat, *[in_hbm(x) for x in earlier])


def unpack_items_kernel(me, *refs, items, peers, counts, joint, earlier, jobs, per_peer):
    ends = [sum(counts[: c + 1]) for c in range(len(counts))]
    groups = [refs[end - count : end] for end, count in zip(ends, counts)]
    outs = refs[ends[-1] + earlier :][:4]
    stages = refs[-3 - len(counts) : -3]
    ready, in_sems, out_sems = refs[-3:]
    head_dim = ready.shape[-1] // 2
    used = [
        sorted({head for job in jobs for which, head in job[1:] if which == c})
        for c in range(len(counts))
    ]

    def peer_of(j):
        return me[0] ^ (peers - 1 - items[j])

    def fetch(which, j):
        group = groups[which]
        source = group[0].at[peer_of(j)] if joint[which] else group[j]
        some = pl.ds(used[which][0], used[which][-1] - used[which][0] + 1)
        return pltpu.make_async_copy(
            source.at[some], stages[which].at[j, some], in_sems.at[which, j]
        )

    def send(j, job, i):
        first = pl.multiple_of(peer_of(j) * per_peer, LANES) + jobs[job][0] * LANES
        return pltpu.make_async_copy(
            ready.at[j, i, job], outs[i].at[:, pl.ds(first, LANES)], out_sems.at[j, i, job]
        )

    steps = [(j, which) for j in range(len(items)) for which in range(len(counts))]
    steps = [(j, which) for j, which in steps if used[which]]
    for j, which in steps:
        fetch(which, j).start()
    for j in range(len(items)):
        for at, which in steps:
            if at == j:
                fetch(which, j).wait()
        for job, (_, left, right) in enumerate(jobs):
            sides = [stages[which][j, head] for which, head in (left, right)]
            for i, (kind, half) in enumerate(((1, 1), (1, 0), (0, 0), (0, 1))):
                ready[j, i, job] = join(sides[0][kind], sides[1][kind], head_dim, half)
                send(j, job, i).start()
    for j in range(len(items)):
        for job in range(len(jobs)):
            for i in range(4):
                send(j, job, i).wait()


def unpack_items(me, messages, starts, heads_here, items, earlier):
    chunk = len(messages) - 1
    peers = lax.axis_size("seq")
    _, _, rows, pair_dim = message_shape(messages[0])
    head_dim = pair_dim // 2
    per_peer = heads_here * head_dim
    dtype = messages[0][0].dtype

    def place_of(head):
        which = max(c for c, start in enumerate(starts) if start <= head)
        return which, head - starts[which]

    jobs = []
    for tile in range(per_peer // LANES):
        left, right = place_of(2 * tile), place_of(2 * tile + 1)
        if max(left[0], right[0]) == chunk:
            jobs.append((tile, left, right))
    groups = [
        list(group) if len(group) == 1 else [group[item] for item in items]
        for group in messages
    ]
    flat = [x for group in groups for x in group]
    anywhere = pl.BlockSpec(memory_space=pltpu.HBM)
    return pl.pallas_call(
        functools.partial(
            unpack_items_kernel,
            items=items,
            peers=peers,
            counts=[len(group) for group in groups],
            joint=[len(group) == 1 for group in messages],
            earlier=len(earlier),
            jobs=jobs,
            per_peer=per_peer,
        ),
        in_specs=[pl.BlockSpec(memory_space=pltpu.SMEM)]
        + [pl.BlockSpec(memory_space=pl.ANY)] * len(flat)
        + [anywhere] * len(earlier),
        out_specs=[anywhere] * 4,
        out_shape=[pltpu.HBM((rows, peers * per_peer), dtype)] * 4,
        input_output_aliases={1 + len(flat) + i: i for i in range(len(earlier))},
        scratch_shapes=[
            pltpu.VMEM((len(items),) + message_shape(m), dtype) for m in messages
        ]
        + [
            pltpu.VMEM((len(items), 4, len(jobs), rows, LANES), dtype),
            pltpu.SemaphoreType.DMA((chunk + 1, len(items))),
            pltpu.SemaphoreType.DMA((len(items), 4, len(jobs))),
        ],
        compiler_params=pltpu.CompilerParams(vmem_limit_bytes=SMALL_VMEM),
        name="unpack_items",
    )(me, *flat, *[in_hbm(x) for x in earlier])


def pick_kernel(me, asked, *refs, count):
    for_next, for_prev, table, sems = refs[-4:]
    heads, window, block_rows, _ = table.shape
    peers, each = sems.shape

    def fetch(item, i):
        source, peer = part_of(refs[:count], me, item)
        rows = pl.ds(i * block_rows, block_rows)
        return pltpu.make_async_copy(
            source.at[:, 0, rows], table.at[:, CROSS + peer * each + i], sems.at[item, i]
        )

    for item in range(peers):
        for i in range(each):
            fetch(item, i).start()
    for item in range(peers):
        for i in range(each):
            fetch(item, i).wait()
    for i in range(CROSS):
        for_next[i] = table[:, CROSS + asked[i]]
        for_prev[i] = table[:, CROSS + asked[CROSS + i]]


def pick(me, messages, asked, block_rows, after):
    heads, _, rows, lanes = message_shape(messages)
    dtype = messages[0].dtype
    peers = lax.axis_size("seq")
    each = rows // block_rows
    window = peers * each + 2 * CROSS
    picked = jax.ShapeDtypeStruct((CROSS, heads, block_rows, lanes), dtype)
    return pl.pallas_call(
        functools.partial(pick_kernel, count=len(messages)),
        in_specs=[pl.BlockSpec(memory_space=pltpu.SMEM)] * 2
        + [pl.BlockSpec(memory_space=pl.ANY)] * (len(messages) + len(after)),
        out_specs=[pl.BlockSpec(memory_space=pltpu.VMEM)] * 3,
        out_shape=[picked, picked, pltpu.VMEM((heads, window, block_rows, lanes), dtype)],
        scratch_shapes=[pltpu.SemaphoreType.DMA((peers, each))],
        compiler_params=pltpu.CompilerParams(vmem_limit_bytes=SMALL_VMEM),
        name="pick",
    )(me, asked, *messages, *[in_hbm(x) for x in after])


def prepare_kernel(me, table, *refs, peers):
    messages = refs[:-4]
    turned, pairs, sums, sems = refs[-4:]
    heads, window, _, _ = table.shape

    def fetch(item):
        source, peer = part_of(messages, me, item)
        return pltpu.make_async_copy(source.at[:, 1], pairs.at[peer], sems.at[item])

    for item in range(peers):
        fetch(item).start()
    for head in range(heads):

        def clear(i, carry):
            sums[head, i] = jnp.zeros(sums.shape[2:], sums.dtype)
            return carry

        def turn(i, carry):
            turned[head, i] = table[head, i].T
            return carry

        lax.fori_loop(0, window, clear, 0)
        lax.fori_loop(CROSS, window - CROSS, turn, 0)
    for item in range(peers):
        fetch(item).wait()


def prepare(me, messages, table):
    heads, _, rows, lanes = message_shape(messages)
    _, window, block_rows, _ = table.shape
    dtype = messages[0].dtype
    peers = lax.axis_size("seq")
    inside = pl.BlockSpec(memory_space=pltpu.VMEM)
    return pl.pallas_call(
        functools.partial(prepare_kernel, peers=peers),
        in_specs=[pl.BlockSpec(memory_space=pltpu.SMEM), inside]
        + [pl.BlockSpec(memory_space=pl.ANY)] * len(messages),
        out_specs=[inside] * 3,
        out_shape=[
            pltpu.VMEM((heads, window, lanes, block_rows), dtype),
            pltpu.VMEM((peers, heads, rows, lanes), dtype),
            pltpu.VMEM((heads, window, block_rows, lanes), jnp.float32),
        ],
        scratch_shapes=[pltpu.SemaphoreType.DMA((peers,))],
        compiler_params=pltpu.CompilerParams(vmem_limit_bytes=SMALL_VMEM),
        name="prepare",
    )(me, in_vmem(table), *messages)


def attend_kernel(
    lists,
    came_prev,
    came_next,
    pairs,
    table_in,
    turned_in,
    sums_in,
    back,
    to_prev,
    to_next,
    table,
    turned,
    sums,
    both_even,
    both_odd,
    low_even,
    low_odd,
    *,
    head_dim,
    per_list,
):
    del table_in, turned_in, sums_in
    peers, heads, rows, lanes = pairs.shape
    _, window, block_rows, _ = table.shape
    each = rows // block_rows
    blocks = peers * each
    units = heads * blocks
    keys = per_list * block_rows
    scaling = head_dim ** (-0.5)
    exponent = scaling * math.log2(math.e)
    both = (both_even, both_odd)
    low = (low_even, low_odd)
    step_rows = 64

    for head in range(heads):
        for i in range(CROSS):
            table[head, i] = came_prev[i, head]
            table[head, CROSS + blocks + i] = came_next[i, head]
            turned[head, i] = came_prev[i, head].T
            turned[head, CROSS + blocks + i] = came_next[i, head].T

    left = lax.broadcasted_iota(jnp.int32, (block_rows, lanes), 1) < head_dim

    def locate(unit):
        head = lax.div(unit, blocks)
        block = lax.rem(unit, blocks)
        ids = [lists[head, block, j] for j in range(per_list)]
        peer = lax.div(block, each)
        start = pl.multiple_of(lax.rem(block, each) * block_rows, block_rows)
        return head, ids, peer, pl.ds(start, block_rows)

    def apart_of(head, peer, here):
        query_grad = pairs[peer, head, here]
        nothing = jnp.zeros_like(query_grad)
        return jnp.concatenate(
            [jnp.where(left, query_grad, nothing), jnp.where(left, nothing, query_grad)],
            axis=0,
        )

    def score(unit, slot):
        head, ids, peer, here = locate(unit)
        key_value = jnp.concatenate([table[head, i] for i in ids], axis=0)
        both[slot][...] = lax.dot_general(
            key_value,
            apart_of(head, peer, here),
            (((1,), (1,)), ((), ())),
            preferred_element_type=jnp.float32,
        )

    def soften(slot):
        source, target = both[slot], low[slot]
        parts = [slice(i, i + step_rows) for i in range(0, keys, step_rows)]
        top = source[parts[0], :block_rows]
        for part in parts[1:]:
            top = jnp.maximum(top, source[part, :block_rows])
        top = jnp.max(top, axis=0, keepdims=True)
        total = jnp.zeros((step_rows, block_rows), jnp.float32)
        mixed = jnp.zeros((step_rows, block_rows), jnp.float32)
        for part in parts:
            raised = jnp.exp2((source[part, :block_rows] - top) * exponent)
            source[part, :block_rows] = raised
            total += raised
            mixed += raised * source[part, block_rows:]
        inverse = 1.0 / jnp.sum(total, axis=0, keepdims=True)
        correction = jnp.sum(mixed, axis=0, keepdims=True) * inverse
        for part in parts:
            weights = source[part, :block_rows] * inverse
            target[part, block_rows:] = weights.astype(jnp.bfloat16)
            target[part, :block_rows] = (
                weights * (source[part, block_rows:] - correction)
            ).astype(jnp.bfloat16)

    def combine(unit, slot):
        head, ids, peer, here = locate(unit)
        products = low[slot][...]
        terms = jnp.dot(
            products, apart_of(head, peer, here), preferred_element_type=jnp.float32
        )
        for j, i in enumerate(ids):
            sums[head, i] += terms[j * block_rows : (j + 1) * block_rows]
        key_value = jnp.concatenate([turned[head, i] for i in ids], axis=1)
        out = jnp.dot(key_value, products, preferred_element_type=jnp.float32)
        out = jnp.concatenate(
            [out[:head_dim, :block_rows] * scaling, out[head_dim:, block_rows:]], axis=0
        )
        back[peer, head, here] = out.T.astype(back.dtype)

    score(0, 0)
    score(1, 1)
    soften(0)

    def step(i, carry):
        for slot in range(2):
            unit = 2 * i + slot
            combine(unit - 2, slot)
            score(unit, slot)
            soften(1 - slot)
        return carry

    lax.fori_loop(1, units // 2, step, 0)
    combine(units - 2, 0)
    soften(1)
    combine(units - 1, 1)

    factor = jnp.where(left, scaling, 1.0)
    for head in range(heads):
        for i in range(CROSS):
            to_prev[i, head] = (sums[head, i] * factor).astype(to_prev.dtype)
            to_next[i, head] = (sums[head, CROSS + blocks + i] * factor).astype(to_next.dtype)


def attend(lists, came_prev, came_next, pairs, table, turned, sums):
    _, _, block_rows, lanes = came_prev.shape
    dtype = pairs.dtype
    per_list = lists.shape[-1]
    keys = per_list * block_rows
    inside = pl.BlockSpec(memory_space=pltpu.VMEM)
    cross_shape = jax.ShapeDtypeStruct(came_prev.shape, dtype)
    kept = (table, turned, sums)
    return pl.pallas_call(
        functools.partial(attend_kernel, head_dim=lanes // 2, per_list=per_list),
        in_specs=[pl.BlockSpec(memory_space=pltpu.SMEM)] + [inside] * 6,
        out_specs=[inside] * 6,
        out_shape=[pltpu.VMEM(pairs.shape, dtype), cross_shape, cross_shape]
        + [pltpu.VMEM(x.shape, x.dtype) for x in kept],
        input_output_aliases={4: 3, 5: 4, 6: 5},
        scratch_shapes=[
            pltpu.VMEM((keys, 2 * block_rows), jnp.float32),
            pltpu.VMEM((keys, 2 * block_rows), jnp.float32),
            pltpu.VMEM((keys, 2 * block_rows), dtype),
            pltpu.VMEM((keys, 2 * block_rows), dtype),
        ],
        compiler_params=pltpu.CompilerParams(vmem_limit_bytes=SMALL_VMEM),
        name="attend",
    )(lists, came_prev, came_next, *[in_vmem(x) for x in (pairs, *kept)])


def finish_kernel(me, asked, back, kept, later, earlier, *refs, block_rows):
    messages = refs[:-3]
    sums, ready, sems = refs[-3:]
    peers, heads, _, rows, lanes = ready.shape
    each = rows // block_rows
    blocks = peers * each
    head_dim = lanes // 2
    left = lax.broadcasted_iota(jnp.int32, (block_rows, lanes), 1) < head_dim
    factor = jnp.where(left, head_dim ** (-0.5), 1.0)

    def send(item, head):
        target, peer = part_of(messages, me, item)
        return pltpu.make_async_copy(
            ready.at[peer, head], target.at[head], sems.at[item, head]
        )

    for head in range(heads):
        sums[...] = kept[head, CROSS : CROSS + blocks] * factor
        for i in range(CROSS):
            sums[asked[i]] += later[i, head].astype(jnp.float32)
        for i in range(CROSS):
            sums[asked[CROSS + i]] += earlier[i, head].astype(jnp.float32)
        for peer in range(peers):
            ready[peer, head, 1] = back[peer, head]
            for i in range(each):
                ready[peer, head, 0, i * block_rows : (i + 1) * block_rows] = sums[
                    peer * each + i
                ].astype(ready.dtype)
        for item in range(peers):
            send(item, head).start()
    for head in range(heads):
        for item in range(peers):
            send(item, head).wait()


def finish(me, back, kept, later, earlier, asked, apart):
    peers, heads, rows, lanes = back.shape
    _, window, block_rows, _ = kept.shape
    blocks = window - 2 * CROSS
    inside = pl.BlockSpec(memory_space=pltpu.VMEM)
    scalars = pl.BlockSpec(memory_space=pltpu.SMEM)
    shape = (heads, 2, rows, lanes)
    outs = message_outs(peers, shape, back.dtype, apart)
    return pl.pallas_call(
        functools.partial(finish_kernel, block_rows=block_rows),
        in_specs=[scalars, scalars] + [inside] * 4,
        out_specs=[pl.BlockSpec(memory_space=pltpu.HBM)] * len(outs),
        out_shape=outs,
        scratch_shapes=[
            pltpu.VMEM((blocks, block_rows, lanes), jnp.float32),
            pltpu.VMEM((peers,) + shape, back.dtype),
            pltpu.SemaphoreType.DMA((peers, heads)),
        ],
        compiler_params=pltpu.CompilerParams(vmem_limit_bytes=SMALL_VMEM),
        name="finish",
    )(
        me,
        asked,
        in_vmem(back),
        in_vmem(kept),
        later,
        earlier,
    )


def local(query, key, value, d_out, pattern):
    heads_here, blocks, _ = pattern.shape
    peers = lax.axis_size("seq")
    rows, columns = query.shape
    head_dim = columns // (peers * heads_here)
    block_rows = rows * peers // blocks
    chunks = min(CHUNKS, heads_here)
    starts = [-(-heads_here * i // chunks) for i in range(chunks)]
    sizes = [end - start for start, end in zip(starts, starts[1:] + [heads_here])]
    arrays = (query, key, value, d_out)

    own_base = lax.axis_index("slab") * blocks
    block_ids = jnp.arange(blocks, dtype=jnp.int32)
    flat_lists = pattern.reshape(-1)
    reverse_rank = blocks - 1 - block_ids
    hits_prev = jnp.any(flat_lists[:, None] == (own_base - blocks + block_ids)[None, :], axis=0)
    hits_next = jnp.any(flat_lists[:, None] == (own_base + blocks + block_ids)[None, :], axis=0)
    need_prev = lax.top_k(hits_prev.astype(jnp.int32) * blocks + reverse_rank, CROSS)[1]
    need_next = lax.top_k(hits_next.astype(jnp.int32) * blocks + reverse_rank, CROSS)[1]
    asked_next = from_behind(need_prev, "slab", -1)
    asked_prev = from_behind(need_next, "slab", 1)
    asked = jnp.concatenate([asked_next, asked_prev])
    rank_ids = jnp.arange(CROSS, dtype=jnp.int32)
    prev_global = own_base - blocks + need_prev
    next_global = own_base + blocks + need_next
    pos_prev = jnp.sum(jnp.where(pattern[..., None] == prev_global, rank_ids, 0), axis=-1)
    pos_next = jnp.sum(jnp.where(pattern[..., None] == next_global, rank_ids, 0), axis=-1)
    in_own = (pattern >= own_base) & (pattern < own_base + blocks)
    local_ids = jnp.where(
        in_own,
        CROSS + pattern - own_base,
        jnp.where(pattern < own_base, pos_prev, CROSS + blocks + pos_next),
    )

    me = lax.axis_index("seq").astype(jnp.int32).reshape(1)
    last = chunks - 1
    came = []
    for chunk, (start, size) in enumerate(zip(starts, sizes)):
        after = (asked, local_ids) if came else ()
        packed = pack(arrays, start, size, heads_here, peers, head_dim, after)
        came.append(exchange(packed))
    received = []
    outs = finished = ()
    for chunk, (messages, start, size) in enumerate(zip(came, starts, sizes)):
        for_next, for_prev, table = pick(me, messages, asked, block_rows, finished[:1])
        came_prev = from_behind(for_next, "slab", 1)
        came_next = from_behind(for_prev, "slab", -1)
        turned, pairs, sums = prepare(me, messages, table)
        lists = local_ids[start : start + size]
        back, to_prev, to_next, _, _, kept = attend(
            lists, came_prev, came_next, pairs, table, turned, sums
        )
        later = from_behind(to_prev, "slab", -1)
        earlier = from_behind(to_next, "slab", 1)
        finished = finish(me, back, kept, later, earlier, asked, chunk == last)
        received.append(exchange(finished))
        if chunk == last and heads_here * head_dim % LANES == 0:
            half = peers // 2
            near = list(range(peers - 2, half - 1, -1))
            parts = (
                [peers - 1, *near[::2]],
                list(range(half // 2)),
                list(range(half // 2, half - 1)),
                [half - 1, *near[1::2]],
            )
            for items in parts:
                outs = unpack_items(me, received, starts, heads_here, items, outs)
        else:
            outs = unpack(me, received, starts, heads_here, outs)
    return tuple(outs)


def solution(mesh):
    tokens = P(("slab", "seq"), None)
    return jax.shard_map(
        local,
        mesh=mesh,
        in_specs=(tokens, tokens, tokens, tokens, P("seq", "slab", None)),
        out_specs=(tokens, tokens, tokens, tokens),
        check_vma=False,
    )
```

```python
import functools
import math

import jax
import jax.numpy as jnp
from jax import lax
from jax.experimental import pallas as pl
from jax.experimental.pallas import tpu as pltpu
from jax.sharding import PartitionSpec as P

CROSS = 4
CHUNKS = 2
LANES = 128
SMALL_VMEM = 24 * 1024 * 1024
LARGE_VMEM = 40 * 1024 * 1024


def in_hbm(x):
    return pltpu.with_memory_space_constraint(x, pltpu.HBM)


def in_vmem(x):
    return pltpu.with_memory_space_constraint(x, pltpu.VMEM)


def from_behind(x, axis, by):
    count = lax.axis_size(axis)
    pairs = [(i, i + by) for i in range(count) if 0 <= i + by < count]
    return lax.ppermute(x, axis, pairs)


def part_of(messages, me, item):
    if len(messages) == 1:
        return messages[0].at[item], item
    return messages[item], me[0] ^ (len(messages) - 1 - item)


def message_shape(messages):
    return messages[0].shape[-4:]


def message_outs(peers, shape, dtype, apart):
    if apart:
        return [pltpu.HBM(shape, dtype)] * peers
    return [pltpu.HBM((peers,) + shape, dtype)]


def exchange(messages):
    if len(messages) == 1:
        return [lax.all_to_all(messages[0], "seq", split_axis=0, concat_axis=0, tiled=True)]
    count = len(messages)
    received = list(messages)
    for item in range(count - 1):
        pairs = [(i, i ^ (count - 1 - item)) for i in range(count)]
        received[item] = lax.ppermute(messages[item], "seq", pairs)
    return received


def join(left, right, head_dim, half):
    first = lax.broadcasted_iota(jnp.int32, left.shape, 1) < head_dim
    if half == 0:
        return jnp.where(first, left, pltpu.roll(right, head_dim, 1))
    return jnp.where(first, pltpu.roll(left, head_dim, 1), right)


def pack_kernel(query, key, value, d_out, *refs, first, heads, per_peer, head_dim):
    message, stage, ready, in_sems, out_sems = refs[-5:]
    sources = (key, value, query, d_out)
    peers = message.shape[0]

    def span(peer):
        begin = peer * per_peer + first
        low = begin // LANES * LANES
        high = -(-(begin + heads * head_dim) // LANES) * LANES
        return low, high - low, begin - low

    def fetch(peer, i):
        low, width, _ = span(peer)
        return pltpu.make_async_copy(
            sources[i].at[:, pl.ds(low, width)],
            stage.at[i, peer, :, pl.ds(0, width)],
            in_sems.at[i, peer],
        )

    def send(peer):
        return pltpu.make_async_copy(ready.at[peer], message.at[peer], out_sems.at[peer])

    for peer in range(peers):
        for i in range(4):
            fetch(peer, i).start()
    for peer in range(peers):
        for i in range(4):
            fetch(peer, i).wait()
        at = span(peer)[2]
        for head in range(heads):
            tile, inside = divmod(at + head * head_dim, LANES)
            lanes = slice(tile * LANES, (tile + 1) * LANES)
            for kind in range(2):
                ready[peer, head, kind] = join(
                    stage[2 * kind, peer, :, lanes],
                    stage[2 * kind + 1, peer, :, lanes],
                    head_dim,
                    inside // head_dim,
                )
        send(peer).start()
    for peer in range(peers):
        send(peer).wait()


def pack(arrays, start, heads, heads_here, peers, head_dim, after):
    rows = arrays[0].shape[0]
    dtype = arrays[0].dtype
    shape = (peers, heads, 2, rows, 2 * head_dim)
    width = (-(-heads * head_dim // LANES) + 1) * LANES
    anywhere = pl.BlockSpec(memory_space=pltpu.HBM)
    return pl.pallas_call(
        functools.partial(
            pack_kernel,
            first=start * head_dim,
            heads=heads,
            per_peer=heads_here * head_dim,
            head_dim=head_dim,
        ),
        in_specs=[anywhere] * 4 + [pl.BlockSpec(memory_space=pl.ANY)] * len(after),
        out_specs=[anywhere],
        out_shape=[pltpu.HBM(shape, dtype)],
        scratch_shapes=[
            pltpu.VMEM((4, peers, rows, width), dtype),
            pltpu.VMEM(shape, dtype),
            pltpu.SemaphoreType.DMA((4, peers)),
            pltpu.SemaphoreType.DMA((peers,)),
        ],
        compiler_params=pltpu.CompilerParams(vmem_limit_bytes=SMALL_VMEM),
        name="pack",
    )(*[in_hbm(x) for x in arrays], *after)


def unpack_kernel(me, *refs, chunk, peers, counts, earlier, jobs):
    ends = [sum(counts[: c + 1]) for c in range(chunk + 1)]
    groups = [refs[end - count : end] for end, count in zip(ends, counts)]
    outs = refs[ends[-1] + earlier :][:4]
    stages = refs[-3 - chunk - 1 : -3]
    ready, in_sems, out_sems = refs[-3:]
    head_dim = ready.shape[-1] // 2
    used = sorted({(which, peer) for job in jobs for which, peer, _ in job[1:]})
    chunks_used = sorted({which for which, _ in used})
    heads_used = {
        c: sorted({head for job in jobs for which, _, head in job[1:] if which == c})
        for c in chunks_used
    }

    def fetch(which, item, slot=None):
        heads = heads_used[which]
        some = pl.ds(heads[0], heads[-1] - heads[0] + 1)
        source, peer = part_of(groups[which], me, item)
        slot = peer if slot is None else slot
        return pltpu.make_async_copy(
            source.at[some], stages[which].at[slot, some], in_sems.at[which, slot]
        )

    def send(job, i):
        tile = jobs[job][0]
        return pltpu.make_async_copy(
            ready.at[i, job],
            outs[i].at[:, pl.ds(tile * LANES, LANES)],
            out_sems.at[4 * job + i],
        )

    for item in range(peers):
        for which in chunks_used:
            fetch(which, item).start()
    waited = set()

    def wait_for(which, peer):
        if (which, peer) not in waited:
            fetch(which, 0, peer).wait()
            waited.add((which, peer))

    for job, (tile, left, right) in enumerate(jobs):
        for which, peer, _ in (left, right):
            wait_for(which, peer)
        sides = [stages[which][peer, head] for which, peer, head in (left, right)]
        for i, (kind, half) in enumerate(((1, 1), (1, 0), (0, 0), (0, 1))):
            ready[i, job] = join(sides[0][kind], sides[1][kind], head_dim, half)
            send(job, i).start()
    for which in chunks_used:
        for peer in range(peers):
            wait_for(which, peer)
    for job in range(len(jobs)):
        for i in range(4):
            send(job, i).wait()


def unpack(me, messages, starts, heads_here, earlier):
    chunk = len(messages) - 1
    peers = lax.axis_size("seq")
    _, _, rows, pair_dim = message_shape(messages[0])
    head_dim = pair_dim // 2
    columns = peers * heads_here * head_dim
    dtype = messages[0][0].dtype

    def place_of(head):
        peer, local_head = divmod(head, heads_here)
        which = max(c for c, start in enumerate(starts) if start <= local_head)
        return which, peer, local_head - starts[which]

    jobs = []
    for tile in range(columns // LANES):
        left, right = place_of(2 * tile), place_of(2 * tile + 1)
        if max(left[0], right[0]) == chunk:
            jobs.append((tile, left, right))
    if not jobs:
        return earlier
    flat = [x for group in messages for x in group]
    anywhere = pl.BlockSpec(memory_space=pltpu.HBM)
    return pl.pallas_call(
        functools.partial(
            unpack_kernel,
            chunk=chunk,
            peers=peers,
            counts=[len(group) for group in messages],
            earlier=len(earlier),
            jobs=jobs,
        ),
        in_specs=[pl.BlockSpec(memory_space=pltpu.SMEM)]
        + [pl.BlockSpec(memory_space=pl.ANY)] * len(flat)
        + [anywhere] * len(earlier),
        out_specs=[anywhere] * 4,
        out_shape=[pltpu.HBM((rows, columns), dtype)] * 4,
        input_output_aliases={1 + len(flat) + i: i for i in range(len(earlier))},
        scratch_shapes=[pltpu.VMEM((peers,) + message_shape(m), dtype) for m in messages]
        + [
            pltpu.VMEM((4, len(jobs), rows, LANES), dtype),
            pltpu.SemaphoreType.DMA((chunk + 1, peers)),
            pltpu.SemaphoreType.DMA((4 * len(jobs),)),
        ],
        compiler_params=pltpu.CompilerParams(vmem_limit_bytes=SMALL_VMEM),
        name="unpack",
    )(me, *flat, *[in_hbm(x) for x in earlier])


def unpack_items_kernel(me, *refs, items, peers, counts, joint, earlier, jobs, per_peer):
    ends = [sum(counts[: c + 1]) for c in range(len(counts))]
    groups = [refs[end - count : end] for end, count in zip(ends, counts)]
    outs = refs[ends[-1] + earlier :][:4]
    ready, out_sems = refs[-2:]
    head_dim = ready.shape[-1] // 2

    def peer_of(j):
        return me[0] ^ (peers - 1 - items[j])

    def side_of(which, j, head, kind):
        if joint[which]:
            return groups[which][0][peer_of(j), head, kind]
        return groups[which][j][head, kind]

    def send(j, job, i):
        first = pl.multiple_of(peer_of(j) * per_peer, LANES) + jobs[job][0] * LANES
        return pltpu.make_async_copy(
            ready.at[j, i, job], outs[i].at[:, pl.ds(first, LANES)], out_sems.at[j, i, job]
        )

    for j in range(len(items)):
        for job, (_, left, right) in enumerate(jobs):
            for i, (kind, half) in enumerate(((1, 1), (1, 0), (0, 0), (0, 1))):
                ready[j, i, job] = join(
                    side_of(left[0], j, left[1], kind),
                    side_of(right[0], j, right[1], kind),
                    head_dim,
                    half,
                )
                send(j, job, i).start()
    for j in range(len(items)):
        for job in range(len(jobs)):
            for i in range(4):
                send(j, job, i).wait()


def unpack_items(me, messages, starts, heads_here, items, earlier):
    chunk = len(messages) - 1
    peers = lax.axis_size("seq")
    _, _, rows, pair_dim = message_shape(messages[0])
    head_dim = pair_dim // 2
    per_peer = heads_here * head_dim
    dtype = messages[0][0].dtype

    def place_of(head):
        which = max(c for c, start in enumerate(starts) if start <= head)
        return which, head - starts[which]

    jobs = []
    for tile in range(per_peer // LANES):
        left, right = place_of(2 * tile), place_of(2 * tile + 1)
        if max(left[0], right[0]) == chunk:
            jobs.append((tile, left, right))
    groups = [
        list(group) if len(group) == 1 else [group[item] for item in items]
        for group in messages
    ]
    flat = [x for group in groups for x in group]
    anywhere = pl.BlockSpec(memory_space=pltpu.HBM)
    return pl.pallas_call(
        functools.partial(
            unpack_items_kernel,
            items=items,
            peers=peers,
            counts=[len(group) for group in groups],
            joint=[len(group) == 1 for group in messages],
            earlier=len(earlier),
            jobs=jobs,
            per_peer=per_peer,
        ),
        in_specs=[pl.BlockSpec(memory_space=pltpu.SMEM)]
        + [pl.BlockSpec(memory_space=pltpu.VMEM)] * len(flat)
        + [anywhere] * len(earlier),
        out_specs=[anywhere] * 4,
        out_shape=[pltpu.HBM((rows, peers * per_peer), dtype)] * 4,
        input_output_aliases={1 + len(flat) + i: i for i in range(len(earlier))},
        scratch_shapes=[
            pltpu.VMEM((len(items), 4, len(jobs), rows, LANES), dtype),
            pltpu.SemaphoreType.DMA((len(items), 4, len(jobs))),
        ],
        compiler_params=pltpu.CompilerParams(vmem_limit_bytes=SMALL_VMEM),
        name="unpack_items",
    )(me, *[in_vmem(x) for x in flat], *[in_hbm(x) for x in earlier])


def pick_kernel(me, asked, *refs, count):
    for_next, for_prev, table, sems = refs[-4:]
    heads, window, block_rows, _ = table.shape
    peers, each = sems.shape

    def fetch(item, i):
        source, peer = part_of(refs[:count], me, item)
        rows = pl.ds(i * block_rows, block_rows)
        return pltpu.make_async_copy(
            source.at[:, 0, rows], table.at[:, CROSS + peer * each + i], sems.at[item, i]
        )

    for item in range(peers):
        for i in range(each):
            fetch(item, i).start()
    for item in range(peers):
        for i in range(each):
            fetch(item, i).wait()
    for i in range(CROSS):
        for_next[i] = table[:, CROSS + asked[i]]
        for_prev[i] = table[:, CROSS + asked[CROSS + i]]


def pick(me, messages, asked, block_rows, after):
    heads, _, rows, lanes = message_shape(messages)
    dtype = messages[0].dtype
    peers = lax.axis_size("seq")
    each = rows // block_rows
    window = peers * each + 2 * CROSS
    picked = jax.ShapeDtypeStruct((CROSS, heads, block_rows, lanes), dtype)
    return pl.pallas_call(
        functools.partial(pick_kernel, count=len(messages)),
        in_specs=[pl.BlockSpec(memory_space=pltpu.SMEM)] * 2
        + [pl.BlockSpec(memory_space=pl.ANY)] * (len(messages) + len(after)),
        out_specs=[pl.BlockSpec(memory_space=pltpu.VMEM)] * 3,
        out_shape=[picked, picked, pltpu.VMEM((heads, window, block_rows, lanes), dtype)],
        scratch_shapes=[pltpu.SemaphoreType.DMA((peers, each))],
        compiler_params=pltpu.CompilerParams(vmem_limit_bytes=SMALL_VMEM),
        name="pick",
    )(me, asked, *messages, *[in_hbm(x) for x in after])


def prepare_kernel(me, table, *refs, peers):
    messages = refs[:-4]
    turned, pairs, sums, sems = refs[-4:]
    heads, window, _, _ = table.shape

    def fetch(item):
        source, peer = part_of(messages, me, item)
        return pltpu.make_async_copy(source.at[:, 1], pairs.at[peer], sems.at[item])

    for item in range(peers):
        fetch(item).start()
    for head in range(heads):

        def clear(i, carry):
            sums[head, i] = jnp.zeros(sums.shape[2:], sums.dtype)
            return carry

        def turn(i, carry):
            turned[head, i] = table[head, i].T
            return carry

        lax.fori_loop(0, window, clear, 0)
        lax.fori_loop(CROSS, window - CROSS, turn, 0)
    for item in range(peers):
        fetch(item).wait()


def prepare(me, messages, table):
    heads, _, rows, lanes = message_shape(messages)
    _, window, block_rows, _ = table.shape
    dtype = messages[0].dtype
    peers = lax.axis_size("seq")
    inside = pl.BlockSpec(memory_space=pltpu.VMEM)
    return pl.pallas_call(
        functools.partial(prepare_kernel, peers=peers),
        in_specs=[pl.BlockSpec(memory_space=pltpu.SMEM), inside]
        + [pl.BlockSpec(memory_space=pl.ANY)] * len(messages),
        out_specs=[inside] * 3,
        out_shape=[
            pltpu.VMEM((heads, window, lanes, block_rows), dtype),
            pltpu.VMEM((peers, heads, rows, lanes), dtype),
            pltpu.VMEM((heads, window, block_rows, lanes), jnp.float32),
        ],
        scratch_shapes=[pltpu.SemaphoreType.DMA((peers,))],
        compiler_params=pltpu.CompilerParams(vmem_limit_bytes=SMALL_VMEM),
        name="prepare",
    )(me, in_vmem(table), *messages)


def attend_kernel(
    lists,
    came_prev,
    came_next,
    pairs,
    table_in,
    turned_in,
    sums_in,
    back,
    to_prev,
    to_next,
    table,
    turned,
    sums,
    both_even,
    both_odd,
    low_even,
    low_odd,
    *,
    head_dim,
    per_list,
):
    del table_in, turned_in, sums_in
    peers, heads, rows, lanes = pairs.shape
    _, window, block_rows, _ = table.shape
    each = rows // block_rows
    blocks = peers * each
    units = heads * blocks
    keys = per_list * block_rows
    scaling = head_dim ** (-0.5)
    exponent = scaling * math.log2(math.e)
    both = (both_even, both_odd)
    low = (low_even, low_odd)
    step_rows = 64

    for head in range(heads):
        for i in range(CROSS):
            table[head, i] = came_prev[i, head]
            table[head, CROSS + blocks + i] = came_next[i, head]
            turned[head, i] = came_prev[i, head].T
            turned[head, CROSS + blocks + i] = came_next[i, head].T

    left = lax.broadcasted_iota(jnp.int32, (block_rows, lanes), 1) < head_dim

    def locate(unit):
        head = lax.div(unit, blocks)
        block = lax.rem(unit, blocks)
        ids = [lists[head, block, j] for j in range(per_list)]
        peer = lax.div(block, each)
        start = pl.multiple_of(lax.rem(block, each) * block_rows, block_rows)
        return head, ids, peer, pl.ds(start, block_rows)

    def apart_of(head, peer, here):
        query_grad = pairs[peer, head, here]
        nothing = jnp.zeros_like(query_grad)
        return jnp.concatenate(
            [jnp.where(left, query_grad, nothing), jnp.where(left, nothing, query_grad)],
            axis=0,
        )

    def score(unit, slot):
        head, ids, peer, here = locate(unit)
        key_value = jnp.concatenate([table[head, i] for i in ids], axis=0)
        both[slot][...] = lax.dot_general(
            key_value,
            apart_of(head, peer, here),
            (((1,), (1,)), ((), ())),
            preferred_element_type=jnp.float32,
        )

    def soften(slot):
        source, target = both[slot], low[slot]
        parts = [slice(i, i + step_rows) for i in range(0, keys, step_rows)]
        top = source[parts[0], :block_rows]
        for part in parts[1:]:
            top = jnp.maximum(top, source[part, :block_rows])
        top = jnp.max(top, axis=0, keepdims=True)
        total = jnp.zeros((step_rows, block_rows), jnp.float32)
        mixed = jnp.zeros((step_rows, block_rows), jnp.float32)
        for part in parts:
            raised = jnp.exp2((source[part, :block_rows] - top) * exponent)
            source[part, :block_rows] = raised
            total += raised
            mixed += raised * source[part, block_rows:]
        inverse = 1.0 / jnp.sum(total, axis=0, keepdims=True)
        correction = jnp.sum(mixed, axis=0, keepdims=True) * inverse
        for part in parts:
            weights = source[part, :block_rows] * inverse
            target[part, block_rows:] = weights.astype(jnp.bfloat16)
            target[part, :block_rows] = (
                weights * (source[part, block_rows:] - correction)
            ).astype(jnp.bfloat16)

    def combine(unit, slot):
        head, ids, peer, here = locate(unit)
        products = low[slot][...]
        terms = jnp.dot(
            products, apart_of(head, peer, here), preferred_element_type=jnp.float32
        )
        for j, i in enumerate(ids):
            sums[head, i] += terms[j * block_rows : (j + 1) * block_rows]
        key_value = jnp.concatenate([turned[head, i] for i in ids], axis=1)
        out = jnp.dot(key_value, products, preferred_element_type=jnp.float32)
        out = jnp.concatenate(
            [out[:head_dim, :block_rows] * scaling, out[head_dim:, block_rows:]], axis=0
        )
        back[peer, head, here] = out.T.astype(back.dtype)

    score(0, 0)
    score(1, 1)
    soften(0)

    def step(i, carry):
        for slot in range(2):
            unit = 2 * i + slot
            combine(unit - 2, slot)
            score(unit, slot)
            soften(1 - slot)
        return carry

    lax.fori_loop(1, units // 2, step, 0)
    combine(units - 2, 0)
    soften(1)
    combine(units - 1, 1)

    factor = jnp.where(left, scaling, 1.0)
    for head in range(heads):
        for i in range(CROSS):
            to_prev[i, head] = (sums[head, i] * factor).astype(to_prev.dtype)
            to_next[i, head] = (sums[head, CROSS + blocks + i] * factor).astype(to_next.dtype)


def attend(lists, came_prev, came_next, pairs, table, turned, sums):
    _, _, block_rows, lanes = came_prev.shape
    dtype = pairs.dtype
    per_list = lists.shape[-1]
    keys = per_list * block_rows
    inside = pl.BlockSpec(memory_space=pltpu.VMEM)
    cross_shape = jax.ShapeDtypeStruct(came_prev.shape, dtype)
    kept = (table, turned, sums)
    return pl.pallas_call(
        functools.partial(attend_kernel, head_dim=lanes // 2, per_list=per_list),
        in_specs=[pl.BlockSpec(memory_space=pltpu.SMEM)] + [inside] * 6,
        out_specs=[inside] * 6,
        out_shape=[pltpu.VMEM(pairs.shape, dtype), cross_shape, cross_shape]
        + [pltpu.VMEM(x.shape, x.dtype) for x in kept],
        input_output_aliases={4: 3, 5: 4, 6: 5},
        scratch_shapes=[
            pltpu.VMEM((keys, 2 * block_rows), jnp.float32),
            pltpu.VMEM((keys, 2 * block_rows), jnp.float32),
            pltpu.VMEM((keys, 2 * block_rows), dtype),
            pltpu.VMEM((keys, 2 * block_rows), dtype),
        ],
        compiler_params=pltpu.CompilerParams(vmem_limit_bytes=SMALL_VMEM),
        name="attend",
    )(lists, came_prev, came_next, *[in_vmem(x) for x in (pairs, *kept)])


def finish_kernel(me, asked, back, kept, later, earlier, *refs, block_rows):
    messages = refs[:-3]
    sums, ready, sems = refs[-3:]
    peers, heads, _, rows, lanes = ready.shape
    each = rows // block_rows
    blocks = peers * each
    head_dim = lanes // 2
    left = lax.broadcasted_iota(jnp.int32, (block_rows, lanes), 1) < head_dim
    factor = jnp.where(left, head_dim ** (-0.5), 1.0)

    def send(item, head):
        target, peer = part_of(messages, me, item)
        return pltpu.make_async_copy(
            ready.at[peer, head], target.at[head], sems.at[item, head]
        )

    for head in range(heads):
        sums[...] = kept[head, CROSS : CROSS + blocks] * factor
        for i in range(CROSS):
            sums[asked[i]] += later[i, head].astype(jnp.float32)
        for i in range(CROSS):
            sums[asked[CROSS + i]] += earlier[i, head].astype(jnp.float32)
        for peer in range(peers):
            ready[peer, head, 1] = back[peer, head]
            for i in range(each):
                ready[peer, head, 0, i * block_rows : (i + 1) * block_rows] = sums[
                    peer * each + i
                ].astype(ready.dtype)
        for item in range(peers):
            send(item, head).start()
    for head in range(heads):
        for item in range(peers):
            send(item, head).wait()


def finish(me, back, kept, later, earlier, asked, apart):
    peers, heads, rows, lanes = back.shape
    _, window, block_rows, _ = kept.shape
    blocks = window - 2 * CROSS
    inside = pl.BlockSpec(memory_space=pltpu.VMEM)
    scalars = pl.BlockSpec(memory_space=pltpu.SMEM)
    shape = (heads, 2, rows, lanes)
    outs = message_outs(peers, shape, back.dtype, apart)
    return pl.pallas_call(
        functools.partial(finish_kernel, block_rows=block_rows),
        in_specs=[scalars, scalars] + [inside] * 4,
        out_specs=[pl.BlockSpec(memory_space=pltpu.HBM)] * len(outs),
        out_shape=outs,
        scratch_shapes=[
            pltpu.VMEM((blocks, block_rows, lanes), jnp.float32),
            pltpu.VMEM((peers,) + shape, back.dtype),
            pltpu.SemaphoreType.DMA((peers, heads)),
        ],
        compiler_params=pltpu.CompilerParams(vmem_limit_bytes=SMALL_VMEM),
        name="finish",
    )(
        me,
        asked,
        in_vmem(back),
        in_vmem(kept),
        later,
        earlier,
    )


def local(query, key, value, d_out, pattern):
    heads_here, blocks, _ = pattern.shape
    peers = lax.axis_size("seq")
    rows, columns = query.shape
    head_dim = columns // (peers * heads_here)
    block_rows = rows * peers // blocks
    chunks = min(CHUNKS, heads_here)
    starts = [-(-heads_here * i // chunks) for i in range(chunks)]
    sizes = [end - start for start, end in zip(starts, starts[1:] + [heads_here])]
    arrays = (query, key, value, d_out)

    own_base = lax.axis_index("slab") * blocks
    block_ids = jnp.arange(blocks, dtype=jnp.int32)
    flat_lists = pattern.reshape(-1)
    reverse_rank = blocks - 1 - block_ids
    hits_prev = jnp.any(flat_lists[:, None] == (own_base - blocks + block_ids)[None, :], axis=0)
    hits_next = jnp.any(flat_lists[:, None] == (own_base + blocks + block_ids)[None, :], axis=0)
    need_prev = lax.top_k(hits_prev.astype(jnp.int32) * blocks + reverse_rank, CROSS)[1]
    need_next = lax.top_k(hits_next.astype(jnp.int32) * blocks + reverse_rank, CROSS)[1]
    asked_next = from_behind(need_prev, "slab", -1)
    asked_prev = from_behind(need_next, "slab", 1)
    asked = jnp.concatenate([asked_next, asked_prev])
    rank_ids = jnp.arange(CROSS, dtype=jnp.int32)
    prev_global = own_base - blocks + need_prev
    next_global = own_base + blocks + need_next
    pos_prev = jnp.sum(jnp.where(pattern[..., None] == prev_global, rank_ids, 0), axis=-1)
    pos_next = jnp.sum(jnp.where(pattern[..., None] == next_global, rank_ids, 0), axis=-1)
    in_own = (pattern >= own_base) & (pattern < own_base + blocks)
    local_ids = jnp.where(
        in_own,
        CROSS + pattern - own_base,
        jnp.where(pattern < own_base, pos_prev, CROSS + blocks + pos_next),
    )

    me = lax.axis_index("seq").astype(jnp.int32).reshape(1)
    last = chunks - 1
    came = []
    for chunk, (start, size) in enumerate(zip(starts, sizes)):
        after = (asked, local_ids) if came else ()
        packed = pack(arrays, start, size, heads_here, peers, head_dim, after)
        came.append(exchange(packed))
    received = []
    outs = finished = ()
    for chunk, (messages, start, size) in enumerate(zip(came, starts, sizes)):
        for_next, for_prev, table = pick(me, messages, asked, block_rows, finished[:1])
        came_prev = from_behind(for_next, "slab", 1)
        came_next = from_behind(for_prev, "slab", -1)
        turned, pairs, sums = prepare(me, messages, table)
        lists = local_ids[start : start + size]
        back, to_prev, to_next, _, _, kept = attend(
            lists, came_prev, came_next, pairs, table, turned, sums
        )
        later = from_behind(to_prev, "slab", -1)
        earlier = from_behind(to_next, "slab", 1)
        finished = finish(me, back, kept, later, earlier, asked, chunk == last)
        received.append(exchange(finished))
        if chunk == last and heads_here * head_dim % LANES == 0:
            half = peers // 2
            near = list(range(peers - 2, half - 1, -1))
            parts = (
                [peers - 1, *near[::2]],
                list(range(half // 2)),
                list(range(half // 2, half - 1)),
                [half - 1, *near[1::2]],
            )
            for items in parts:
                outs = unpack_items(me, received, starts, heads_here, items, outs)
        else:
            outs = unpack(me, received, starts, heads_here, outs)
    return tuple(outs)


def solution(mesh):
    tokens = P(("slab", "seq"), None)
    return jax.shard_map(
        local,
        mesh=mesh,
        in_specs=(tokens, tokens, tokens, tokens, P("seq", "slab", None)),
        out_specs=(tokens, tokens, tokens, tokens),
        check_vma=False,
    )
```

```python
import functools
import math

import jax
import jax.numpy as jnp
from jax import lax
from jax.experimental import pallas as pl
from jax.experimental.pallas import tpu as pltpu
from jax.sharding import PartitionSpec as P

CROSS = 4
CHUNKS = 2
LANES = 128
SMALL_VMEM = 24 * 1024 * 1024
LARGE_VMEM = 40 * 1024 * 1024


def in_hbm(x):
    return pltpu.with_memory_space_constraint(x, pltpu.HBM)


def in_vmem(x):
    return pltpu.with_memory_space_constraint(x, pltpu.VMEM)


def from_behind(x, axis, by):
    count = lax.axis_size(axis)
    pairs = [(i, i + by) for i in range(count) if 0 <= i + by < count]
    return lax.ppermute(x, axis, pairs)


def part_of(messages, me, item):
    if len(messages) == 1:
        return messages[0].at[item], item
    return messages[item], me[0] ^ (len(messages) - 1 - item)


def message_shape(messages):
    return messages[0].shape[-4:]


def message_outs(peers, shape, dtype, apart):
    if apart:
        return [pltpu.HBM(shape, dtype)] * peers
    return [pltpu.HBM((peers,) + shape, dtype)]


def exchange(messages):
    if len(messages) == 1:
        return [lax.all_to_all(messages[0], "seq", split_axis=0, concat_axis=0, tiled=True)]
    count = len(messages)
    received = list(messages)
    for item in range(count - 1):
        pairs = [(i, i ^ (count - 1 - item)) for i in range(count)]
        received[item] = lax.ppermute(messages[item], "seq", pairs)
    return received


def join(left, right, head_dim, half):
    first = lax.broadcasted_iota(jnp.int32, left.shape, 1) < head_dim
    if half == 0:
        return jnp.where(first, left, pltpu.roll(right, head_dim, 1))
    return jnp.where(first, pltpu.roll(left, head_dim, 1), right)


def pack_kernel(query, key, value, d_out, *refs, first, heads, per_peer, head_dim):
    message, stage, ready, in_sems, out_sems = refs[-5:]
    sources = (key, value, query, d_out)
    peers = message.shape[0]

    def span(peer):
        begin = peer * per_peer + first
        low = begin // LANES * LANES
        high = -(-(begin + heads * head_dim) // LANES) * LANES
        return low, high - low, begin - low

    def fetch(peer, i):
        low, width, _ = span(peer)
        return pltpu.make_async_copy(
            sources[i].at[:, pl.ds(low, width)],
            stage.at[i, peer, :, pl.ds(0, width)],
            in_sems.at[i, peer],
        )

    def send(peer):
        return pltpu.make_async_copy(ready.at[peer], message.at[peer], out_sems.at[peer])

    for peer in range(peers):
        for i in range(4):
            fetch(peer, i).start()
    for peer in range(peers):
        for i in range(4):
            fetch(peer, i).wait()
        at = span(peer)[2]
        for head in range(heads):
            tile, inside = divmod(at + head * head_dim, LANES)
            lanes = slice(tile * LANES, (tile + 1) * LANES)
            for kind in range(2):
                ready[peer, head, kind] = join(
                    stage[2 * kind, peer, :, lanes],
                    stage[2 * kind + 1, peer, :, lanes],
                    head_dim,
                    inside // head_dim,
                )
        send(peer).start()
    for peer in range(peers):
        send(peer).wait()


def pack(arrays, start, heads, heads_here, peers, head_dim, after):
    rows = arrays[0].shape[0]
    dtype = arrays[0].dtype
    shape = (peers, heads, 2, rows, 2 * head_dim)
    width = (-(-heads * head_dim // LANES) + 1) * LANES
    anywhere = pl.BlockSpec(memory_space=pltpu.HBM)
    return pl.pallas_call(
        functools.partial(
            pack_kernel,
            first=start * head_dim,
            heads=heads,
            per_peer=heads_here * head_dim,
            head_dim=head_dim,
        ),
        in_specs=[anywhere] * 4 + [pl.BlockSpec(memory_space=pl.ANY)] * len(after),
        out_specs=[anywhere],
        out_shape=[pltpu.HBM(shape, dtype)],
        scratch_shapes=[
            pltpu.VMEM((4, peers, rows, width), dtype),
            pltpu.VMEM(shape, dtype),
            pltpu.SemaphoreType.DMA((4, peers)),
            pltpu.SemaphoreType.DMA((peers,)),
        ],
        compiler_params=pltpu.CompilerParams(vmem_limit_bytes=SMALL_VMEM),
        name="pack",
    )(*[in_hbm(x) for x in arrays], *after)


def unpack_kernel(me, *refs, chunk, peers, counts, earlier, jobs):
    ends = [sum(counts[: c + 1]) for c in range(chunk + 1)]
    groups = [refs[end - count : end] for end, count in zip(ends, counts)]
    outs = refs[ends[-1] + earlier :][:4]
    stages = refs[-3 - chunk - 1 : -3]
    ready, in_sems, out_sems = refs[-3:]
    head_dim = ready.shape[-1] // 2
    used = sorted({(which, peer) for job in jobs for which, peer, _ in job[1:]})
    chunks_used = sorted({which for which, _ in used})
    heads_used = {
        c: sorted({head for job in jobs for which, _, head in job[1:] if which == c})
        for c in chunks_used
    }

    def fetch(which, item, slot=None):
        heads = heads_used[which]
        some = pl.ds(heads[0], heads[-1] - heads[0] + 1)
        source, peer = part_of(groups[which], me, item)
        slot = peer if slot is None else slot
        return pltpu.make_async_copy(
            source.at[some], stages[which].at[slot, some], in_sems.at[which, slot]
        )

    def send(job, i):
        tile = jobs[job][0]
        return pltpu.make_async_copy(
            ready.at[i, job],
            outs[i].at[:, pl.ds(tile * LANES, LANES)],
            out_sems.at[4 * job + i],
        )

    for item in range(peers):
        for which in chunks_used:
            fetch(which, item).start()
    waited = set()

    def wait_for(which, peer):
        if (which, peer) not in waited:
            fetch(which, 0, peer).wait()
            waited.add((which, peer))

    for job, (tile, left, right) in enumerate(jobs):
        for which, peer, _ in (left, right):
            wait_for(which, peer)
        sides = [stages[which][peer, head] for which, peer, head in (left, right)]
        for i, (kind, half) in enumerate(((1, 1), (1, 0), (0, 0), (0, 1))):
            ready[i, job] = join(sides[0][kind], sides[1][kind], head_dim, half)
            send(job, i).start()
    for which in chunks_used:
        for peer in range(peers):
            wait_for(which, peer)
    for job in range(len(jobs)):
        for i in range(4):
            send(job, i).wait()


def unpack(me, messages, starts, heads_here, earlier):
    chunk = len(messages) - 1
    peers = lax.axis_size("seq")
    _, _, rows, pair_dim = message_shape(messages[0])
    head_dim = pair_dim // 2
    columns = peers * heads_here * head_dim
    dtype = messages[0][0].dtype

    def place_of(head):
        peer, local_head = divmod(head, heads_here)
        which = max(c for c, start in enumerate(starts) if start <= local_head)
        return which, peer, local_head - starts[which]

    jobs = []
    for tile in range(columns // LANES):
        left, right = place_of(2 * tile), place_of(2 * tile + 1)
        if max(left[0], right[0]) == chunk:
            jobs.append((tile, left, right))
    if not jobs:
        return earlier
    flat = [x for group in messages for x in group]
    anywhere = pl.BlockSpec(memory_space=pltpu.HBM)
    return pl.pallas_call(
        functools.partial(
            unpack_kernel,
            chunk=chunk,
            peers=peers,
            counts=[len(group) for group in messages],
            earlier=len(earlier),
            jobs=jobs,
        ),
        in_specs=[pl.BlockSpec(memory_space=pltpu.SMEM)]
        + [pl.BlockSpec(memory_space=pl.ANY)] * len(flat)
        + [anywhere] * len(earlier),
        out_specs=[anywhere] * 4,
        out_shape=[pltpu.HBM((rows, columns), dtype)] * 4,
        input_output_aliases={1 + len(flat) + i: i for i in range(len(earlier))},
        scratch_shapes=[pltpu.VMEM((peers,) + message_shape(m), dtype) for m in messages]
        + [
            pltpu.VMEM((4, len(jobs), rows, LANES), dtype),
            pltpu.SemaphoreType.DMA((chunk + 1, peers)),
            pltpu.SemaphoreType.DMA((4 * len(jobs),)),
        ],
        compiler_params=pltpu.CompilerParams(vmem_limit_bytes=SMALL_VMEM),
        name="unpack",
    )(me, *flat, *[in_hbm(x) for x in earlier])


def unpack_items_kernel(me, *refs, items, peers, counts, joint, earlier, jobs, per_peer):
    ends = [sum(counts[: c + 1]) for c in range(len(counts))]
    groups = [refs[end - count : end] for end, count in zip(ends, counts)]
    outs = refs[ends[-1] + earlier :][:4]
    ready, out_sems = refs[-2:]
    head_dim = ready.shape[-1] // 2

    def peer_of(j):
        return me[0] ^ (peers - 1 - items[j])

    def side_of(which, j, head, kind):
        if joint[which]:
            return groups[which][0][peer_of(j), head, kind]
        return groups[which][j][head, kind]

    def send(j, job, i):
        first = pl.multiple_of(peer_of(j) * per_peer, LANES) + jobs[job][0] * LANES
        return pltpu.make_async_copy(
            ready.at[j, i, job], outs[i].at[:, pl.ds(first, LANES)], out_sems.at[j, i, job]
        )

    for j in range(len(items)):
        for job, (_, left, right) in enumerate(jobs):
            for i, (kind, half) in enumerate(((1, 1), (1, 0), (0, 0), (0, 1))):
                ready[j, i, job] = join(
                    side_of(left[0], j, left[1], kind),
                    side_of(right[0], j, right[1], kind),
                    head_dim,
                    half,
                )
                send(j, job, i).start()
    for j in range(len(items)):
        for job in range(len(jobs)):
            for i in range(4):
                send(j, job, i).wait()


def unpack_items(me, messages, starts, heads_here, items, earlier):
    chunk = len(messages) - 1
    peers = lax.axis_size("seq")
    _, _, rows, pair_dim = message_shape(messages[0])
    head_dim = pair_dim // 2
    per_peer = heads_here * head_dim
    dtype = messages[0][0].dtype

    def place_of(head):
        which = max(c for c, start in enumerate(starts) if start <= head)
        return which, head - starts[which]

    jobs = []
    for tile in range(per_peer // LANES):
        left, right = place_of(2 * tile), place_of(2 * tile + 1)
        if max(left[0], right[0]) == chunk:
            jobs.append((tile, left, right))
    groups = [
        list(group) if len(group) == 1 else [group[item] for item in items]
        for group in messages
    ]
    flat = [x for group in groups for x in group]
    anywhere = pl.BlockSpec(memory_space=pltpu.HBM)
    return pl.pallas_call(
        functools.partial(
            unpack_items_kernel,
            items=items,
            peers=peers,
            counts=[len(group) for group in groups],
            joint=[len(group) == 1 for group in messages],
            earlier=len(earlier),
            jobs=jobs,
            per_peer=per_peer,
        ),
        in_specs=[pl.BlockSpec(memory_space=pltpu.SMEM)]
        + [pl.BlockSpec(memory_space=pltpu.VMEM)] * len(flat)
        + [anywhere] * len(earlier),
        out_specs=[anywhere] * 4,
        out_shape=[pltpu.HBM((rows, peers * per_peer), dtype)] * 4,
        input_output_aliases={1 + len(flat) + i: i for i in range(len(earlier))},
        scratch_shapes=[
            pltpu.VMEM((len(items), 4, len(jobs), rows, LANES), dtype),
            pltpu.SemaphoreType.DMA((len(items), 4, len(jobs))),
        ],
        compiler_params=pltpu.CompilerParams(vmem_limit_bytes=SMALL_VMEM),
        name="unpack_items",
    )(me, *[in_vmem(x) for x in flat], *[in_hbm(x) for x in earlier])


def pick_kernel(me, asked, *refs, count):
    for_next, for_prev, table, sems = refs[-4:]
    heads, window, block_rows, _ = table.shape
    peers, each = sems.shape

    def fetch(item, i):
        source, peer = part_of(refs[:count], me, item)
        rows = pl.ds(i * block_rows, block_rows)
        return pltpu.make_async_copy(
            source.at[:, 0, rows], table.at[:, CROSS + peer * each + i], sems.at[item, i]
        )

    for item in range(peers):
        for i in range(each):
            fetch(item, i).start()
    for item in range(peers):
        for i in range(each):
            fetch(item, i).wait()
    for i in range(CROSS):
        for_next[i] = table[:, CROSS + asked[i]]
        for_prev[i] = table[:, CROSS + asked[CROSS + i]]


def pick(me, messages, asked, block_rows, after):
    heads, _, rows, lanes = message_shape(messages)
    dtype = messages[0].dtype
    peers = lax.axis_size("seq")
    each = rows // block_rows
    window = peers * each + 2 * CROSS
    picked = jax.ShapeDtypeStruct((CROSS, heads, block_rows, lanes), dtype)
    return pl.pallas_call(
        functools.partial(pick_kernel, count=len(messages)),
        in_specs=[pl.BlockSpec(memory_space=pltpu.SMEM)] * 2
        + [pl.BlockSpec(memory_space=pl.ANY)] * (len(messages) + len(after)),
        out_specs=[pl.BlockSpec(memory_space=pltpu.VMEM)] * 3,
        out_shape=[picked, picked, pltpu.VMEM((heads, window, block_rows, lanes), dtype)],
        scratch_shapes=[pltpu.SemaphoreType.DMA((peers, each))],
        compiler_params=pltpu.CompilerParams(vmem_limit_bytes=SMALL_VMEM),
        name="pick",
    )(me, asked, *messages, *[in_hbm(x) for x in after])


def prepare_kernel(me, table, *refs, peers):
    messages = refs[:-4]
    turned, pairs, sums, sems = refs[-4:]
    heads, window, _, _ = table.shape

    def fetch(item):
        source, peer = part_of(messages, me, item)
        return pltpu.make_async_copy(source.at[:, 1], pairs.at[peer], sems.at[item])

    for item in range(peers):
        fetch(item).start()
    for head in range(heads):

        def clear(i, carry):
            sums[head, i] = jnp.zeros(sums.shape[2:], sums.dtype)
            return carry

        def turn(i, carry):
            turned[head, i] = table[head, i].T
            return carry

        lax.fori_loop(0, window, clear, 0)
        lax.fori_loop(CROSS, window - CROSS, turn, 0)
    for item in range(peers):
        fetch(item).wait()


def prepare(me, messages, table):
    heads, _, rows, lanes = message_shape(messages)
    _, window, block_rows, _ = table.shape
    dtype = messages[0].dtype
    peers = lax.axis_size("seq")
    inside = pl.BlockSpec(memory_space=pltpu.VMEM)
    return pl.pallas_call(
        functools.partial(prepare_kernel, peers=peers),
        in_specs=[pl.BlockSpec(memory_space=pltpu.SMEM), inside]
        + [pl.BlockSpec(memory_space=pl.ANY)] * len(messages),
        out_specs=[inside] * 3,
        out_shape=[
            pltpu.VMEM((heads, window, lanes, block_rows), dtype),
            pltpu.VMEM((peers, heads, rows, lanes), dtype),
            pltpu.VMEM((heads, window, block_rows, lanes), jnp.float32),
        ],
        scratch_shapes=[pltpu.SemaphoreType.DMA((peers,))],
        compiler_params=pltpu.CompilerParams(vmem_limit_bytes=SMALL_VMEM),
        name="prepare",
    )(me, in_vmem(table), *messages)


def attend_kernel(
    lists,
    came_prev,
    came_next,
    pairs,
    table_in,
    turned_in,
    sums_in,
    back,
    to_prev,
    to_next,
    table,
    turned,
    sums,
    both_even,
    both_odd,
    low_even,
    low_odd,
    *,
    head_dim,
    per_list,
):
    del table_in, turned_in, sums_in
    peers, heads, rows, lanes = pairs.shape
    _, window, block_rows, _ = table.shape
    each = rows // block_rows
    blocks = peers * each
    units = heads * blocks
    keys = per_list * block_rows
    scaling = head_dim ** (-0.5)
    exponent = scaling * math.log2(math.e)
    both = (both_even, both_odd)
    low = (low_even, low_odd)
    step_rows = 64

    for head in range(heads):
        for i in range(CROSS):
            table[head, i] = came_prev[i, head]
            table[head, CROSS + blocks + i] = came_next[i, head]
            turned[head, i] = came_prev[i, head].T
            turned[head, CROSS + blocks + i] = came_next[i, head].T

    left = lax.broadcasted_iota(jnp.int32, (block_rows, lanes), 1) < head_dim

    def locate(unit):
        head = lax.div(unit, blocks)
        block = lax.rem(unit, blocks)
        ids = [lists[head, block, j] for j in range(per_list)]
        peer = lax.div(block, each)
        start = pl.multiple_of(lax.rem(block, each) * block_rows, block_rows)
        return head, ids, peer, pl.ds(start, block_rows)

    def apart_of(head, peer, here):
        query_grad = pairs[peer, head, here]
        nothing = jnp.zeros_like(query_grad)
        return jnp.concatenate(
            [jnp.where(left, query_grad, nothing), jnp.where(left, nothing, query_grad)],
            axis=0,
        )

    def score(unit, slot):
        head, ids, peer, here = locate(unit)
        key_value = jnp.concatenate([table[head, i] for i in ids], axis=0)
        both[slot][...] = lax.dot_general(
            key_value,
            apart_of(head, peer, here),
            (((1,), (1,)), ((), ())),
            preferred_element_type=jnp.float32,
        )

    def soften(slot):
        source, target = both[slot], low[slot]
        parts = [slice(i, i + step_rows) for i in range(0, keys, step_rows)]
        top = source[parts[0], :block_rows]
        for part in parts[1:]:
            top = jnp.maximum(top, source[part, :block_rows])
        top = jnp.max(top, axis=0, keepdims=True)
        total = jnp.zeros((step_rows, block_rows), jnp.float32)
        mixed = jnp.zeros((step_rows, block_rows), jnp.float32)
        for part in parts:
            raised = jnp.exp2((source[part, :block_rows] - top) * exponent)
            source[part, :block_rows] = raised
            total += raised
            mixed += raised * source[part, block_rows:]
        inverse = 1.0 / jnp.sum(total, axis=0, keepdims=True)
        correction = jnp.sum(mixed, axis=0, keepdims=True) * inverse
        for part in parts:
            weights = source[part, :block_rows] * inverse
            target[part, block_rows:] = weights.astype(jnp.bfloat16)
            target[part, :block_rows] = (
                weights * (source[part, block_rows:] - correction)
            ).astype(jnp.bfloat16)

    def combine(unit, slot):
        head, ids, peer, here = locate(unit)
        products = low[slot][...]
        terms = jnp.dot(
            products, apart_of(head, peer, here), preferred_element_type=jnp.float32
        )
        for j, i in enumerate(ids):
            sums[head, i] += terms[j * block_rows : (j + 1) * block_rows]
        key_value = jnp.concatenate([turned[head, i] for i in ids], axis=1)
        out = jnp.dot(key_value, products, preferred_element_type=jnp.float32)
        out = jnp.concatenate(
            [out[:head_dim, :block_rows] * scaling, out[head_dim:, block_rows:]], axis=0
        )
        back[peer, head, here] = out.T.astype(back.dtype)

    score(0, 0)
    score(1, 1)
    soften(0)

    def step(i, carry):
        for slot in range(2):
            unit = 2 * i + slot
            combine(unit - 2, slot)
            score(unit, slot)
            soften(1 - slot)
        return carry

    lax.fori_loop(1, units // 2, step, 0)
    combine(units - 2, 0)
    soften(1)
    combine(units - 1, 1)

    factor = jnp.where(left, scaling, 1.0)
    for head in range(heads):
        for i in range(CROSS):
            to_prev[i, head] = (sums[head, i] * factor).astype(to_prev.dtype)
            to_next[i, head] = (sums[head, CROSS + blocks + i] * factor).astype(to_next.dtype)


def attend(lists, came_prev, came_next, pairs, table, turned, sums):
    _, _, block_rows, lanes = came_prev.shape
    dtype = pairs.dtype
    per_list = lists.shape[-1]
    keys = per_list * block_rows
    inside = pl.BlockSpec(memory_space=pltpu.VMEM)
    cross_shape = jax.ShapeDtypeStruct(came_prev.shape, dtype)
    kept = (table, turned, sums)
    return pl.pallas_call(
        functools.partial(attend_kernel, head_dim=lanes // 2, per_list=per_list),
        in_specs=[pl.BlockSpec(memory_space=pltpu.SMEM)] + [inside] * 6,
        out_specs=[inside] * 6,
        out_shape=[pltpu.VMEM(pairs.shape, dtype), cross_shape, cross_shape]
        + [pltpu.VMEM(x.shape, x.dtype) for x in kept],
        input_output_aliases={4: 3, 5: 4, 6: 5},
        scratch_shapes=[
            pltpu.VMEM((keys, 2 * block_rows), jnp.float32),
            pltpu.VMEM((keys, 2 * block_rows), jnp.float32),
            pltpu.VMEM((keys, 2 * block_rows), dtype),
            pltpu.VMEM((keys, 2 * block_rows), dtype),
        ],
        compiler_params=pltpu.CompilerParams(vmem_limit_bytes=SMALL_VMEM),
        name="attend",
    )(lists, came_prev, came_next, *[in_vmem(x) for x in (pairs, *kept)])


def finish_kernel(me, asked, back, kept, later, earlier, *refs, block_rows):
    messages = refs[:-3]
    sums, ready, sems = refs[-3:]
    peers, heads, _, rows, lanes = ready.shape
    each = rows // block_rows
    blocks = peers * each
    head_dim = lanes // 2
    left = lax.broadcasted_iota(jnp.int32, (block_rows, lanes), 1) < head_dim
    factor = jnp.where(left, head_dim ** (-0.5), 1.0)

    def send(item, head):
        target, peer = part_of(messages, me, item)
        return pltpu.make_async_copy(
            ready.at[peer, head], target.at[head], sems.at[item, head]
        )

    for head in range(heads):
        sums[...] = kept[head, CROSS : CROSS + blocks] * factor
        for i in range(CROSS):
            sums[asked[i]] += later[i, head].astype(jnp.float32)
        for i in range(CROSS):
            sums[asked[CROSS + i]] += earlier[i, head].astype(jnp.float32)
        for peer in range(peers):
            ready[peer, head, 1] = back[peer, head]
            for i in range(each):
                ready[peer, head, 0, i * block_rows : (i + 1) * block_rows] = sums[
                    peer * each + i
                ].astype(ready.dtype)
        for item in range(peers):
            send(item, head).start()
    for head in range(heads):
        for item in range(peers):
            send(item, head).wait()


def finish(me, back, kept, later, earlier, asked, apart):
    peers, heads, rows, lanes = back.shape
    _, window, block_rows, _ = kept.shape
    blocks = window - 2 * CROSS
    inside = pl.BlockSpec(memory_space=pltpu.VMEM)
    scalars = pl.BlockSpec(memory_space=pltpu.SMEM)
    shape = (heads, 2, rows, lanes)
    outs = message_outs(peers, shape, back.dtype, apart)
    return pl.pallas_call(
        functools.partial(finish_kernel, block_rows=block_rows),
        in_specs=[scalars, scalars] + [inside] * 4,
        out_specs=[pl.BlockSpec(memory_space=pltpu.HBM)] * len(outs),
        out_shape=outs,
        scratch_shapes=[
            pltpu.VMEM((blocks, block_rows, lanes), jnp.float32),
            pltpu.VMEM((peers,) + shape, back.dtype),
            pltpu.SemaphoreType.DMA((peers, heads)),
        ],
        compiler_params=pltpu.CompilerParams(vmem_limit_bytes=SMALL_VMEM),
        name="finish",
    )(
        me,
        asked,
        in_vmem(back),
        in_vmem(kept),
        later,
        earlier,
    )


def local(query, key, value, d_out, pattern):
    heads_here, blocks, _ = pattern.shape
    peers = lax.axis_size("seq")
    rows, columns = query.shape
    head_dim = columns // (peers * heads_here)
    block_rows = rows * peers // blocks
    chunks = min(CHUNKS, heads_here)
    starts = [-(-heads_here * i // chunks) for i in range(chunks)]
    sizes = [end - start for start, end in zip(starts, starts[1:] + [heads_here])]
    arrays = (query, key, value, d_out)

    own_base = lax.axis_index("slab") * blocks
    block_ids = jnp.arange(blocks, dtype=jnp.int32)
    flat_lists = pattern.reshape(-1)
    reverse_rank = blocks - 1 - block_ids
    hits_prev = jnp.any(flat_lists[:, None] == (own_base - blocks + block_ids)[None, :], axis=0)
    hits_next = jnp.any(flat_lists[:, None] == (own_base + blocks + block_ids)[None, :], axis=0)
    need_prev = lax.top_k(hits_prev.astype(jnp.int32) * blocks + reverse_rank, CROSS)[1]
    need_next = lax.top_k(hits_next.astype(jnp.int32) * blocks + reverse_rank, CROSS)[1]
    asked_next = from_behind(need_prev, "slab", -1)
    asked_prev = from_behind(need_next, "slab", 1)
    asked = jnp.concatenate([asked_next, asked_prev])
    rank_ids = jnp.arange(CROSS, dtype=jnp.int32)
    prev_global = own_base - blocks + need_prev
    next_global = own_base + blocks + need_next
    pos_prev = jnp.sum(jnp.where(pattern[..., None] == prev_global, rank_ids, 0), axis=-1)
    pos_next = jnp.sum(jnp.where(pattern[..., None] == next_global, rank_ids, 0), axis=-1)
    in_own = (pattern >= own_base) & (pattern < own_base + blocks)
    local_ids = jnp.where(
        in_own,
        CROSS + pattern - own_base,
        jnp.where(pattern < own_base, pos_prev, CROSS + blocks + pos_next),
    )

    me = lax.axis_index("seq").astype(jnp.int32).reshape(1)
    last = chunks - 1
    came = []
    for chunk, (start, size) in enumerate(zip(starts, sizes)):
        after = (asked, local_ids) if came else ()
        packed = pack(arrays, start, size, heads_here, peers, head_dim, after)
        came.append(exchange(packed))
    received = []
    outs = finished = ()
    for chunk, (messages, start, size) in enumerate(zip(came, starts, sizes)):
        for_next, for_prev, table = pick(me, messages, asked, block_rows, finished[:1])
        came_prev = from_behind(for_next, "slab", 1)
        came_next = from_behind(for_prev, "slab", -1)
        turned, pairs, sums = prepare(me, messages, table)
        lists = local_ids[start : start + size]
        back, to_prev, to_next, _, _, kept = attend(
            lists, came_prev, came_next, pairs, table, turned, sums
        )
        later = from_behind(to_prev, "slab", -1)
        earlier = from_behind(to_next, "slab", 1)
        finished = finish(me, back, kept, later, earlier, asked, chunk == last)
        received.append(exchange(finished))
        if chunk == last and heads_here * head_dim % LANES == 0:
            half = peers // 2
            near = list(range(peers - 2, half - 1, -1))
            parts = (
                [peers - 1, near[0]],
                list(range(half // 2)),
                list(range(half // 2, half - 1)),
                [half - 1, *near[1:]],
            )
            for items in parts:
                outs = unpack_items(me, received, starts, heads_here, items, outs)
        else:
            outs = unpack(me, received, starts, heads_here, outs)
    return tuple(outs)


def solution(mesh):
    tokens = P(("slab", "seq"), None)
    return jax.shard_map(
        local,
        mesh=mesh,
        in_specs=(tokens, tokens, tokens, tokens, P("seq", "slab", None)),
        out_specs=(tokens, tokens, tokens, tokens),
        check_vma=False,
    )
```
